32 devices in a mesh: role: 2 (over core), dp: 4 (over z), mp: 4 (over y, x).
Axes of the slice: x: 2, y: 2, z: 4, core: 2. Of those that a mesh axis runs over, the one named last changes fastest.
Arguments:
- pixels: bfloat16 [32, 196, 768], P('dp', None, 'mp'), may hold values from -6 to 6
- context_slots: int32 [32, 160], P('dp'), may hold values from 0 to 195, as said below
- context_count: int32 [32], P('dp'), may hold values from 40 to 160
- target_slots: int32 [32, 4, 64], P('dp'), may hold values from 0 to 195, as said below
- target_count: int32 [32, 4], P('dp'), may hold values from 16 to 64
- encoder_in: float32 [768, 5376], P(('role', 'dp'), 'mp'), may hold values from -0.21875 to 0.21875
- encoder_out: float32 [4608, 768], P('mp', ('role', 'dp')), may hold values from -0.21875 to 0.21875
- predictor_in: float32 [384, 3456], P(('role', 'dp'), 'mp'), may hold values from -0.3125 to 0.3125
- predictor_out: float32 [2688, 384], P('mp', ('role', 'dp')), may hold values from -0.3125 to 0.3125
- vectors: float32 [3072], P(('role', 'dp', 'mp')), may hold values from 0.5 to 1.5
- first_encoder_in: float32 [768, 5376], P(('role', 'dp'), 'mp'), may hold values from -1.9073486e-05 to 1.9073486e-05
- first_encoder_out: float32 [4608, 768], P('mp', ('role', 'dp')), may hold values from -1.9073486e-05 to 1.9073486e-05
- first_predictor_in: float32 [384, 3456], P(('role', 'dp'), 'mp'), may hold values from -1.9073486e-05 to 1.9073486e-05
- first_predictor_out: float32 [2688, 384], P('mp', ('role', 'dp')), may hold values from -1.9073486e-05 to 1.9073486e-05
- first_vectors: float32 [3072], P(('role', 'dp', 'mp')), may hold values from -6.1035156e-05 to 6.1035156e-05
- second_encoder_in: float32 [768, 5376], P(('role', 'dp'), 'mp'), may hold values from 9.97001e-13 to 3.988004e-12
- second_encoder_out: float32 [4608, 768], P('mp', ('role', 'dp')), may hold values from 9.97001e-13 to 3.988004e-12
- second_predictor_in: float32 [384, 3456], P(('role', 'dp'), 'mp'), may hold values from 9.97001e-13 to 3.988004e-12
- second_predictor_out: float32 [2688, 384], P('mp', ('role', 'dp')), may hold values from 9.97001e-13 to 3.988004e-12
- second_vectors: float32 [3072], P(('role', 'dp', 'mp')), may hold values from 8.973009e-12 to 3.5892036e-11
- target_encoder_in: float32 [768, 5376], P(('role', 'dp'), 'mp'), may hold values from -0.21875 to 0.21875
- target_encoder_out: float32 [4608, 768], P('mp', ('role', 'dp')), may hold values from -0.21875 to 0.21875
- target_vectors: float32 [3072], P(('role', 'dp', 'mp')), may hold values from 0.5 to 1.5
Outputs:
- new_encoder_in: float32 [768, 5376], P(('role', 'dp'), 'mp')
- new_encoder_out: float32 [4608, 768], P('mp', ('role', 'dp'))
- new_predictor_in: float32 [384, 3456], P(('role', 'dp'), 'mp')
- new_predictor_out: float32 [2688, 384], P('mp', ('role', 'dp'))
- new_vectors: float32 [3072], P(('role', 'dp', 'mp'))
- new_first_encoder_in: float32 [768, 5376], P(('role', 'dp'), 'mp')
- new_first_encoder_out: float32 [4608, 768], P('mp', ('role', 'dp'))
- new_first_predictor_in: float32 [384, 3456], P(('role', 'dp'), 'mp')
- new_first_predictor_out: float32 [2688, 384], P('mp', ('role', 'dp'))
- new_first_vectors: float32 [3072], P(('role', 'dp', 'mp'))
- new_second_encoder_in: float32 [768, 5376], P(('role', 'dp'), 'mp')
- new_second_encoder_out: float32 [4608, 768], P('mp', ('role', 'dp'))
- new_second_predictor_in: float32 [384, 3456], P(('role', 'dp'), 'mp')
- new_second_predictor_out: float32 [2688, 384], P('mp', ('role', 'dp'))
- new_second_vectors: float32 [3072], P(('role', 'dp', 'mp'))
- new_target_encoder_in: float32 [768, 5376], P(('role', 'dp'), 'mp')
- new_target_encoder_out: float32 [4608, 768], P('mp', ('role', 'dp'))
- new_target_vectors: float32 [3072], P(('role', 'dp', 'mp'))
- loss_total: float32 [], replicated
- target_total: float32 [], replicated
- grad_norm: float32 [], replicated
The draws below stay inside these ranges and needn't reach their ends.
Inputs may be any that keep to these rules, and one draw needn't show every extreme that they name: `context_slots`: each row holds distinct patch numbers; an image's context is its first context_count entries. `target_slots`: each block's row holds distinct patch numbers; a block is its first target_count entries.
All inputs are finite; a program needn't handle non-finite values.
Results may differ from the reference program's by a relative error of at most 0.0024.
The reference program's roundings to bfloat16 on the way count: a program that leaves them out, or rounds other values in their place, can miss the bound.
Values may be sent and summed in bfloat16 or wider, within the bound.
A program may use at most 320 MiB of HBM per device.

```python
import math
import jax
import jax.numpy as jnp
from jax import lax

D = 768
HEADS = 12
FF = 3072
PD = 384
PF = 1536
PIX = 768
GRID = 14
CTX = 160
CTX_MIN = 40
TGT = 64
BLOCKS = 4
STEP = 10
IMG_DEV = 8
NP = 196
IMGS = 32
VEC = 3072
NPARAM = 10030080
N_DP = 4
N_MP = 4


def draw_context_slots(key, part):
    keys = jax.random.split(key, IMGS)
    picks = jax.vmap(lambda single: jax.random.permutation(single, NP)[:CTX])(keys)
    return picks.astype(jnp.int32)


def draw_context_count(key, part):
    counts = jax.random.randint(key, (IMGS,), CTX_MIN, CTX + 1)
    return counts.at[0].set(CTX).at[IMGS - 1].set(CTX_MIN).astype(jnp.int32)


def draw_target_slots(key, part):
    keys = jax.random.split(key, IMGS * BLOCKS)
    picks = jax.vmap(lambda single: jax.random.permutation(single, NP)[:TGT])(keys)
    return picks.reshape(IMGS, BLOCKS, TGT).astype(jnp.int32)


def draw_target_count(key, part):
    lowest = TGT // 4 + (TGT - TGT // 4) * jnp.arange(IMGS) // IMGS
    counts = jax.random.randint(key, (IMGS, BLOCKS), lowest[:, None], TGT + 1)
    return counts.at[0, 0].set(TGT).astype(jnp.int32)


def level_of(own_key, shape, shards, low, top_value):
    level, own = 1.0, jax.random.fold_in(own_key, 6)
    for position, shards_of in shards:
        heights = jnp.exp(jax.random.uniform(jax.random.fold_in(own, position), (shards_of,), jnp.float32, low / len(shards), top_value / len(shards)))
        level = level * jnp.repeat(heights, shape[position] // shards_of).reshape([-1 if axis == position else 1 for axis in range(len(shape))])
    return level


def scatter_about(own_key, shape, scale, most, pieces=(), dtype=jnp.bfloat16):
    array = scale * jax.random.normal(own_key, shape, jnp.float32)
    if pieces:
        array = array * level_of(own_key, shape, pieces, -0.22, 0.18)
    return jnp.clip(array, -most, most).astype(dtype)


def setup_inputs(seed: int = 0) -> dict:
    streams_of = jax.random.split(jax.random.key(seed), 24)
    return {
        "pixels": scatter_about(streams_of[0], (IMGS, NP, PIX), 1.0, 6.0, ((0, 4), (2, 4))),
        "context_slots": draw_context_slots(jax.random.fold_in(streams_of[23], 71), 0),
        "context_count": draw_context_count(jax.random.fold_in(streams_of[23], 71), 0),
        "target_slots": draw_target_slots(jax.random.fold_in(streams_of[23], 71), 0),
        "target_count": draw_target_count(jax.random.fold_in(streams_of[23], 71), 0),
        "encoder_in": scatter_about(streams_of[5], (D, 3 * D + FF), D ** -0.5, 0.21875, ((0, 8), (1, 4)), jnp.float32),
        "encoder_out": scatter_about(streams_of[6], (PIX + D + FF, D), D ** -0.5, 0.21875, ((0, 4), (1, 8)), jnp.float32),
        "predictor_in": scatter_about(streams_of[7], (PD, 3 * PD + PF + D), PD ** -0.5, 0.3125, ((0, 8), (1, 4)), jnp.float32),
        "predictor_out": scatter_about(streams_of[8], (D + PD + PF, PD), PD ** -0.5, 0.3125, ((0, 4), (1, 8)), jnp.float32),
        "vectors": jnp.clip(1.0 + 0.1 * jax.random.normal(streams_of[9], (VEC,), jnp.float32), 0.5, 1.5),
        "first_encoder_in": scatter_about(streams_of[10], (D, 3 * D + FF), (0.011 * NPARAM ** -0.5), 1.9073486328125e-05, ((0, 8), (1, 4)), jnp.float32),
        "first_encoder_out": scatter_about(streams_of[11], (PIX + D + FF, D), (0.011 * NPARAM ** -0.5), 1.9073486328125e-05, ((0, 4), (1, 8)), jnp.float32),
        "first_predictor_in": scatter_about(streams_of[12], (PD, 3 * PD + PF + D), (0.011 * NPARAM ** -0.5), 1.9073486328125e-05, ((0, 8), (1, 4)), jnp.float32),
        "first_predictor_out": scatter_about(streams_of[13], (D + PD + PF, PD), (0.011 * NPARAM ** -0.5), 1.9073486328125e-05, ((0, 4), (1, 8)), jnp.float32),
        "first_vectors": scatter_about(streams_of[14], (VEC,), (0.033 * NPARAM ** -0.5), 6.103515625e-05, ((0, 32),), jnp.float32),
        "second_encoder_in": jnp.clip(jnp.exp(math.log(3.98800393749954e-12) - 1.3862944 * jax.random.uniform(streams_of[15], (D, 3 * D + FF), jnp.float32) ** level_of(streams_of[15], (D, 3 * D + FF), ((0, 8), (1, 4)), -0.2, 0.2)), 9.97000984374885e-13, 3.98800393749954e-12),
        "second_encoder_out": jnp.clip(jnp.exp(math.log(3.98800393749954e-12) - 1.3862944 * jax.random.uniform(streams_of[16], (PIX + D + FF, D), jnp.float32) ** level_of(streams_of[16], (PIX + D + FF, D), ((0, 4), (1, 8)), -0.2, 0.2)), 9.97000984374885e-13, 3.98800393749954e-12),
        "second_predictor_in": jnp.clip(jnp.exp(math.log(3.98800393749954e-12) - 1.3862944 * jax.random.uniform(streams_of[17], (PD, 3 * PD + PF + D), jnp.float32) ** level_of(streams_of[17], (PD, 3 * PD + PF + D), ((0, 8), (1, 4)), -0.2, 0.2)), 9.97000984374885e-13, 3.98800393749954e-12),
        "second_predictor_out": jnp.clip(jnp.exp(math.log(3.98800393749954e-12) - 1.3862944 * jax.random.uniform(streams_of[18], (D + PD + PF, PD), jnp.float32) ** level_of(streams_of[18], (D + PD + PF, PD), ((0, 4), (1, 8)), -0.2, 0.2)), 9.97000984374885e-13, 3.98800393749954e-12),
        "second_vectors": jnp.clip(jnp.exp(math.log(3.589203587117673e-11) - 1.3862944 * jax.random.uniform(streams_of[19], (VEC,), jnp.float32) ** level_of(streams_of[19], (VEC,), ((0, 32),), -0.2, 0.2)), 8.973008967794183e-12, 3.589203587117673e-11),
        "target_encoder_in": scatter_about(streams_of[20], (D, 3 * D + FF), D ** -0.5, 0.21875, ((0, 8), (1, 4)), jnp.float32),
        "target_encoder_out": scatter_about(streams_of[21], (PIX + D + FF, D), D ** -0.5, 0.21875, ((0, 4), (1, 8)), jnp.float32),
        "target_vectors": jnp.clip(1.0 + 0.1 * jax.random.normal(streams_of[22], (VEC,), jnp.float32), 0.5, 1.5),
    }


@jax.custom_vjp
def low(v):
    return lax.optimization_barrier(v.astype(jnp.bfloat16)).astype(jnp.float32)

@jax.custom_vjp
def low_back(v):
    return v

def low_keep(v):
    return (low(v), None)

def low_pass(kept, grad):
    return (grad,)

def back_keep(v):
    return (v, None)

def back_low(kept, grad):
    return (low(grad),)
low.defvjp(low_keep, low_pass)
low_back.defvjp(back_keep, back_low)
HIGH = lax.Precision.HIGHEST
BETA_ONE = 0.9
BETA_TWO = 0.999
ADAM_EPS = 1e-08
RATE_MATRIX = 0.03
RATE_VECTOR = 0.3
DECAY = 0.05
MOMENTUM_EMA = 0.9
CLIP = 0.1

def product(left, right):
    return jnp.dot(left, right, precision=HIGH, preferred_element_type=jnp.float32)

def layer_norm(stream, gain):
    mean = lax.optimization_barrier(jnp.mean(stream, -1, keepdims=True))
    cent = stream - mean
    return cent * lax.rsqrt(lax.optimization_barrier(jnp.mean(cent * cent, -1, keepdims=True)) + 1e-06) * gain

def sincos(width):
    quarter = width // 4
    omega = 1.0 / 10000.0 ** (jnp.arange(quarter).astype(jnp.float32) / quarter)
    place = jnp.arange(GRID * GRID)
    rows = (place // GRID).astype(jnp.float32)[:, None] * omega[None, :]
    cols = (place % GRID).astype(jnp.float32)[:, None] * omega[None, :]
    return jnp.concatenate([jnp.sin(rows), jnp.cos(rows), jnp.sin(cols), jnp.cos(cols)], -1)

def encoder_parts(w_in, w_out):
    local, hidden, pixel = (D // N_MP, FF // N_MP, PIX // N_MP)
    cols = w_in.reshape(D, N_MP, 3 * local + hidden)
    rows = w_out.reshape(N_MP, pixel + local + hidden, D)

    def col(start, stop):
        return cols[:, :, start:stop].reshape(D, -1)

    def row(start, stop):
        return rows[:, start:stop].reshape(-1, D)
    weights = (col(0, local), col(local, 2 * local), col(2 * local, 3 * local), row(pixel, pixel + local), col(3 * local, 3 * local + hidden), row(pixel + local, pixel + local + hidden))
    return (weights, row(0, pixel))

def predictor_parts(p_in, p_out):
    local, hidden, enc_local = (PD // N_MP, PF // N_MP, D // N_MP)
    cols = p_in.reshape(PD, N_MP, 3 * local + hidden + enc_local)
    rows = p_out.reshape(N_MP, enc_local + local + hidden, PD)

    def col(start, stop):
        return cols[:, :, start:stop].reshape(PD, -1)

    def row(start, stop):
        return rows[:, start:stop].reshape(-1, PD)
    weights = (col(0, local), col(local, 2 * local), col(2 * local, 3 * local), row(enc_local, enc_local + local), col(3 * local, 3 * local + hidden), row(enc_local + local, enc_local + local + hidden))
    return (weights, col(3 * local + hidden, 3 * local + hidden + enc_local), row(0, enc_local))

def block(stream, keep, weights, first, second):
    w_query, w_key, w_value, w_out, w_up, w_down = weights
    batch, length, width = stream.shape
    size = width // HEADS
    mixer_in = low(layer_norm(stream, first))

    def heads(weight):
        return low_back(low(product(mixer_in, weight))).reshape(batch, length, HEADS, size)
    queries, keyset, values = (heads(w_query), heads(w_key), heads(w_value))
    score = jnp.einsum('blhd,bmhd->bhlm', queries, keyset, precision=HIGH) * size ** (-0.5) + (keep[:, None, None, :] - 1.0) * 1000000000.0
    probs = low(jax.nn.softmax(low_back(score), -1))
    mixed = low_back(low(jnp.einsum('bhlm,bmhd->blhd', probs, values, precision=HIGH))).reshape(batch, length, width)
    middle = stream + low_back(product(mixed, w_out))
    dense_in = low(layer_norm(middle, second))
    hidden = low_back(product(dense_in, w_up))
    active = low(jax.nn.gelu(hidden, approximate=False))
    return middle + low_back(product(active, w_down))

def encode(pix, keep, weights, embed, first, second):
    start = low_back(product(pix, embed)) + sincos(D)
    return block(start, keep, weights, first, second)

def teacher(ema_in, ema_out, ema_vec, pix, tslots):
    weights, embed = encoder_parts(ema_in, ema_out)
    latent = encode(pix, jnp.ones(pix.shape[:2], jnp.float32), weights, embed, ema_vec[:D], ema_vec[D:2 * D])
    normed = low(layer_norm(latent, 1.0))
    count = pix.shape[0]
    return normed[jnp.arange(count)[:, None, None], tslots]

def student(banks, pix, slots, counts, tslots, tcounts, target, total):
    w_in, w_out, p_in, p_out, vec = banks
    weights, embed = encoder_parts(w_in, w_out)
    pweights, head, proj_in = predictor_parts(p_in, p_out)
    count = pix.shape[0]
    ctx_keep = (jnp.arange(CTX)[None, :] < counts[:, None]).astype(jnp.float32)
    hits = (slots[:, :, None] == jnp.arange(NP)[None, None, :]).astype(jnp.float32)
    keep = lax.optimization_barrier(jnp.sum(hits * ctx_keep[:, :, None], 1))
    latent = encode(pix, keep, weights, embed, vec[:D], vec[D:2 * D])
    context = low(latent[jnp.arange(count)[:, None], slots])
    table = sincos(PD)
    entry = low_back(product(context, proj_in)) + table[slots]
    queries = vec[2 * D + 3 * PD:] + table[tslots]
    seq = jnp.concatenate([jnp.broadcast_to(entry[:, None], (count, BLOCKS, CTX, PD)), queries], 2).reshape(count * BLOCKS, CTX + TGT, PD)
    tkeep = (jnp.arange(TGT)[None, None, :] < tcounts[:, :, None]).astype(jnp.float32)
    keys = jnp.concatenate([jnp.broadcast_to(ctx_keep[:, None], (count, BLOCKS, CTX)), tkeep], 2).reshape(count * BLOCKS, CTX + TGT)
    out = block(seq, keys, pweights, vec[2 * D:2 * D + PD], vec[2 * D + PD:2 * D + 2 * PD])
    normed = low(layer_norm(out[:, CTX:], vec[2 * D + 2 * PD:2 * D + 3 * PD]))
    pred = low_back(product(normed, head)).reshape(count, BLOCKS, TGT, D)
    diff = pred - target
    squares = jnp.sum(tkeep[..., None] * diff * diff)
    return (squares / total, squares)

def adamw(weight, grad, first, second, scale, rate, decay):
    grad = grad * scale
    first = BETA_ONE * first + (1.0 - BETA_ONE) * grad
    second = BETA_TWO * second + (1.0 - BETA_TWO) * grad * grad
    mean_hat = first / (1.0 - BETA_ONE ** STEP)
    square_hat = second / (1.0 - BETA_TWO ** STEP)
    return (weight - rate * (mean_hat / (jnp.sqrt(square_hat) + ADAM_EPS) + decay * weight), first, second)

def reference(pixels, context_slots, context_count, target_slots, target_count, encoder_in, encoder_out, predictor_in, predictor_out, vectors, first_encoder_in, first_encoder_out, first_predictor_in, first_predictor_out, first_vectors, second_encoder_in, second_encoder_out, second_predictor_in, second_predictor_out, second_vectors, target_encoder_in, target_encoder_out, target_vectors):

    def working(weight):
        return weight.astype(jnp.bfloat16).astype(jnp.float32)
    masters = (encoder_in, encoder_out, predictor_in, predictor_out, vectors)
    banks = tuple((working(w) for w in masters))
    ema_banks = (working(target_encoder_in), working(target_encoder_out), working(target_vectors))
    total = jnp.sum(target_count).astype(jnp.float32)
    pix = pixels.astype(jnp.float32)

    def group(carry, index):
        start = (index * IMG_DEV).astype(jnp.int32)

        def take(arr):
            return lax.dynamic_slice_in_dim(arr, start, IMG_DEV, 0)
        part_pix, slots, counts, tslots, tcounts = (take(pix), take(context_slots), take(context_count), take(target_slots), take(target_count))
        target = teacher(ema_banks[0], ema_banks[1], ema_banks[2], part_pix, tslots)

        def loss_fn(*weights):
            return student(weights, part_pix, slots, counts, tslots, tcounts, target, total)
        scaled, pullback, squares = jax.vjp(loss_fn, *banks, has_aux=True)
        grads = pullback(jnp.ones_like(scaled))
        return ((tuple((a + g for a, g in zip(carry[0], grads))), carry[1] + squares), None)
    init = (tuple((jnp.zeros_like(b) for b in banks)), jnp.zeros((), jnp.float32))
    (grads, loss_total), _ = lax.scan(group, init, jnp.arange(N_DP))
    norm = jnp.sqrt(sum((jnp.sum(g * g) for g in grads)))
    scale = jnp.minimum(1.0, CLIP / (norm + 1e-06))
    firsts = (first_encoder_in, first_encoder_out, first_predictor_in, first_predictor_out, first_vectors)
    seconds = (second_encoder_in, second_encoder_out, second_predictor_in, second_predictor_out, second_vectors)
    results = []
    for index in range(5):
        rate = RATE_VECTOR if index == 4 else RATE_MATRIX
        decay = 0.0 if index == 4 else DECAY
        results.append(adamw(masters[index], grads[index], firsts[index], seconds[index], scale, rate, decay))
    new_w = [r[0] for r in results]
    new_m = [r[1] for r in results]
    new_v = [r[2] for r in results]
    ema_in = MOMENTUM_EMA * target_encoder_in + (1.0 - MOMENTUM_EMA) * new_w[0]
    ema_out = MOMENTUM_EMA * target_encoder_out + (1.0 - MOMENTUM_EMA) * new_w[1]
    ema_vec = MOMENTUM_EMA * target_vectors + (1.0 - MOMENTUM_EMA) * new_w[4]
    return (new_w[0], new_w[1], new_w[2], new_w[3], new_w[4], new_m[0], new_m[1], new_m[2], new_m[3], new_m[4], new_v[0], new_v[1], new_v[2], new_v[3], new_v[4], ema_in, ema_out, ema_vec, loss_total, total, norm)
```

```python
import jax
import jax.numpy as jnp
import numpy as np
from jax import lax
from jax.sharding import PartitionSpec as P

HEADS = 12
GRID = 14
STEP = 10

BETA_ONE = 0.9
BETA_TWO = 0.999
ADAM_EPS = 1e-08
RATE_MATRIX = 0.03
RATE_VECTOR = 0.3
DECAY = 0.05
MOMENTUM_EMA = 0.9
CLIP = 0.1
ROOT_HALF = 0.7071067811865476
INVERSE_ROOT = 0.3989422804014327

BF = jnp.bfloat16
F32 = jnp.float32
EVERY = ("mp", "role", "dp")


def dots(spec, left, right):
    return jnp.einsum(spec, left, right, preferred_element_type=F32)


def sincos(width):
    quarter = width // 4
    omega = 1.0 / 10000.0 ** (np.arange(quarter, dtype=np.float64) / quarter)
    place = np.arange(GRID * GRID)
    rows = (place // GRID)[:, None] * omega[None, :]
    cols = (place % GRID)[:, None] * omega[None, :]
    return np.concatenate([np.sin(rows), np.cos(rows), np.sin(cols), np.cos(cols)], -1).astype(
        np.float32
    )


def pick(table, places):
    hot = (places[:, None] == jnp.arange(table.shape[0])[None, :]).astype(F32)
    return jnp.dot(hot, table, precision=lax.Precision.HIGHEST, preferred_element_type=F32)


def layer_stats(stream):
    mean = jnp.mean(stream, -1, keepdims=True)
    cent = stream - mean
    scale = lax.rsqrt(jnp.mean(cent * cent, -1, keepdims=True) + 1e-06)
    return (cent * scale, scale)


def norm_back(normed, scale, gain, grad):
    gain_grad = jnp.sum(grad * normed, 0)
    scaled = grad * gain
    inner = (
        scaled
        - jnp.mean(scaled, -1, keepdims=True)
        - normed * jnp.mean(scaled * normed, -1, keepdims=True)
    )
    return (scale * inner, gain_grad)


def gelu(hidden):
    return 0.5 * hidden * (1.0 + lax.erf(hidden * ROOT_HALF))


def gelu_slope(hidden):
    return (
        0.5 * (1.0 + lax.erf(hidden * ROOT_HALF))
        + hidden * jnp.exp(-0.5 * hidden * hidden) * INVERSE_ROOT
    )


def pack_encoder(w_in, w_out, local, pixel):
    turned = w_out.T
    return jnp.concatenate(
        [
            w_in[:, : 3 * local],
            turned[:, pixel : pixel + local],
            w_in[:, 3 * local :],
            turned[:, pixel + local :],
            turned[:, :pixel],
        ],
        1,
    )


def unpack_encoder(packed, local, hidden, pixel):
    up = 4 * local
    down = up + hidden
    emb = down + hidden
    w_in = jnp.concatenate([packed[:, : 3 * local], packed[:, up:down]], 1)
    turned = jnp.concatenate(
        [packed[:, emb:], packed[:, 3 * local : up], packed[:, down:emb]], 1
    )
    return (w_in, turned.T)


def pack_predictor(p_in, p_out, local, plocal, phidden):
    turned = p_out.T
    return jnp.concatenate(
        [
            p_in[:, : 3 * plocal],
            turned[:, local : local + plocal],
            p_in[:, 3 * plocal : 3 * plocal + phidden],
            turned[:, local + plocal :],
            p_in[:, 3 * plocal + phidden :],
            turned[:, :local],
        ],
        1,
    )


def unpack_predictor(packed, local, plocal, phidden):
    up = 4 * plocal
    down = up + phidden
    head = down + phidden
    entry = head + local
    p_in = jnp.concatenate(
        [packed[:, : 3 * plocal], packed[:, up:down], packed[:, head:entry]], 1
    )
    turned = jnp.concatenate(
        [packed[:, entry:], packed[:, 3 * plocal : up], packed[:, down:head]], 1
    )
    return (p_in, turned.T)


def adamw(weight, grad, first, second, scale, rate, decay):
    grad = grad * scale
    first = BETA_ONE * first + (1.0 - BETA_ONE) * grad
    second = BETA_TWO * second + (1.0 - BETA_TWO) * grad * grad
    mean_hat = first / (1.0 - BETA_ONE**STEP)
    square_hat = second / (1.0 - BETA_TWO**STEP)
    return (
        weight - rate * (mean_hat / (jnp.sqrt(square_hat) + ADAM_EPS) + decay * weight),
        first,
        second,
    )


def split_heads(packed, heads):
    groups, rows, cols = packed.shape
    return packed.reshape(groups, rows, heads, cols // heads)


def merge_heads(split):
    groups, rows, heads, size = split.shape
    return split.reshape(groups, rows, heads * size)


def rest_forward(stream, mixed, w_o, w_up, w_down, second):
    middle = stream + dots("gnk,gdk->nd", mixed, w_o)
    norm2, scale2 = layer_stats(middle)
    dense = (norm2 * second).astype(BF)
    hidden = dots("nd,gdk->gnk", dense, w_up)
    active = gelu(hidden).astype(BF)
    out = middle + dots("gnk,gdk->nd", active, w_down)
    return (out, (norm2, scale2, dense, hidden, active))


def rest_backward(grad_out, saved, mixed, w_o, w_up, w_down, second):
    norm2, scale2, dense, hidden, active = saved
    branch = grad_out.astype(BF)
    g_down = dots("nd,gnk->gdk", branch, active)
    grad_hidden = (dots("nd,gdk->gnk", branch, w_down) * gelu_slope(hidden)).astype(BF)
    g_up = dots("nd,gnk->gdk", dense, grad_hidden)
    grad_norm, g_second = norm_back(norm2, scale2, second, dots("gnk,gdk->nd", grad_hidden, w_up))
    grad_mid = grad_out + grad_norm
    mixer = grad_mid.astype(BF)
    g_o = dots("nd,gnk->gdk", mixer, mixed)
    grad_mixed = dots("nd,gdk->gnk", mixer, w_o).astype(BF)
    return (grad_mid, grad_mixed, g_o, g_up, g_down, g_second)


def encoder_forward(pix, place, keep, bank, gains, sizes, asked):
    local, hidden, pixel = sizes
    heads = HEADS // bank.shape[0]
    size = local // heads
    up = 4 * local
    down = up + hidden
    emb = down + hidden
    start = dots("gnk,gdk->nd", pix, bank[:, :, emb:]) + place
    norm1, scale1 = layer_stats(start)
    mixer_in = (norm1 * gains[0]).astype(BF)
    triple = dots("nd,gdk->gnk", mixer_in, bank[:, :, : 3 * local]).astype(BF)
    queries = split_heads(triple[:, :asked, :local], heads)
    keyset = split_heads(triple[:, :, local : 2 * local], heads)
    values = split_heads(triple[:, :, 2 * local :], heads)
    score = dots("gnhs,gmhs->ghnm", queries, keyset) * size**-0.5 + (keep - 1.0) * 1e9
    probs32 = jax.nn.softmax(score, -1)
    probs = probs32.astype(BF)
    mixed = merge_heads(dots("ghnm,gmhs->gnhs", probs, values).astype(BF))
    out, rest = rest_forward(
        start[:asked], mixed, bank[:, :, 3 * local : up], bank[:, :, up:down],
        bank[:, :, down:emb], gains[1],
    )
    return (out, (norm1, scale1, mixer_in, queries, keyset, values, probs32, mixed, rest))


def encoder_backward(grad_out, saved, pix, bank, gains, sizes):
    norm1, scale1, mixer_in, queries, keyset, values, probs32, mixed, rest = saved
    local, hidden, pixel = sizes
    asked = queries.shape[1]
    size = queries.shape[3]
    up = 4 * local
    down = up + hidden
    emb = down + hidden
    heads = queries.shape[2]
    grad_mid, grad_mixed, g_o, g_up, g_down, g_second = rest_backward(
        grad_out, rest, mixed, bank[:, :, 3 * local : up], bank[:, :, up:down],
        bank[:, :, down:emb], gains[1],
    )
    grad_mixed = split_heads(grad_mixed, heads)
    probs = probs32.astype(BF)
    grad_probs = dots("gnhs,gmhs->ghnm", grad_mixed, values)
    grad_values = dots("ghnm,gnhs->gmhs", probs, grad_mixed).astype(BF)
    grad_scores = (
        probs32 * (grad_probs - jnp.sum(grad_probs * probs32, -1, keepdims=True))
    ).astype(BF)
    grad_queries = (dots("ghnm,gmhs->gnhs", grad_scores, keyset) * size**-0.5).astype(BF)
    grad_keys = (dots("ghnm,gnhs->gmhs", grad_scores, queries) * size**-0.5).astype(BF)
    total = mixer_in.shape[0]
    grad_queries = jnp.pad(merge_heads(grad_queries), ((0, 0), (0, total - asked), (0, 0)))
    triple = jnp.concatenate([grad_queries, merge_heads(grad_keys), merge_heads(grad_values)], 2)
    g_qkv = dots("nd,gnk->gdk", mixer_in, triple)
    grad_norm, g_first = norm_back(
        norm1, scale1, gains[0], dots("gnk,gdk->nd", triple, bank[:, :, : 3 * local])
    )
    grad_start = (jnp.pad(grad_mid, ((0, total - asked), (0, 0))) + grad_norm).astype(BF)
    g_emb = dots("nd,gnk->gdk", grad_start, pix)
    return (jnp.concatenate([g_qkv, g_o, g_up, g_down, g_emb], 2), g_first, g_second)


def predictor(context, targets, table, slots, tslots, ckeep, tkeep, total, bank, gains, sizes):
    local, plocal, phidden = sizes
    first, second, final, token = gains
    heads = HEADS // bank.shape[0]
    size = plocal // heads
    up = 4 * plocal
    down = up + phidden
    head_at = down + phidden
    entry_at = head_at + local
    w_qkv = bank[:, :, : 3 * plocal]
    w_o = bank[:, :, 3 * plocal : up]
    w_up = bank[:, :, up:down]
    w_down = bank[:, :, down:head_at]
    w_head = bank[:, :, head_at:entry_at]
    w_entry = bank[:, :, entry_at:]
    groups = bank.shape[0]
    blocks, tlen = tslots.shape
    nctx = slots.shape[0]
    asked = blocks * tlen
    spread = context.reshape(nctx, groups, local).transpose(1, 0, 2)
    entry = dots("gnk,gdk->nd", spread, w_entry) + pick(table, slots)
    tgt_in = token + pick(table, tslots.reshape(-1))
    norm1, scale1 = layer_stats(jnp.concatenate([entry, tgt_in], 0))
    mixer_in = (norm1 * first).astype(BF)
    triple = dots("nd,gdk->gnk", mixer_in, w_qkv).astype(BF)
    queries = split_heads(triple[:, nctx:, :plocal], heads)
    keyset = split_heads(triple[:, :, plocal : 2 * plocal], heads)
    values = split_heads(triple[:, :, 2 * plocal :], heads)
    shape_b = (groups, blocks, tlen, heads, size)
    q_b = queries.reshape(shape_b)
    k_c, v_c = (keyset[:, :nctx], values[:, :nctx])
    k_t, v_t = (keyset[:, nctx:].reshape(shape_b), values[:, nctx:].reshape(shape_b))
    s_c = dots("gbnhs,gmhs->ghbnm", q_b, k_c) * size**-0.5 + (ckeep - 1.0) * 1e9
    s_t = (
        dots("gbnhs,gbmhs->ghbnm", q_b, k_t) * size**-0.5 + (tkeep[:, None, :] - 1.0) * 1e9
    )
    score = jnp.concatenate([s_c, s_t], -1)
    probs32 = jax.nn.softmax(score, -1)
    probs = probs32.astype(BF)
    mixed = dots("ghbnm,gmhs->gbnhs", probs[..., :nctx], v_c) + dots(
        "ghbnm,gbmhs->gbnhs", probs[..., nctx:], v_t
    )
    mixed = mixed.astype(BF).reshape(groups, asked, plocal)
    out, rest = rest_forward(tgt_in, mixed, w_o, w_up, w_down, second)
    norm_f, scale_f = layer_stats(out)
    head_in = (norm_f * final).astype(BF)
    pred = dots("nd,gdk->gnk", head_in, w_head)
    weight = tkeep.reshape(-1)[None, :, None]
    wanted = targets.reshape(asked, groups, local).transpose(1, 0, 2).astype(F32)
    diff = pred - wanted
    loss = jnp.sum(weight * diff * diff)
    grad_pred = (2.0 * weight * diff / total).astype(BF)
    g_head = dots("nd,gnk->gdk", head_in, grad_pred)
    grad_out, g_final = norm_back(
        norm_f, scale_f, final, dots("gnk,gdk->nd", grad_pred, w_head)
    )
    grad_mid, grad_mixed, g_o, g_up, g_down, g_second = rest_backward(
        grad_out, rest, mixed, w_o, w_up, w_down, second
    )
    gm = grad_mixed.reshape(shape_b)
    grad_probs = jnp.concatenate(
        [dots("gbnhs,gmhs->ghbnm", gm, v_c), dots("gbnhs,gbmhs->ghbnm", gm, v_t)], -1
    )
    grad_scores = (
        probs32 * (grad_probs - jnp.sum(grad_probs * probs32, -1, keepdims=True))
    ).astype(BF)
    ds_c, ds_t = (grad_scores[..., :nctx], grad_scores[..., nctx:])
    p_c, p_t = (probs[..., :nctx], probs[..., nctx:])
    root = size**-0.5
    grad_q = (
        (dots("ghbnm,gmhs->gbnhs", ds_c, k_c) + dots("ghbnm,gbmhs->gbnhs", ds_t, k_t)) * root
    ).astype(BF)
    grad_k_t = (dots("ghbnm,gbnhs->gbmhs", ds_t, q_b) * root).astype(BF)
    grad_v_t = dots("ghbnm,gbnhs->gbmhs", p_t, gm).astype(BF)
    grad_k_c = jnp.sum(
        (dots("ghbnm,gbnhs->gbmhs", ds_c, q_b) * root).astype(BF).astype(F32), 1
    )
    grad_v_c = jnp.sum(dots("ghbnm,gbnhs->gbmhs", p_c, gm).astype(BF).astype(F32), 1)
    kv_c = jnp.concatenate([merge_heads(grad_k_c), merge_heads(grad_v_c)], 2)
    high = kv_c.astype(BF)
    low = (kv_c - high.astype(F32)).astype(BF)
    flat = (groups, asked, plocal)
    t_rows = jnp.concatenate(
        [grad_q.reshape(flat), grad_k_t.reshape(flat), grad_v_t.reshape(flat)], 2
    )
    a_c, a_t = (mixer_in[:nctx], mixer_in[nctx:])
    g_q = dots("nd,gnk->gdk", a_t, t_rows[:, :, :plocal])
    g_kv = dots(
        "nd,gnk->gdk",
        jnp.concatenate([a_c, a_c, a_t], 0),
        jnp.concatenate([high, low, t_rows[:, :, plocal:]], 1),
    )
    w_kv = bank[:, :, plocal : 3 * plocal]
    grad_a = jnp.concatenate(
        [
            dots("gnk,gdk->nd", high, w_kv) + dots("gnk,gdk->nd", low, w_kv),
            dots("gnk,gdk->nd", t_rows, w_qkv),
        ],
        0,
    )
    grad_in, g_first = norm_back(norm1, scale1, first, grad_a)
    g_token = jnp.sum(grad_in[nctx:] + grad_mid, 0)
    grad_entry = grad_in[:nctx].astype(BF)
    g_entry = dots("nd,gnk->gdk", grad_entry, spread)
    grad_context = dots("nd,gdk->gnk", grad_entry, w_entry).transpose(1, 0, 2).reshape(nctx, -1)
    g_bank = jnp.concatenate([g_q, g_kv, g_o, g_up, g_down, g_head, g_entry], 2)
    return (grad_context, loss, g_bank, (g_first, g_second, g_final, g_token))


def per_device(
    pixels,
    context_slots,
    context_count,
    target_slots,
    target_count,
    encoder_in,
    encoder_out,
    predictor_in,
    predictor_out,
    vectors,
    first_encoder_in,
    first_encoder_out,
    first_predictor_in,
    first_predictor_out,
    first_vectors,
    second_encoder_in,
    second_encoder_out,
    second_predictor_in,
    second_predictor_out,
    second_vectors,
    target_encoder_in,
    target_encoder_out,
    target_vectors,
):
    groups = lax.axis_size("mp")
    owners = lax.axis_size("role") * lax.axis_size("dp")
    width = encoder_in.shape[0] * owners
    pwidth = predictor_in.shape[0] * owners
    local, plocal = (width // groups, pwidth // groups)
    pixel = pixels.shape[2]
    hidden = encoder_in.shape[1] - 3 * local
    phidden = predictor_in.shape[1] - 3 * plocal - local
    patches = pixels.shape[1]
    image = lax.axis_index("role") * groups + lax.axis_index("mp")

    def gather(packed):
        whole = lax.all_gather(packed.astype(BF), EVERY, axis=0, tiled=True)
        return whole.reshape(groups, -1, packed.shape[1])

    bank = gather(pack_encoder(encoder_in, encoder_out, local, pixel))
    pbank = gather(pack_predictor(predictor_in, predictor_out, local, plocal, phidden))
    tbank = gather(pack_encoder(target_encoder_in, target_encoder_out, local, pixel))
    both = lax.all_gather(
        jnp.stack([vectors, target_vectors]).astype(BF), ("role", "dp", "mp"), axis=0
    )
    s_vec = both[:, 0].reshape(-1).astype(F32)
    t_vec = both[:, 1].reshape(-1).astype(F32)
    target_total = lax.psum(jnp.sum(target_count).astype(F32), "dp")

    half = lax.dynamic_slice_in_dim(pixels, lax.axis_index("role") * groups, groups, 0)
    pix = lax.all_to_all(half, "mp", 0, 0, tiled=True)
    slots = lax.dynamic_index_in_dim(context_slots, image, 0, keepdims=False)
    count = lax.dynamic_index_in_dim(context_count, image, 0, keepdims=False)
    tslots = lax.dynamic_index_in_dim(target_slots, image, 0, keepdims=False)
    tcount = lax.dynamic_index_in_dim(target_count, image, 0, keepdims=False)
    nctx = slots.shape[0]
    blocks, tlen = tslots.shape

    patch = jnp.arange(patches)
    hits = slots[:, None] == patch[None, :]
    member = jnp.any(hits, 0)
    order = jnp.where(
        member,
        jnp.sum(jnp.where(hits, jnp.arange(nctx)[:, None], 0), 0),
        nctx + jnp.cumsum(1 - member.astype(jnp.int32)) - 1,
    )
    shuffle = order[None, :] == patch[:, None]
    places = jnp.sum(jnp.where(shuffle, patch[None, :], 0), 1)
    ckeep = (jnp.arange(nctx) < count).astype(F32)
    keep = (patch < count).astype(F32)
    tkeep = (jnp.arange(tlen)[None, :] < tcount[:, None]).astype(F32)

    table = sincos(width)
    sizes = (local, hidden, pixel)
    t_out, _ = encoder_forward(
        pix, table, jnp.ones_like(keep), tbank, (t_vec[:width], t_vec[width : 2 * width]),
        sizes, patches,
    )
    t_norm = layer_stats(t_out)[0].astype(BF)
    t_hot = (tslots.reshape(-1)[:, None] == patch[None, :]).astype(BF)
    targets = jnp.dot(t_hot, t_norm, preferred_element_type=F32).astype(BF)

    mixed_pix = dots("jp,gpk->gjk", shuffle.astype(BF), pix).astype(BF)
    enc_gains = (s_vec[:width], s_vec[width : 2 * width])
    latent, enc_saved = encoder_forward(
        mixed_pix, pick(table, places), keep, bank, enc_gains, sizes, nctx
    )
    pv = s_vec[2 * width :]
    pgains = (pv[:pwidth], pv[pwidth : 2 * pwidth], pv[2 * pwidth : 3 * pwidth], pv[3 * pwidth :])
    grad_context, loss, g_pbank, p_small = predictor(
        latent.astype(BF), targets, sincos(pwidth), slots, tslots, ckeep, tkeep, target_total,
        pbank, pgains, (local, plocal, phidden),
    )
    g_bank, g_first, g_second = encoder_backward(
        grad_context, enc_saved, mixed_pix, bank, enc_gains, sizes
    )
    g_vec = jnp.concatenate([g_first, g_second, *p_small])

    def scatter(grads):
        flat = grads.reshape(-1, grads.shape[-1])
        return lax.psum_scatter(flat, EVERY, scatter_dimension=0, tiled=True)

    r_pin, r_pout = unpack_predictor(scatter(g_pbank), local, plocal, phidden)
    r_in, r_out = unpack_encoder(scatter(g_bank), local, hidden, pixel)
    r_vec = lax.psum_scatter(g_vec, ("role", "dp", "mp"), scatter_dimension=0, tiled=True)
    squares = sum(jnp.sum(g * g) for g in (r_in, r_out, r_pin, r_pout, r_vec))
    squares, loss_total = lax.psum((squares, loss), ("role", "dp", "mp"))
    grad_norm = jnp.sqrt(squares)
    scale = jnp.minimum(1.0, CLIP / (grad_norm + 1e-06))
    new_in, m_in, v_in = adamw(
        encoder_in, r_in, first_encoder_in, second_encoder_in, scale, RATE_MATRIX, DECAY
    )
    new_out, m_out, v_out = adamw(
        encoder_out, r_out, first_encoder_out, second_encoder_out, scale, RATE_MATRIX, DECAY
    )
    new_pin, m_pin, v_pin = adamw(
        predictor_in, r_pin, first_predictor_in, second_predictor_in, scale, RATE_MATRIX, DECAY
    )
    new_pout, m_pout, v_pout = adamw(
        predictor_out, r_pout, first_predictor_out, second_predictor_out, scale, RATE_MATRIX, DECAY
    )
    new_vec, m_vec, v_vec = adamw(
        vectors, r_vec, first_vectors, second_vectors, scale, RATE_VECTOR, 0.0
    )
    ema_in = MOMENTUM_EMA * target_encoder_in + (1.0 - MOMENTUM_EMA) * new_in
    ema_out = MOMENTUM_EMA * target_encoder_out + (1.0 - MOMENTUM_EMA) * new_out
    ema_vec = MOMENTUM_EMA * target_vectors + (1.0 - MOMENTUM_EMA) * new_vec
    return (
        new_in, new_out, new_pin, new_pout, new_vec,
        m_in, m_out, m_pin, m_pout, m_vec,
        v_in, v_out, v_pin, v_pout, v_vec,
        ema_in, ema_out, ema_vec,
        loss_total, target_total, grad_norm,
    )


def solution(mesh):
    bank_in, bank_out, small = (
        P(("role", "dp"), "mp"),
        P("mp", ("role", "dp")),
        P(("role", "dp", "mp")),
    )
    five = (bank_in, bank_out, bank_in, bank_out, small)
    three = (bank_in, bank_out, small)
    return jax.shard_map(
        per_device,
        mesh=mesh,
        in_specs=(
            P("dp", None, "mp"),
            P("dp", None),
            P("dp"),
            P("dp", None, None),
            P("dp", None),
        )
        + five * 3
        + three,
        out_specs=five * 3 + three + (P(), P(), P()),
        check_vma=False,
    )
```

```python
import functools

import jax
import jax.numpy as jnp
import numpy as np
from jax import lax
from jax.experimental import pallas as pl
from jax.experimental.pallas import tpu as pltpu
from jax.sharding import PartitionSpec as P

HEADS = 12
GRID = 14
STEP = 10

BETA_ONE = 0.9
BETA_TWO = 0.999
ADAM_EPS = 1e-08
RATE_MATRIX = 0.03
RATE_VECTOR = 0.3
DECAY = 0.05
MOMENTUM_EMA = 0.9
CLIP = 0.1
ROOT_HALF = 0.7071067811865476
INVERSE_ROOT = 0.3989422804014327

BF = jnp.bfloat16
F32 = jnp.float32
LANES = 128


def dots(spec, left, right):
    return jnp.einsum(spec, left, right, preferred_element_type=F32)


def sincos(width):
    quarter = width // 4
    omega = 1.0 / 10000.0 ** (np.arange(quarter, dtype=np.float64) / quarter)
    place = np.arange(GRID * GRID)
    rows = (place // GRID)[:, None] * omega[None, :]
    cols = (place % GRID)[:, None] * omega[None, :]
    return np.concatenate([np.sin(rows), np.cos(rows), np.sin(cols), np.cos(cols)], -1).astype(
        np.float32
    )


def pick(table, places):
    hot = (places[:, None] == jnp.arange(table.shape[0])[None, :]).astype(F32)
    return jnp.dot(hot, table, precision=lax.Precision.HIGHEST, preferred_element_type=F32)


def layer_stats(stream):
    mean = jnp.mean(stream, -1, keepdims=True)
    cent = stream - mean
    scale = lax.rsqrt(jnp.mean(cent * cent, -1, keepdims=True) + 1e-06)
    return (cent * scale, scale)


def norm_back(normed, scale, gain, grad):
    gain_grad = jnp.sum(grad * normed, 0)
    scaled = grad * gain
    inner = (
        scaled
        - jnp.mean(scaled, -1, keepdims=True)
        - normed * jnp.mean(scaled * normed, -1, keepdims=True)
    )
    return (scale * inner, gain_grad)


def gelu(hidden):
    return 0.5 * hidden * (1.0 + lax.erf(hidden * ROOT_HALF))


def gelu_slope(hidden):
    return (
        0.5 * (1.0 + lax.erf(hidden * ROOT_HALF))
        + hidden * jnp.exp(-0.5 * hidden * hidden) * INVERSE_ROOT
    )


def pack_encoder(w_in, w_out, local, pixel, extras):
    turned = w_out.T
    used = w_in.shape[1] + turned.shape[1] + len(extras)
    return jnp.concatenate(
        [
            w_in[:, : 3 * local],
            turned[:, pixel : pixel + local],
            w_in[:, 3 * local :],
            turned[:, pixel + local :],
            turned[:, :pixel],
            *[e[:, None] for e in extras],
            jnp.zeros((w_in.shape[0], -used % (2 * LANES)), F32),
        ],
        1,
    ).astype(BF)


def unpack_encoder(packed, local, hidden, pixel):
    up = 4 * local
    down = up + hidden
    emb = down + hidden
    w_in = jnp.concatenate([packed[:, : 3 * local], packed[:, up:down]], 1)
    turned = jnp.concatenate(
        [packed[:, emb : emb + pixel], packed[:, 3 * local : up], packed[:, down:emb]], 1
    )
    return (w_in, turned.T)


def pack_predictor(p_in, p_out, local, plocal, phidden):
    turned = p_out.T
    return jnp.concatenate(
        [
            p_in[:, : 3 * plocal],
            turned[:, local : local + plocal],
            p_in[:, 3 * plocal : 3 * plocal + phidden],
            turned[:, local + plocal :],
            p_in[:, 3 * plocal + phidden :],
            turned[:, :local],
        ],
        1,
    ).astype(BF)


def unpack_predictor(packed, local, plocal, phidden):
    up = 4 * plocal
    down = up + phidden
    head = down + phidden
    entry = head + local
    p_in = jnp.concatenate(
        [packed[:, : 3 * plocal], packed[:, up:down], packed[:, head:entry]], 1
    )
    turned = jnp.concatenate(
        [packed[:, entry:], packed[:, 3 * plocal : up], packed[:, down:head]], 1
    )
    return (p_in, turned.T)


def adamw(weight, grad, first, second, scale, rate, decay):
    grad = grad * scale
    first = BETA_ONE * first + (1.0 - BETA_ONE) * grad
    second = BETA_TWO * second + (1.0 - BETA_TWO) * grad * grad
    mean_hat = first / (1.0 - BETA_ONE**STEP)
    square_hat = second / (1.0 - BETA_TWO**STEP)
    return (
        weight - rate * (mean_hat / (jnp.sqrt(square_hat) + ADAM_EPS) + decay * weight),
        first,
        second,
    )


def split_heads(packed, heads):
    groups, rows, cols = packed.shape
    return packed.reshape(groups, rows, heads, cols // heads)


def merge_heads(split):
    groups, rows, heads, size = split.shape
    return split.reshape(groups, rows, heads * size)


def rest_forward(stream, mixed, w_o, w_up, w_down, second):
    middle = stream + dots("gnk,gdk->nd", mixed, w_o)
    norm2, scale2 = layer_stats(middle)
    dense = (norm2 * second).astype(BF)
    hidden = dots("nd,gdk->gnk", dense, w_up)
    active = gelu(hidden).astype(BF)
    out = middle + dots("gnk,gdk->nd", active, w_down)
    return (out, (norm2, scale2, dense, hidden, active))


def rest_backward(grad_out, saved, mixed, w_o, w_up, w_down, second):
    norm2, scale2, dense, hidden, active = saved
    branch = grad_out.astype(BF)
    g_down = dots("nd,gnk->gdk", branch, active)
    grad_hidden = (dots("nd,gdk->gnk", branch, w_down) * gelu_slope(hidden)).astype(BF)
    g_up = dots("nd,gnk->gdk", dense, grad_hidden)
    grad_norm, g_second = norm_back(norm2, scale2, second, dots("gnk,gdk->nd", grad_hidden, w_up))
    grad_mid = grad_out + grad_norm
    mixer = grad_mid.astype(BF)
    g_o = dots("nd,gnk->gdk", mixer, mixed)
    grad_mixed = dots("nd,gdk->gnk", mixer, w_o).astype(BF)
    return (grad_mid, grad_mixed, g_o, g_up, g_down, g_second)


def shift_of(rank, by):
    return jnp.bitwise_xor(rank, by)


def greet(peers):
    barrier = pltpu.get_barrier_semaphore()
    for peer in peers:
        pl.semaphore_signal(barrier, inc=1, device_id=peer, device_id_type=pl.DeviceIdType.MESH)
    pl.semaphore_wait(barrier, len(peers))


def gather_kernel(nz, count, *refs):
    ins = refs[:count]
    outs = refs[count : 2 * count]
    (own_sem, zs, zr, xs, xr, ys, yr, rxs, rxr, rys, ryr, cs, cr) = refs[2 * count :]
    r = lax.axis_index("role")
    d = lax.axis_index("dp")
    m = lax.axis_index("mp")
    mx = shift_of(m, 1)
    my = shift_of(m, 2)
    base = r * nz
    line_of = [{"dp": lax.rem(d + j, nz)} for j in range(1, nz)]
    greet([{"role": 1 - r}, {"mp": mx}, {"mp": my}] + line_of)

    def remote(src, dst, send, recv, where):
        return pltpu.make_async_remote_copy(
            src_ref=src, dst_ref=dst, send_sem=send, recv_sem=recv,
            device_id=where, device_id_type=pl.DeviceIdType.MESH,
        )

    def line(k, piece, way, from_input=False):
        out = outs[k]
        src = ins[k] if from_input else out.at[m, base + piece]
        return remote(
            src, out.at[m, base + piece], zs.at[k, way, piece], zr.at[k, way, piece],
            {"dp": d + 1 - 2 * way},
        )

    def across(k, piece, from_input=False):
        out = outs[k]
        src = ins[k] if from_input else out.at[m, base + piece]
        dst = out.at[m, base + piece]
        return (
            remote(src, dst, xs.at[k, piece], xr.at[k, piece], {"mp": mx}),
            remote(src, dst, ys.at[k, piece], yr.at[k, piece], {"mp": my}),
        )

    def arrived(k, piece):
        out = outs[k]
        return (
            remote(out.at[mx, base + piece], out.at[mx, base + piece], xs.at[k, piece], xr.at[k, piece], {"mp": mx}),
            remote(out.at[my, base + piece], out.at[my, base + piece], ys.at[k, piece], yr.at[k, piece], {"mp": my}),
        )

    def relay(k, piece):
        out = outs[k]
        half = out.shape[3] // 2
        first = out.at[mx, base + piece, :, pl.ds(0, half)]
        second = out.at[my, base + piece, :, pl.ds(half, half)]
        return (
            remote(first, first, rys.at[k, piece], ryr.at[k, piece], {"mp": my}),
            remote(second, second, rxs.at[k, piece], rxr.at[k, piece], {"mp": mx}),
        )

    def diagonal(k, piece):
        out = outs[k]
        half = out.shape[3] // 2
        far = shift_of(m, 3)
        first = out.at[far, base + piece, :, pl.ds(0, half)]
        second = out.at[far, base + piece, :, pl.ds(half, half)]
        return (
            remote(first, first, rys.at[k, piece], ryr.at[k, piece], {"mp": my}),
            remote(second, second, rxs.at[k, piece], rxr.at[k, piece], {"mp": mx}),
        )

    def core(k, column, slot):
        block = outs[k].at[column, pl.ds(base, nz)]
        return remote(block, block, cs.at[k, slot], cr.at[k, slot], {"role": 1 - r})

    def core_in(k, column, slot):
        block = outs[k].at[column, pl.ds((1 - r) * nz, nz)]
        return remote(block, block, cs.at[k, slot], cr.at[k, slot], {"role": 1 - r})

    def owncopy(k):
        return pltpu.make_async_copy(ins[k], outs[k].at[m, base + d], own_sem.at[k])

    for k in range(count):
        @pl.when(d < nz - 1)
        def _():
            line(k, d, 0, True).start()

        @pl.when(d > 0)
        def _():
            line(k, d, 1, True).start()

        for copy in across(k, d, True):
            copy.start()
        owncopy(k).start()

    for k in range(count):
        def pass_on(piece):
            for copy in arrived(k, piece):
                copy.wait_recv()
            for copy in relay(k, piece):
                copy.start()

        def step(t, carry):
            left = d - 1 - t
            right = d + 1 + t

            @pl.when(left >= 0)
            def _():
                line(k, left, 0).wait_recv()

                @pl.when(d < nz - 1)
                def _():
                    line(k, left, 0).start()

                for copy in across(k, left):
                    copy.start()

            @pl.when(right < nz)
            def _():
                line(k, right, 1).wait_recv()

                @pl.when(d > 0)
                def _():
                    line(k, right, 1).start()

                for copy in across(k, right):
                    copy.start()

            @pl.when(t == 0)
            def _():
                pass_on(d)

            @pl.when(jnp.logical_and(t > 0, left + 1 >= 0))
            def _():
                pass_on(left + 1)

            @pl.when(jnp.logical_and(t > 0, right - 1 < nz))
            def _():
                pass_on(right - 1)

            return carry

        lax.fori_loop(0, nz - 1, step, 0)
        if nz == 1:
            pass_on(d)
        else:
            @pl.when(d == nz - 1)
            def _():
                pass_on(0)

            @pl.when(d == 0)
            def _():
                pass_on(nz - 1)

        owncopy(k).wait()
        core(k, m, 0).start()
        core(k, mx, 1).start()
        core(k, my, 2).start()

    for k in range(count):
        def take(piece, carry):
            for copy in diagonal(k, piece):
                copy.wait_recv()
            return carry

        lax.fori_loop(0, nz, take, 0)
        core(k, shift_of(m, 3), 3).start()
    for k in range(count):
        columns = (m, mx, my, shift_of(m, 3))
        for slot, column in enumerate(columns):
            core_in(k, column, slot).wait_recv()
            core(k, column, slot).wait_send()

        def done(piece, carry):
            for copy in across(k, piece):
                copy.wait_send()
            for copy in relay(k, piece):
                copy.wait_send()

            @pl.when(jnp.logical_and(piece <= d, d < nz - 1))
            def _():
                line(k, piece, 0).wait_send()

            @pl.when(jnp.logical_and(piece >= d, d > 0))
            def _():
                line(k, piece, 1).wait_send()

            return carry

        lax.fori_loop(0, nz, done, 0)


def gather_all(packs):
    nz = lax.axis_size("dp")
    groups = lax.axis_size("mp")
    count = len(packs)
    dma = pltpu.SemaphoreType.DMA
    piece = dma((count, nz))
    return pl.pallas_call(
        functools.partial(gather_kernel, nz, count),
        out_shape=[
            jax.ShapeDtypeStruct((groups, lax.axis_size("role") * nz, *p.shape), p.dtype)
            for p in packs
        ],
        in_specs=[pl.BlockSpec(memory_space=pl.ANY)] * count,
        out_specs=[pl.BlockSpec(memory_space=pl.ANY)] * count,
        scratch_shapes=[dma((count,)), dma((count, 2, nz)), dma((count, 2, nz))]
        + [piece] * 8
        + [dma((count, 4)), dma((count, 4))],
        compiler_params=pltpu.CompilerParams(collective_id=1, has_side_effects=True),
    )(*packs)


def reduce_kernel(nz, count, stats_in, *refs):
    ins = refs[:count]
    outs = refs[count : 2 * count]
    stats_out = refs[2 * count]
    rest = refs[2 * count + 1 :]
    accs = rest[:count]
    loads = rest[count : 2 * count]
    sends1 = rest[2 * count : 3 * count]
    recvs1 = rest[3 * count : 4 * count]
    sends2 = rest[4 * count : 5 * count]
    recvs2 = rest[5 * count : 6 * count]
    lines = rest[6 * count : 7 * count]
    (near, near_in, far_in, ld, cs, cr, s1s, s1r, s2s, s2r, zs, zr, ns, nr, fs, fr) = rest[
        7 * count :
    ]
    r = lax.axis_index("role")
    d = lax.axis_index("dp")
    m = lax.axis_index("mp")
    groups = 4
    mx = shift_of(m, 1)
    my = shift_of(m, 2)
    mf = shift_of(m, 3)
    columns = (mf, mx, my, m)
    group = [
        {"role": role, "mp": shift_of(m, by)}
        for role in (r, 1 - r)
        for by in range(groups)
    ][1:]
    far = [{"dp": lax.rem(d + j, nz)} for j in range(1, nz)]
    greet(group + far)

    def remote(src, dst, send, recv, where):
        return pltpu.make_async_remote_copy(
            src_ref=src, dst_ref=dst, send_sem=send, recv_sem=recv,
            device_id=where, device_id_type=pl.DeviceIdType.MESH,
        )

    def core(k, j):
        return remote(
            ins[k].at[columns[j], pl.ds((1 - r) * nz, nz)], accs[k].at[columns[j]],
            cs.at[k, j], cr.at[k, j], {"role": 1 - r},
        )

    def load(k, j):
        return pltpu.make_async_copy(
            ins[k].at[columns[j], pl.ds(r * nz, nz)], loads[k].at[j % 2], ld.at[k, j % 2]
        )

    def first(k, piece):
        half = ins[k].shape[3] // 2
        low, high = (pl.ds(0, half), pl.ds(half, half))
        return (
            remote(sends1[k].at[piece, :, low], recvs1[k].at[piece, :, low],
                   s1s.at[k, 0, piece], s1r.at[k, 0, piece], {"mp": my}),
            remote(sends1[k].at[piece, :, high], recvs1[k].at[piece, :, high],
                   s1s.at[k, 1, piece], s1r.at[k, 1, piece], {"mp": mx}),
        )

    def second(k, piece):
        return (
            remote(sends2[k].at[0, piece], recvs2[k].at[0, piece],
                   s2s.at[k, 0, piece], s2r.at[k, 0, piece], {"mp": mx}),
            remote(sends2[k].at[1, piece], recvs2[k].at[1, piece],
                   s2s.at[k, 1, piece], s2r.at[k, 1, piece], {"mp": my}),
        )

    def right(k, piece):
        return remote(accs[k].at[m, piece], lines[k].at[piece], zs.at[k, piece],
                      zr.at[k, piece], {"dp": d + 1})

    def left(k, piece):
        slot = jnp.where(piece == d - 1, nz, piece)
        return remote(accs[k].at[m, piece], lines[k].at[slot], zs.at[k, piece],
                      zr.at[k, slot], {"dp": d - 1})

    def line_in(k, slot):
        return pltpu.make_async_remote_copy(
            src_ref=lines[k].at[slot], dst_ref=lines[k].at[slot], send_sem=zs.at[k, 0],
            recv_sem=zr.at[k, slot], device_id={"role": 1 - r},
            device_id_type=pl.DeviceIdType.MESH,
        )

    def each(body):
        def step(t, carry):
            off = nz - 1 - t

            @pl.when(d + off < nz)
            def _():
                body(d + off)

            @pl.when(d - off >= 0)
            def _():
                body(d - off)

            return carry

        lax.fori_loop(0, nz - 1, step, 0)
        body(d)

    for k in range(count):
        core(k, 0).start()
        load(k, 0).start()
        load(k, 1).start()
    for j in range(1, groups):
        for k in range(count):
            core(k, j).start()

    def combine(k, j):
        core(k, j).wait_recv()
        load(k, j).wait()

    for k in range(count):
        combine(k, 0)

        def send_far(piece):
            sends1[k][piece] = (accs[k][mf, piece] + loads[k][0, piece]).astype(sends1[k].dtype)
            for copy in first(k, piece):
                copy.start()

        each(send_far)
        load(k, 2).start()
    for k in range(count):
        half = ins[k].shape[3] // 2
        combine(k, 1)

        def add_x(piece, carry):
            accs[k][mx, piece] += loads[k][1, piece]
            return carry

        lax.fori_loop(0, nz, add_x, 0)
        load(k, 3).start()
        combine(k, 2)

        def send_near(piece):
            for copy in first(k, piece):
                copy.wait_recv()
            relayed = recvs1[k][piece].astype(jnp.float32)
            lane = lax.broadcasted_iota(jnp.int32, relayed.shape, 1)
            sends2[k][0, piece] = (
                accs[k][mx, piece] + jnp.where(lane < half, relayed, 0.0)
            ).astype(sends2[k].dtype)
            sends2[k][1, piece] = (
                accs[k][my, piece] + loads[k][0, piece] + jnp.where(lane < half, 0.0, relayed)
            ).astype(sends2[k].dtype)
            for copy in second(k, piece):
                copy.start()

        each(send_near)
    squares = jnp.zeros((1, 1), jnp.float32)
    for k in range(count):
        combine(k, 3)

        def finish(piece):
            for copy in second(k, piece):
                copy.wait_recv()
            accs[k][m, piece] += (
                loads[k][1, piece]
                + recvs2[k][0, piece].astype(jnp.float32)
                + recvs2[k][1, piece].astype(jnp.float32)
            )

            @pl.when(piece > d)
            def _():
                @pl.when(d > 0)
                def _():
                    line_in(k, piece).wait_recv()
                    accs[k][m, piece] += lines[k][piece]

                right(k, piece).start()

            @pl.when(piece < d)
            def _():
                @pl.when(d < nz - 1)
                def _():
                    line_in(k, piece).wait_recv()
                    accs[k][m, piece] += lines[k][piece]

                left(k, piece).start()

        each(finish)
    for k in range(count):
        outs[k][...] = accs[k][m, d]

        @pl.when(d > 0)
        def _():
            line_in(k, d).wait_recv()
            outs[k][...] += lines[k][d]

        @pl.when(d < nz - 1)
        def _():
            line_in(k, nz).wait_recv()
            outs[k][...] += lines[k][nz]

        total = outs[k][...]
        squares += jnp.sum(total * total, keepdims=True)

    mine = r * groups + m
    row = lax.broadcasted_iota(jnp.int32, (8, 128), 0)
    near[...] = jnp.where(row == 0, stats_in[...], squares)
    near_in[mine] = near[...]
    copies = []
    for j, peer in enumerate(group):
        copies.append(remote(near, near_in.at[mine], ns.at[j], nr.at[mine], peer))
        copies[-1].start()
    for j, peer in enumerate(group):
        slot = peer["role"] * groups + peer["mp"]
        remote(near, near_in.at[slot], ns.at[j], nr.at[slot], peer).wait_recv()
    for copy in copies:
        copy.wait_send()
    summed = near_in[0]
    for j in range(1, 2 * groups):
        summed += near_in[j]
    near[...] = summed
    far_in[d] = summed
    copies = []
    for j, peer in enumerate(far):
        copies.append(remote(near, far_in.at[d], fs.at[j], fr.at[d], peer))
        copies[-1].start()
    for j, peer in enumerate(far):
        slot = peer["dp"]
        remote(near, far_in.at[slot], fs.at[j], fr.at[slot], peer).wait_recv()
    for copy in copies:
        copy.wait_send()
    summed = far_in[0]
    for j in range(1, nz):
        summed += far_in[j]
    stats_out[...] = summed

    for k in range(count):
        for j in range(groups):
            core(k, j).wait_send()

        def done(piece, carry):
            for copy in first(k, piece):
                copy.wait_send()
            for copy in second(k, piece):
                copy.wait_send()

            @pl.when(piece != d)
            def _():
                right(k, piece).wait_send()

            return carry

        lax.fori_loop(0, nz, done, 0)


def reduce_all(grads, wire_types, stats):
    nz = lax.axis_size("dp")
    groups = lax.axis_size("mp")
    count = len(grads)
    dma = pltpu.SemaphoreType.DMA
    shapes = [g.shape[2:] for g in grads]
    vmem = pl.BlockSpec(memory_space=pltpu.VMEM)
    scratch = (
        [pltpu.VMEM((groups, nz, *s), jnp.float32) for s in shapes]
        + [pltpu.VMEM((2, nz, *s), jnp.float32) for s in shapes]
        + [pltpu.VMEM((nz, *s), t) for s, t in zip(shapes, wire_types)] * 2
        + [pltpu.VMEM((2, nz, *s), t) for s, t in zip(shapes, wire_types)] * 2
        + [pltpu.VMEM((nz + 1, *s), jnp.float32) for s in shapes]
        + [
            pltpu.VMEM((8, 128), jnp.float32),
            pltpu.VMEM((2 * groups, 8, 128), jnp.float32),
            pltpu.VMEM((nz, 8, 128), jnp.float32),
            dma((count, 2)),
            dma((count, groups)),
            dma((count, groups)),
            dma((count, 2, nz)),
            dma((count, 2, nz)),
            dma((count, 2, nz)),
            dma((count, 2, nz)),
            dma((count, nz)),
            dma((count, nz + 1)),
            dma((2 * groups,)),
            dma((2 * groups,)),
            dma((nz,)),
            dma((nz,)),
        ]
    )
    return pl.pallas_call(
        functools.partial(reduce_kernel, nz, count),
        out_shape=[jax.ShapeDtypeStruct(s, jnp.float32) for s in shapes]
        + [jax.ShapeDtypeStruct((8, 128), jnp.float32)],
        in_specs=[vmem] + [pl.BlockSpec(memory_space=pl.ANY)] * count,
        out_specs=[vmem] * (count + 1),
        scratch_shapes=scratch,
        compiler_params=pltpu.CompilerParams(
            collective_id=2, has_side_effects=True, vmem_limit_bytes=60 * 2**20
        ),
    )(stats, *grads)


def encoder_forward(pix, place, keep, bank, gains, sizes, asked):
    local, hidden, pixel = sizes
    heads = HEADS // bank.shape[0]
    size = local // heads
    up = 4 * local
    down = up + hidden
    emb = down + hidden
    start = dots("gnk,gdk->nd", pix, bank[:, :, emb : emb + pixel]) + place
    norm1, scale1 = layer_stats(start)
    mixer_in = (norm1 * gains[0]).astype(BF)
    triple = dots("nd,gdk->gnk", mixer_in, bank[:, :, : 3 * local]).astype(BF)
    queries = split_heads(triple[:, :asked, :local], heads)
    keyset = split_heads(triple[:, :, local : 2 * local], heads)
    values = split_heads(triple[:, :, 2 * local :], heads)
    score = dots("gnhs,gmhs->ghnm", queries, keyset) * size**-0.5 + (keep - 1.0) * 1e9
    probs32 = jax.nn.softmax(score, -1)
    probs = probs32.astype(BF)
    mixed = merge_heads(dots("ghnm,gmhs->gnhs", probs, values).astype(BF))
    out, rest = rest_forward(
        start[:asked], mixed, bank[:, :, 3 * local : up], bank[:, :, up:down],
        bank[:, :, down:emb], gains[1],
    )
    return (out, (norm1, scale1, mixer_in, queries, keyset, values, probs32, mixed, rest))


def encoder_backward(grad_out, saved, pix, bank, gains, sizes):
    norm1, scale1, mixer_in, queries, keyset, values, probs32, mixed, rest = saved
    local, hidden, pixel = sizes
    asked = queries.shape[1]
    size = queries.shape[3]
    up = 4 * local
    down = up + hidden
    emb = down + hidden
    heads = queries.shape[2]
    grad_mid, grad_mixed, g_o, g_up, g_down, g_second = rest_backward(
        grad_out, rest, mixed, bank[:, :, 3 * local : up], bank[:, :, up:down],
        bank[:, :, down:emb], gains[1],
    )
    grad_mixed = split_heads(grad_mixed, heads)
    probs = probs32.astype(BF)
    grad_probs = dots("gnhs,gmhs->ghnm", grad_mixed, values)
    grad_values = dots("ghnm,gnhs->gmhs", probs, grad_mixed).astype(BF)
    grad_scores = (
        probs32 * (grad_probs - jnp.sum(grad_probs * probs32, -1, keepdims=True))
    ).astype(BF)
    grad_queries = (dots("ghnm,gmhs->gnhs", grad_scores, keyset) * size**-0.5).astype(BF)
    grad_keys = (dots("ghnm,gnhs->gmhs", grad_scores, queries) * size**-0.5).astype(BF)
    total = mixer_in.shape[0]
    grad_queries = jnp.pad(merge_heads(grad_queries), ((0, 0), (0, total - asked), (0, 0)))
    triple = jnp.concatenate([grad_queries, merge_heads(grad_keys), merge_heads(grad_values)], 2)
    g_qkv = dots("nd,gnk->gdk", mixer_in, triple)
    grad_norm, g_first = norm_back(
        norm1, scale1, gains[0], dots("gnk,gdk->nd", triple, bank[:, :, : 3 * local])
    )
    grad_start = (jnp.pad(grad_mid, ((0, total - asked), (0, 0))) + grad_norm).astype(BF)
    g_emb = dots("nd,gnk->gdk", grad_start, pix)
    return (jnp.concatenate([g_qkv, g_o, g_up, g_down, g_emb], 2), g_first, g_second)


def predictor(context, targets, table, slots, tslots, ckeep, tkeep, total, bank, gains, sizes):
    local, plocal, phidden = sizes
    first, second, final, token = gains
    heads = HEADS // bank.shape[0]
    size = plocal // heads
    up = 4 * plocal
    down = up + phidden
    head_at = down + phidden
    entry_at = head_at + local
    w_qkv = bank[:, :, : 3 * plocal]
    w_o = bank[:, :, 3 * plocal : up]
    w_up = bank[:, :, up:down]
    w_down = bank[:, :, down:head_at]
    w_head = bank[:, :, head_at:entry_at]
    w_entry = bank[:, :, entry_at:]
    groups = bank.shape[0]
    blocks, tlen = tslots.shape
    nctx = slots.shape[0]
    asked = blocks * tlen
    spread = context.reshape(nctx, groups, local).transpose(1, 0, 2)
    entry = dots("gnk,gdk->nd", spread, w_entry) + pick(table, slots)
    tgt_in = token + pick(table, tslots.reshape(-1))
    norm1, scale1 = layer_stats(jnp.concatenate([entry, tgt_in], 0))
    mixer_in = (norm1 * first).astype(BF)
    triple = dots("nd,gdk->gnk", mixer_in, w_qkv).astype(BF)
    queries = split_heads(triple[:, nctx:, :plocal], heads)
    keyset = split_heads(triple[:, :, plocal : 2 * plocal], heads)
    values = split_heads(triple[:, :, 2 * plocal :], heads)
    shape_b = (groups, blocks, tlen, heads, size)
    q_b = queries.reshape(shape_b)
    k_c, v_c = (keyset[:, :nctx], values[:, :nctx])
    k_t, v_t = (keyset[:, nctx:].reshape(shape_b), values[:, nctx:].reshape(shape_b))
    s_c = dots("gbnhs,gmhs->ghbnm", q_b, k_c) * size**-0.5 + (ckeep - 1.0) * 1e9
    s_t = (
        dots("gbnhs,gbmhs->ghbnm", q_b, k_t) * size**-0.5 + (tkeep[:, None, :] - 1.0) * 1e9
    )
    score = jnp.concatenate([s_c, s_t], -1)
    probs32 = jax.nn.softmax(score, -1)
    probs = probs32.astype(BF)
    mixed = dots("ghbnm,gmhs->gbnhs", probs[..., :nctx], v_c) + dots(
        "ghbnm,gbmhs->gbnhs", probs[..., nctx:], v_t
    )
    mixed = mixed.astype(BF).reshape(groups, asked, plocal)
    out, rest = rest_forward(tgt_in, mixed, w_o, w_up, w_down, second)
    norm_f, scale_f = layer_stats(out)
    head_in = (norm_f * final).astype(BF)
    pred = dots("nd,gdk->gnk", head_in, w_head)
    weight = tkeep.reshape(-1)[None, :, None]
    wanted = targets.reshape(asked, groups, local).transpose(1, 0, 2).astype(F32)
    diff = pred - wanted
    loss = jnp.sum(weight * diff * diff)
    grad_pred = (2.0 * weight * diff / total).astype(BF)
    g_head = dots("nd,gnk->gdk", head_in, grad_pred)
    grad_out, g_final = norm_back(
        norm_f, scale_f, final, dots("gnk,gdk->nd", grad_pred, w_head)
    )
    grad_mid, grad_mixed, g_o, g_up, g_down, g_second = rest_backward(
        grad_out, rest, mixed, w_o, w_up, w_down, second
    )
    gm = grad_mixed.reshape(shape_b)
    grad_probs = jnp.concatenate(
        [dots("gbnhs,gmhs->ghbnm", gm, v_c), dots("gbnhs,gbmhs->ghbnm", gm, v_t)], -1
    )
    grad_scores = (
        probs32 * (grad_probs - jnp.sum(grad_probs * probs32, -1, keepdims=True))
    ).astype(BF)
    ds_c, ds_t = (grad_scores[..., :nctx], grad_scores[..., nctx:])
    p_c, p_t = (probs[..., :nctx], probs[..., nctx:])
    root = size**-0.5
    grad_q = (
        (dots("ghbnm,gmhs->gbnhs", ds_c, k_c) + dots("ghbnm,gbmhs->gbnhs", ds_t, k_t)) * root
    ).astype(BF)
    grad_k_t = (dots("ghbnm,gbnhs->gbmhs", ds_t, q_b) * root).astype(BF)
    grad_v_t = dots("ghbnm,gbnhs->gbmhs", p_t, gm).astype(BF)
    grad_k_c = jnp.sum(
        (dots("ghbnm,gbnhs->gbmhs", ds_c, q_b) * root).astype(BF).astype(F32), 1
    )
    grad_v_c = jnp.sum(dots("ghbnm,gbnhs->gbmhs", p_c, gm).astype(BF).astype(F32), 1)
    kv_c = jnp.concatenate([merge_heads(grad_k_c), merge_heads(grad_v_c)], 2)
    high = kv_c.astype(BF)
    low = (kv_c - high.astype(F32)).astype(BF)
    flat = (groups, asked, plocal)
    t_rows = jnp.concatenate(
        [grad_q.reshape(flat), grad_k_t.reshape(flat), grad_v_t.reshape(flat)], 2
    )
    a_c, a_t = (mixer_in[:nctx], mixer_in[nctx:])
    g_q = dots("nd,gnk->gdk", a_t, t_rows[:, :, :plocal])
    g_kv = dots(
        "nd,gnk->gdk",
        jnp.concatenate([a_c, a_c, a_t], 0),
        jnp.concatenate([high, low, t_rows[:, :, plocal:]], 1),
    )
    w_kv = bank[:, :, plocal : 3 * plocal]
    grad_a = jnp.concatenate(
        [
            dots("gnk,gdk->nd", high, w_kv) + dots("gnk,gdk->nd", low, w_kv),
            dots("gnk,gdk->nd", t_rows, w_qkv),
        ],
        0,
    )
    grad_in, g_first = norm_back(norm1, scale1, first, grad_a)
    g_token = jnp.sum(grad_in[nctx:] + grad_mid, 0)
    grad_entry = grad_in[:nctx].astype(BF)
    g_entry = dots("nd,gnk->gdk", grad_entry, spread)
    grad_context = dots("nd,gdk->gnk", grad_entry, w_entry).transpose(1, 0, 2).reshape(nctx, -1)
    g_bank = jnp.concatenate([g_q, g_kv, g_o, g_up, g_down, g_head, g_entry], 2)
    return (grad_context, loss, g_bank, (g_first, g_second, g_final, g_token))


def per_device(
    pixels,
    context_slots,
    context_count,
    target_slots,
    target_count,
    encoder_in,
    encoder_out,
    predictor_in,
    predictor_out,
    vectors,
    first_encoder_in,
    first_encoder_out,
    first_predictor_in,
    first_predictor_out,
    first_vectors,
    second_encoder_in,
    second_encoder_out,
    second_predictor_in,
    second_predictor_out,
    second_vectors,
    target_encoder_in,
    target_encoder_out,
    target_vectors,
):
    groups = lax.axis_size("mp")
    owners = lax.axis_size("role") * lax.axis_size("dp")
    width = encoder_in.shape[0] * owners
    pwidth = predictor_in.shape[0] * owners
    local, plocal = (width // groups, pwidth // groups)
    pixel = pixels.shape[2]
    hidden = encoder_in.shape[1] - 3 * local
    phidden = predictor_in.shape[1] - 3 * plocal - local
    patches = pixels.shape[1]
    image = lax.axis_index("role") * groups + lax.axis_index("mp")

    slots = lax.dynamic_index_in_dim(context_slots, image, 0, keepdims=False)
    count = lax.dynamic_index_in_dim(context_count, image, 0, keepdims=False)
    tslots = lax.dynamic_index_in_dim(target_slots, image, 0, keepdims=False)
    tcount = lax.dynamic_index_in_dim(target_count, image, 0, keepdims=False)
    tsum = jnp.broadcast_to(jnp.sum(tcount).astype(F32), vectors.shape)
    gathered = gather_all(
        [
            pack_encoder(encoder_in, encoder_out, local, pixel, [vectors, tsum]),
            pack_predictor(predictor_in, predictor_out, local, plocal, phidden),
            pack_encoder(target_encoder_in, target_encoder_out, local, pixel, [target_vectors]),
        ]
    )
    bank, pbank, tbank = (g.reshape(groups, -1, g.shape[-1]) for g in gathered)
    extra = 4 * local + 2 * hidden + pixel

    def spread_vector(whole):
        return whole[:, :, extra].reshape(groups, owners, -1).transpose(1, 0, 2).reshape(-1)

    s_vec = spread_vector(bank).astype(F32)
    t_vec = spread_vector(tbank).astype(F32)
    target_total = jnp.sum(gathered[0][:, :, 0, extra + 1].astype(F32))

    half = lax.dynamic_slice_in_dim(pixels, lax.axis_index("role") * groups, groups, 0)
    pix = lax.all_to_all(half, "mp", 0, 0, tiled=True)
    nctx = slots.shape[0]
    blocks, tlen = tslots.shape

    patch = jnp.arange(patches)
    hits = slots[:, None] == patch[None, :]
    member = jnp.any(hits, 0)
    order = jnp.where(
        member,
        jnp.sum(jnp.where(hits, jnp.arange(nctx)[:, None], 0), 0),
        nctx + jnp.cumsum(1 - member.astype(jnp.int32)) - 1,
    )
    shuffle = order[None, :] == patch[:, None]
    places = jnp.sum(jnp.where(shuffle, patch[None, :], 0), 1)
    ckeep = (jnp.arange(nctx) < count).astype(F32)
    keep = (patch < count).astype(F32)
    tkeep = (jnp.arange(tlen)[None, :] < tcount[:, None]).astype(F32)

    table = sincos(width)
    sizes = (local, hidden, pixel)
    t_out, _ = encoder_forward(
        pix, table, jnp.ones_like(keep), tbank, (t_vec[:width], t_vec[width : 2 * width]),
        sizes, patches,
    )
    t_norm = layer_stats(t_out)[0].astype(BF)
    t_hot = (tslots.reshape(-1)[:, None] == patch[None, :]).astype(BF)
    targets = jnp.dot(t_hot, t_norm, preferred_element_type=F32).astype(BF)

    mixed_pix = dots("jp,gpk->gjk", shuffle.astype(BF), pix).astype(BF)
    enc_gains = (s_vec[:width], s_vec[width : 2 * width])
    latent, enc_saved = encoder_forward(
        mixed_pix, pick(table, places), keep, bank, enc_gains, sizes, nctx
    )
    pv = s_vec[2 * width :]
    pgains = (pv[:pwidth], pv[pwidth : 2 * pwidth], pv[2 * pwidth : 3 * pwidth], pv[3 * pwidth :])
    grad_context, loss, g_pbank, p_small = predictor(
        latent.astype(BF), targets, sincos(pwidth), slots, tslots, ckeep, tkeep, target_total,
        pbank, pgains, (local, plocal, phidden),
    )
    g_bank, g_first, g_second = encoder_backward(
        grad_context, enc_saved, mixed_pix, bank, enc_gains, sizes
    )
    g_vec = jnp.concatenate([g_first, g_second, *p_small])

    small = g_vec.reshape(owners, groups, -1).transpose(1, 0, 2).reshape(groups, width, 1)
    rest = jnp.zeros((groups, width, bank.shape[2] - extra - 1), F32)
    g_bank = jnp.concatenate([g_bank, small, rest], 2)
    r_bank, r_pbank, stats = reduce_all(
        [
            g_bank.reshape(gathered[0].shape),
            g_pbank.reshape(gathered[1].shape),
        ],
        (BF, F32),
        jnp.broadcast_to(loss, (8, LANES)),
    )
    r_pin, r_pout = unpack_predictor(r_pbank, local, plocal, phidden)
    r_in, r_out = unpack_encoder(r_bank, local, hidden, pixel)
    r_vec = r_bank[:, extra]
    loss_total, squares = (stats[0, 0], stats[1, 0])
    grad_norm = jnp.sqrt(squares)
    scale = jnp.minimum(1.0, CLIP / (grad_norm + 1e-06))
    new_in, m_in, v_in = adamw(
        encoder_in, r_in, first_encoder_in, second_encoder_in, scale, RATE_MATRIX, DECAY
    )
    new_out, m_out, v_out = adamw(
        encoder_out, r_out, first_encoder_out, second_encoder_out, scale, RATE_MATRIX, DECAY
    )
    new_pin, m_pin, v_pin = adamw(
        predictor_in, r_pin, first_predictor_in, second_predictor_in, scale, RATE_MATRIX, DECAY
    )
    new_pout, m_pout, v_pout = adamw(
        predictor_out, r_pout, first_predictor_out, second_predictor_out, scale, RATE_MATRIX, DECAY
    )
    new_vec, m_vec, v_vec = adamw(
        vectors, r_vec, first_vectors, second_vectors, scale, RATE_VECTOR, 0.0
    )
    ema_in = MOMENTUM_EMA * target_encoder_in + (1.0 - MOMENTUM_EMA) * new_in
    ema_out = MOMENTUM_EMA * target_encoder_out + (1.0 - MOMENTUM_EMA) * new_out
    ema_vec = MOMENTUM_EMA * target_vectors + (1.0 - MOMENTUM_EMA) * new_vec
    return (
        new_in, new_out, new_pin, new_pout, new_vec,
        m_in, m_out, m_pin, m_pout, m_vec,
        v_in, v_out, v_pin, v_pout, v_vec,
        ema_in, ema_out, ema_vec,
        loss_total, target_total, grad_norm,
    )


def solution(mesh):
    bank_in, bank_out, small = (
        P(("role", "dp"), "mp"),
        P("mp", ("role", "dp")),
        P(("role", "dp", "mp")),
    )
    five = (bank_in, bank_out, bank_in, bank_out, small)
    three = (bank_in, bank_out, small)
    return jax.shard_map(
        per_device,
        mesh=mesh,
        in_specs=(
            P("dp", None, "mp"),
            P("dp", None),
            P("dp"),
            P("dp", None, None),
            P("dp", None),
        )
        + five * 3
        + three,
        out_specs=five * 3 + three + (P(), P(), P()),
        check_vma=False,
    )
```

```python
import functools

import jax
import jax.numpy as jnp
import numpy as np
from jax import lax
from jax.experimental import pallas as pl
from jax.experimental.pallas import tpu as pltpu
from jax.sharding import PartitionSpec as P

HEADS = 12
GRID = 14
STEP = 10

BETA_ONE = 0.9
BETA_TWO = 0.999
ADAM_EPS = 1e-08
RATE_MATRIX = 0.03
RATE_VECTOR = 0.3
DECAY = 0.05
MOMENTUM_EMA = 0.9
CLIP = 0.1
ROOT_HALF = 0.7071067811865476
INVERSE_ROOT = 0.3989422804014327

BF = jnp.bfloat16
F32 = jnp.float32
LANES = 128


def sincos(width):
    quarter = width // 4
    omega = 1.0 / 10000.0 ** (np.arange(quarter, dtype=np.float64) / quarter)
    place = np.arange(GRID * GRID)
    rows = (place // GRID)[:, None] * omega[None, :]
    cols = (place % GRID)[:, None] * omega[None, :]
    return np.concatenate([np.sin(rows), np.cos(rows), np.sin(cols), np.cos(cols)], -1).astype(
        np.float32
    )


def pick(table, places):
    parts, rest = ([], table)
    for _ in range(3):
        parts.append(rest.astype(jnp.bfloat16))
        rest = rest - parts[-1].astype(np.float32)
    hot = (places[:, None] == jnp.arange(table.shape[0])[None, :]).astype(BF)
    rows = jnp.dot(hot, np.concatenate(parts, 1), preferred_element_type=F32)
    width = table.shape[1]
    return rows[:, :width] + rows[:, width : 2 * width] + rows[:, 2 * width :]


def pack_encoder(w_in, w_out, local, pixel, extras):
    turned = w_out.T
    used = w_in.shape[1] + turned.shape[1] + len(extras)
    return jnp.concatenate(
        [
            w_in[:, : 3 * local],
            turned[:, pixel : pixel + local],
            w_in[:, 3 * local :],
            turned[:, pixel + local :],
            turned[:, :pixel],
            *[e[:, None] for e in extras],
            jnp.zeros((w_in.shape[0], -used % (2 * LANES)), F32),
        ],
        1,
    ).astype(BF)


def unpack_encoder(packed, local, hidden, pixel):
    up = 4 * local
    down = up + hidden
    emb = down + hidden
    w_in = jnp.concatenate([packed[:, : 3 * local], packed[:, up:down]], 1)
    turned = jnp.concatenate(
        [packed[:, emb : emb + pixel], packed[:, 3 * local : up], packed[:, down:emb]], 1
    )
    return (w_in, turned.T)


def pack_predictor(p_in, p_out, local, plocal, phidden):
    turned = p_out.T
    return jnp.concatenate(
        [
            p_in[:, : 3 * plocal],
            turned[:, local : local + plocal],
            p_in[:, 3 * plocal : 3 * plocal + phidden],
            turned[:, local + plocal :],
            p_in[:, 3 * plocal + phidden :],
            turned[:, :local],
        ],
        1,
    ).astype(BF)


def unpack_predictor(packed, local, plocal, phidden):
    up = 4 * plocal
    down = up + phidden
    head = down + phidden
    entry = head + local
    p_in = jnp.concatenate(
        [packed[:, : 3 * plocal], packed[:, up:down], packed[:, head:entry]], 1
    )
    turned = jnp.concatenate(
        [packed[:, entry:], packed[:, 3 * plocal : up], packed[:, down:head]], 1
    )
    return (p_in, turned.T)


def adamw(weight, grad, first, second, scale, rate, decay):
    grad = grad * scale
    first = BETA_ONE * first + (1.0 - BETA_ONE) * grad
    second = BETA_TWO * second + (1.0 - BETA_TWO) * grad * grad
    mean_hat = first / (1.0 - BETA_ONE**STEP)
    square_hat = second / (1.0 - BETA_TWO**STEP)
    return (
        weight - rate * (mean_hat / (jnp.sqrt(square_hat) + ADAM_EPS) + decay * weight),
        first,
        second,
    )


def shift_of(rank, by):
    return jnp.bitwise_xor(rank, by)


def greet(peers):
    barrier = pltpu.get_barrier_semaphore()
    for peer in peers:
        pl.semaphore_signal(barrier, inc=1, device_id=peer, device_id_type=pl.DeviceIdType.MESH)
    pl.semaphore_wait(barrier, len(peers))


def gather_kernel(nz, count, *refs):
    ins = refs[:count]
    outs = refs[count : 2 * count]
    (own_sem, zs, zr, xs, xr, ys, yr, rxs, rxr, rys, ryr, cs, cr) = refs[2 * count :]
    r = lax.axis_index("role")
    d = lax.axis_index("dp")
    m = lax.axis_index("mp")
    mx = shift_of(m, 1)
    my = shift_of(m, 2)
    base = r * nz
    line_of = [{"dp": lax.rem(d + j, nz)} for j in range(1, nz)]
    greet([{"role": 1 - r}, {"mp": mx}, {"mp": my}] + line_of)

    def remote(src, dst, send, recv, where):
        return pltpu.make_async_remote_copy(
            src_ref=src, dst_ref=dst, send_sem=send, recv_sem=recv,
            device_id=where, device_id_type=pl.DeviceIdType.MESH,
        )

    def line(k, piece, way, from_input=False):
        out = outs[k]
        src = ins[k] if from_input else out.at[m, base + piece]
        return remote(
            src, out.at[m, base + piece], zs.at[k, way, piece], zr.at[k, way, piece],
            {"dp": d + 1 - 2 * way},
        )

    def across(k, piece, from_input=False):
        out = outs[k]
        src = ins[k] if from_input else out.at[m, base + piece]
        dst = out.at[m, base + piece]
        return (
            remote(src, dst, xs.at[k, piece], xr.at[k, piece], {"mp": mx}),
            remote(src, dst, ys.at[k, piece], yr.at[k, piece], {"mp": my}),
        )

    def arrived(k, piece):
        out = outs[k]
        return (
            remote(out.at[mx, base + piece], out.at[mx, base + piece], xs.at[k, piece], xr.at[k, piece], {"mp": mx}),
            remote(out.at[my, base + piece], out.at[my, base + piece], ys.at[k, piece], yr.at[k, piece], {"mp": my}),
        )

    def relay(k, piece):
        out = outs[k]
        half = out.shape[3] // 2
        first = out.at[mx, base + piece, :, pl.ds(0, half)]
        second = out.at[my, base + piece, :, pl.ds(half, half)]
        return (
            remote(first, first, rys.at[k, piece], ryr.at[k, piece], {"mp": my}),
            remote(second, second, rxs.at[k, piece], rxr.at[k, piece], {"mp": mx}),
        )

    def diagonal(k, piece):
        out = outs[k]
        half = out.shape[3] // 2
        far = shift_of(m, 3)
        first = out.at[far, base + piece, :, pl.ds(0, half)]
        second = out.at[far, base + piece, :, pl.ds(half, half)]
        return (
            remote(first, first, rys.at[k, piece], ryr.at[k, piece], {"mp": my}),
            remote(second, second, rxs.at[k, piece], rxr.at[k, piece], {"mp": mx}),
        )

    def core(k, column, slot):
        block = outs[k].at[column, pl.ds(base, nz)]
        return remote(block, block, cs.at[k, slot], cr.at[k, slot], {"role": 1 - r})

    def core_in(k, column, slot):
        block = outs[k].at[column, pl.ds((1 - r) * nz, nz)]
        return remote(block, block, cs.at[k, slot], cr.at[k, slot], {"role": 1 - r})

    def owncopy(k):
        return pltpu.make_async_copy(ins[k], outs[k].at[m, base + d], own_sem.at[k])

    for k in range(count):
        @pl.when(d < nz - 1)
        def _():
            line(k, d, 0, True).start()

        @pl.when(d > 0)
        def _():
            line(k, d, 1, True).start()

        for copy in across(k, d, True):
            copy.start()
        owncopy(k).start()

    for k in range(count):
        def pass_on(piece):
            for copy in arrived(k, piece):
                copy.wait_recv()
            for copy in relay(k, piece):
                copy.start()

        def step(t, carry):
            left = d - 1 - t
            right = d + 1 + t

            @pl.when(left >= 0)
            def _():
                line(k, left, 0).wait_recv()

                @pl.when(d < nz - 1)
                def _():
                    line(k, left, 0).start()

                for copy in across(k, left):
                    copy.start()

            @pl.when(right < nz)
            def _():
                line(k, right, 1).wait_recv()

                @pl.when(d > 0)
                def _():
                    line(k, right, 1).start()

                for copy in across(k, right):
                    copy.start()

            @pl.when(t == 0)
            def _():
                pass_on(d)

            @pl.when(jnp.logical_and(t > 0, left + 1 >= 0))
            def _():
                pass_on(left + 1)

            @pl.when(jnp.logical_and(t > 0, right - 1 < nz))
            def _():
                pass_on(right - 1)

            return carry

        lax.fori_loop(0, nz - 1, step, 0)
        if nz == 1:
            pass_on(d)
        else:
            @pl.when(d == nz - 1)
            def _():
                pass_on(0)

            @pl.when(d == 0)
            def _():
                pass_on(nz - 1)

        owncopy(k).wait()
        core(k, m, 0).start()
        core(k, mx, 1).start()
        core(k, my, 2).start()

    for k in range(count):
        def take(piece, carry):
            for copy in diagonal(k, piece):
                copy.wait_recv()
            return carry

        lax.fori_loop(0, nz, take, 0)
        core(k, shift_of(m, 3), 3).start()
    for k in range(count):
        columns = (m, mx, my, shift_of(m, 3))
        for slot, column in enumerate(columns):
            core_in(k, column, slot).wait_recv()
            core(k, column, slot).wait_send()

        def done(piece, carry):
            for copy in across(k, piece):
                copy.wait_send()
            for copy in relay(k, piece):
                copy.wait_send()

            @pl.when(jnp.logical_and(piece <= d, d < nz - 1))
            def _():
                line(k, piece, 0).wait_send()

            @pl.when(jnp.logical_and(piece >= d, d > 0))
            def _():
                line(k, piece, 1).wait_send()

            return carry

        lax.fori_loop(0, nz, done, 0)


def gather_all(packs):
    nz = lax.axis_size("dp")
    groups = lax.axis_size("mp")
    count = len(packs)
    dma = pltpu.SemaphoreType.DMA
    piece = dma((count, nz))
    return pl.pallas_call(
        functools.partial(gather_kernel, nz, count),
        out_shape=[
            jax.ShapeDtypeStruct((groups, lax.axis_size("role") * nz, *p.shape), p.dtype)
            for p in packs
        ],
        in_specs=[pl.BlockSpec(memory_space=pl.ANY)] * count,
        out_specs=[pl.BlockSpec(memory_space=pl.ANY)] * count,
        scratch_shapes=[dma((count,)), dma((count, 2, nz)), dma((count, 2, nz))]
        + [piece] * 8
        + [dma((count, 4)), dma((count, 4))],
        compiler_params=pltpu.CompilerParams(collective_id=1, has_side_effects=True),
    )(*packs)


def reduce_kernel(nz, count, stats_in, *refs):
    ins = refs[:count]
    outs = refs[count : 2 * count]
    stats_out = refs[2 * count]
    rest = refs[2 * count + 1 :]
    accs = rest[:count]
    loads = rest[count : 2 * count]
    sends1 = rest[2 * count : 3 * count]
    recvs1 = rest[3 * count : 4 * count]
    sends2 = rest[4 * count : 5 * count]
    recvs2 = rest[5 * count : 6 * count]
    lines = rest[6 * count : 7 * count]
    (near, near_in, far_in, ld, cs, cr, s1s, s1r, s2s, s2r, zs, zr, ns, nr, fs, fr) = rest[
        7 * count :
    ]
    r = lax.axis_index("role")
    d = lax.axis_index("dp")
    m = lax.axis_index("mp")
    groups = 4
    mx = shift_of(m, 1)
    my = shift_of(m, 2)
    mf = shift_of(m, 3)
    columns = (mf, mx, my, m)
    group = [
        {"role": role, "mp": shift_of(m, by)}
        for role in (r, 1 - r)
        for by in range(groups)
    ][1:]
    far = [{"dp": lax.rem(d + j, nz)} for j in range(1, nz)]
    greet(group + far)

    def remote(src, dst, send, recv, where):
        return pltpu.make_async_remote_copy(
            src_ref=src, dst_ref=dst, send_sem=send, recv_sem=recv,
            device_id=where, device_id_type=pl.DeviceIdType.MESH,
        )

    def core(k, j):
        return remote(
            ins[k].at[columns[j], pl.ds((1 - r) * nz, nz)], accs[k].at[columns[j]],
            cs.at[k, j], cr.at[k, j], {"role": 1 - r},
        )

    def load(k, j):
        return pltpu.make_async_copy(
            ins[k].at[columns[j], pl.ds(r * nz, nz)], loads[k].at[j % 2], ld.at[k, j % 2]
        )

    def first(k, piece):
        half = ins[k].shape[3] // 2
        low, high = (pl.ds(0, half), pl.ds(half, half))
        return (
            remote(sends1[k].at[piece, :, low], recvs1[k].at[piece, :, low],
                   s1s.at[k, 0, piece], s1r.at[k, 0, piece], {"mp": my}),
            remote(sends1[k].at[piece, :, high], recvs1[k].at[piece, :, high],
                   s1s.at[k, 1, piece], s1r.at[k, 1, piece], {"mp": mx}),
        )

    def second(k, piece):
        return (
            remote(sends2[k].at[0, piece], recvs2[k].at[0, piece],
                   s2s.at[k, 0, piece], s2r.at[k, 0, piece], {"mp": mx}),
            remote(sends2[k].at[1, piece], recvs2[k].at[1, piece],
                   s2s.at[k, 1, piece], s2r.at[k, 1, piece], {"mp": my}),
        )

    def right(k, piece):
        return remote(accs[k].at[m, piece], lines[k].at[piece], zs.at[k, piece],
                      zr.at[k, piece], {"dp": d + 1})

    def left(k, piece):
        slot = jnp.where(piece == d - 1, nz, piece)
        return remote(accs[k].at[m, piece], lines[k].at[slot], zs.at[k, piece],
                      zr.at[k, slot], {"dp": d - 1})

    def line_in(k, slot):
        return pltpu.make_async_remote_copy(
            src_ref=lines[k].at[slot], dst_ref=lines[k].at[slot], send_sem=zs.at[k, 0],
            recv_sem=zr.at[k, slot], device_id={"role": 1 - r},
            device_id_type=pl.DeviceIdType.MESH,
        )

    def each(body):
        def step(t, carry):
            off = nz - 1 - t

            @pl.when(d + off < nz)
            def _():
                body(d + off)

            @pl.when(d - off >= 0)
            def _():
                body(d - off)

            return carry

        lax.fori_loop(0, nz - 1, step, 0)
        body(d)

    for k in range(count):
        core(k, 0).start()
        load(k, 0).start()
        load(k, 1).start()
    for j in range(1, groups):
        for k in range(count):
            core(k, j).start()

    def combine(k, j):
        core(k, j).wait_recv()
        load(k, j).wait()

    for k in range(count):
        combine(k, 0)

        def send_far(piece):
            sends1[k][piece] = (accs[k][mf, piece] + loads[k][0, piece]).astype(sends1[k].dtype)
            for copy in first(k, piece):
                copy.start()

        each(send_far)
        load(k, 2).start()
    for k in range(count):
        half = ins[k].shape[3] // 2
        combine(k, 1)

        def add_x(piece, carry):
            accs[k][mx, piece] += loads[k][1, piece]
            return carry

        lax.fori_loop(0, nz, add_x, 0)
        load(k, 3).start()
        combine(k, 2)

        def send_near(piece):
            for copy in first(k, piece):
                copy.wait_recv()
            relayed = recvs1[k][piece].astype(jnp.float32)
            lane = lax.broadcasted_iota(jnp.int32, relayed.shape, 1)
            sends2[k][0, piece] = (
                accs[k][mx, piece] + jnp.where(lane < half, relayed, 0.0)
            ).astype(sends2[k].dtype)
            sends2[k][1, piece] = (
                accs[k][my, piece] + loads[k][0, piece] + jnp.where(lane < half, 0.0, relayed)
            ).astype(sends2[k].dtype)
            for copy in second(k, piece):
                copy.start()

        each(send_near)
    squares = jnp.zeros((1, 1), jnp.float32)
    for k in range(count):
        combine(k, 3)

        def finish(piece):
            for copy in second(k, piece):
                copy.wait_recv()
            accs[k][m, piece] += (
                loads[k][1, piece]
                + recvs2[k][0, piece].astype(jnp.float32)
                + recvs2[k][1, piece].astype(jnp.float32)
            )

            @pl.when(piece > d)
            def _():
                @pl.when(d > 0)
                def _():
                    line_in(k, piece).wait_recv()
                    accs[k][m, piece] += lines[k][piece]

                right(k, piece).start()

            @pl.when(piece < d)
            def _():
                @pl.when(d < nz - 1)
                def _():
                    line_in(k, piece).wait_recv()
                    accs[k][m, piece] += lines[k][piece]

                left(k, piece).start()

        each(finish)
    for k in range(count):
        outs[k][...] = accs[k][m, d]

        @pl.when(d > 0)
        def _():
            line_in(k, d).wait_recv()
            outs[k][...] += lines[k][d]

        @pl.when(d < nz - 1)
        def _():
            line_in(k, nz).wait_recv()
            outs[k][...] += lines[k][nz]

        total = outs[k][...]
        squares += jnp.sum(total * total, keepdims=True)

    mine = r * groups + m
    row = lax.broadcasted_iota(jnp.int32, (8, 128), 0)
    near[...] = jnp.where(row == 0, stats_in[...], squares)
    near_in[mine] = near[...]
    copies = []
    for j, peer in enumerate(group):
        copies.append(remote(near, near_in.at[mine], ns.at[j], nr.at[mine], peer))
        copies[-1].start()
    for j, peer in enumerate(group):
        slot = peer["role"] * groups + peer["mp"]
        remote(near, near_in.at[slot], ns.at[j], nr.at[slot], peer).wait_recv()
    for copy in copies:
        copy.wait_send()
    summed = near_in[0]
    for j in range(1, 2 * groups):
        summed += near_in[j]
    near[...] = summed
    far_in[d] = summed
    copies = []
    for j, peer in enumerate(far):
        copies.append(remote(near, far_in.at[d], fs.at[j], fr.at[d], peer))
        copies[-1].start()
    for j, peer in enumerate(far):
        slot = peer["dp"]
        remote(near, far_in.at[slot], fs.at[j], fr.at[slot], peer).wait_recv()
    for copy in copies:
        copy.wait_send()
    summed = far_in[0]
    for j in range(1, nz):
        summed += far_in[j]
    stats_out[...] = summed

    for k in range(count):
        for j in range(groups):
            core(k, j).wait_send()

        def done(piece, carry):
            for copy in first(k, piece):
                copy.wait_send()
            for copy in second(k, piece):
                copy.wait_send()

            @pl.when(piece != d)
            def _():
                right(k, piece).wait_send()

            return carry

        lax.fori_loop(0, nz, done, 0)


def reduce_all(grads, wire_types, stats):
    nz = lax.axis_size("dp")
    groups = lax.axis_size("mp")
    count = len(grads)
    dma = pltpu.SemaphoreType.DMA
    shapes = [g.shape[2:] for g in grads]
    vmem = pl.BlockSpec(memory_space=pltpu.VMEM)
    scratch = (
        [pltpu.VMEM((groups, nz, *s), jnp.float32) for s in shapes]
        + [pltpu.VMEM((2, nz, *s), jnp.float32) for s in shapes]
        + [pltpu.VMEM((nz, *s), t) for s, t in zip(shapes, wire_types)] * 2
        + [pltpu.VMEM((2, nz, *s), t) for s, t in zip(shapes, wire_types)] * 2
        + [pltpu.VMEM((nz + 1, *s), jnp.float32) for s in shapes]
        + [
            pltpu.VMEM((8, 128), jnp.float32),
            pltpu.VMEM((2 * groups, 8, 128), jnp.float32),
            pltpu.VMEM((nz, 8, 128), jnp.float32),
            dma((count, 2)),
            dma((count, groups)),
            dma((count, groups)),
            dma((count, 2, nz)),
            dma((count, 2, nz)),
            dma((count, 2, nz)),
            dma((count, 2, nz)),
            dma((count, nz)),
            dma((count, nz + 1)),
            dma((2 * groups,)),
            dma((2 * groups,)),
            dma((nz,)),
            dma((nz,)),
        ]
    )
    return pl.pallas_call(
        functools.partial(reduce_kernel, nz, count),
        out_shape=[jax.ShapeDtypeStruct(s, jnp.float32) for s in shapes]
        + [jax.ShapeDtypeStruct((8, 128), jnp.float32)],
        in_specs=[vmem] + [pl.BlockSpec(memory_space=pl.ANY)] * count,
        out_specs=[vmem] * (count + 1),
        scratch_shapes=scratch,
        compiler_params=pltpu.CompilerParams(
            collective_id=2, has_side_effects=True, vmem_limit_bytes=60 * 2**20
        ),
    )(stats, *grads)


def dot(left, right):
    return lax.dot_general(left, right, (((1,), (0,)), ((), ())), preferred_element_type=F32)


def dot_rt(left, right):
    return lax.dot_general(left, right, (((1,), (1,)), ((), ())), preferred_element_type=F32)


def dot_lt(left, right):
    return lax.dot_general(left, right, (((0,), (0,)), ((), ())), preferred_element_type=F32)


def chain(term, count):
    total = term(0)
    for g in range(1, count):
        total += term(g)
    return total


def head_lanes(lanes, size, head):
    lane = lax.broadcasted_iota(jnp.int32, (1, lanes), 1)
    return jnp.logical_and(lane >= head * size, lane < (head + 1) * size)


def only(mask, value):
    return jnp.where(mask, value, jnp.zeros_like(value))


def turn(value, by):
    return pltpu.roll(value, by % value.shape[1], 1)


def stats_of(stream):
    mean = jnp.mean(stream, -1, keepdims=True)
    cent = stream - mean
    scale = lax.rsqrt(jnp.mean(cent * cent, -1, keepdims=True) + 1e-06)
    return (cent * scale, scale)


def norm_back_of(normed, scale, gain, grad):
    gain_grad = jnp.sum(grad * normed, 0, keepdims=True)
    scaled = grad * gain
    inner = (
        scaled
        - jnp.mean(scaled, -1, keepdims=True)
        - normed * jnp.mean(scaled * normed, -1, keepdims=True)
    )
    return (scale * inner, gain_grad)


def normal_cdf(hidden):
    return 0.5 * (1.0 + lax.erf(hidden * ROOT_HALF))


def encoder_kernel(sizes, asked, saving, pix, place, bias, bank, gains, *refs):
    local, hidden, size = sizes
    groups = bank.shape[0]
    heads = local // size
    up = 4 * local
    down = up + hidden
    emb = down + hidden
    wide = local + 64
    if saving:
        (out, norm1, scale1, mixer_in, qs, ks, vs, probs_out, mixed_out, norm2, scale2, dense,
         slope, active) = refs
    else:
        hot, out = refs[:2]
    start = place[...] + chain(lambda g: dot_rt(pix[g], bank[g, :, emb : emb + wide]), groups)
    normed, scale = stats_of(start)
    a = (normed * gains[0:1]).astype(BF)
    if saving:
        norm1[...] = normed
        scale1[...] = scale
        mixer_in[...] = a
    def attend(g):
        t = dot(a, bank[g, :, : 3 * local + 64]).astype(BF).astype(F32)
        q = t[:asked, :wide].astype(BF)
        k = turn(t, -local)[:, :wide].astype(BF)
        v = t[:, 2 * local :].astype(BF)
        if saving:
            qs[g] = q
            ks[g] = k
            vs[g] = v
        mixed = jnp.zeros((asked, wide), F32)
        for h in range(heads):
            mask = head_lanes(wide, size, h)
            score = dot_rt(only(mask, q), k) * size**-0.5 + bias[...]
            score = jnp.exp(score - jnp.max(score, -1, keepdims=True))
            probs = score / jnp.sum(score, -1, keepdims=True)
            if saving:
                probs_out[g * heads + h] = probs
            mixed += only(mask, dot(probs.astype(BF), v))
        mixed = turn(mixed, 64).astype(BF)
        if saving:
            mixed_out[g] = mixed
        return dot_rt(mixed, bank[g, :, up - wide : up])

    middle = start[:asked] + chain(attend, groups)
    normed, scale = stats_of(middle)
    b = (normed * gains[1:2]).astype(BF)
    if saving:
        norm2[...] = normed
        scale2[...] = scale
        dense[...] = b

    def feed(g):
        pre = dot(b, bank[g, :, up:down])
        cdf = normal_cdf(pre)
        act = (pre * cdf).astype(BF)
        if saving:
            slope[g] = cdf + pre * jnp.exp(-0.5 * pre * pre) * INVERSE_ROOT
            active[g] = act
        return dot_rt(act, bank[g, :, down:emb])

    latent = middle + chain(feed, groups)
    lane = lax.broadcasted_iota(jnp.int32, (1, wide), 1)
    if saving:
        for g in range(groups):
            part = turn(latent, 64 - g * local)[:, :wide]
            out[g] = only(lane >= 64, part).astype(BF)
    else:
        t_norm = stats_of(latent)[0].astype(BF)
        chosen = dot(hot[...], t_norm)
        for g in range(groups):
            out[g] = turn(chosen, -g * local)[:, :wide].astype(BF)


def run_encoder(pix, place, keep, bank, gains, sizes, asked, hot=None):
    local, hidden, size = sizes
    groups, width, _ = bank.shape
    rows = place.shape[0]
    wide = local + 64
    heads = HEADS
    bias = ((keep - 1.0) * 1e9)[None, :]
    saving = hot is None
    make = jax.ShapeDtypeStruct
    if saving:
        outs = [
            make((groups, asked, wide), BF),
            make((rows, width), F32),
            make((rows, 1), F32),
            make((rows, width), BF),
            make((groups, asked, wide), BF),
            make((groups, rows, wide), BF),
            make((groups, rows, wide), BF),
            make((heads, asked, rows), F32),
            make((groups, asked, wide), BF),
            make((asked, width), F32),
            make((asked, 1), F32),
            make((asked, width), BF),
            make((groups, asked, hidden), F32),
            make((groups, asked, hidden), BF),
        ]
    else:
        outs = [make((groups, hot.shape[0], wide), BF)]
    ins = [pix, place, bias, bank, gains] + ([] if saving else [hot])
    vmem = pl.BlockSpec(memory_space=pltpu.VMEM)
    return pl.pallas_call(
        functools.partial(encoder_kernel, sizes, asked, saving),
        out_shape=outs,
        in_specs=[vmem] * len(ins),
        out_specs=[vmem] * len(outs),
        compiler_params=pltpu.CompilerParams(vmem_limit_bytes=56 * 2**20),
    )(*ins)


def predictor_kernel(
    sizes, ctx, wanted, place_c, place_t, bias, weight, total, bank, gains,
    grad_ctx, grads, small, loss_out, probs_s, q_s, k_s, v_s, mixed_s, slope_s, active_s, dt_s
):
    local, plocal, phidden, size, blocks = sizes
    groups = bank.shape[0]
    heads = plocal // size
    lanes = 128
    up = 4 * plocal
    down = up + phidden
    head_at = down + phidden
    entry_at = head_at + local
    wide = local + 64
    nctx = place_c.shape[0]
    asked = place_t.shape[0]
    rows = nctx + asked
    tlen = asked // blocks
    first, second, final, token = (gains[i : i + 1] for i in range(4))
    root = size**-0.5

    entry = place_c[...] + chain(
        lambda g: dot_rt(ctx[g], bank[g, :, entry_at - 64 : entry_at + local]), groups
    )
    tgt_in = place_t[...] + token
    norm_c, scale_c = stats_of(entry)
    norm_t, scale_t = stats_of(tgt_in)
    a_c = (norm_c * first).astype(BF)
    a_t = (norm_t * first).astype(BF)
    a = jnp.concatenate([a_c, a_t], 0)

    def attend(g):
        t = dot(a, bank[g, :, :up]).astype(BF).astype(F32)
        q = t[nctx:, :lanes].astype(BF)
        k = turn(t, -plocal)[:, :lanes].astype(BF)
        v = turn(t, -2 * plocal)[:, :lanes].astype(BF)
        q_s[g] = q
        k_s[g] = k
        v_s[g] = v
        mixed = jnp.zeros((asked, lanes), F32)
        for h in range(heads):
            mask = head_lanes(lanes, size, h)
            score = dot_rt(only(mask, q), k) * root + bias[...]
            score = jnp.exp(score - jnp.max(score, -1, keepdims=True))
            probs = score / jnp.sum(score, -1, keepdims=True)
            probs_s[g * heads + h] = probs
            mixed += only(mask, dot(probs.astype(BF), v))
        mixed = turn(mixed, lanes - plocal).astype(BF)
        mixed_s[g] = mixed
        return dot_rt(mixed, bank[g, :, up - lanes : up])

    middle = tgt_in + chain(attend, groups)
    norm2, scale2 = stats_of(middle)
    b = (norm2 * second).astype(BF)

    def feed(g):
        pre = dot(b, bank[g, :, up:down])
        cdf = normal_cdf(pre)
        slope_s[g] = cdf + pre * jnp.exp(-0.5 * pre * pre) * INVERSE_ROOT
        act = (pre * cdf).astype(BF)
        active_s[g] = act
        return dot_rt(act, bank[g, :, down:head_at])

    out = middle + chain(feed, groups)
    norm_f, scale_f = stats_of(out)
    head_in = (norm_f * final).astype(BF)
    lane = lax.broadcasted_iota(jnp.int32, (1, wide), 1)
    losses = jnp.zeros((1, 1), F32)
    row_weight = weight[...]

    def judge(g):
        nonlocal losses
        pred = dot(head_in, bank[g, :, head_at : head_at + wide])
        diff = only(lane < local, pred - wanted[g].astype(F32))
        losses += jnp.sum(row_weight * diff * diff, keepdims=True)
        grad = (2.0 * row_weight * diff / total[...]).astype(BF)
        g_head = dot_lt(head_in, grad)
        grads[g, :, head_at : head_at + lanes] = g_head[:, :lanes]
        grads[g, :, head_at + lanes : head_at + wide] = g_head[:, lanes:]
        return dot_rt(grad, bank[g, :, head_at : head_at + wide])

    grad_out, g_final = norm_back_of(norm_f, scale_f, final, chain(judge, groups))
    loss_out[...] = jnp.broadcast_to(losses, loss_out.shape)

    branch = grad_out.astype(BF)

    def feed_back(g):
        grads[g, :, down:head_at] = dot_lt(branch, active_s[g])
        grad_pre = (dot(branch, bank[g, :, down:head_at]) * slope_s[g]).astype(BF)
        grads[g, :, up:down] = dot_lt(b, grad_pre)
        return dot_rt(grad_pre, bank[g, :, up:down])

    grad_norm, g_second = norm_back_of(norm2, scale2, second, chain(feed_back, groups))
    grad_mid = grad_out + grad_norm
    mixer = grad_mid.astype(BF)

    def attend_back(g):
        g_o = dot_lt(mixer, mixed_s[g])
        gm = turn(dot(mixer, bank[g, :, up - lanes : up]), plocal - lanes).astype(BF)
        q, k, v = (q_s[g], k_s[g], v_s[g])
        valid = head_lanes(lanes, plocal, 0)
        gm = only(valid, gm)
        qv = only(valid, q)
        block = lax.broadcasted_iota(jnp.int32, (asked, 1), 0) // tlen
        q_spread = jnp.concatenate([only(block == i, qv) for i in range(blocks)], 1)
        gm_spread = jnp.concatenate([only(block == i, gm) for i in range(blocks)], 1)
        dqs, dkt, dvt, dkc, dvc = ([], [], [], [], [])
        for h in range(heads):
            mask = head_lanes(lanes, size, h)
            masks = jnp.concatenate([mask] * blocks, 1)
            probs = probs_s[g * heads + h]
            gmh = only(mask, gm)
            grad_probs = dot_rt(gmh, v)
            ds = (probs * (grad_probs - jnp.sum(grad_probs * probs, -1, keepdims=True))).astype(BF)
            pb = probs.astype(BF)
            qh = only(mask, qv)
            dqs.append(dot(ds, only(mask, k)))
            dkt.append(dot_lt(ds[:, nctx:], qh))
            dvt.append(dot_lt(pb[:, nctx:], gmh))
            dkc.append(dot_lt(ds[:, :nctx], only(masks, q_spread)))
            dvc.append(dot_lt(pb[:, :nctx], only(masks, gm_spread)))
        dq = (sum(dqs[1:], dqs[0]) * root).astype(BF).astype(F32)
        dk = (sum(dkt[1:], dkt[0]) * root).astype(BF).astype(F32)
        dv = sum(dvt[1:], dvt[0]).astype(BF).astype(F32)
        kc = (sum(dkc[1:], dkc[0]) * root).astype(BF).astype(F32)
        vc = sum(dvc[1:], dvc[0]).astype(BF).astype(F32)
        kc = chain(lambda i: kc[:, i * lanes : (i + 1) * lanes], blocks)
        vc = chain(lambda i: vc[:, i * lanes : (i + 1) * lanes], blocks)

        def lay(query, keyed, valued):
            count = keyed.shape[0]
            blank = jnp.zeros((count, up - lanes), F32)
            wideq = 0.0 if query is None else jnp.concatenate([query, blank], 1)
            return (
                wideq
                + turn(jnp.concatenate([keyed, blank], 1), plocal)
                + turn(jnp.concatenate([valued, blank], 1), 2 * plocal)
            )

        dt_t = lay(dq, dk, dv).astype(BF)
        dt_c = lay(None, kc, vc)
        high = dt_c.astype(BF)
        low = (dt_c - high.astype(F32)).astype(BF)
        dt = jnp.concatenate([high, dt_t], 0)
        dt_s[g] = jnp.concatenate([dt, low], 0)
        g_qkv = dot_lt(jnp.concatenate([a, a_c], 0), jnp.concatenate([dt, low], 0))
        grads[g, :, : up - lanes] = g_qkv[:, : up - lanes]
        grads[g, :, up - lanes : up] = g_qkv[:, up - lanes :] + g_o

    for g in range(groups):
        attend_back(g)
    grad_a = chain(lambda g: dot_rt(dt_s[g], bank[g, :, :up]), groups)
    grad_in_t, g_first_t = norm_back_of(norm_t, scale_t, first, grad_a[nctx:rows])
    grad_in_c, g_first_c = norm_back_of(
        norm_c, scale_c, first, grad_a[:nctx] + grad_a[rows:]
    )
    g_token = jnp.sum(grad_in_t + grad_mid, 0, keepdims=True)
    small[...] = jnp.concatenate([g_first_t + g_first_c, g_second, g_final, g_token], 0)
    grad_entry = grad_in_c.astype(BF)
    width = groups * local
    grad_context = jnp.zeros((nctx, width), F32)
    for g in range(groups):
        g_entry = dot_lt(grad_entry, ctx[g])
        grads[g, :, entry_at - 64 : entry_at + 64] += g_entry[:, :lanes]
        grads[g, :, entry_at + 64 : entry_at + local] = g_entry[:, lanes:]
        part = only(lane >= 64, dot(grad_entry, bank[g, :, entry_at - 64 : entry_at + local]))
        full = jnp.concatenate([part, jnp.zeros((nctx, width - wide), F32)], 1)
        grad_context += turn(full, g * local - 64)
    grad_ctx[...] = grad_context


def run_predictor(ctx, wanted, place_c, place_t, bias, weight, total, bank, gains, sizes):
    local, plocal, phidden, size, blocks = sizes
    groups = bank.shape[0]
    nctx, pwidth = place_c.shape
    asked = place_t.shape[0]
    rows = nctx + asked
    make = jax.ShapeDtypeStruct
    outs = [
        make((nctx, groups * local), F32),
        make(bank.shape, F32),
        make((4, pwidth), F32),
        make((8, 128), F32),
    ]
    ins = [ctx, wanted, place_c, place_t, bias, weight, total, bank, gains]
    vmem = pl.BlockSpec(memory_space=pltpu.VMEM)
    scratch = [
        pltpu.VMEM((HEADS, asked, rows), F32),
        pltpu.VMEM((groups, asked, 128), BF),
        pltpu.VMEM((groups, rows, 128), BF),
        pltpu.VMEM((groups, rows, 128), BF),
        pltpu.VMEM((groups, asked, 128), BF),
        pltpu.VMEM((groups, asked, phidden), F32),
        pltpu.VMEM((groups, asked, phidden), BF),
        pltpu.VMEM((groups, rows + nctx, 4 * plocal), BF),
    ]
    return pl.pallas_call(
        functools.partial(predictor_kernel, sizes),
        out_shape=outs,
        in_specs=[vmem] * len(ins),
        out_specs=[vmem] * len(outs),
        scratch_shapes=scratch,
        compiler_params=pltpu.CompilerParams(vmem_limit_bytes=56 * 2**20),
    )(*ins)


def encoder_back_kernel(
    sizes, grad_ctx, pix, norm1, scale1, mixer_in, qs, ks, vs, probs_in, mixed_in, norm2, scale2,
    dense, slope, active, bank, gains, grads, small, wide_s, tail_s, dt_s, sems
):
    local, hidden, size = sizes
    groups = bank.shape[0]
    heads = local // size
    up = 4 * local
    down = up + hidden
    emb = down + hidden
    wide = local + 64
    span = 3 * local + 64
    asked = grad_ctx.shape[0]
    rows = norm1.shape[0]
    first, second = (gains[0:1], gains[1:2])
    root = size**-0.5
    grad_out = grad_ctx[...]
    branch = grad_out.astype(BF)

    def ship(g, start, width):
        return pltpu.make_async_copy(
            wide_s.at[g % 2, :, pl.ds(start, width)],
            grads.at[g, :, pl.ds(start, width)],
            sems.at[g % 2],
        )

    def feed_back(g):
        if g >= 2:
            ship(g - 2, up, 2 * hidden).wait()
        wide_s[g % 2, :, down:emb] = dot_lt(branch, active[g])
        grad_pre = (dot(branch, bank[g, :, down:emb]) * slope[g]).astype(BF)
        wide_s[g % 2, :, up:down] = dot_lt(dense[...], grad_pre)
        ship(g, up, 2 * hidden).start()
        return dot_rt(grad_pre, bank[g, :, up:down])

    grad_norm, g_second = norm_back_of(norm2[...], scale2[...], second, chain(feed_back, groups))
    grad_mid = grad_out + grad_norm
    mixer = grad_mid.astype(BF)
    for g in range(groups - 2, groups):
        ship(g, up, 2 * hidden).wait()
    valid = head_lanes(wide, local, 0)

    def attend_back(g):
        g_o = dot_lt(mixer, mixed_in[g])
        gm = turn(dot(mixer, bank[g, :, up - wide : up]), -64).astype(BF)
        q, k, v = (only(valid, qs[g]), ks[g], vs[g])
        gm = only(valid, gm)
        dqs, dks, dvs = ([], [], [])
        for h in range(heads):
            mask = head_lanes(wide, size, h)
            probs = probs_in[g * heads + h]
            gmh = only(mask, gm)
            grad_probs = dot_rt(gmh, v)
            ds = (probs * (grad_probs - jnp.sum(grad_probs * probs, -1, keepdims=True))).astype(BF)
            dqs.append(dot(ds, only(mask, k)))
            dks.append(dot_lt(ds, only(mask, q)))
            dvs.append(dot_lt(probs.astype(BF), gmh))
        dq = (sum(dqs[1:], dqs[0]) * root).astype(BF).astype(F32)
        dk = (sum(dks[1:], dks[0]) * root).astype(BF).astype(F32)
        dv = sum(dvs[1:], dvs[0]).astype(BF).astype(F32)
        dq = jnp.concatenate([dq, jnp.zeros((rows - asked, wide), F32)], 0)
        blank = jnp.zeros((rows, span - wide), F32)
        dt = (
            jnp.concatenate([dq, blank], 1)
            + turn(jnp.concatenate([dk, blank], 1), local)
            + jnp.concatenate([blank, dv], 1)
        ).astype(BF)
        dt_s[g] = dt
        g_qkv = dot_lt(mixer_in[...], dt)
        if g >= 2:
            ship(g - 2, 0, up).wait()
        slot = wide_s.at[g % 2]
        slot[:, : up - wide] = g_qkv[:, : up - wide]
        slot[:, up - wide : span] = g_qkv[:, up - wide :] + g_o[:, : span - up + wide]
        slot[:, span:up] = g_o[:, span - up + wide :]
        ship(g, 0, up).start()

    for g in range(groups):
        attend_back(g)
    grad_a = chain(lambda g: dot_rt(dt_s[g], bank[g, :, :span]), groups)
    grad_start, g_first = norm_back_of(norm1[...], scale1[...], first, grad_a)
    grad_start = (
        grad_start + jnp.concatenate([grad_mid, jnp.zeros((rows - asked, grad_mid.shape[1]), F32)], 0)
    ).astype(BF)
    small[...] = jnp.concatenate([g_first, g_second], 0)

    def tail(g):
        return pltpu.make_async_copy(
            tail_s.at[g], grads.at[g, :, pl.ds(emb, wide)], sems.at[2 + g]
        )

    for g in range(groups):
        tail_s[g] = dot_lt(grad_start, pix[g])
        tail(g).start()
    for g in range(groups - 2, groups):
        ship(g, 0, up).wait()
    for g in range(groups):
        tail(g).wait()


def run_encoder_back(grad_ctx, pix, saved, bank, gains, sizes):
    local, hidden, size = sizes
    groups, width, columns = bank.shape
    rows = pix.shape[1]
    make = jax.ShapeDtypeStruct
    ins = [grad_ctx, pix, *saved, bank, gains]
    vmem = pl.BlockSpec(memory_space=pltpu.VMEM)
    return pl.pallas_call(
        functools.partial(encoder_back_kernel, sizes),
        out_shape=[make(bank.shape, F32), make((2, width), F32)],
        in_specs=[vmem] * len(ins),
        out_specs=[pl.BlockSpec(memory_space=pl.ANY), vmem],
        scratch_shapes=[
            pltpu.VMEM((2, width, 4 * local + 2 * hidden), F32),
            pltpu.VMEM((groups, width, local + 64), F32),
            pltpu.VMEM((groups, rows, 3 * local + 64), BF),
            pltpu.SemaphoreType.DMA((2 + groups,)),
        ],
        compiler_params=pltpu.CompilerParams(vmem_limit_bytes=58 * 2**20),
    )(*ins)


def per_device(
    pixels,
    context_slots,
    context_count,
    target_slots,
    target_count,
    encoder_in,
    encoder_out,
    predictor_in,
    predictor_out,
    vectors,
    first_encoder_in,
    first_encoder_out,
    first_predictor_in,
    first_predictor_out,
    first_vectors,
    second_encoder_in,
    second_encoder_out,
    second_predictor_in,
    second_predictor_out,
    second_vectors,
    target_encoder_in,
    target_encoder_out,
    target_vectors,
):
    groups = lax.axis_size("mp")
    owners = lax.axis_size("role") * lax.axis_size("dp")
    width = encoder_in.shape[0] * owners
    pwidth = predictor_in.shape[0] * owners
    local, plocal = (width // groups, pwidth // groups)
    pixel = pixels.shape[2]
    hidden = encoder_in.shape[1] - 3 * local
    phidden = predictor_in.shape[1] - 3 * plocal - local
    patches = pixels.shape[1]
    image = lax.axis_index("role") * groups + lax.axis_index("mp")

    slots = lax.dynamic_index_in_dim(context_slots, image, 0, keepdims=False)
    count = lax.dynamic_index_in_dim(context_count, image, 0, keepdims=False)
    tslots = lax.dynamic_index_in_dim(target_slots, image, 0, keepdims=False)
    tcount = lax.dynamic_index_in_dim(target_count, image, 0, keepdims=False)
    tsum = jnp.broadcast_to(jnp.sum(tcount).astype(F32), vectors.shape)
    gathered = gather_all(
        [
            pack_encoder(encoder_in, encoder_out, local, pixel, [vectors, tsum]),
            pack_predictor(predictor_in, predictor_out, local, plocal, phidden),
            pack_encoder(target_encoder_in, target_encoder_out, local, pixel, [target_vectors]),
        ]
    )
    bank, pbank, tbank = (g.reshape(groups, -1, g.shape[-1]) for g in gathered)
    extra = 4 * local + 2 * hidden + pixel

    def spread_vector(whole):
        return whole[:, :, extra].reshape(groups, owners, -1).transpose(1, 0, 2).reshape(-1)

    s_vec = spread_vector(bank).astype(F32)
    t_vec = spread_vector(tbank).astype(F32)
    target_total = jnp.sum(gathered[0][:, :, 0, extra + 1].astype(F32))

    half = lax.dynamic_slice_in_dim(pixels, lax.axis_index("role") * groups, groups, 0)
    pix = lax.all_to_all(half, "mp", 0, 0, tiled=True)
    nctx = slots.shape[0]
    blocks, tlen = tslots.shape
    rows = -(-patches // 16) * 16

    patch = jnp.arange(patches)
    hits = slots[:, None] == patch[None, :]
    member = jnp.any(hits, 0)
    order = jnp.where(
        member,
        jnp.sum(jnp.where(hits, jnp.arange(nctx)[:, None], 0), 0),
        nctx + jnp.cumsum(1 - member.astype(jnp.int32)) - 1,
    )
    shuffle = order[None, :] == jnp.arange(rows)[:, None]
    places = jnp.sum(jnp.where(shuffle, patch[None, :] + 1, 0), 1) - 1
    mixed_pix = jnp.einsum(
        "jp,gpk->gjk", shuffle.astype(BF), pix, preferred_element_type=F32
    ).astype(BF)

    def widen(value):
        return jnp.pad(value, ((0, 0), (0, rows - value.shape[1]), (0, 64)))

    ckeep = (jnp.arange(nctx) < count).astype(F32)
    tkeep = (jnp.arange(tlen)[None, :] < tcount[:, None]).astype(F32)
    tflat = tslots.reshape(-1)
    of_block = jnp.arange(blocks * tlen) // tlen
    keys = jnp.concatenate(
        [
            jnp.broadcast_to(ckeep[None], (blocks * tlen, nctx)),
            (of_block[:, None] == of_block[None, :]) * tkeep.reshape(1, -1),
        ],
        1,
    )

    table = sincos(width)
    ptable = sincos(pwidth)
    sizes = (local, hidden, width // HEADS)
    slot_of = jnp.arange(rows)
    hot = (tflat[:, None] == slot_of[None, :]).astype(BF)
    (wanted,) = run_encoder(
        widen(pix),
        np.pad(table, ((0, rows - patches), (0, 0))),
        (slot_of < patches).astype(F32),
        tbank,
        t_vec[: 2 * width].reshape(2, width),
        sizes,
        rows,
        hot,
    )
    student_pix = widen(mixed_pix)
    enc_gains = s_vec[: 2 * width].reshape(2, width)
    context, *saved = run_encoder(
        student_pix,
        pick(table, places),
        (slot_of < count).astype(F32),
        bank,
        enc_gains,
        sizes,
        nctx,
    )
    grad_context, g_pbank, p_small, loss = run_predictor(
        context,
        wanted,
        pick(ptable, slots),
        pick(ptable, tflat),
        (keys - 1.0) * 1e9,
        tkeep.reshape(-1, 1),
        target_total.reshape(1, 1),
        pbank,
        s_vec[2 * width :].reshape(4, pwidth),
        (local, plocal, phidden, pwidth // HEADS, blocks),
    )
    g_bank, e_small = run_encoder_back(grad_context, student_pix, saved, bank, enc_gains, sizes)
    g_vec = jnp.concatenate([e_small.reshape(-1), p_small.reshape(-1)])
    g_vec = g_vec.reshape(owners, groups, 1, -1).transpose(1, 0, 2, 3)
    share = g_vec.shape[3]
    r_bank, r_pbank, r_vec, stats = reduce_all(
        [
            g_bank.reshape(gathered[0].shape),
            g_pbank.reshape(gathered[1].shape),
            jnp.pad(g_vec, ((0, 0), (0, 0), (0, 7), (0, -share % (2 * LANES)))),
        ],
        (BF, F32, F32),
        loss,
    )
    r_pin, r_pout = unpack_predictor(r_pbank, local, plocal, phidden)
    r_in, r_out = unpack_encoder(r_bank, local, hidden, pixel)
    r_vec = r_vec[0, :share]
    loss_total, squares = (stats[0, 0], stats[1, 0])
    grad_norm = jnp.sqrt(squares)
    scale = jnp.minimum(1.0, CLIP / (grad_norm + 1e-06))
    new_in, m_in, v_in = adamw(
        encoder_in, r_in, first_encoder_in, second_encoder_in, scale, RATE_MATRIX, DECAY
    )
    new_out, m_out, v_out = adamw(
        encoder_out, r_out, first_encoder_out, second_encoder_out, scale, RATE_MATRIX, DECAY
    )
    new_pin, m_pin, v_pin = adamw(
        predictor_in, r_pin, first_predictor_in, second_predictor_in, scale, RATE_MATRIX, DECAY
    )
    new_pout, m_pout, v_pout = adamw(
        predictor_out, r_pout, first_predictor_out, second_predictor_out, scale, RATE_MATRIX, DECAY
    )
    new_vec, m_vec, v_vec = adamw(
        vectors, r_vec, first_vectors, second_vectors, scale, RATE_VECTOR, 0.0
    )
    ema_in = MOMENTUM_EMA * target_encoder_in + (1.0 - MOMENTUM_EMA) * new_in
    ema_out = MOMENTUM_EMA * target_encoder_out + (1.0 - MOMENTUM_EMA) * new_out
    ema_vec = MOMENTUM_EMA * target_vectors + (1.0 - MOMENTUM_EMA) * new_vec
    return (
        new_in, new_out, new_pin, new_pout, new_vec,
        m_in, m_out, m_pin, m_pout, m_vec,
        v_in, v_out, v_pin, v_pout, v_vec,
        ema_in, ema_out, ema_vec,
        loss_total, target_total, grad_norm,
    )


def solution(mesh):
    bank_in, bank_out, small = (
        P(("role", "dp"), "mp"),
        P("mp", ("role", "dp")),
        P(("role", "dp", "mp")),
    )
    five = (bank_in, bank_out, bank_in, bank_out, small)
    three = (bank_in, bank_out, small)
    return jax.shard_map(
        per_device,
        mesh=mesh,
        in_specs=(
            P("dp", None, "mp"),
            P("dp", None),
            P("dp"),
            P("dp", None, None),
            P("dp", None),
        )
        + five * 3
        + three,
        out_specs=five * 3 + three + (P(), P(), P()),
        check_vma=False,
    )
```

```python
import functools

import jax
import jax.numpy as jnp
import numpy as np
from jax import lax
from jax.experimental import pallas as pl
from jax.experimental.pallas import tpu as pltpu
from jax.sharding import PartitionSpec as P

HEADS = 12
GRID = 14
STEP = 10

BETA_ONE = 0.9
BETA_TWO = 0.999
ADAM_EPS = 1e-08
RATE_MATRIX = 0.03
RATE_VECTOR = 0.3
DECAY = 0.05
MOMENTUM_EMA = 0.9
CLIP = 0.1
ROOT_HALF = 0.7071067811865476
INVERSE_ROOT = 0.3989422804014327

BF = jnp.bfloat16
F32 = jnp.float32
LANES = 128


def sincos(width):
    quarter = width // 4
    omega = 1.0 / 10000.0 ** (np.arange(quarter, dtype=np.float64) / quarter)
    place = np.arange(GRID * GRID)
    rows = (place // GRID)[:, None] * omega[None, :]
    cols = (place % GRID)[:, None] * omega[None, :]
    return np.concatenate([np.sin(rows), np.cos(rows), np.sin(cols), np.cos(cols)], -1).astype(
        np.float32
    )


def in_three(table):
    parts, rest = ([], table)
    for _ in range(3):
        parts.append(rest.astype(jnp.bfloat16))
        rest = rest - parts[-1].astype(np.float32)
    return np.concatenate(parts, 1)


def pick(table, places):
    hot = (places[:, None] == jnp.arange(table.shape[0])[None, :]).astype(BF)
    rows = jnp.dot(hot, in_three(table), preferred_element_type=F32)
    width = table.shape[1]
    return rows[:, :width] + rows[:, width : 2 * width] + rows[:, 2 * width :]


def chunk_list(arrays):
    return tuple(
        (array, start, min(step, columns - start))
        for array, columns, step in arrays
        for start in range(0, columns, step)
    )


def pack_encoder(w_in, w_out, local, pixel):
    turned = w_out.T
    used = w_in.shape[1] + turned.shape[1]
    return jnp.concatenate(
        [
            w_in[:, : 3 * local],
            turned[:, pixel : pixel + local],
            w_in[:, 3 * local :],
            turned[:, pixel + local :],
            turned[:, :pixel],
            jnp.zeros((w_in.shape[0], -used % (2 * LANES)), F32),
        ],
        1,
    ).astype(BF)


def unpack_encoder(packed, local, hidden, pixel):
    up = 4 * local
    down = up + hidden
    emb = down + hidden
    w_in = jnp.concatenate([packed[:, : 3 * local], packed[:, up:down]], 1)
    turned = jnp.concatenate(
        [packed[:, emb : emb + pixel], packed[:, 3 * local : up], packed[:, down:emb]], 1
    )
    return (w_in, turned.T)


def pack_predictor(p_in, p_out, local, plocal, phidden):
    turned = p_out.T
    return jnp.concatenate(
        [
            p_in[:, : 3 * plocal],
            turned[:, local : local + plocal],
            p_in[:, 3 * plocal : 3 * plocal + phidden],
            turned[:, local + plocal :],
            p_in[:, 3 * plocal + phidden :],
            turned[:, :local],
        ],
        1,
    ).astype(BF)


def unpack_predictor(packed, local, plocal, phidden):
    up = 4 * plocal
    down = up + phidden
    head = down + phidden
    entry = head + local
    p_in = jnp.concatenate(
        [packed[:, : 3 * plocal], packed[:, up:down], packed[:, head:entry]], 1
    )
    turned = jnp.concatenate(
        [packed[:, entry:], packed[:, 3 * plocal : up], packed[:, down:head]], 1
    )
    return (p_in, turned.T)


def adamw(weight, grad, first, second, scale, rate, decay):
    grad = grad * scale
    first = BETA_ONE * first + (1.0 - BETA_ONE) * grad
    second = BETA_TWO * second + (1.0 - BETA_TWO) * grad * grad
    mean_hat = first / (1.0 - BETA_ONE**STEP)
    square_hat = second / (1.0 - BETA_TWO**STEP)
    return (
        weight - rate * (mean_hat / (jnp.sqrt(square_hat) + ADAM_EPS) + decay * weight),
        first,
        second,
    )


def shift_of(rank, by):
    return jnp.bitwise_xor(rank, by)


def greet(peers):
    barrier = pltpu.get_barrier_semaphore()
    for peer in peers:
        pl.semaphore_signal(barrier, inc=1, device_id=peer, device_id_type=pl.DeviceIdType.MESH)
    pl.semaphore_wait(barrier, len(peers))


def remote(src, dst, send, recv, where):
    return pltpu.make_async_remote_copy(
        src_ref=src, dst_ref=dst, send_sem=send, recv_sem=recv,
        device_id=where, device_id_type=pl.DeviceIdType.MESH,
    )


class Gather:
    def __init__(self, place, source, target, rows, cols, first, sems, where, nz):
        (self.zs, self.zr, self.xs, self.xr, self.ys, self.yr, self.rxs, self.rxr, self.rys,
         self.ryr, self.bs, self.br, self.bzs, self.bzr, self.cs, self.cr, self.own) = sems
        self.k = place
        self.source, self.target = (source, target)
        self.rows, self.cols, self.first, self.nz = (rows, cols, first, nz)
        self.r, self.d, self.m = where
        self.base = self.r * nz
        self.mx, self.my, self.mf = (shift_of(self.m, by) for by in (1, 2, 3))

    def at(self, column, owner, count, start, width):
        if len(self.target.shape) == 4:
            return self.target.at[column, pl.ds(owner, count), :, pl.ds(start, width)]
        row = pl.multiple_of(owner * self.rows, self.rows)
        return self.target.at[column, pl.ds(row, count * self.rows), pl.ds(start, width)]

    def mine(self, start, width):
        if len(self.target.shape) == 4:
            return self.source.at[:, :, pl.ds(start, width)]
        return self.source.at[:, pl.ds(start, width)]

    def line(self, piece, way, own=False):
        spot = self.at(self.m, self.base + piece, 1, 0, self.first)
        return remote(
            self.mine(0, self.first) if own else spot, spot,
            self.zs.at[self.k, way, piece], self.zr.at[self.k, way, piece],
            {"dp": self.d + 1 - 2 * way},
        )

    def across(self, piece, own=False):
        spot = self.at(self.m, self.base + piece, 1, 0, self.first)
        source = self.mine(0, self.first) if own else spot
        return (
            remote(source, spot, self.xs.at[self.k, piece], self.xr.at[self.k, piece], {"mp": self.mx}),
            remote(source, spot, self.ys.at[self.k, piece], self.yr.at[self.k, piece], {"mp": self.my}),
        )

    def arrived(self, piece):
        return [
            remote(spot, spot, send.at[self.k, piece], recv.at[self.k, piece], {"mp": peer})
            for spot, send, recv, peer in (
                (self.at(self.mx, self.base + piece, 1, 0, self.first), self.xs, self.xr, self.mx),
                (self.at(self.my, self.base + piece, 1, 0, self.first), self.ys, self.yr, self.my),
            )
        ]

    def halves(self, low, high, piece):
        half = self.first // 2 if self.first % 256 == 0 else self.first
        one = self.at(low, self.base + piece, 1, 0, half)
        copies = [remote(one, one, self.rys.at[self.k, piece], self.ryr.at[self.k, piece], {"mp": self.my})]
        if half < self.first:
            two = self.at(high, self.base + piece, 1, half, half)
            copies.append(
                remote(two, two, self.rxs.at[self.k, piece], self.rxr.at[self.k, piece], {"mp": self.mx})
            )
        return copies

    def relay(self, piece):
        return self.halves(self.mx, self.my, piece)

    def diagonal(self, piece):
        return self.halves(self.mf, self.mf, piece)

    def late_across(self):
        width = self.cols - self.first
        spot = self.at(self.m, self.base + self.d, 1, self.first, width)
        source = self.mine(self.first, width)
        return (
            remote(source, spot, self.bs.at[self.k, 0], self.br.at[self.k, 0], {"mp": self.mx}),
            remote(source, spot, self.bs.at[self.k, 1], self.br.at[self.k, 1], {"mp": self.my}),
        )

    def late_arrived(self):
        width = self.cols - self.first
        spots = [self.at(c, self.base + self.d, 1, self.first, width) for c in (self.mx, self.my)]
        return [
            remote(spot, spot, self.bs.at[self.k, i], self.br.at[self.k, i], {"mp": peer})
            for i, (spot, peer) in enumerate(zip(spots, (self.mx, self.my)))
        ]

    def late_halves(self, low, high):
        half = (self.cols - self.first) // 2
        one = self.at(low, self.base + self.d, 1, self.first, half)
        two = self.at(high, self.base + self.d, 1, self.first + half, half)
        return (
            remote(one, one, self.bs.at[self.k, 2], self.br.at[self.k, 2], {"mp": self.my}),
            remote(two, two, self.bs.at[self.k, 3], self.br.at[self.k, 3], {"mp": self.mx}),
        )

    def late_line(self, piece, way):
        spot = self.at(slice(None), self.base + piece, 1, self.first, self.cols - self.first)
        return remote(
            spot, spot, self.bzs.at[self.k, way, piece], self.bzr.at[self.k, way, piece],
            {"dp": self.d + 1 - 2 * way},
        )

    def core(self, slot, incoming=False):
        base = (1 - self.r) * self.nz if incoming else self.base
        if slot == 4:
            spot = self.at(slice(None), base, self.nz, self.first, self.cols - self.first)
        else:
            column = (self.m, self.mx, self.my, self.mf)[slot]
            spot = self.at(column, base, self.nz, 0, self.first)
        return remote(spot, spot, self.cs.at[self.k, slot], self.cr.at[self.k, slot], {"role": 1 - self.r})

    def copy_own(self):
        return pltpu.make_async_copy(
            self.mine(0, self.cols), self.at(self.m, self.base + self.d, 1, 0, self.cols),
            self.own.at[self.k],
        )

    def start(self):
        d, nz = (self.d, self.nz)

        @pl.when(d < nz - 1)
        def _():
            self.line(d, 0, True).start()

        @pl.when(d > 0)
        def _():
            self.line(d, 1, True).start()

        for copy in self.across(d, True):
            copy.start()
        if self.first < self.cols:
            for copy in self.late_across():
                copy.start()
        self.copy_own().start()

    def pass_on(self, piece):
        for copy in self.arrived(piece):
            copy.wait_recv()
        for copy in self.relay(piece):
            copy.start()

    def step(self, t):
        d, nz = (self.d, self.nz)
        left = d - 1 - t
        right = d + 1 + t

        @pl.when(left >= 0)
        def _():
            self.line(left, 0).wait_recv()

            @pl.when(d < nz - 1)
            def _():
                self.line(left, 0).start()

            for copy in self.across(left):
                copy.start()

        @pl.when(right < nz)
        def _():
            self.line(right, 1).wait_recv()

            @pl.when(d > 0)
            def _():
                self.line(right, 1).start()

            for copy in self.across(right):
                copy.start()

        if t == 0:
            self.pass_on(d)
        else:
            @pl.when(left + 1 >= 0)
            def _():
                self.pass_on(left + 1)

            @pl.when(right - 1 < nz)
            def _():
                self.pass_on(right - 1)

    def late_turn(self):
        for copy in self.late_arrived():
            copy.wait_recv()
        for copy in self.late_halves(self.mx, self.my):
            copy.start()

    def late_start(self):
        for copy in self.late_halves(self.mf, self.mf):
            copy.wait_recv()
        self.copy_own().wait()

        @pl.when(self.d < self.nz - 1)
        def _():
            self.late_line(self.d, 0).start()

        @pl.when(self.d > 0)
        def _():
            self.late_line(self.d, 1).start()

    def late_step(self, t):
        d, nz = (self.d, self.nz)
        left = d - 1 - t
        right = d + 1 + t

        @pl.when(left >= 0)
        def _():
            self.late_line(left, 0).wait_recv()

            @pl.when(d < nz - 1)
            def _():
                self.late_line(left, 0).start()

        @pl.when(right < nz)
        def _():
            self.late_line(right, 1).wait_recv()

            @pl.when(d > 0)
            def _():
                self.late_line(right, 1).start()

    def last_pass(self):
        @pl.when(self.d == self.nz - 1)
        def _():
            self.pass_on(0)

        if self.nz > 1:
            @pl.when(self.d == 0)
            def _():
                self.pass_on(self.nz - 1)

        if self.first == self.cols:
            self.copy_own().wait()
        for slot in range(3):
            self.core(slot).start()

    def take_diagonal(self):
        def take(piece, carry):
            for copy in self.diagonal(piece):
                copy.wait_recv()
            return carry

        lax.fori_loop(0, self.nz, take, 0)
        self.core(3).start()
        if self.first < self.cols:
            self.core(4).start()

    def steps(self):
        late = self.first < self.cols
        early = [functools.partial(self.step, t) for t in range(self.nz - 1)] + [self.last_pass]
        late = []
        if self.first < self.cols:
            late = [self.late_turn, self.late_start]
            late += [functools.partial(self.late_step, t) for t in range(self.nz - 1)]
        todo = []
        while early or late:
            todo += early[:1] + late[:1]
            early, late = (early[1:], late[1:])
        return todo

    def complete(self):
        for slot in range(5 if self.first < self.cols else 4):
            self.core(slot, True).wait_recv()

    def finish(self):
        d, nz = (self.d, self.nz)
        late = self.first < self.cols
        for slot in range(5 if late else 4):
            self.core(slot).wait_send()
        if late:
            for copy in self.late_across() + self.late_halves(self.mx, self.my):
                copy.wait_send()

        def done(piece, carry):
            for copy in self.across(piece):
                copy.wait_send()
            for copy in self.relay(piece):
                copy.wait_send()

            @pl.when(jnp.logical_and(piece <= d, d < nz - 1))
            def _():
                self.line(piece, 0).wait_send()
                if late:
                    self.late_line(piece, 0).wait_send()

            @pl.when(jnp.logical_and(piece >= d, d > 0))
            def _():
                self.line(piece, 1).wait_send()
                if late:
                    self.late_line(piece, 1).wait_send()

            return carry

        lax.fori_loop(0, nz, done, 0)


def gather_sems(count, nz):
    dma = pltpu.SemaphoreType.DMA
    piece = [dma((count, nz))] * 8
    return (
        [dma((count, 2, nz))] * 2 + piece + [dma((count, 4))] * 2 + [dma((count, 2, nz))] * 2
        + [dma((count, 5))] * 2 + [dma((count,))]
    )


def reduce_kernel(nz, chunks, ring, count, stats_in, *refs):
    n = len(chunks)
    ins = refs[:count]
    outs = refs[count : 2 * count]
    stats_out = refs[2 * count]
    rest = refs[2 * count + 1 :]
    accs = rest[:n]
    sends1 = rest[n : 2 * n]
    recvs1 = rest[2 * n : 3 * n]
    sends2 = rest[3 * n : 4 * n]
    recvs2 = rest[4 * n : 5 * n]
    lines = rest[5 * n : 6 * n]
    rest = rest[6 * n :]
    kinds = sorted(set(ring))
    buffers = {kind: rest[3 * i : 3 * i + 3] for i, kind in enumerate(kinds)}
    (near, near_in, far_in, ld, cs, cr, s1s, s1r, s2s, s2r, zs, zr, ns, nr, fs, fr) = rest[
        3 * len(kinds) :
    ]
    turns = [ring[:k].count(kind) for k, kind in enumerate(ring)]
    r = lax.axis_index("role")
    d = lax.axis_index("dp")
    m = lax.axis_index("mp")
    groups = 4
    mx = shift_of(m, 1)
    my = shift_of(m, 2)
    mf = shift_of(m, 3)
    columns = (mf, mx, my, m)
    group = [
        {"role": role, "mp": shift_of(m, by)}
        for role in (r, 1 - r)
        for by in range(groups)
    ][1:]
    far = [{"dp": lax.rem(d + j, nz)} for j in range(1, nz)]
    greet(group + far)

    def part(k, column, first):
        array, start, width = chunks[k]
        return ins[array].at[column, pl.ds(first, nz), :, pl.ds(start, width)]

    def core(k, j):
        return remote(
            part(k, columns[j], (1 - r) * nz), accs[k].at[j], cs.at[k, j], cr.at[k, j],
            {"role": 1 - r},
        )

    def loaded(k, j):
        far_ring, near_ring, own_ring = buffers[ring[k]]
        if j == 0:
            return far_ring.at[turns[k] % 3]
        if j == 3:
            return own_ring.at[turns[k] % 2]
        return near_ring.at[turns[k] % 2, j - 1]

    def load(k, j):
        return pltpu.make_async_copy(part(k, columns[j], r * nz), loaded(k, j), ld.at[k, j])

    def first(k, piece):
        half = chunks[k][2] // 2
        low, high = (pl.ds(0, half), pl.ds(half, half))
        return (
            remote(sends1[k].at[piece, :, low], recvs1[k].at[piece, :, low],
                   s1s.at[k, 0, piece], s1r.at[k, 0, piece], {"mp": my}),
            remote(sends1[k].at[piece, :, high], recvs1[k].at[piece, :, high],
                   s1s.at[k, 1, piece], s1r.at[k, 1, piece], {"mp": mx}),
        )

    def second(k, piece):
        return (
            remote(sends2[k].at[0, piece], recvs2[k].at[0, piece],
                   s2s.at[k, 0, piece], s2r.at[k, 0, piece], {"mp": mx}),
            remote(sends2[k].at[1, piece], recvs2[k].at[1, piece],
                   s2s.at[k, 1, piece], s2r.at[k, 1, piece], {"mp": my}),
        )

    def right(k, piece):
        return remote(accs[k].at[3, piece], lines[k].at[piece], zs.at[k, piece],
                      zr.at[k, piece], {"dp": d + 1})

    def left(k, piece):
        slot = jnp.where(piece == d - 1, nz, piece)
        return remote(accs[k].at[3, piece], lines[k].at[slot], zs.at[k, piece],
                      zr.at[k, slot], {"dp": d - 1})

    def line_in(k, slot):
        return remote(lines[k].at[slot], lines[k].at[slot], zs.at[k, 0], zr.at[k, slot],
                      {"role": 1 - r})

    def each(body):
        def step(t, carry):
            off = nz - 1 - t

            @pl.when(d + off < nz)
            def _():
                body(d + off)

            @pl.when(d - off >= 0)
            def _():
                body(d - off)

            return carry

        lax.fori_loop(0, nz - 1, step, 0)
        body(d)

    def fetch(k):
        for j in range(groups):
            core(k, j).start()
        load(k, 0).start()

    def combine(k, j):
        core(k, j).wait_recv()
        load(k, j).wait()

    def to_far(k):
        load(k, 1).start()
        load(k, 2).start()
        combine(k, 0)

        def send_far(piece):
            sends1[k][piece] = (accs[k][0, piece] + loaded(k, 0)[piece]).astype(sends1[k].dtype)
            for copy in first(k, piece):
                copy.start()

        each(send_far)

    def to_near(k):
        half = chunks[k][2] // 2
        load(k, 3).start()
        combine(k, 1)
        combine(k, 2)

        def send_near(piece):
            for copy in first(k, piece):
                copy.wait_recv()
            relayed = recvs1[k][piece].astype(jnp.float32)
            lane = lax.broadcasted_iota(jnp.int32, relayed.shape, 1)
            sends2[k][0, piece] = (
                accs[k][1, piece] + loaded(k, 1)[piece] + jnp.where(lane < half, relayed, 0.0)
            ).astype(sends2[k].dtype)
            sends2[k][1, piece] = (
                accs[k][2, piece] + loaded(k, 2)[piece] + jnp.where(lane < half, 0.0, relayed)
            ).astype(sends2[k].dtype)
            for copy in second(k, piece):
                copy.start()

        each(send_near)

    def to_line(k):
        combine(k, 3)

        def pass_on(piece):
            for copy in second(k, piece):
                copy.wait_recv()
            accs[k][3, piece] += (
                loaded(k, 3)[piece]
                + recvs2[k][0, piece].astype(jnp.float32)
                + recvs2[k][1, piece].astype(jnp.float32)
            )

            @pl.when(piece > d)
            def _():
                @pl.when(d > 0)
                def _():
                    line_in(k, piece).wait_recv()
                    accs[k][3, piece] += lines[k][piece]

                right(k, piece).start()

            @pl.when(piece < d)
            def _():
                @pl.when(d < nz - 1)
                def _():
                    line_in(k, piece).wait_recv()
                    accs[k][3, piece] += lines[k][piece]

                left(k, piece).start()

        each(pass_on)

    def land(k):
        array, start, width = chunks[k]

        @pl.when(d > 0)
        def _():
            line_in(k, d).wait_recv()
            accs[k][3, d] += lines[k][d]

        @pl.when(d < nz - 1)
        def _():
            line_in(k, nz).wait_recv()
            accs[k][3, d] += lines[k][nz]

        total = accs[k][3, d]
        outs[array][:, start : start + width] = total
        return jnp.sum(total * total, keepdims=True)

    ahead = 2
    for k in range(min(ahead, n)):
        fetch(k)
    squares = jnp.zeros((1, 1), jnp.float32)
    for step in range(n + 3):
        if step + ahead < n:
            fetch(step + ahead)
        if step < n:
            to_far(step)
        if 0 <= step - 1 < n:
            to_near(step - 1)
        if 0 <= step - 2 < n:
            to_line(step - 2)
        if 0 <= step - 3 < n:
            squares += land(step - 3)

    mine = r * groups + m
    row = lax.broadcasted_iota(jnp.int32, (8, 128), 0)
    near[...] = jnp.where(row == 0, stats_in[...], squares)
    near_in[mine] = near[...]
    copies = []
    for j, peer in enumerate(group):
        copies.append(remote(near, near_in.at[mine], ns.at[j], nr.at[mine], peer))
        copies[-1].start()
    for j, peer in enumerate(group):
        slot = peer["role"] * groups + peer["mp"]
        remote(near, near_in.at[slot], ns.at[j], nr.at[slot], peer).wait_recv()
    for copy in copies:
        copy.wait_send()
    summed = near_in[0]
    for j in range(1, 2 * groups):
        summed += near_in[j]
    near[...] = summed
    far_in[d] = summed
    copies = []
    for j, peer in enumerate(far):
        copies.append(remote(near, far_in.at[d], fs.at[j], fr.at[d], peer))
        copies[-1].start()
    for j, peer in enumerate(far):
        slot = peer["dp"]
        remote(near, far_in.at[slot], fs.at[j], fr.at[slot], peer).wait_recv()
    for copy in copies:
        copy.wait_send()
    summed = far_in[0]
    for j in range(1, nz):
        summed += far_in[j]
    stats_out[...] = summed

    for k in range(n):
        for j in range(groups):
            core(k, j).wait_send()

        def done(piece, carry):
            for copy in first(k, piece):
                copy.wait_send()
            for copy in second(k, piece):
                copy.wait_send()

            @pl.when(piece != d)
            def _():
                right(k, piece).wait_send()

            return carry

        lax.fori_loop(0, nz, done, 0)


def reduce_all(grads, wire_types, chunks, stats):
    nz = lax.axis_size("dp")
    groups = lax.axis_size("mp")
    count = len(grads)
    n = len(chunks)
    dma = pltpu.SemaphoreType.DMA
    shapes = [(grads[array].shape[2], width) for array, _, width in chunks]
    kinds = sorted(set(shapes))
    ring = tuple(kinds.index(s) for s in shapes)
    wires = [wire_types[array] for array, _, _ in chunks]
    vmem = pl.BlockSpec(memory_space=pltpu.VMEM)
    scratch = (
        [pltpu.VMEM((groups, nz, *s), jnp.float32) for s in shapes]
        + [pltpu.VMEM((nz, *s), t) for s, t in zip(shapes, wires)] * 2
        + [pltpu.VMEM((2, nz, *s), t) for s, t in zip(shapes, wires)] * 2
        + [pltpu.VMEM((nz + 1, *s), jnp.float32) for s in shapes]
        + [
            pltpu.VMEM((*slots, nz, *kinds[kind]), jnp.float32)
            for kind in range(len(kinds))
            for slots in ((min(3, ring.count(kind)),), (min(2, ring.count(kind)), 2), (min(2, ring.count(kind)),))
        ]
        + [
            pltpu.VMEM((8, 128), jnp.float32),
            pltpu.VMEM((2 * groups, 8, 128), jnp.float32),
            pltpu.VMEM((nz, 8, 128), jnp.float32),
            dma((n, groups)),
            dma((n, groups)),
            dma((n, groups)),
            dma((n, 2, nz)),
            dma((n, 2, nz)),
            dma((n, 2, nz)),
            dma((n, 2, nz)),
            dma((n, nz)),
            dma((n, nz + 1)),
            dma((2 * groups,)),
            dma((2 * groups,)),
            dma((nz,)),
            dma((nz,)),
        ]
    )
    return pl.pallas_call(
        functools.partial(reduce_kernel, nz, chunks, ring, count),
        out_shape=[jax.ShapeDtypeStruct(g.shape[2:], jnp.float32) for g in grads]
        + [jax.ShapeDtypeStruct((8, 128), jnp.float32)],
        in_specs=[vmem] + [pl.BlockSpec(memory_space=pl.ANY)] * count,
        out_specs=[vmem] * (count + 1),
        scratch_shapes=scratch,
        compiler_params=pltpu.CompilerParams(
            collective_id=2, has_side_effects=True, vmem_limit_bytes=60 * 2**20
        ),
    )(stats, *grads)


def dot(left, right):
    return lax.dot_general(left, right, (((1,), (0,)), ((), ())), preferred_element_type=F32)


def dot_rt(left, right):
    return lax.dot_general(left, right, (((1,), (1,)), ((), ())), preferred_element_type=F32)


def dot_lt(left, right):
    return lax.dot_general(left, right, (((0,), (0,)), ((), ())), preferred_element_type=F32)


def chain(term, count):
    total = term(0)
    for g in range(1, count):
        total += term(g)
    return total


def head_lanes(lanes, size, head):
    lane = lax.broadcasted_iota(jnp.int32, (1, lanes), 1)
    return jnp.logical_and(lane >= head * size, lane < (head + 1) * size)


def only(mask, value):
    return jnp.where(mask, value, jnp.zeros_like(value))


def turn(value, by):
    return pltpu.roll(value, by % value.shape[1], 1)


def stats_of(stream):
    mean = jnp.mean(stream, -1, keepdims=True)
    cent = stream - mean
    scale = lax.rsqrt(jnp.mean(cent * cent, -1, keepdims=True) + 1e-06)
    return (cent * scale, scale)


def norm_back_of(normed, scale, gain, grad):
    gain_grad = jnp.sum(grad * normed, 0, keepdims=True)
    scaled = grad * gain
    inner = (
        scaled
        - jnp.mean(scaled, -1, keepdims=True)
        - normed * jnp.mean(scaled * normed, -1, keepdims=True)
    )
    return (scale * inner, gain_grad)


def normal_cdf(hidden):
    return 0.5 * (1.0 + lax.erf(hidden * ROOT_HALF))


def encoder_forward(sizes, asked, pix, place, bias, bank, gains, keep_refs, finish):
    local, hidden, size = sizes
    groups = bank.shape[0]
    heads = local // size
    up = 4 * local
    down = up + hidden
    emb = down + hidden
    wide = local + 64
    saving = keep_refs is not None
    if saving:
        (norm1, scale1, mixer_in, qs, ks, vs, probs_out, mixed_out, norm2, scale2, dense, slope,
         active) = keep_refs
    terms = None
    for g in range(groups):
        term = dot_rt(pix[g], bank[g, :, emb : emb + wide])
        terms = term if terms is None else terms + term
    start = place() + terms
    normed, scale = stats_of(start)
    a = (normed * gains[0]).astype(BF)
    if saving:
        norm1[...] = normed
        scale1[...] = scale
        mixer_in[...] = a
    yield
    terms = None
    for g in range(groups):
        t = dot(a, bank[g, :, : 3 * local + 64]).astype(BF).astype(F32)
        q = t[:asked, :wide].astype(BF)
        k = turn(t, -local)[:, :wide].astype(BF)
        v = t[:, 2 * local :].astype(BF)
        if saving:
            qs[g] = q
            ks[g] = k
            vs[g] = v
        mixed = jnp.zeros((asked, wide), F32)
        for h in range(heads):
            mask = head_lanes(wide, size, h)
            score = dot_rt(only(mask, q), k) * size**-0.5 + bias[...]
            score = jnp.exp(score - jnp.max(score, -1, keepdims=True))
            probs = score / jnp.sum(score, -1, keepdims=True)
            if saving:
                probs_out[g * heads + h] = probs
            mixed += only(mask, dot(probs.astype(BF), v))
        mixed = turn(mixed, 64).astype(BF)
        if saving:
            mixed_out[g] = mixed
        term = dot_rt(mixed, bank[g, :, up - wide : up])
        terms = term if terms is None else terms + term
        yield
    middle = start[:asked] + terms
    normed, scale = stats_of(middle)
    b = (normed * gains[1]).astype(BF)
    if saving:
        norm2[...] = normed
        scale2[...] = scale
        dense[...] = b
    terms = None
    for g in range(groups):
        pre = dot(b, bank[g, :, up:down])
        cdf = normal_cdf(pre)
        act = (pre * cdf).astype(BF)
        if saving:
            slope[g] = cdf + pre * jnp.exp(-0.5 * pre * pre) * INVERSE_ROOT
            active[g] = act
        term = dot_rt(act, bank[g, :, down:emb])
        terms = term if terms is None else terms + term
        yield
    finish(middle + terms)


def front_kernel(nz, sizes, asked, firsts, *refs):
    local, hidden, size = sizes
    wide = local + 64
    sources, refs = (refs[:4], refs[4:])
    (half, tables, shuffle, bias_t, bias_s, hot), refs = (refs[:6], refs[6:])
    (bank_out, pbank_out, context, wanted, pix_s, vec_rows, total), refs = (refs[:7], refs[7:])
    keep_refs, refs = (refs[:13], refs[13:])
    (vec_all, tbank, bank, pix_t, px, pr, own_sem, out_sem), sems = (refs[:8], refs[8:])
    r = lax.axis_index("role")
    d = lax.axis_index("dp")
    m = lax.axis_index("mp")
    groups = tbank.shape[0]
    width = tbank.shape[1]
    nears = [{"mp": shift_of(m, by)} for by in range(1, groups)]
    greet([{"role": 1 - r}] + nears + [{"dp": lax.rem(d + j, nz)} for j in range(1, nz)])
    targets = (vec_all, tbank, bank, pbank_out)
    arrays = [
        Gather(k, sources[k], targets[k], sources[k].shape[-2], sources[k].shape[-1], firsts[k],
               sems, (r, d, m), nz)
        for k in range(4)
    ]
    small, teach, learn, guess = arrays

    def pixel(j):
        peer = shift_of(m, j)
        return remote(half.at[peer], pix_t.at[m], px.at[j], pr.at[j], {"mp": peer})

    def pixel_in(j):
        peer = shift_of(m, j)
        return remote(half.at[peer], pix_t.at[peer], px.at[j], pr.at[j], {"mp": peer})

    own_pixel = pltpu.make_async_copy(half.at[m], pix_t.at[m], own_sem.at[0])
    own_pixel.start()
    small.start()
    for j in range(1, groups):
        pixel(j).start()
    teach.start()
    for step in small.steps():
        step()

    def place():
        rows = tables[...].astype(F32)
        return rows[:, :width] + rows[:, width : 2 * width] + rows[:, 2 * width :]

    def place_shuffled():
        rows = dot(shuffle[...], tables[...])
        return rows[:, :width] + rows[:, width : 2 * width] + rows[:, 2 * width :]

    for j, step in enumerate(teach.steps()):
        if j == 3:
            learn.start()
        step()
        if j == 1:
            small.take_diagonal()
    small.complete()

    share = vec_rows.shape[1] * 4 // (vec_all.shape[0] * vec_all.shape[1])
    lanes = vec_all.shape[3]
    lane = lax.broadcasted_iota(jnp.int32, (1, lanes), 1)

    def vector_row(kind, j):
        row = jnp.zeros((1, width), F32)
        count = width // share
        for c in range(count):
            flat = j * count + c
            piece = vec_all[flat % groups, flat // groups].astype(F32)[kind : kind + 1]
            piece = only(lane < share, piece)
            row += turn(jnp.concatenate([piece, jnp.zeros((1, width - lanes), F32)], 1), c * share)
        return row

    gains_t = [vector_row(1, j) for j in range(2)]
    rows_s = [vector_row(0, j) for j in range(4)]
    vec_rows[...] = jnp.concatenate(rows_s, 0)
    counts = jnp.zeros((1, 1), F32)
    for c in range(groups):
        for o in range(vec_all.shape[1]):
            counts += vec_all[c, o].astype(F32)[2:3, :1]
    total[...] = jnp.broadcast_to(counts, total.shape)
    own_pixel.wait()
    for j in range(1, groups):
        pixel_in(j).wait_recv()
    for g in range(groups):
        pix_s[g] = dot(shuffle[...], pix_t[g]).astype(BF)

    def teacher_rows(latent):
        chosen = dot(hot[...], stats_of(latent)[0].astype(BF))
        for g in range(groups):
            wanted[g] = turn(chosen, -g * local)[:, :wide].astype(BF)

    def student_rows(latent):
        at = lax.broadcasted_iota(jnp.int32, (1, wide), 1)
        for g in range(groups):
            context[g] = only(at >= 64, turn(latent, 64 - g * local)[:, :wide]).astype(BF)

    teacher = encoder_forward(
        sizes, pix_t.shape[1], pix_t, place, bias_t, tbank, gains_t, None, teacher_rows
    )
    student = encoder_forward(
        sizes, asked, pix_s, place_shuffled, bias_s, bank, rows_s[:2], keep_refs, student_rows
    )

    def advance(work, parts):
        for _ in range(parts):
            next(work, None)

    def bank_copy(g):
        return pltpu.make_async_copy(bank.at[g], bank_out.at[g], out_sem.at[g])

    steps = learn.steps()
    for j, step in enumerate(steps):
        if j == 3:
            guess.start()
        step()
        if j == 1:
            teach.take_diagonal()
        if j == 3:
            teach.complete()
        if j > 3:
            advance(teacher, 2)
    for j, step in enumerate(guess.steps()):
        step()
        if j == 1:
            learn.take_diagonal()
            advance(teacher, 100)
            learn.complete()
            for g in range(groups):
                bank_copy(g).start()
        if j > 1:
            advance(student, 1)
    guess.take_diagonal()
    advance(student, 100)
    for g in range(groups):
        bank_copy(g).wait()
    guess.complete()
    for j in range(1, groups):
        pixel(j).wait_send()
    for array in arrays:
        array.finish()


def run_front(packs, half, tables, shuffle, keep_t, keep_s, hot, sizes, asked):
    local, hidden, size = sizes
    nz = lax.axis_size("dp")
    groups = lax.axis_size("mp")
    owners = lax.axis_size("role") * nz
    vec, target, master, predictor = packs
    rows = half.shape[1]
    width = target.shape[0] * owners
    columns = target.shape[1]
    wide = local + 64
    make = jax.ShapeDtypeStruct
    hbm = pl.BlockSpec(memory_space=pl.ANY)
    vmem = pl.BlockSpec(memory_space=pltpu.VMEM)
    dma = pltpu.SemaphoreType.DMA
    bank = make((groups, width, columns), BF)
    outs = [
        bank,
        make((groups, owners, *predictor.shape[1:]), BF),
        make((groups, asked, wide), BF),
        make((groups, hot.shape[0], wide), BF),
        make((groups, rows, wide), BF),
        make((4, width), F32),
        make((8, 128), F32),
        make((rows, width), F32),
        make((rows, 1), F32),
        make((rows, width), BF),
        make((groups, asked, wide), BF),
        make((groups, rows, wide), BF),
        make((groups, rows, wide), BF),
        make((HEADS, asked, rows), F32),
        make((groups, asked, wide), BF),
        make((asked, width), F32),
        make((asked, 1), F32),
        make((asked, width), BF),
        make((groups, asked, hidden), F32),
        make((groups, asked, hidden), BF),
    ]

    def first(cols):
        return cols - (cols // 5 // 256) * 256

    firsts = (vec.shape[2], first(columns), first(columns), first(predictor.shape[2]))
    bias_t, bias_s = (((keep - 1.0) * 1e9)[None, :] for keep in (keep_t, keep_s))
    return pl.pallas_call(
        functools.partial(front_kernel, nz, sizes, asked, firsts),
        out_shape=outs,
        in_specs=[hbm] * 5 + [vmem] * 5,
        out_specs=[hbm] * 2 + [vmem] * (len(outs) - 2),
        scratch_shapes=[
            pltpu.VMEM((groups, owners, *vec.shape[1:]), BF),
            pltpu.VMEM(bank.shape, BF),
            pltpu.VMEM(bank.shape, BF),
            pltpu.VMEM((groups, rows, wide), BF),
            dma((groups,)),
            dma((groups,)),
            dma((1,)),
            dma((groups,)),
        ]
        + gather_sems(4, nz),
        compiler_params=pltpu.CompilerParams(
            collective_id=1, has_side_effects=True, vmem_limit_bytes=60 * 2**20
        ),
    )(vec, target, master, predictor, half, tables, shuffle, bias_t, bias_s, hot)


def predictor_kernel(
    sizes, ctx, wanted, place_c, place_t, bias, weight, total, bank, gains,
    grad_ctx, grads, small, loss_out, probs_s, q_s, k_s, v_s, mixed_s, slope_s, active_s, dt_s
):
    local, plocal, phidden, size, blocks = sizes
    groups = bank.shape[0]
    heads = plocal // size
    lanes = 128
    up = 4 * plocal
    down = up + phidden
    head_at = down + phidden
    entry_at = head_at + local
    wide = local + 64
    nctx = place_c.shape[0]
    asked = place_t.shape[0]
    rows = nctx + asked
    tlen = asked // blocks
    first, second, final, token = (gains[i : i + 1] for i in range(4))
    root = size**-0.5

    entry = place_c[...] + chain(
        lambda g: dot_rt(ctx[g], bank[g, :, entry_at - 64 : entry_at + local]), groups
    )
    tgt_in = place_t[...] + token
    norm_c, scale_c = stats_of(entry)
    norm_t, scale_t = stats_of(tgt_in)
    a_c = (norm_c * first).astype(BF)
    a_t = (norm_t * first).astype(BF)
    a = jnp.concatenate([a_c, a_t], 0)

    def attend(g):
        t = dot(a, bank[g, :, :up]).astype(BF).astype(F32)
        q = t[nctx:, :lanes].astype(BF)
        k = turn(t, -plocal)[:, :lanes].astype(BF)
        v = turn(t, -2 * plocal)[:, :lanes].astype(BF)
        q_s[g] = q
        k_s[g] = k
        v_s[g] = v
        mixed = jnp.zeros((asked, lanes), F32)
        for h in range(heads):
            mask = head_lanes(lanes, size, h)
            score = dot_rt(only(mask, q), k) * root + bias[...]
            score = jnp.exp(score - jnp.max(score, -1, keepdims=True))
            probs = score / jnp.sum(score, -1, keepdims=True)
            probs_s[g * heads + h] = probs
            mixed += only(mask, dot(probs.astype(BF), v))
        mixed = turn(mixed, lanes - plocal).astype(BF)
        mixed_s[g] = mixed
        return dot_rt(mixed, bank[g, :, up - lanes : up])

    middle = tgt_in + chain(attend, groups)
    norm2, scale2 = stats_of(middle)
    b = (norm2 * second).astype(BF)

    def feed(g):
        pre = dot(b, bank[g, :, up:down])
        cdf = normal_cdf(pre)
        slope_s[g] = cdf + pre * jnp.exp(-0.5 * pre * pre) * INVERSE_ROOT
        act = (pre * cdf).astype(BF)
        active_s[g] = act
        return dot_rt(act, bank[g, :, down:head_at])

    out = middle + chain(feed, groups)
    norm_f, scale_f = stats_of(out)
    head_in = (norm_f * final).astype(BF)
    lane = lax.broadcasted_iota(jnp.int32, (1, wide), 1)
    losses = jnp.zeros((1, 1), F32)
    row_weight = weight[...]

    def judge(g):
        nonlocal losses
        pred = dot(head_in, bank[g, :, head_at : head_at + wide])
        diff = only(lane < local, pred - wanted[g].astype(F32))
        losses += jnp.sum(row_weight * diff * diff, keepdims=True)
        grad = (2.0 * row_weight * diff / total[...]).astype(BF)
        g_head = dot_lt(head_in, grad)
        grads[g, :, head_at : head_at + lanes] = g_head[:, :lanes]
        grads[g, :, head_at + lanes : head_at + wide] = g_head[:, lanes:]
        return dot_rt(grad, bank[g, :, head_at : head_at + wide])

    grad_out, g_final = norm_back_of(norm_f, scale_f, final, chain(judge, groups))
    loss_out[...] = jnp.broadcast_to(losses, loss_out.shape)

    branch = grad_out.astype(BF)

    def feed_back(g):
        grads[g, :, down:head_at] = dot_lt(branch, active_s[g])
        grad_pre = (dot(branch, bank[g, :, down:head_at]) * slope_s[g]).astype(BF)
        grads[g, :, up:down] = dot_lt(b, grad_pre)
        return dot_rt(grad_pre, bank[g, :, up:down])

    grad_norm, g_second = norm_back_of(norm2, scale2, second, chain(feed_back, groups))
    grad_mid = grad_out + grad_norm
    mixer = grad_mid.astype(BF)

    def attend_back(g):
        g_o = dot_lt(mixer, mixed_s[g])
        gm = turn(dot(mixer, bank[g, :, up - lanes : up]), plocal - lanes).astype(BF)
        q, k, v = (q_s[g], k_s[g], v_s[g])
        valid = head_lanes(lanes, plocal, 0)
        gm = only(valid, gm)
        qv = only(valid, q)
        block = lax.broadcasted_iota(jnp.int32, (asked, 1), 0) // tlen
        q_spread = jnp.concatenate([only(block == i, qv) for i in range(blocks)], 1)
        gm_spread = jnp.concatenate([only(block == i, gm) for i in range(blocks)], 1)
        dqs, dkt, dvt, dkc, dvc = ([], [], [], [], [])
        for h in range(heads):
            mask = head_lanes(lanes, size, h)
            masks = jnp.concatenate([mask] * blocks, 1)
            probs = probs_s[g * heads + h]
            gmh = only(mask, gm)
            grad_probs = dot_rt(gmh, v)
            ds = (probs * (grad_probs - jnp.sum(grad_probs * probs, -1, keepdims=True))).astype(BF)
            pb = probs.astype(BF)
            qh = only(mask, qv)
            dqs.append(dot(ds, only(mask, k)))
            dkt.append(dot_lt(ds[:, nctx:], qh))
            dvt.append(dot_lt(pb[:, nctx:], gmh))
            dkc.append(dot_lt(ds[:, :nctx], only(masks, q_spread)))
            dvc.append(dot_lt(pb[:, :nctx], only(masks, gm_spread)))
        dq = (sum(dqs[1:], dqs[0]) * root).astype(BF).astype(F32)
        dk = (sum(dkt[1:], dkt[0]) * root).astype(BF).astype(F32)
        dv = sum(dvt[1:], dvt[0]).astype(BF).astype(F32)
        kc = (sum(dkc[1:], dkc[0]) * root).astype(BF).astype(F32)
        vc = sum(dvc[1:], dvc[0]).astype(BF).astype(F32)
        kc = chain(lambda i: kc[:, i * lanes : (i + 1) * lanes], blocks)
        vc = chain(lambda i: vc[:, i * lanes : (i + 1) * lanes], blocks)

        def lay(query, keyed, valued):
            count = keyed.shape[0]
            blank = jnp.zeros((count, up - lanes), F32)
            wideq = 0.0 if query is None else jnp.concatenate([query, blank], 1)
            return (
                wideq
                + turn(jnp.concatenate([keyed, blank], 1), plocal)
                + turn(jnp.concatenate([valued, blank], 1), 2 * plocal)
            )

        dt_t = lay(dq, dk, dv).astype(BF)
        dt_c = lay(None, kc, vc)
        high = dt_c.astype(BF)
        low = (dt_c - high.astype(F32)).astype(BF)
        dt = jnp.concatenate([high, dt_t], 0)
        dt_s[g] = jnp.concatenate([dt, low], 0)
        g_qkv = dot_lt(jnp.concatenate([a, a_c], 0), jnp.concatenate([dt, low], 0))
        grads[g, :, : up - lanes] = g_qkv[:, : up - lanes]
        grads[g, :, up - lanes : up] = g_qkv[:, up - lanes :] + g_o

    for g in range(groups):
        attend_back(g)
    grad_a = chain(lambda g: dot_rt(dt_s[g], bank[g, :, :up]), groups)
    grad_in_t, g_first_t = norm_back_of(norm_t, scale_t, first, grad_a[nctx:rows])
    grad_in_c, g_first_c = norm_back_of(
        norm_c, scale_c, first, grad_a[:nctx] + grad_a[rows:]
    )
    g_token = jnp.sum(grad_in_t + grad_mid, 0, keepdims=True)
    small[...] = jnp.concatenate([g_first_t + g_first_c, g_second, g_final, g_token], 0)
    grad_entry = grad_in_c.astype(BF)
    width = groups * local
    grad_context = jnp.zeros((nctx, width), F32)
    for g in range(groups):
        g_entry = dot_lt(grad_entry, ctx[g])
        grads[g, :, entry_at - 64 : entry_at + 64] += g_entry[:, :lanes]
        grads[g, :, entry_at + 64 : entry_at + local] = g_entry[:, lanes:]
        part = only(lane >= 64, dot(grad_entry, bank[g, :, entry_at - 64 : entry_at + local]))
        full = jnp.concatenate([part, jnp.zeros((nctx, width - wide), F32)], 1)
        grad_context += turn(full, g * local - 64)
    grad_ctx[...] = grad_context


def run_predictor(ctx, wanted, place_c, place_t, bias, weight, total, bank, gains, sizes):
    local, plocal, phidden, size, blocks = sizes
    groups = bank.shape[0]
    nctx, pwidth = place_c.shape
    asked = place_t.shape[0]
    rows = nctx + asked
    make = jax.ShapeDtypeStruct
    outs = [
        make((nctx, groups * local), F32),
        make(bank.shape, F32),
        make((4, pwidth), F32),
        make((8, 128), F32),
    ]
    ins = [ctx, wanted, place_c, place_t, bias, weight, total, bank, gains]
    vmem = pl.BlockSpec(memory_space=pltpu.VMEM)
    scratch = [
        pltpu.VMEM((HEADS, asked, rows), F32),
        pltpu.VMEM((groups, asked, 128), BF),
        pltpu.VMEM((groups, rows, 128), BF),
        pltpu.VMEM((groups, rows, 128), BF),
        pltpu.VMEM((groups, asked, 128), BF),
        pltpu.VMEM((groups, asked, phidden), F32),
        pltpu.VMEM((groups, asked, phidden), BF),
        pltpu.VMEM((groups, rows + nctx, 4 * plocal), BF),
    ]
    return pl.pallas_call(
        functools.partial(predictor_kernel, sizes),
        out_shape=outs,
        in_specs=[vmem] * len(ins),
        out_specs=[vmem] * len(outs),
        scratch_shapes=scratch,
        compiler_params=pltpu.CompilerParams(vmem_limit_bytes=56 * 2**20),
    )(*ins)


def encoder_back_kernel(
    sizes, grad_ctx, pix, norm1, scale1, mixer_in, qs, ks, vs, probs_in, mixed_in, norm2, scale2,
    dense, slope, active, bank, gains, grads, small, wide_s, tail_s, dt_s, sems
):
    local, hidden, size = sizes
    groups = bank.shape[0]
    heads = local // size
    up = 4 * local
    down = up + hidden
    emb = down + hidden
    wide = local + 64
    span = 3 * local + 64
    asked = grad_ctx.shape[0]
    rows = norm1.shape[0]
    first, second = (gains[0:1], gains[1:2])
    root = size**-0.5
    grad_out = grad_ctx[...]
    branch = grad_out.astype(BF)

    def ship(g, start, width):
        return pltpu.make_async_copy(
            wide_s.at[g % 2, :, pl.ds(start, width)],
            grads.at[g, :, pl.ds(start, width)],
            sems.at[g % 2],
        )

    def feed_back(g):
        if g >= 2:
            ship(g - 2, up, 2 * hidden).wait()
        wide_s[g % 2, :, down:emb] = dot_lt(branch, active[g])
        grad_pre = (dot(branch, bank[g, :, down:emb]) * slope[g]).astype(BF)
        wide_s[g % 2, :, up:down] = dot_lt(dense[...], grad_pre)
        ship(g, up, 2 * hidden).start()
        return dot_rt(grad_pre, bank[g, :, up:down])

    grad_norm, g_second = norm_back_of(norm2[...], scale2[...], second, chain(feed_back, groups))
    grad_mid = grad_out + grad_norm
    mixer = grad_mid.astype(BF)
    for g in range(groups - 2, groups):
        ship(g, up, 2 * hidden).wait()
    valid = head_lanes(wide, local, 0)

    def attend_back(g):
        g_o = dot_lt(mixer, mixed_in[g])
        gm = turn(dot(mixer, bank[g, :, up - wide : up]), -64).astype(BF)
        q, k, v = (only(valid, qs[g]), ks[g], vs[g])
        gm = only(valid, gm)
        dqs, dks, dvs = ([], [], [])
        for h in range(heads):
            mask = head_lanes(wide, size, h)
            probs = probs_in[g * heads + h]
            gmh = only(mask, gm)
            grad_probs = dot_rt(gmh, v)
            ds = (probs * (grad_probs - jnp.sum(grad_probs * probs, -1, keepdims=True))).astype(BF)
            dqs.append(dot(ds, only(mask, k)))
            dks.append(dot_lt(ds, only(mask, q)))
            dvs.append(dot_lt(probs.astype(BF), gmh))
        dq = (sum(dqs[1:], dqs[0]) * root).astype(BF).astype(F32)
        dk = (sum(dks[1:], dks[0]) * root).astype(BF).astype(F32)
        dv = sum(dvs[1:], dvs[0]).astype(BF).astype(F32)
        dq = jnp.concatenate([dq, jnp.zeros((rows - asked, wide), F32)], 0)
        blank = jnp.zeros((rows, span - wide), F32)
        dt = (
            jnp.concatenate([dq, blank], 1)
            + turn(jnp.concatenate([dk, blank], 1), local)
            + jnp.concatenate([blank, dv], 1)
        ).astype(BF)
        dt_s[g] = dt
        g_qkv = dot_lt(mixer_in[...], dt)
        if g >= 2:
            ship(g - 2, 0, up).wait()
        slot = wide_s.at[g % 2]
        slot[:, : up - wide] = g_qkv[:, : up - wide]
        slot[:, up - wide : span] = g_qkv[:, up - wide :] + g_o[:, : span - up + wide]
        slot[:, span:up] = g_o[:, span - up + wide :]
        ship(g, 0, up).start()

    for g in range(groups):
        attend_back(g)
    grad_a = chain(lambda g: dot_rt(dt_s[g], bank[g, :, :span]), groups)
    grad_start, g_first = norm_back_of(norm1[...], scale1[...], first, grad_a)
    grad_start = (
        grad_start + jnp.concatenate([grad_mid, jnp.zeros((rows - asked, grad_mid.shape[1]), F32)], 0)
    ).astype(BF)
    small[...] = jnp.concatenate([g_first, g_second], 0)

    def tail(g):
        return pltpu.make_async_copy(
            tail_s.at[g], grads.at[g, :, pl.ds(emb, wide)], sems.at[2 + g]
        )

    for g in range(groups):
        tail_s[g] = dot_lt(grad_start, pix[g])
        tail(g).start()
    for g in range(groups - 2, groups):
        ship(g, 0, up).wait()
    for g in range(groups):
        tail(g).wait()


def run_encoder_back(grad_ctx, pix, saved, bank, gains, sizes):
    local, hidden, size = sizes
    groups, width, columns = bank.shape
    rows = pix.shape[1]
    make = jax.ShapeDtypeStruct
    ins = [grad_ctx, pix, *saved, bank, gains]
    vmem = pl.BlockSpec(memory_space=pltpu.VMEM)
    return pl.pallas_call(
        functools.partial(encoder_back_kernel, sizes),
        out_shape=[make(bank.shape, F32), make((2, width), F32)],
        in_specs=[vmem] * len(ins),
        out_specs=[pl.BlockSpec(memory_space=pl.ANY), vmem],
        scratch_shapes=[
            pltpu.VMEM((2, width, 4 * local + 2 * hidden), F32),
            pltpu.VMEM((groups, width, local + 64), F32),
            pltpu.VMEM((groups, rows, 3 * local + 64), BF),
            pltpu.SemaphoreType.DMA((2 + groups,)),
        ],
        compiler_params=pltpu.CompilerParams(vmem_limit_bytes=58 * 2**20),
    )(*ins)


def per_device(
    pixels,
    context_slots,
    context_count,
    target_slots,
    target_count,
    encoder_in,
    encoder_out,
    predictor_in,
    predictor_out,
    vectors,
    first_encoder_in,
    first_encoder_out,
    first_predictor_in,
    first_predictor_out,
    first_vectors,
    second_encoder_in,
    second_encoder_out,
    second_predictor_in,
    second_predictor_out,
    second_vectors,
    target_encoder_in,
    target_encoder_out,
    target_vectors,
):
    groups = lax.axis_size("mp")
    owners = lax.axis_size("role") * lax.axis_size("dp")
    width = encoder_in.shape[0] * owners
    pwidth = predictor_in.shape[0] * owners
    local, plocal = (width // groups, pwidth // groups)
    pixel = pixels.shape[2]
    hidden = encoder_in.shape[1] - 3 * local
    phidden = predictor_in.shape[1] - 3 * plocal - local
    patches = pixels.shape[1]
    image = lax.axis_index("role") * groups + lax.axis_index("mp")

    slots = lax.dynamic_index_in_dim(context_slots, image, 0, keepdims=False)
    count = lax.dynamic_index_in_dim(context_count, image, 0, keepdims=False)
    tslots = lax.dynamic_index_in_dim(target_slots, image, 0, keepdims=False)
    tcount = lax.dynamic_index_in_dim(target_count, image, 0, keepdims=False)
    nctx = slots.shape[0]
    blocks, tlen = tslots.shape
    rows = -(-patches // 16) * 16
    share = vectors.shape[0]

    patch = jnp.arange(patches)
    hits = slots[:, None] == patch[None, :]
    member = jnp.any(hits, 0)
    order = jnp.where(
        member,
        jnp.sum(jnp.where(hits, jnp.arange(nctx)[:, None], 0), 0),
        nctx + jnp.cumsum(1 - member.astype(jnp.int32)) - 1,
    )
    order = jnp.pad(order, (0, rows - patches), constant_values=-1)
    slot_of = jnp.arange(rows)
    shuffle = (order[None, :] == slot_of[:, None]).astype(BF)
    ckeep = (jnp.arange(nctx) < count).astype(F32)
    tkeep = (jnp.arange(tlen)[None, :] < tcount[:, None]).astype(F32)
    tflat = tslots.reshape(-1)
    of_block = jnp.arange(blocks * tlen) // tlen
    keys = jnp.concatenate(
        [
            jnp.broadcast_to(ckeep[None], (blocks * tlen, nctx)),
            (of_block[:, None] == of_block[None, :]) * tkeep.reshape(1, -1),
        ],
        1,
    )
    hot = (tflat[:, None] == slot_of[None, :]).astype(BF)

    vec = jnp.stack([vectors, target_vectors, jnp.broadcast_to(jnp.sum(tcount).astype(F32), (share,))])
    vec = jnp.pad(vec, ((0, 13), (0, -share % LANES))).astype(BF)
    half = lax.dynamic_slice_in_dim(pixels, lax.axis_index("role") * groups, groups, 0)
    half = jnp.pad(half, ((0, 0), (0, rows - patches), (0, 64)))
    ptable = sincos(pwidth)
    sizes = (local, hidden, width // HEADS)
    bank, pbank, context, wanted, student_pix, vec_rows, target_total, *saved = run_front(
        (
            vec[None],
            pack_encoder(target_encoder_in, target_encoder_out, local, pixel),
            pack_encoder(encoder_in, encoder_out, local, pixel),
            pack_predictor(predictor_in, predictor_out, local, plocal, phidden)[None],
        ),
        half,
        np.pad(in_three(sincos(width)), ((0, rows - patches), (0, 0))),
        shuffle,
        (slot_of < patches).astype(F32),
        (slot_of < count).astype(F32),
        hot,
        sizes,
        nctx,
    )
    enc_gains = vec_rows[:2]
    target_total = target_total[0, 0]
    grad_context, g_pbank, p_small, loss = run_predictor(
        context,
        wanted,
        pick(ptable, slots),
        pick(ptable, tflat),
        (keys - 1.0) * 1e9,
        tkeep.reshape(-1, 1),
        target_total.reshape(1, 1),
        pbank.reshape(groups, pwidth, -1),
        vec_rows[2:].reshape(4, pwidth),
        (local, plocal, phidden, pwidth // HEADS, blocks),
    )
    g_bank, e_small = run_encoder_back(grad_context, student_pix, saved, bank, enc_gains, sizes)
    g_vec = jnp.concatenate([e_small.reshape(-1), p_small.reshape(-1)])
    g_vec = g_vec.reshape(owners, groups, 1, -1).transpose(1, 0, 2, 3)
    r_bank, r_pbank, r_vec, stats = reduce_all(
        [
            g_bank.reshape(groups, owners, width // owners, -1),
            g_pbank.reshape(pbank.shape),
            jnp.pad(g_vec, ((0, 0), (0, 0), (0, 7), (0, -share % (2 * LANES)))),
        ],
        (BF, BF, F32),
        chunk_list([(1, g_pbank.shape[2], 768), (0, g_bank.shape[2], 512), (2, -(-share // 256) * 256, 256)]),
        loss,
    )
    r_pin, r_pout = unpack_predictor(r_pbank, local, plocal, phidden)
    r_in, r_out = unpack_encoder(r_bank, local, hidden, pixel)
    r_vec = r_vec[0, :share]
    loss_total, squares = (stats[0, 0], stats[1, 0])
    grad_norm = jnp.sqrt(squares)
    scale = jnp.minimum(1.0, CLIP / (grad_norm + 1e-06))
    new_in, m_in, v_in = adamw(
        encoder_in, r_in, first_encoder_in, second_encoder_in, scale, RATE_MATRIX, DECAY
    )
    new_out, m_out, v_out = adamw(
        encoder_out, r_out, first_encoder_out, second_encoder_out, scale, RATE_MATRIX, DECAY
    )
    new_pin, m_pin, v_pin = adamw(
        predictor_in, r_pin, first_predictor_in, second_predictor_in, scale, RATE_MATRIX, DECAY
    )
    new_pout, m_pout, v_pout = adamw(
        predictor_out, r_pout, first_predictor_out, second_predictor_out, scale, RATE_MATRIX, DECAY
    )
    new_vec, m_vec, v_vec = adamw(
        vectors, r_vec, first_vectors, second_vectors, scale, RATE_VECTOR, 0.0
    )
    ema_in = MOMENTUM_EMA * target_encoder_in + (1.0 - MOMENTUM_EMA) * new_in
    ema_out = MOMENTUM_EMA * target_encoder_out + (1.0 - MOMENTUM_EMA) * new_out
    ema_vec = MOMENTUM_EMA * target_vectors + (1.0 - MOMENTUM_EMA) * new_vec
    return (
        new_in, new_out, new_pin, new_pout, new_vec,
        m_in, m_out, m_pin, m_pout, m_vec,
        v_in, v_out, v_pin, v_pout, v_vec,
        ema_in, ema_out, ema_vec,
        loss_total, target_total, grad_norm,
    )


def solution(mesh):
    bank_in, bank_out, small = (
        P(("role", "dp"), "mp"),
        P("mp", ("role", "dp")),
        P(("role", "dp", "mp")),
    )
    five = (bank_in, bank_out, bank_in, bank_out, small)
    three = (bank_in, bank_out, small)
    return jax.shard_map(
        per_device,
        mesh=mesh,
        in_specs=(
            P("dp", None, "mp"),
            P("dp", None),
            P("dp"),
            P("dp", None, None),
            P("dp", None),
        )
        + five * 3
        + three,
        out_specs=five * 3 + three + (P(), P(), P()),
        check_vma=False,
    )
```

```python
import functools

import jax
import jax.numpy as jnp
import numpy as np
from jax import lax
from jax.experimental import pallas as pl
from jax.experimental.pallas import tpu as pltpu
from jax.sharding import PartitionSpec as P

HEADS = 12
GRID = 14
STEP = 10

BETA_ONE = 0.9
BETA_TWO = 0.999
ADAM_EPS = 1e-08
RATE_MATRIX = 0.03
RATE_VECTOR = 0.3
DECAY = 0.05
MOMENTUM_EMA = 0.9
CLIP = 0.1
ROOT_HALF = 0.7071067811865476
INVERSE_ROOT = 0.3989422804014327

BF = jnp.bfloat16
F32 = jnp.float32
LANES = 128


def sincos(width):
    quarter = width // 4
    omega = 1.0 / 10000.0 ** (np.arange(quarter, dtype=np.float64) / quarter)
    place = np.arange(GRID * GRID)
    rows = (place // GRID)[:, None] * omega[None, :]
    cols = (place % GRID)[:, None] * omega[None, :]
    return np.concatenate([np.sin(rows), np.cos(rows), np.sin(cols), np.cos(cols)], -1).astype(
        np.float32
    )


def in_three(table):
    parts, rest = ([], table)
    for _ in range(3):
        parts.append(rest.astype(jnp.bfloat16))
        rest = rest - parts[-1].astype(np.float32)
    return np.concatenate(parts, 1)


def pick(table, places):
    hot = (places[:, None] == jnp.arange(table.shape[0])[None, :]).astype(BF)
    rows = jnp.dot(hot, in_three(table), preferred_element_type=F32)
    width = table.shape[1]
    return rows[:, :width] + rows[:, width : 2 * width] + rows[:, 2 * width :]


def chunk_list(arrays):
    return tuple(
        (array, start, min(step, columns - start))
        for array, columns, step in arrays
        for start in range(0, columns, step)
    )


def pack_encoder(w_in, w_out, local, pixel):
    turned = w_out.T
    used = w_in.shape[1] + turned.shape[1]
    return jnp.concatenate(
        [
            w_in[:, : 3 * local],
            turned[:, pixel : pixel + local],
            w_in[:, 3 * local :],
            turned[:, pixel + local :],
            turned[:, :pixel],
            jnp.zeros((w_in.shape[0], -used % (2 * LANES)), F32),
        ],
        1,
    ).astype(BF)


def unpack_encoder(packed, local, hidden, pixel):
    up = 4 * local
    down = up + hidden
    emb = down + hidden
    w_in = jnp.concatenate([packed[:, : 3 * local], packed[:, up:down]], 1)
    turned = jnp.concatenate(
        [packed[:, emb : emb + pixel], packed[:, 3 * local : up], packed[:, down:emb]], 1
    )
    return (w_in, turned.T)


def pack_predictor(p_in, p_out, local, plocal, phidden):
    turned = p_out.T
    return jnp.concatenate(
        [
            p_in[:, : 3 * plocal],
            turned[:, local : local + plocal],
            p_in[:, 3 * plocal : 3 * plocal + phidden],
            turned[:, local + plocal :],
            p_in[:, 3 * plocal + phidden :],
            turned[:, :local],
        ],
        1,
    ).astype(BF)


def unpack_predictor(packed, local, plocal, phidden):
    up = 4 * plocal
    down = up + phidden
    head = down + phidden
    entry = head + local
    p_in = jnp.concatenate(
        [packed[:, : 3 * plocal], packed[:, up:down], packed[:, head:entry]], 1
    )
    turned = jnp.concatenate(
        [packed[:, entry:], packed[:, 3 * plocal : up], packed[:, down:head]], 1
    )
    return (p_in, turned.T)


def adamw(weight, grad, first, second, scale, rate, decay):
    grad = grad * scale
    first = BETA_ONE * first + (1.0 - BETA_ONE) * grad
    second = BETA_TWO * second + (1.0 - BETA_TWO) * grad * grad
    mean_hat = first / (1.0 - BETA_ONE**STEP)
    square_hat = second / (1.0 - BETA_TWO**STEP)
    return (
        weight - rate * (mean_hat / (jnp.sqrt(square_hat) + ADAM_EPS) + decay * weight),
        first,
        second,
    )


def shift_of(rank, by):
    return jnp.bitwise_xor(rank, by)


def greet(peers):
    barrier = pltpu.get_barrier_semaphore()
    for peer in peers:
        pl.semaphore_signal(barrier, inc=1, device_id=peer, device_id_type=pl.DeviceIdType.MESH)
    pl.semaphore_wait(barrier, len(peers))


def remote(src, dst, send, recv, where):
    return pltpu.make_async_remote_copy(
        src_ref=src, dst_ref=dst, send_sem=send, recv_sem=recv,
        device_id=where, device_id_type=pl.DeviceIdType.MESH,
    )


class Gather:
    def __init__(self, place, source, target, rows, cols, first, sems, where, nz):
        (self.zs, self.zr, self.xs, self.xr, self.ys, self.yr, self.rxs, self.rxr, self.rys,
         self.ryr, self.bs, self.br, self.bzs, self.bzr, self.cs, self.cr, self.own) = sems
        self.k = place
        self.source, self.target = (source, target)
        self.rows, self.cols, self.first, self.nz = (rows, cols, first, nz)
        self.r, self.d, self.m = where
        self.base = self.r * nz
        self.mx, self.my, self.mf = (shift_of(self.m, by) for by in (1, 2, 3))

    def at(self, column, owner, count, start, width):
        if len(self.target.shape) == 4:
            return self.target.at[column, pl.ds(owner, count), :, pl.ds(start, width)]
        row = pl.multiple_of(owner * self.rows, self.rows)
        return self.target.at[column, pl.ds(row, count * self.rows), pl.ds(start, width)]

    def mine(self, start, width):
        if len(self.target.shape) == 4:
            return self.source.at[:, :, pl.ds(start, width)]
        return self.source.at[:, pl.ds(start, width)]

    def line(self, piece, way, own=False):
        spot = self.at(self.m, self.base + piece, 1, 0, self.first)
        return remote(
            self.mine(0, self.first) if own else spot, spot,
            self.zs.at[self.k, way, piece], self.zr.at[self.k, way, piece],
            {"dp": self.d + 1 - 2 * way},
        )

    def across(self, piece, own=False):
        spot = self.at(self.m, self.base + piece, 1, 0, self.first)
        source = self.mine(0, self.first) if own else spot
        return (
            remote(source, spot, self.xs.at[self.k, piece], self.xr.at[self.k, piece], {"mp": self.mx}),
            remote(source, spot, self.ys.at[self.k, piece], self.yr.at[self.k, piece], {"mp": self.my}),
        )

    def arrived(self, piece):
        return [
            remote(spot, spot, send.at[self.k, piece], recv.at[self.k, piece], {"mp": peer})
            for spot, send, recv, peer in (
                (self.at(self.mx, self.base + piece, 1, 0, self.first), self.xs, self.xr, self.mx),
                (self.at(self.my, self.base + piece, 1, 0, self.first), self.ys, self.yr, self.my),
            )
        ]

    def halves(self, low, high, piece):
        half = self.first // 2 if self.first % 256 == 0 else self.first
        one = self.at(low, self.base + piece, 1, 0, half)
        copies = [remote(one, one, self.rys.at[self.k, piece], self.ryr.at[self.k, piece], {"mp": self.my})]
        if half < self.first:
            two = self.at(high, self.base + piece, 1, half, half)
            copies.append(
                remote(two, two, self.rxs.at[self.k, piece], self.rxr.at[self.k, piece], {"mp": self.mx})
            )
        return copies

    def relay(self, piece):
        return self.halves(self.mx, self.my, piece)

    def diagonal(self, piece):
        return self.halves(self.mf, self.mf, piece)

    def late_across(self):
        width = self.cols - self.first
        spot = self.at(self.m, self.base + self.d, 1, self.first, width)
        source = self.mine(self.first, width)
        return (
            remote(source, spot, self.bs.at[self.k, 0], self.br.at[self.k, 0], {"mp": self.mx}),
            remote(source, spot, self.bs.at[self.k, 1], self.br.at[self.k, 1], {"mp": self.my}),
        )

    def late_arrived(self):
        width = self.cols - self.first
        spots = [self.at(c, self.base + self.d, 1, self.first, width) for c in (self.mx, self.my)]
        return [
            remote(spot, spot, self.bs.at[self.k, i], self.br.at[self.k, i], {"mp": peer})
            for i, (spot, peer) in enumerate(zip(spots, (self.mx, self.my)))
        ]

    def late_halves(self, low, high):
        half = (self.cols - self.first) // 2
        one = self.at(low, self.base + self.d, 1, self.first, half)
        two = self.at(high, self.base + self.d, 1, self.first + half, half)
        return (
            remote(one, one, self.bs.at[self.k, 2], self.br.at[self.k, 2], {"mp": self.my}),
            remote(two, two, self.bs.at[self.k, 3], self.br.at[self.k, 3], {"mp": self.mx}),
        )

    def late_line(self, piece, way):
        spot = self.at(slice(None), self.base + piece, 1, self.first, self.cols - self.first)
        return remote(
            spot, spot, self.bzs.at[self.k, way, piece], self.bzr.at[self.k, way, piece],
            {"dp": self.d + 1 - 2 * way},
        )

    def core(self, slot, incoming=False):
        base = (1 - self.r) * self.nz if incoming else self.base
        if slot == 4:
            spot = self.at(slice(None), base, self.nz, self.first, self.cols - self.first)
        else:
            column = (self.m, self.mx, self.my, self.mf)[slot]
            spot = self.at(column, base, self.nz, 0, self.first)
        return remote(spot, spot, self.cs.at[self.k, slot], self.cr.at[self.k, slot], {"role": 1 - self.r})

    def copy_own(self):
        return pltpu.make_async_copy(
            self.mine(0, self.cols), self.at(self.m, self.base + self.d, 1, 0, self.cols),
            self.own.at[self.k],
        )

    def start(self):
        d, nz = (self.d, self.nz)

        @pl.when(d < nz - 1)
        def _():
            self.line(d, 0, True).start()

        @pl.when(d > 0)
        def _():
            self.line(d, 1, True).start()

        for copy in self.across(d, True):
            copy.start()
        if self.first < self.cols:
            for copy in self.late_across():
                copy.start()
        self.copy_own().start()

    def pass_on(self, piece):
        for copy in self.arrived(piece):
            copy.wait_recv()
        for copy in self.relay(piece):
            copy.start()

    def step(self, t):
        d, nz = (self.d, self.nz)
        left = d - 1 - t
        right = d + 1 + t

        @pl.when(left >= 0)
        def _():
            self.line(left, 0).wait_recv()

            @pl.when(d < nz - 1)
            def _():
                self.line(left, 0).start()

            for copy in self.across(left):
                copy.start()

        @pl.when(right < nz)
        def _():
            self.line(right, 1).wait_recv()

            @pl.when(d > 0)
            def _():
                self.line(right, 1).start()

            for copy in self.across(right):
                copy.start()

        if t == 0:
            self.pass_on(d)
        else:
            @pl.when(left + 1 >= 0)
            def _():
                self.pass_on(left + 1)

            @pl.when(right - 1 < nz)
            def _():
                self.pass_on(right - 1)

    def late_turn(self):
        for copy in self.late_arrived():
            copy.wait_recv()
        for copy in self.late_halves(self.mx, self.my):
            copy.start()

    def late_start(self):
        for copy in self.late_halves(self.mf, self.mf):
            copy.wait_recv()
        self.copy_own().wait()

        @pl.when(self.d < self.nz - 1)
        def _():
            self.late_line(self.d, 0).start()

        @pl.when(self.d > 0)
        def _():
            self.late_line(self.d, 1).start()

    def late_step(self, t):
        d, nz = (self.d, self.nz)
        left = d - 1 - t
        right = d + 1 + t

        @pl.when(left >= 0)
        def _():
            self.late_line(left, 0).wait_recv()

            @pl.when(d < nz - 1)
            def _():
                self.late_line(left, 0).start()

        @pl.when(right < nz)
        def _():
            self.late_line(right, 1).wait_recv()

            @pl.when(d > 0)
            def _():
                self.late_line(right, 1).start()

    def last_pass(self):
        @pl.when(self.d == self.nz - 1)
        def _():
            self.pass_on(0)

        if self.nz > 1:
            @pl.when(self.d == 0)
            def _():
                self.pass_on(self.nz - 1)

        if self.first == self.cols:
            self.copy_own().wait()
        for slot in range(3):
            self.core(slot).start()

    def take_diagonal(self):
        def take(piece, carry):
            for copy in self.diagonal(piece):
                copy.wait_recv()
            return carry

        lax.fori_loop(0, self.nz, take, 0)
        self.core(3).start()
        if self.first < self.cols:
            self.core(4).start()

    def steps(self):
        late = self.first < self.cols
        early = [functools.partial(self.step, t) for t in range(self.nz - 1)] + [self.last_pass]
        late = []
        if self.first < self.cols:
            late = [self.late_turn, self.late_start]
            late += [functools.partial(self.late_step, t) for t in range(self.nz - 1)]
        todo = []
        while early or late:
            todo += early[:1] + late[:1]
            early, late = (early[1:], late[1:])
        return todo

    def complete(self):
        for slot in range(5 if self.first < self.cols else 4):
            self.core(slot, True).wait_recv()

    def finish(self):
        d, nz = (self.d, self.nz)
        late = self.first < self.cols
        for slot in range(5 if late else 4):
            self.core(slot).wait_send()
        if late:
            for copy in self.late_across() + self.late_halves(self.mx, self.my):
                copy.wait_send()

        def done(piece, carry):
            for copy in self.across(piece):
                copy.wait_send()
            for copy in self.relay(piece):
                copy.wait_send()

            @pl.when(jnp.logical_and(piece <= d, d < nz - 1))
            def _():
                self.line(piece, 0).wait_send()
                if late:
                    self.late_line(piece, 0).wait_send()

            @pl.when(jnp.logical_and(piece >= d, d > 0))
            def _():
                self.line(piece, 1).wait_send()
                if late:
                    self.late_line(piece, 1).wait_send()

            return carry

        lax.fori_loop(0, nz, done, 0)


def gather_sems(count, nz):
    dma = pltpu.SemaphoreType.DMA
    piece = [dma((count, nz))] * 8
    return (
        [dma((count, 2, nz))] * 2 + piece + [dma((count, 4))] * 2 + [dma((count, 2, nz))] * 2
        + [dma((count, 5))] * 2 + [dma((count,))]
    )


class Reduce:
    def __init__(self, nz, chunks, ring, ins, outs, refs):
        n = len(chunks)
        self.nz, self.chunks, self.ring, self.ins, self.outs, self.n = (nz, chunks, ring, ins, outs, n)
        self.accs, self.sends1, self.recvs1, self.sends2, self.recvs2, self.lines = (
            refs[i * n : (i + 1) * n] for i in range(6)
        )
        refs = refs[6 * n :]
        kinds = sorted(set(ring))
        self.buffers = {kind: refs[3 * i : 3 * i + 3] for i, kind in enumerate(kinds)}
        (self.ld, self.cs, self.cr, self.s1s, self.s1r, self.s2s, self.s2r, self.zs, self.zr) = refs[
            3 * len(kinds) :
        ]
        self.turns = [ring[:k].count(kind) for k, kind in enumerate(ring)]
        self.r = lax.axis_index("role")
        self.d = lax.axis_index("dp")
        m = lax.axis_index("mp")
        self.mx, self.my = (shift_of(m, 1), shift_of(m, 2))
        self.columns = (shift_of(m, 3), self.mx, self.my, m)

    def part(self, k, column, first):
        array, start, width = self.chunks[k]
        return self.ins[array].at[column, pl.ds(first, self.nz), :, pl.ds(start, width)]

    def core(self, k, j):
        return remote(
            self.part(k, self.columns[j], (1 - self.r) * self.nz), self.accs[k].at[j], self.cs.at[k, j], self.cr.at[k, j],
            {"role": 1 - self.r},
        )

    def loaded(self, k, j):
        far_ring, near_ring, own_ring = self.buffers[self.ring[k]]
        if j == 0:
            return far_ring.at[self.turns[k] % 3]
        if j == 3:
            return own_ring.at[self.turns[k] % 2]
        return near_ring.at[self.turns[k] % 2, j - 1]

    def load(self, k, j):
        return pltpu.make_async_copy(self.part(k, self.columns[j], self.r * self.nz), self.loaded(k, j), self.ld.at[k, j])

    def first(self, k, piece):
        half = self.chunks[k][2] // 2
        low, high = (pl.ds(0, half), pl.ds(half, half))
        return (
            remote(self.sends1[k].at[piece, :, low], self.recvs1[k].at[piece, :, low],
                   self.s1s.at[k, 0, piece], self.s1r.at[k, 0, piece], {"mp": self.my}),
            remote(self.sends1[k].at[piece, :, high], self.recvs1[k].at[piece, :, high],
                   self.s1s.at[k, 1, piece], self.s1r.at[k, 1, piece], {"mp": self.mx}),
        )

    def second(self, k, piece):
        return (
            remote(self.sends2[k].at[0, piece], self.recvs2[k].at[0, piece],
                   self.s2s.at[k, 0, piece], self.s2r.at[k, 0, piece], {"mp": self.mx}),
            remote(self.sends2[k].at[1, piece], self.recvs2[k].at[1, piece],
                   self.s2s.at[k, 1, piece], self.s2r.at[k, 1, piece], {"mp": self.my}),
        )

    def right(self, k, piece):
        return remote(self.accs[k].at[3, piece], self.lines[k].at[piece], self.zs.at[k, piece],
                      self.zr.at[k, piece], {"dp": self.d + 1})

    def left(self, k, piece):
        slot = jnp.where(piece == self.d - 1, self.nz, piece)
        return remote(self.accs[k].at[3, piece], self.lines[k].at[slot], self.zs.at[k, piece],
                      self.zr.at[k, slot], {"dp": self.d - 1})

    def line_in(self, k, slot):
        return remote(self.lines[k].at[slot], self.lines[k].at[slot], self.zs.at[k, 0], self.zr.at[k, slot],
                      {"role": 1 - self.r})

    def each(self, body):
        def step(t, carry):
            off = self.nz - 1 - t

            @pl.when(self.d + off < self.nz)
            def _():
                body(self.d + off)

            @pl.when(self.d - off >= 0)
            def _():
                body(self.d - off)

            return carry

        lax.fori_loop(0, self.nz - 1, step, 0)
        body(self.d)

    def fetch(self, k):
        for j in range(4):
            self.core(k, j).start()
        self.load(k, 0).start()

    def combine(self, k, j):
        self.core(k, j).wait_recv()
        self.load(k, j).wait()

    def to_far(self, k):
        self.load(k, 1).start()
        self.load(k, 2).start()
        self.combine(k, 0)

        def send_far(piece):
            self.sends1[k][piece] = (self.accs[k][0, piece] + self.loaded(k, 0)[piece]).astype(self.sends1[k].dtype)
            for copy in self.first(k, piece):
                copy.start()

        self.each(send_far)

    def to_near(self, k):
        half = self.chunks[k][2] // 2
        self.load(k, 3).start()
        self.combine(k, 1)
        self.combine(k, 2)

        def send_near(piece):
            for copy in self.first(k, piece):
                copy.wait_recv()
            relayed = self.recvs1[k][piece].astype(jnp.float32)
            lane = lax.broadcasted_iota(jnp.int32, relayed.shape, 1)
            self.sends2[k][0, piece] = (
                self.accs[k][1, piece] + self.loaded(k, 1)[piece] + jnp.where(lane < half, relayed, 0.0)
            ).astype(self.sends2[k].dtype)
            self.sends2[k][1, piece] = (
                self.accs[k][2, piece] + self.loaded(k, 2)[piece] + jnp.where(lane < half, 0.0, relayed)
            ).astype(self.sends2[k].dtype)
            for copy in self.second(k, piece):
                copy.start()

        self.each(send_near)

    def to_line(self, k):
        self.combine(k, 3)

        def pass_on(piece):
            for copy in self.second(k, piece):
                copy.wait_recv()
            self.accs[k][3, piece] += (
                self.loaded(k, 3)[piece]
                + self.recvs2[k][0, piece].astype(jnp.float32)
                + self.recvs2[k][1, piece].astype(jnp.float32)
            )

            @pl.when(piece > self.d)
            def _():
                @pl.when(self.d > 0)
                def _():
                    self.line_in(k, piece).wait_recv()
                    self.accs[k][3, piece] += self.lines[k][piece]

                self.right(k, piece).start()

            @pl.when(piece < self.d)
            def _():
                @pl.when(self.d < self.nz - 1)
                def _():
                    self.line_in(k, piece).wait_recv()
                    self.accs[k][3, piece] += self.lines[k][piece]

                self.left(k, piece).start()

        self.each(pass_on)

    def land(self, k):
        array, start, width = self.chunks[k]

        @pl.when(self.d > 0)
        def _():
            self.line_in(k, self.d).wait_recv()
            self.accs[k][3, self.d] += self.lines[k][self.d]

        @pl.when(self.d < self.nz - 1)
        def _():
            self.line_in(k, self.nz).wait_recv()
            self.accs[k][3, self.d] += self.lines[k][self.nz]

        total = self.accs[k][3, self.d]
        self.outs[array][:, start : start + width] = total
        return jnp.sum(total * total, keepdims=True)

    def finish(self):
        for k in range(self.n):
            for j in range(4):
                self.core(k, j).wait_send()

            def done(piece, carry):
                for copy in self.first(k, piece):
                    copy.wait_send()
                for copy in self.second(k, piece):
                    copy.wait_send()

                @pl.when(piece != self.d)
                def _():
                    self.right(k, piece).wait_send()

                return carry

            lax.fori_loop(0, self.nz, done, 0)


def reduce_ring(grads, chunks):
    shapes = [(grads[array].shape[2], width) for array, _, width in chunks]
    kinds = sorted(set(shapes))
    return (shapes, kinds, tuple(kinds.index(s) for s in shapes))


def reduce_scratch(grads, wire_types, chunks, nz):
    groups = 4
    n = len(chunks)
    dma = pltpu.SemaphoreType.DMA
    shapes, kinds, ring = reduce_ring(grads, chunks)
    wires = [wire_types[array] for array, _, _ in chunks]
    return (
        [pltpu.VMEM((groups, nz, *s), jnp.float32) for s in shapes]
        + [pltpu.VMEM((nz, *s), t) for s, t in zip(shapes, wires)] * 2
        + [pltpu.VMEM((2, nz, *s), t) for s, t in zip(shapes, wires)] * 2
        + [pltpu.VMEM((nz + 1, *s), jnp.float32) for s in shapes]
        + [
            pltpu.VMEM((*slots, nz, *kinds[kind]), jnp.float32)
            for kind in range(len(kinds))
            for slots in (
                (min(3, ring.count(kind)),),
                (min(2, ring.count(kind)), 2),
                (min(2, ring.count(kind)),),
            )
        ]
        + [dma((n, groups))] * 3
        + [dma((n, 2, nz))] * 4
        + [dma((n, nz)), dma((n, nz + 1))]
    )


def peers(nz):
    r = lax.axis_index("role")
    d = lax.axis_index("dp")
    m = lax.axis_index("mp")
    group = [{"role": role, "mp": shift_of(m, by)} for role in (r, 1 - r) for by in range(4)][1:]
    return (group, [{"dp": lax.rem(d + j, nz)} for j in range(1, nz)])


def reduce_kernel(nz, chunks, ring, count, stats_in, *refs):
    ins = refs[:count]
    outs = refs[count : 2 * count]
    stats_out, near, near_in, far_in, ns, nr, fs, fr = refs[2 * count : 2 * count + 8]
    work = Reduce(nz, chunks, ring, ins, outs, refs[2 * count + 8 :])
    n = len(chunks)
    r = lax.axis_index("role")
    d = lax.axis_index("dp")
    m = lax.axis_index("mp")
    groups = 4
    group, far = peers(nz)
    greet(group + far)
    ahead = 2
    for k in range(min(ahead, n)):
        work.fetch(k)
    squares = jnp.zeros((1, 1), jnp.float32)
    for step in range(n + 3):
        if step + ahead < n:
            work.fetch(step + ahead)
        if step < n:
            work.to_far(step)
        if 0 <= step - 1 < n:
            work.to_near(step - 1)
        if 0 <= step - 2 < n:
            work.to_line(step - 2)
        if 0 <= step - 3 < n:
            squares += work.land(step - 3)

    mine = r * groups + m
    row = lax.broadcasted_iota(jnp.int32, (8, 128), 0)
    near[...] = stats_in[...] + jnp.where(row == 1, squares, 0.0)
    near_in[mine] = near[...]
    copies = []
    for j, peer in enumerate(group):
        copies.append(remote(near, near_in.at[mine], ns.at[j], nr.at[mine], peer))
        copies[-1].start()
    for j, peer in enumerate(group):
        slot = peer["role"] * groups + peer["mp"]
        remote(near, near_in.at[slot], ns.at[j], nr.at[slot], peer).wait_recv()
    for copy in copies:
        copy.wait_send()
    summed = near_in[0]
    for j in range(1, 2 * groups):
        summed += near_in[j]
    near[...] = summed
    far_in[d] = summed
    copies = []
    for j, peer in enumerate(far):
        copies.append(remote(near, far_in.at[d], fs.at[j], fr.at[d], peer))
        copies[-1].start()
    for j, peer in enumerate(far):
        slot = peer["dp"]
        remote(near, far_in.at[slot], fs.at[j], fr.at[slot], peer).wait_recv()
    for copy in copies:
        copy.wait_send()
    summed = far_in[0]
    for j in range(1, nz):
        summed += far_in[j]
    stats_out[...] = summed
    work.finish()


def reduce_all(grads, wire_types, chunks, stats):
    nz = lax.axis_size("dp")
    groups = lax.axis_size("mp")
    count = len(grads)
    dma = pltpu.SemaphoreType.DMA
    vmem = pl.BlockSpec(memory_space=pltpu.VMEM)
    return pl.pallas_call(
        functools.partial(reduce_kernel, nz, chunks, reduce_ring(grads, chunks)[2], count),
        out_shape=[jax.ShapeDtypeStruct(g.shape[2:], jnp.float32) for g in grads]
        + [jax.ShapeDtypeStruct((8, 128), jnp.float32)],
        in_specs=[vmem] + [pl.BlockSpec(memory_space=pl.ANY)] * count,
        out_specs=[vmem] * (count + 1),
        scratch_shapes=[
            pltpu.VMEM((8, 128), jnp.float32),
            pltpu.VMEM((2 * groups, 8, 128), jnp.float32),
            pltpu.VMEM((nz, 8, 128), jnp.float32),
            dma((2 * groups,)),
            dma((2 * groups,)),
            dma((nz,)),
            dma((nz,)),
        ]
        + reduce_scratch(grads, wire_types, chunks, nz),
        compiler_params=pltpu.CompilerParams(
            collective_id=2, has_side_effects=True, vmem_limit_bytes=60 * 2**20
        ),
    )(stats, *grads)


def dot(left, right):
    return lax.dot_general(left, right, (((1,), (0,)), ((), ())), preferred_element_type=F32)


def dot_rt(left, right):
    return lax.dot_general(left, right, (((1,), (1,)), ((), ())), preferred_element_type=F32)


def dot_lt(left, right):
    return lax.dot_general(left, right, (((0,), (0,)), ((), ())), preferred_element_type=F32)


def chain(term, count):
    total = term(0)
    for g in range(1, count):
        total += term(g)
    return total


def head_lanes(lanes, size, head):
    lane = lax.broadcasted_iota(jnp.int32, (1, lanes), 1)
    return jnp.logical_and(lane >= head * size, lane < (head + 1) * size)


def only(mask, value):
    return jnp.where(mask, value, jnp.zeros_like(value))


def turn(value, by):
    return pltpu.roll(value, by % value.shape[1], 1)


def stats_of(stream):
    mean = jnp.mean(stream, -1, keepdims=True)
    cent = stream - mean
    scale = lax.rsqrt(jnp.mean(cent * cent, -1, keepdims=True) + 1e-06)
    return (cent * scale, scale)


def norm_back_of(normed, scale, gain, grad):
    gain_grad = jnp.sum(grad * normed, 0, keepdims=True)
    scaled = grad * gain
    inner = (
        scaled
        - jnp.mean(scaled, -1, keepdims=True)
        - normed * jnp.mean(scaled * normed, -1, keepdims=True)
    )
    return (scale * inner, gain_grad)


def normal_cdf(hidden):
    return 0.5 * (1.0 + lax.erf(hidden * ROOT_HALF))


def encoder_forward(sizes, asked, pix, place, bias, bank, gains, keep_refs, finish):
    local, hidden, size = sizes
    groups = bank.shape[0]
    heads = local // size
    up = 4 * local
    down = up + hidden
    emb = down + hidden
    wide = local + 64
    saving = keep_refs is not None
    if saving:
        (norm1, scale1, mixer_in, qs, ks, vs, probs_out, mixed_out, norm2, scale2, dense, slope,
         active) = keep_refs
    terms = None
    for g in range(groups):
        term = dot_rt(pix[g], bank[g, :, emb : emb + wide])
        terms = term if terms is None else terms + term
    start = place() + terms
    normed, scale = stats_of(start)
    a = (normed * gains[0]).astype(BF)
    if saving:
        norm1[...] = normed
        scale1[...] = scale
        mixer_in[...] = a
    yield
    terms = None
    for g in range(groups):
        t = dot(a, bank[g, :, : 3 * local + 64]).astype(BF).astype(F32)
        q = t[:asked, :wide].astype(BF)
        k = turn(t, -local)[:, :wide].astype(BF)
        v = t[:, 2 * local :].astype(BF)
        if saving:
            qs[g] = q
            ks[g] = k
            vs[g] = v
        mixed = jnp.zeros((asked, wide), F32)
        for h in range(heads):
            mask = head_lanes(wide, size, h)
            score = dot_rt(only(mask, q), k) * size**-0.5 + bias[...]
            score = jnp.exp(score - jnp.max(score, -1, keepdims=True))
            probs = score / jnp.sum(score, -1, keepdims=True)
            if saving:
                probs_out[g * heads + h] = probs
            mixed += only(mask, dot(probs.astype(BF), v))
        mixed = turn(mixed, 64).astype(BF)
        if saving:
            mixed_out[g] = mixed
        term = dot_rt(mixed, bank[g, :, up - wide : up])
        terms = term if terms is None else terms + term
        yield
    middle = start[:asked] + terms
    normed, scale = stats_of(middle)
    b = (normed * gains[1]).astype(BF)
    if saving:
        norm2[...] = normed
        scale2[...] = scale
        dense[...] = b
    terms = None
    for g in range(groups):
        pre = dot(b, bank[g, :, up:down])
        cdf = normal_cdf(pre)
        act = (pre * cdf).astype(BF)
        if saving:
            slope[g] = cdf + pre * jnp.exp(-0.5 * pre * pre) * INVERSE_ROOT
            active[g] = act
        term = dot_rt(act, bank[g, :, down:emb])
        terms = term if terms is None else terms + term
        yield
    finish(middle + terms)


def front_kernel(nz, sizes, asked, firsts, *refs):
    local, hidden, size = sizes
    wide = local + 64
    sources, refs = (refs[:4], refs[4:])
    (half, tables, shuffle, bias_t, bias_s, hot), refs = (refs[:6], refs[6:])
    (bank_out, pbank_out, context, wanted, pix_s, vec_rows, total), refs = (refs[:7], refs[7:])
    keep_refs, refs = (refs[:13], refs[13:])
    (vec_all, tbank, bank, pix_t, px, pr, own_sem, out_sem), sems = (refs[:8], refs[8:])
    r = lax.axis_index("role")
    d = lax.axis_index("dp")
    m = lax.axis_index("mp")
    groups = tbank.shape[0]
    width = tbank.shape[1]
    nears = [{"mp": shift_of(m, by)} for by in range(1, groups)]
    greet([{"role": 1 - r}] + nears + [{"dp": lax.rem(d + j, nz)} for j in range(1, nz)])
    targets = (vec_all, tbank, bank, pbank_out)
    arrays = [
        Gather(k, sources[k], targets[k], sources[k].shape[-2], sources[k].shape[-1], firsts[k],
               sems, (r, d, m), nz)
        for k in range(4)
    ]
    small, teach, learn, guess = arrays

    def pixel(j):
        peer = shift_of(m, j)
        return remote(half.at[peer], pix_t.at[m], px.at[j], pr.at[j], {"mp": peer})

    def pixel_in(j):
        peer = shift_of(m, j)
        return remote(half.at[peer], pix_t.at[peer], px.at[j], pr.at[j], {"mp": peer})

    own_pixel = pltpu.make_async_copy(half.at[m], pix_t.at[m], own_sem.at[0])
    own_pixel.start()
    small.start()
    for j in range(1, groups):
        pixel(j).start()
    teach.start()
    for step in small.steps():
        step()

    def place():
        rows = tables[...].astype(F32)
        return rows[:, :width] + rows[:, width : 2 * width] + rows[:, 2 * width :]

    def place_shuffled():
        rows = dot(shuffle[...], tables[...])
        return rows[:, :width] + rows[:, width : 2 * width] + rows[:, 2 * width :]

    for j, step in enumerate(teach.steps()):
        if j == 3:
            learn.start()
        step()
        if j == 1:
            small.take_diagonal()
    small.complete()

    share = vec_rows.shape[1] * 4 // (vec_all.shape[0] * vec_all.shape[1])
    lanes = vec_all.shape[3]
    lane = lax.broadcasted_iota(jnp.int32, (1, lanes), 1)

    def vector_row(kind, j):
        row = jnp.zeros((1, width), F32)
        count = width // share
        for c in range(count):
            flat = j * count + c
            piece = vec_all[flat % groups, flat // groups].astype(F32)[kind : kind + 1]
            piece = only(lane < share, piece)
            row += turn(jnp.concatenate([piece, jnp.zeros((1, width - lanes), F32)], 1), c * share)
        return row

    gains_t = [vector_row(1, j) for j in range(2)]
    rows_s = [vector_row(0, j) for j in range(4)]
    vec_rows[...] = jnp.concatenate(rows_s, 0)
    counts = jnp.zeros((1, 1), F32)
    for c in range(groups):
        for o in range(vec_all.shape[1]):
            counts += vec_all[c, o].astype(F32)[2:3, :1]
    total[...] = jnp.broadcast_to(counts, total.shape)
    own_pixel.wait()
    for j in range(1, groups):
        pixel_in(j).wait_recv()
    for g in range(groups):
        pix_s[g] = dot(shuffle[...], pix_t[g]).astype(BF)

    def teacher_rows(latent):
        chosen = dot(hot[...], stats_of(latent)[0].astype(BF))
        for g in range(groups):
            wanted[g] = turn(chosen, -g * local)[:, :wide].astype(BF)

    def student_rows(latent):
        at = lax.broadcasted_iota(jnp.int32, (1, wide), 1)
        for g in range(groups):
            context[g] = only(at >= 64, turn(latent, 64 - g * local)[:, :wide]).astype(BF)

    teacher = encoder_forward(
        sizes, pix_t.shape[1], pix_t, place, bias_t, tbank, gains_t, None, teacher_rows
    )
    student = encoder_forward(
        sizes, asked, pix_s, place_shuffled, bias_s, bank, rows_s[:2], keep_refs, student_rows
    )

    def advance(work, parts):
        for _ in range(parts):
            next(work, None)

    def bank_copy(g):
        return pltpu.make_async_copy(bank.at[g], bank_out.at[g], out_sem.at[g])

    steps = learn.steps()
    for j, step in enumerate(steps):
        if j == 3:
            guess.start()
        step()
        if j == 1:
            teach.take_diagonal()
        if j == 3:
            teach.complete()
        if j > 3:
            advance(teacher, 2)
    for j, step in enumerate(guess.steps()):
        step()
        if j == 1:
            learn.take_diagonal()
            advance(teacher, 100)
            learn.complete()
            for g in range(groups):
                bank_copy(g).start()
        if j > 1:
            advance(student, 1)
    guess.take_diagonal()
    advance(student, 100)
    for g in range(groups):
        bank_copy(g).wait()
    guess.complete()
    for j in range(1, groups):
        pixel(j).wait_send()
    for array in arrays:
        array.finish()


def run_front(packs, half, tables, shuffle, keep_t, keep_s, hot, sizes, asked):
    local, hidden, size = sizes
    nz = lax.axis_size("dp")
    groups = lax.axis_size("mp")
    owners = lax.axis_size("role") * nz
    vec, target, master, predictor = packs
    rows = half.shape[1]
    width = target.shape[0] * owners
    columns = target.shape[1]
    wide = local + 64
    make = jax.ShapeDtypeStruct
    hbm = pl.BlockSpec(memory_space=pl.ANY)
    vmem = pl.BlockSpec(memory_space=pltpu.VMEM)
    dma = pltpu.SemaphoreType.DMA
    bank = make((groups, width, columns), BF)
    outs = [
        bank,
        make((groups, owners, *predictor.shape[1:]), BF),
        make((groups, asked, wide), BF),
        make((groups, hot.shape[0], wide), BF),
        make((groups, rows, wide), BF),
        make((4, width), F32),
        make((8, 128), F32),
        make((rows, width), F32),
        make((rows, 1), F32),
        make((rows, width), BF),
        make((groups, asked, wide), BF),
        make((groups, rows, wide), BF),
        make((groups, rows, wide), BF),
        make((HEADS, asked, rows), F32),
        make((groups, asked, wide), BF),
        make((asked, width), F32),
        make((asked, 1), F32),
        make((asked, width), BF),
        make((groups, asked, hidden), F32),
        make((groups, asked, hidden), BF),
    ]

    def first(cols):
        return cols - (cols // 5 // 256) * 256

    firsts = (vec.shape[2], first(columns), first(columns), first(predictor.shape[2]))
    bias_t, bias_s = (((keep - 1.0) * 1e9)[None, :] for keep in (keep_t, keep_s))
    return pl.pallas_call(
        functools.partial(front_kernel, nz, sizes, asked, firsts),
        out_shape=outs,
        in_specs=[hbm] * 5 + [vmem] * 5,
        out_specs=[hbm] * 2 + [vmem] * (len(outs) - 2),
        scratch_shapes=[
            pltpu.VMEM((groups, owners, *vec.shape[1:]), BF),
            pltpu.VMEM(bank.shape, BF),
            pltpu.VMEM(bank.shape, BF),
            pltpu.VMEM((groups, rows, wide), BF),
            dma((groups,)),
            dma((groups,)),
            dma((1,)),
            dma((groups,)),
        ]
        + gather_sems(4, nz),
        compiler_params=pltpu.CompilerParams(
            collective_id=1, has_side_effects=True, vmem_limit_bytes=60 * 2**20
        ),
    )(vec, target, master, predictor, half, tables, shuffle, bias_t, bias_s, hot)


def predictor_kernel(
    sizes, ctx, wanted, place_c, place_t, bias, weight, total, bank, gains,
    grad_ctx, grads, small, loss_out, probs_s, q_s, k_s, v_s, mixed_s, slope_s, active_s, dt_s
):
    local, plocal, phidden, size, blocks = sizes
    groups = bank.shape[0]
    heads = plocal // size
    lanes = 128
    up = 4 * plocal
    down = up + phidden
    head_at = down + phidden
    entry_at = head_at + local
    wide = local + 64
    nctx = place_c.shape[0]
    asked = place_t.shape[0]
    rows = nctx + asked
    tlen = asked // blocks
    first, second, final, token = (gains[i : i + 1] for i in range(4))
    root = size**-0.5

    entry = place_c[...] + chain(
        lambda g: dot_rt(ctx[g], bank[g, :, entry_at - 64 : entry_at + local]), groups
    )
    tgt_in = place_t[...] + token
    norm_c, scale_c = stats_of(entry)
    norm_t, scale_t = stats_of(tgt_in)
    a_c = (norm_c * first).astype(BF)
    a_t = (norm_t * first).astype(BF)
    a = jnp.concatenate([a_c, a_t], 0)

    def attend(g):
        t = dot(a, bank[g, :, :up]).astype(BF).astype(F32)
        q = t[nctx:, :lanes].astype(BF)
        k = turn(t, -plocal)[:, :lanes].astype(BF)
        v = turn(t, -2 * plocal)[:, :lanes].astype(BF)
        q_s[g] = q
        k_s[g] = k
        v_s[g] = v
        mixed = jnp.zeros((asked, lanes), F32)
        for h in range(heads):
            mask = head_lanes(lanes, size, h)
            score = dot_rt(only(mask, q), k) * root + bias[...]
            score = jnp.exp(score - jnp.max(score, -1, keepdims=True))
            probs = score / jnp.sum(score, -1, keepdims=True)
            probs_s[g * heads + h] = probs
            mixed += only(mask, dot(probs.astype(BF), v))
        mixed = turn(mixed, lanes - plocal).astype(BF)
        mixed_s[g] = mixed
        return dot_rt(mixed, bank[g, :, up - lanes : up])

    middle = tgt_in + chain(attend, groups)
    norm2, scale2 = stats_of(middle)
    b = (norm2 * second).astype(BF)

    def feed(g):
        pre = dot(b, bank[g, :, up:down])
        cdf = normal_cdf(pre)
        slope_s[g] = cdf + pre * jnp.exp(-0.5 * pre * pre) * INVERSE_ROOT
        act = (pre * cdf).astype(BF)
        active_s[g] = act
        return dot_rt(act, bank[g, :, down:head_at])

    out = middle + chain(feed, groups)
    norm_f, scale_f = stats_of(out)
    head_in = (norm_f * final).astype(BF)
    lane = lax.broadcasted_iota(jnp.int32, (1, wide), 1)
    losses = jnp.zeros((1, 1), F32)
    row_weight = weight[...]

    def judge(g):
        nonlocal losses
        pred = dot(head_in, bank[g, :, head_at : head_at + wide])
        diff = only(lane < local, pred - wanted[g].astype(F32))
        losses += jnp.sum(row_weight * diff * diff, keepdims=True)
        grad = (2.0 * row_weight * diff / total[...]).astype(BF)
        g_head = dot_lt(head_in, grad)
        grads[g, :, head_at : head_at + lanes] = g_head[:, :lanes]
        grads[g, :, head_at + lanes : head_at + wide] = g_head[:, lanes:]
        return dot_rt(grad, bank[g, :, head_at : head_at + wide])

    grad_out, g_final = norm_back_of(norm_f, scale_f, final, chain(judge, groups))
    loss_out[...] = jnp.broadcast_to(losses, loss_out.shape)

    branch = grad_out.astype(BF)

    def feed_back(g):
        grads[g, :, down:head_at] = dot_lt(branch, active_s[g])
        grad_pre = (dot(branch, bank[g, :, down:head_at]) * slope_s[g]).astype(BF)
        grads[g, :, up:down] = dot_lt(b, grad_pre)
        return dot_rt(grad_pre, bank[g, :, up:down])

    grad_norm, g_second = norm_back_of(norm2, scale2, second, chain(feed_back, groups))
    grad_mid = grad_out + grad_norm
    mixer = grad_mid.astype(BF)

    def attend_back(g):
        g_o = dot_lt(mixer, mixed_s[g])
        gm = turn(dot(mixer, bank[g, :, up - lanes : up]), plocal - lanes).astype(BF)
        q, k, v = (q_s[g], k_s[g], v_s[g])
        valid = head_lanes(lanes, plocal, 0)
        gm = only(valid, gm)
        qv = only(valid, q)
        block = lax.broadcasted_iota(jnp.int32, (asked, 1), 0) // tlen
        q_spread = jnp.concatenate([only(block == i, qv) for i in range(blocks)], 1)
        gm_spread = jnp.concatenate([only(block == i, gm) for i in range(blocks)], 1)
        dqs, dkt, dvt, dkc, dvc = ([], [], [], [], [])
        for h in range(heads):
            mask = head_lanes(lanes, size, h)
            masks = jnp.concatenate([mask] * blocks, 1)
            probs = probs_s[g * heads + h]
            gmh = only(mask, gm)
            grad_probs = dot_rt(gmh, v)
            ds = (probs * (grad_probs - jnp.sum(grad_probs * probs, -1, keepdims=True))).astype(BF)
            pb = probs.astype(BF)
            qh = only(mask, qv)
            dqs.append(dot(ds, only(mask, k)))
            dkt.append(dot_lt(ds[:, nctx:], qh))
            dvt.append(dot_lt(pb[:, nctx:], gmh))
            dkc.append(dot_lt(ds[:, :nctx], only(masks, q_spread)))
            dvc.append(dot_lt(pb[:, :nctx], only(masks, gm_spread)))
        dq = (sum(dqs[1:], dqs[0]) * root).astype(BF).astype(F32)
        dk = (sum(dkt[1:], dkt[0]) * root).astype(BF).astype(F32)
        dv = sum(dvt[1:], dvt[0]).astype(BF).astype(F32)
        kc = (sum(dkc[1:], dkc[0]) * root).astype(BF).astype(F32)
        vc = sum(dvc[1:], dvc[0]).astype(BF).astype(F32)
        kc = chain(lambda i: kc[:, i * lanes : (i + 1) * lanes], blocks)
        vc = chain(lambda i: vc[:, i * lanes : (i + 1) * lanes], blocks)

        def lay(query, keyed, valued):
            count = keyed.shape[0]
            blank = jnp.zeros((count, up - lanes), F32)
            wideq = 0.0 if query is None else jnp.concatenate([query, blank], 1)
            return (
                wideq
                + turn(jnp.concatenate([keyed, blank], 1), plocal)
                + turn(jnp.concatenate([valued, blank], 1), 2 * plocal)
            )

        dt_t = lay(dq, dk, dv).astype(BF)
        dt_c = lay(None, kc, vc)
        high = dt_c.astype(BF)
        low = (dt_c - high.astype(F32)).astype(BF)
        dt = jnp.concatenate([high, dt_t], 0)
        dt_s[g] = jnp.concatenate([dt, low], 0)
        g_qkv = dot_lt(jnp.concatenate([a, a_c], 0), jnp.concatenate([dt, low], 0))
        grads[g, :, : up - lanes] = g_qkv[:, : up - lanes]
        grads[g, :, up - lanes : up] = g_qkv[:, up - lanes :] + g_o

    for g in range(groups):
        attend_back(g)
    grad_a = chain(lambda g: dot_rt(dt_s[g], bank[g, :, :up]), groups)
    grad_in_t, g_first_t = norm_back_of(norm_t, scale_t, first, grad_a[nctx:rows])
    grad_in_c, g_first_c = norm_back_of(
        norm_c, scale_c, first, grad_a[:nctx] + grad_a[rows:]
    )
    g_token = jnp.sum(grad_in_t + grad_mid, 0, keepdims=True)
    small[...] = jnp.concatenate([g_first_t + g_first_c, g_second, g_final, g_token], 0)
    grad_entry = grad_in_c.astype(BF)
    width = groups * local
    grad_context = jnp.zeros((nctx, width), F32)
    for g in range(groups):
        g_entry = dot_lt(grad_entry, ctx[g])
        grads[g, :, entry_at - 64 : entry_at + 64] += g_entry[:, :lanes]
        grads[g, :, entry_at + 64 : entry_at + local] = g_entry[:, lanes:]
        part = only(lane >= 64, dot(grad_entry, bank[g, :, entry_at - 64 : entry_at + local]))
        full = jnp.concatenate([part, jnp.zeros((nctx, width - wide), F32)], 1)
        grad_context += turn(full, g * local - 64)
    grad_ctx[...] = grad_context


def run_predictor(ctx, wanted, place_c, place_t, bias, weight, total, bank, gains, sizes):
    local, plocal, phidden, size, blocks = sizes
    groups = bank.shape[0]
    nctx, pwidth = place_c.shape
    asked = place_t.shape[0]
    rows = nctx + asked
    make = jax.ShapeDtypeStruct
    outs = [
        make((nctx, groups * local), F32),
        make(bank.shape, F32),
        make((4, pwidth), F32),
        make((8, 128), F32),
    ]
    ins = [ctx, wanted, place_c, place_t, bias, weight, total, bank, gains]
    vmem = pl.BlockSpec(memory_space=pltpu.VMEM)
    scratch = [
        pltpu.VMEM((HEADS, asked, rows), F32),
        pltpu.VMEM((groups, asked, 128), BF),
        pltpu.VMEM((groups, rows, 128), BF),
        pltpu.VMEM((groups, rows, 128), BF),
        pltpu.VMEM((groups, asked, 128), BF),
        pltpu.VMEM((groups, asked, phidden), F32),
        pltpu.VMEM((groups, asked, phidden), BF),
        pltpu.VMEM((groups, rows + nctx, 4 * plocal), BF),
    ]
    return pl.pallas_call(
        functools.partial(predictor_kernel, sizes),
        out_shape=outs,
        in_specs=[vmem] * len(ins),
        out_specs=[vmem] * len(outs),
        scratch_shapes=scratch,
        compiler_params=pltpu.CompilerParams(vmem_limit_bytes=56 * 2**20),
    )(*ins)


def encoder_back_kernel(
    sizes, nz, chunks, ring, grad_ctx, pix, norm1, scale1, mixer_in, qs, ks, vs, probs_in, mixed_in, norm2, scale2,
    dense, slope, active, bank, gains, pgrads, grads, small, psum, squares, wide_s, tail_s, dt_s,
    sems, *refs
):
    local, hidden, size = sizes
    groups = bank.shape[0]
    heads = local // size
    up = 4 * local
    down = up + hidden
    emb = down + hidden
    wide = local + 64
    span = 3 * local + 64
    asked = grad_ctx.shape[0]
    rows = norm1.shape[0]
    first, second = (gains[0:1], gains[1:2])
    root = size**-0.5
    work = Reduce(nz, chunks, ring, (pgrads,), (psum,), refs)
    group, far = peers(nz)
    greet(group + far)
    n = len(chunks)
    stages = [functools.partial(work.to_far, k) for k in range(n)]
    stages += [functools.partial(work.to_near, k) for k in range(n)]
    stages += [functools.partial(work.to_line, k) for k in range(n)]
    for k in range(n):
        work.fetch(k)

    def serve():
        if stages:
            stages.pop(0)()

    grad_out = grad_ctx[...]
    branch = grad_out.astype(BF)

    def ship(g, start, width):
        return pltpu.make_async_copy(
            wide_s.at[g % 2, :, pl.ds(0, width)],
            grads.at[g, :, pl.ds(start, width)],
            sems.at[g % 2],
        )

    def feed_back(g):
        if g >= 2:
            ship(g - 2, up, 2 * hidden).wait()
        wide_s[g % 2, :, hidden : 2 * hidden] = dot_lt(branch, active[g])
        grad_pre = (dot(branch, bank[g, :, down:emb]) * slope[g]).astype(BF)
        wide_s[g % 2, :, :hidden] = dot_lt(dense[...], grad_pre)
        ship(g, up, 2 * hidden).start()
        serve()
        return dot_rt(grad_pre, bank[g, :, up:down])

    grad_norm, g_second = norm_back_of(norm2[...], scale2[...], second, chain(feed_back, groups))
    grad_mid = grad_out + grad_norm
    mixer = grad_mid.astype(BF)
    for g in range(groups - 2, groups):
        ship(g, up, 2 * hidden).wait()
    valid = head_lanes(wide, local, 0)

    def attend_back(g):
        g_o = dot_lt(mixer, mixed_in[g])
        gm = turn(dot(mixer, bank[g, :, up - wide : up]), -64).astype(BF)
        q, k, v = (only(valid, qs[g]), ks[g], vs[g])
        gm = only(valid, gm)
        dqs, dks, dvs = ([], [], [])
        for h in range(heads):
            mask = head_lanes(wide, size, h)
            probs = probs_in[g * heads + h]
            gmh = only(mask, gm)
            grad_probs = dot_rt(gmh, v)
            ds = (probs * (grad_probs - jnp.sum(grad_probs * probs, -1, keepdims=True))).astype(BF)
            dqs.append(dot(ds, only(mask, k)))
            dks.append(dot_lt(ds, only(mask, q)))
            dvs.append(dot_lt(probs.astype(BF), gmh))
        dq = (sum(dqs[1:], dqs[0]) * root).astype(BF).astype(F32)
        dk = (sum(dks[1:], dks[0]) * root).astype(BF).astype(F32)
        dv = sum(dvs[1:], dvs[0]).astype(BF).astype(F32)
        dq = jnp.concatenate([dq, jnp.zeros((rows - asked, wide), F32)], 0)
        blank = jnp.zeros((rows, span - wide), F32)
        dt = (
            jnp.concatenate([dq, blank], 1)
            + turn(jnp.concatenate([dk, blank], 1), local)
            + jnp.concatenate([blank, dv], 1)
        ).astype(BF)
        dt_s[g] = dt
        g_qkv = dot_lt(mixer_in[...], dt)
        if g >= 2:
            ship(g - 2, 0, up).wait()
        slot = wide_s.at[g % 2]
        slot[:, : up - wide] = g_qkv[:, : up - wide]
        slot[:, up - wide : span] = g_qkv[:, up - wide :] + g_o[:, : span - up + wide]
        slot[:, span:up] = g_o[:, span - up + wide :]
        ship(g, 0, up).start()

    for g in range(groups):
        attend_back(g)
        serve()
    grad_a = chain(lambda g: dot_rt(dt_s[g], bank[g, :, :span]), groups)
    grad_start, g_first = norm_back_of(norm1[...], scale1[...], first, grad_a)
    grad_start = (
        grad_start + jnp.concatenate([grad_mid, jnp.zeros((rows - asked, grad_mid.shape[1]), F32)], 0)
    ).astype(BF)
    small[...] = jnp.concatenate([g_first, g_second], 0)
    while stages:
        serve()

    def tail(g):
        return pltpu.make_async_copy(
            tail_s.at[g], grads.at[g, :, pl.ds(emb, wide)], sems.at[2 + g]
        )

    for g in range(groups):
        tail_s[g] = dot_lt(grad_start, pix[g])
        tail(g).start()
    for g in range(groups - 2, groups):
        ship(g, 0, up).wait()
    total = jnp.zeros((1, 1), F32)
    for k in range(n):
        total += work.land(k)
    squares[...] = jnp.broadcast_to(total, squares.shape)
    for g in range(groups):
        tail(g).wait()
    work.finish()


def run_encoder_back(grad_ctx, pix, saved, bank, gains, sizes, pgrads, chunks):
    local, hidden, size = sizes
    groups, width, columns = bank.shape
    rows = pix.shape[1]
    make = jax.ShapeDtypeStruct
    nz = lax.axis_size("dp")
    ins = [grad_ctx, pix, *saved, bank, gains]
    hbm = pl.BlockSpec(memory_space=pl.ANY)
    vmem = pl.BlockSpec(memory_space=pltpu.VMEM)
    return pl.pallas_call(
        functools.partial(encoder_back_kernel, sizes, nz, chunks, reduce_ring([pgrads], chunks)[2]),
        out_shape=[
            make(bank.shape, F32),
            make((2, width), F32),
            make(pgrads.shape[2:], F32),
            make((8, 128), F32),
        ],
        in_specs=[vmem] * len(ins) + [hbm],
        out_specs=[hbm, vmem, vmem, vmem],
        scratch_shapes=[
            pltpu.VMEM((2, width, 2 * hidden), F32),
            pltpu.VMEM((groups, width, local + 64), F32),
            pltpu.VMEM((groups, rows, 3 * local + 64), BF),
            pltpu.SemaphoreType.DMA((2 + groups,)),
        ]
        + reduce_scratch([pgrads], (BF,), chunks, nz),
        compiler_params=pltpu.CompilerParams(
            collective_id=3, has_side_effects=True, vmem_limit_bytes=60 * 2**20
        ),
    )(*ins, pgrads)


def per_device(
    pixels,
    context_slots,
    context_count,
    target_slots,
    target_count,
    encoder_in,
    encoder_out,
    predictor_in,
    predictor_out,
    vectors,
    first_encoder_in,
    first_encoder_out,
    first_predictor_in,
    first_predictor_out,
    first_vectors,
    second_encoder_in,
    second_encoder_out,
    second_predictor_in,
    second_predictor_out,
    second_vectors,
    target_encoder_in,
    target_encoder_out,
    target_vectors,
):
    groups = lax.axis_size("mp")
    owners = lax.axis_size("role") * lax.axis_size("dp")
    width = encoder_in.shape[0] * owners
    pwidth = predictor_in.shape[0] * owners
    local, plocal = (width // groups, pwidth // groups)
    pixel = pixels.shape[2]
    hidden = encoder_in.shape[1] - 3 * local
    phidden = predictor_in.shape[1] - 3 * plocal - local
    patches = pixels.shape[1]
    image = lax.axis_index("role") * groups + lax.axis_index("mp")

    slots = lax.dynamic_index_in_dim(context_slots, image, 0, keepdims=False)
    count = lax.dynamic_index_in_dim(context_count, image, 0, keepdims=False)
    tslots = lax.dynamic_index_in_dim(target_slots, image, 0, keepdims=False)
    tcount = lax.dynamic_index_in_dim(target_count, image, 0, keepdims=False)
    nctx = slots.shape[0]
    blocks, tlen = tslots.shape
    rows = -(-patches // 16) * 16
    share = vectors.shape[0]

    patch = jnp.arange(patches)
    hits = slots[:, None] == patch[None, :]
    member = jnp.any(hits, 0)
    order = jnp.where(
        member,
        jnp.sum(jnp.where(hits, jnp.arange(nctx)[:, None], 0), 0),
        nctx + jnp.cumsum(1 - member.astype(jnp.int32)) - 1,
    )
    order = jnp.pad(order, (0, rows - patches), constant_values=-1)
    slot_of = jnp.arange(rows)
    shuffle = (order[None, :] == slot_of[:, None]).astype(BF)
    ckeep = (jnp.arange(nctx) < count).astype(F32)
    tkeep = (jnp.arange(tlen)[None, :] < tcount[:, None]).astype(F32)
    tflat = tslots.reshape(-1)
    of_block = jnp.arange(blocks * tlen) // tlen
    keys = jnp.concatenate(
        [
            jnp.broadcast_to(ckeep[None], (blocks * tlen, nctx)),
            (of_block[:, None] == of_block[None, :]) * tkeep.reshape(1, -1),
        ],
        1,
    )
    hot = (tflat[:, None] == slot_of[None, :]).astype(BF)

    vec = jnp.stack([vectors, target_vectors, jnp.broadcast_to(jnp.sum(tcount).astype(F32), (share,))])
    vec = jnp.pad(vec, ((0, 13), (0, -share % LANES))).astype(BF)
    half = lax.dynamic_slice_in_dim(pixels, lax.axis_index("role") * groups, groups, 0)
    half = jnp.pad(half, ((0, 0), (0, rows - patches), (0, 64)))
    ptable = sincos(pwidth)
    sizes = (local, hidden, width // HEADS)
    bank, pbank, context, wanted, student_pix, vec_rows, target_total, *saved = run_front(
        (
            vec[None],
            pack_encoder(target_encoder_in, target_encoder_out, local, pixel),
            pack_encoder(encoder_in, encoder_out, local, pixel),
            pack_predictor(predictor_in, predictor_out, local, plocal, phidden)[None],
        ),
        half,
        np.pad(in_three(sincos(width)), ((0, rows - patches), (0, 0))),
        shuffle,
        (slot_of < patches).astype(F32),
        (slot_of < count).astype(F32),
        hot,
        sizes,
        nctx,
    )
    enc_gains = vec_rows[:2]
    target_total = target_total[0, 0]
    grad_context, g_pbank, p_small, loss = run_predictor(
        context,
        wanted,
        pick(ptable, slots),
        pick(ptable, tflat),
        (keys - 1.0) * 1e9,
        tkeep.reshape(-1, 1),
        target_total.reshape(1, 1),
        pbank.reshape(groups, pwidth, -1),
        vec_rows[2:].reshape(4, pwidth),
        (local, plocal, phidden, pwidth // HEADS, blocks),
    )
    g_bank, e_small, r_pbank, p_squares = run_encoder_back(
        grad_context, student_pix, saved, bank, enc_gains, sizes,
        g_pbank.reshape(pbank.shape), chunk_list([(0, g_pbank.shape[2], 768)]),
    )
    g_vec = jnp.concatenate([e_small.reshape(-1), p_small.reshape(-1)])
    g_vec = g_vec.reshape(owners, groups, 1, -1).transpose(1, 0, 2, 3)
    row = jnp.arange(8)[:, None]
    r_bank, r_vec, stats = reduce_all(
        [
            g_bank.reshape(groups, owners, width // owners, -1),
            jnp.pad(g_vec, ((0, 0), (0, 0), (0, 7), (0, -share % (2 * LANES)))),
        ],
        (BF, F32),
        chunk_list([(0, g_bank.shape[2], 512), (1, -(-share // 256) * 256, 256)]),
        jnp.where(row == 0, loss, jnp.where(row == 1, p_squares, 0.0)),
    )
    r_pin, r_pout = unpack_predictor(r_pbank, local, plocal, phidden)
    r_in, r_out = unpack_encoder(r_bank, local, hidden, pixel)
    r_vec = r_vec[0, :share]
    loss_total, squares = (stats[0, 0], stats[1, 0])
    grad_norm = jnp.sqrt(squares)
    scale = jnp.minimum(1.0, CLIP / (grad_norm + 1e-06))
    new_in, m_in, v_in = adamw(
        encoder_in, r_in, first_encoder_in, second_encoder_in, scale, RATE_MATRIX, DECAY
    )
    new_out, m_out, v_out = adamw(
        encoder_out, r_out, first_encoder_out, second_encoder_out, scale, RATE_MATRIX, DECAY
    )
    new_pin, m_pin, v_pin = adamw(
        predictor_in, r_pin, first_predictor_in, second_predictor_in, scale, RATE_MATRIX, DECAY
    )
    new_pout, m_pout, v_pout = adamw(
        predictor_out, r_pout, first_predictor_out, second_predictor_out, scale, RATE_MATRIX, DECAY
    )
    new_vec, m_vec, v_vec = adamw(
        vectors, r_vec, first_vectors, second_vectors, scale, RATE_VECTOR, 0.0
    )
    ema_in = MOMENTUM_EMA * target_encoder_in + (1.0 - MOMENTUM_EMA) * new_in
    ema_out = MOMENTUM_EMA * target_encoder_out + (1.0 - MOMENTUM_EMA) * new_out
    ema_vec = MOMENTUM_EMA * target_vectors + (1.0 - MOMENTUM_EMA) * new_vec
    return (
        new_in, new_out, new_pin, new_pout, new_vec,
        m_in, m_out, m_pin, m_pout, m_vec,
        v_in, v_out, v_pin, v_pout, v_vec,
        ema_in, ema_out, ema_vec,
        loss_total, target_total, grad_norm,
    )


def solution(mesh):
    bank_in, bank_out, small = (
        P(("role", "dp"), "mp"),
        P("mp", ("role", "dp")),
        P(("role", "dp", "mp")),
    )
    five = (bank_in, bank_out, bank_in, bank_out, small)
    three = (bank_in, bank_out, small)
    return jax.shard_map(
        per_device,
        mesh=mesh,
        in_specs=(
            P("dp", None, "mp"),
            P("dp", None),
            P("dp"),
            P("dp", None, None),
            P("dp", None),
        )
        + five * 3
        + three,
        out_specs=five * 3 + three + (P(), P(), P()),
        check_vma=False,
    )
```

```python
import functools

import jax
import jax.numpy as jnp
import numpy as np
from jax import lax
from jax.experimental import pallas as pl
from jax.experimental.pallas import tpu as pltpu
from jax.sharding import PartitionSpec as P

HEADS = 12
GRID = 14
STEP = 10

BETA_ONE = 0.9
BETA_TWO = 0.999
ADAM_EPS = 1e-08
RATE_MATRIX = 0.03
RATE_VECTOR = 0.3
DECAY = 0.05
MOMENTUM_EMA = 0.9
CLIP = 0.1
ROOT_HALF = 0.7071067811865476
INVERSE_ROOT = 0.3989422804014327

BF = jnp.bfloat16
F32 = jnp.float32
LANES = 128


def sincos(width):
    quarter = width // 4
    omega = 1.0 / 10000.0 ** (np.arange(quarter, dtype=np.float64) / quarter)
    place = np.arange(GRID * GRID)
    rows = (place // GRID)[:, None] * omega[None, :]
    cols = (place % GRID)[:, None] * omega[None, :]
    return np.concatenate([np.sin(rows), np.cos(rows), np.sin(cols), np.cos(cols)], -1).astype(
        np.float32
    )


def in_three(table):
    parts, rest = ([], table)
    for _ in range(3):
        parts.append(rest.astype(jnp.bfloat16))
        rest = rest - parts[-1].astype(np.float32)
    return np.concatenate(parts, 1)


def chunk_list(arrays):
    return tuple(
        (array, start, min(step, columns - start))
        for array, columns, step in arrays
        for start in range(0, columns, step)
    )


def pack_encoder(w_in, w_out, local, pixel):
    turned = w_out.T
    used = w_in.shape[1] + turned.shape[1]
    return jnp.concatenate(
        [
            w_in[:, : 3 * local],
            turned[:, pixel : pixel + local],
            w_in[:, 3 * local :],
            turned[:, pixel + local :],
            turned[:, :pixel],
            jnp.zeros((w_in.shape[0], -used % (2 * LANES)), F32),
        ],
        1,
    ).astype(BF)


def unpack_encoder(packed, local, hidden, pixel):
    up = 4 * local
    down = up + hidden
    emb = down + hidden
    w_in = jnp.concatenate([packed[:, : 3 * local], packed[:, up:down]], 1)
    turned = jnp.concatenate(
        [packed[:, emb : emb + pixel], packed[:, 3 * local : up], packed[:, down:emb]], 1
    )
    return (w_in, turned.T)


def pack_predictor(p_in, p_out, local, plocal, phidden):
    turned = p_out.T
    return jnp.concatenate(
        [
            p_in[:, : 3 * plocal],
            turned[:, local : local + plocal],
            p_in[:, 3 * plocal : 3 * plocal + phidden],
            turned[:, local + plocal :],
            p_in[:, 3 * plocal + phidden :],
            turned[:, :local],
        ],
        1,
    ).astype(BF)


def unpack_predictor(packed, local, plocal, phidden):
    up = 4 * plocal
    down = up + phidden
    head = down + phidden
    entry = head + local
    p_in = jnp.concatenate(
        [packed[:, : 3 * plocal], packed[:, up:down], packed[:, head:entry]], 1
    )
    turned = jnp.concatenate(
        [packed[:, entry:], packed[:, 3 * plocal : up], packed[:, down:head]], 1
    )
    return (p_in, turned.T)


def adamw(weight, grad, first, second, scale, rate, decay):
    grad = grad * scale
    first = BETA_ONE * first + (1.0 - BETA_ONE) * grad
    second = BETA_TWO * second + (1.0 - BETA_TWO) * grad * grad
    mean_hat = first / (1.0 - BETA_ONE**STEP)
    square_hat = second / (1.0 - BETA_TWO**STEP)
    return (
        weight - rate * (mean_hat / (jnp.sqrt(square_hat) + ADAM_EPS) + decay * weight),
        first,
        second,
    )


def shift_of(rank, by):
    return jnp.bitwise_xor(rank, by)


def greet(peers):
    barrier = pltpu.get_barrier_semaphore()
    for peer in peers:
        pl.semaphore_signal(barrier, inc=1, device_id=peer, device_id_type=pl.DeviceIdType.MESH)
    pl.semaphore_wait(barrier, len(peers))


def remote(src, dst, send, recv, where):
    return pltpu.make_async_remote_copy(
        src_ref=src, dst_ref=dst, send_sem=send, recv_sem=recv,
        device_id=where, device_id_type=pl.DeviceIdType.MESH,
    )


class Gather:
    def __init__(self, place, source, target, rows, cols, first, sems, where, nz):
        (self.zs, self.zr, self.xs, self.xr, self.ys, self.yr, self.rxs, self.rxr, self.rys,
         self.ryr, self.bs, self.br, self.bzs, self.bzr, self.cs, self.cr, self.own) = sems
        self.k = place
        self.source, self.target = (source, target)
        self.rows, self.cols, self.first, self.nz = (rows, cols, first, nz)
        self.r, self.d, self.m = where
        self.base = self.r * nz
        self.mx, self.my, self.mf = (shift_of(self.m, by) for by in (1, 2, 3))

    def at(self, column, owner, count, start, width):
        if len(self.target.shape) == 4:
            return self.target.at[column, pl.ds(owner, count), :, pl.ds(start, width)]
        row = pl.multiple_of(owner * self.rows, self.rows)
        return self.target.at[column, pl.ds(row, count * self.rows), pl.ds(start, width)]

    def mine(self, start, width):
        if len(self.target.shape) == 4:
            return self.source.at[:, :, pl.ds(start, width)]
        return self.source.at[:, pl.ds(start, width)]

    def line(self, piece, way, own=False):
        spot = self.at(self.m, self.base + piece, 1, 0, self.first)
        return remote(
            self.mine(0, self.first) if own else spot, spot,
            self.zs.at[self.k, way, piece], self.zr.at[self.k, way, piece],
            {"dp": self.d + 1 - 2 * way},
        )

    def across(self, piece, own=False):
        spot = self.at(self.m, self.base + piece, 1, 0, self.first)
        source = self.mine(0, self.first) if own else spot
        return (
            remote(source, spot, self.xs.at[self.k, piece], self.xr.at[self.k, piece], {"mp": self.mx}),
            remote(source, spot, self.ys.at[self.k, piece], self.yr.at[self.k, piece], {"mp": self.my}),
        )

    def arrived(self, piece):
        return [
            remote(spot, spot, send.at[self.k, piece], recv.at[self.k, piece], {"mp": peer})
            for spot, send, recv, peer in (
                (self.at(self.mx, self.base + piece, 1, 0, self.first), self.xs, self.xr, self.mx),
                (self.at(self.my, self.base + piece, 1, 0, self.first), self.ys, self.yr, self.my),
            )
        ]

    def halves(self, low, high, piece):
        half = self.first // 2 if self.first % 256 == 0 else self.first
        one = self.at(low, self.base + piece, 1, 0, half)
        copies = [remote(one, one, self.rys.at[self.k, piece], self.ryr.at[self.k, piece], {"mp": self.my})]
        if half < self.first:
            two = self.at(high, self.base + piece, 1, half, half)
            copies.append(
                remote(two, two, self.rxs.at[self.k, piece], self.rxr.at[self.k, piece], {"mp": self.mx})
            )
        return copies

    def relay(self, piece):
        return self.halves(self.mx, self.my, piece)

    def diagonal(self, piece):
        return self.halves(self.mf, self.mf, piece)

    def late_across(self):
        width = self.cols - self.first
        spot = self.at(self.m, self.base + self.d, 1, self.first, width)
        source = self.mine(self.first, width)
        return (
            remote(source, spot, self.bs.at[self.k, 0], self.br.at[self.k, 0], {"mp": self.mx}),
            remote(source, spot, self.bs.at[self.k, 1], self.br.at[self.k, 1], {"mp": self.my}),
        )

    def late_arrived(self):
        width = self.cols - self.first
        spots = [self.at(c, self.base + self.d, 1, self.first, width) for c in (self.mx, self.my)]
        return [
            remote(spot, spot, self.bs.at[self.k, i], self.br.at[self.k, i], {"mp": peer})
            for i, (spot, peer) in enumerate(zip(spots, (self.mx, self.my)))
        ]

    def late_halves(self, low, high):
        half = (self.cols - self.first) // 2
        one = self.at(low, self.base + self.d, 1, self.first, half)
        two = self.at(high, self.base + self.d, 1, self.first + half, half)
        return (
            remote(one, one, self.bs.at[self.k, 2], self.br.at[self.k, 2], {"mp": self.my}),
            remote(two, two, self.bs.at[self.k, 3], self.br.at[self.k, 3], {"mp": self.mx}),
        )

    def late_line(self, piece, way):
        spot = self.at(slice(None), self.base + piece, 1, self.first, self.cols - self.first)
        return remote(
            spot, spot, self.bzs.at[self.k, way, piece], self.bzr.at[self.k, way, piece],
            {"dp": self.d + 1 - 2 * way},
        )

    def core(self, slot, incoming=False):
        base = (1 - self.r) * self.nz if incoming else self.base
        if slot == 4:
            spot = self.at(slice(None), base, self.nz, self.first, self.cols - self.first)
        else:
            column = (self.m, self.mx, self.my, self.mf)[slot]
            spot = self.at(column, base, self.nz, 0, self.first)
        return remote(spot, spot, self.cs.at[self.k, slot], self.cr.at[self.k, slot], {"role": 1 - self.r})

    def copy_own(self):
        return pltpu.make_async_copy(
            self.mine(0, self.cols), self.at(self.m, self.base + self.d, 1, 0, self.cols),
            self.own.at[self.k],
        )

    def start(self):
        d, nz = (self.d, self.nz)

        @pl.when(d < nz - 1)
        def _():
            self.line(d, 0, True).start()

        @pl.when(d > 0)
        def _():
            self.line(d, 1, True).start()

        for copy in self.across(d, True):
            copy.start()
        if self.first < self.cols:
            for copy in self.late_across():
                copy.start()
        self.copy_own().start()

    def pass_on(self, piece):
        for copy in self.arrived(piece):
            copy.wait_recv()
        for copy in self.relay(piece):
            copy.start()

    def step(self, t):
        d, nz = (self.d, self.nz)
        left = d - 1 - t
        right = d + 1 + t

        @pl.when(left >= 0)
        def _():
            self.line(left, 0).wait_recv()

            @pl.when(d < nz - 1)
            def _():
                self.line(left, 0).start()

            for copy in self.across(left):
                copy.start()

        @pl.when(right < nz)
        def _():
            self.line(right, 1).wait_recv()

            @pl.when(d > 0)
            def _():
                self.line(right, 1).start()

            for copy in self.across(right):
                copy.start()

        if t == 0:
            self.pass_on(d)
        else:
            @pl.when(left + 1 >= 0)
            def _():
                self.pass_on(left + 1)

            @pl.when(right - 1 < nz)
            def _():
                self.pass_on(right - 1)

    def late_turn(self):
        for copy in self.late_arrived():
            copy.wait_recv()
        for copy in self.late_halves(self.mx, self.my):
            copy.start()

    def late_start(self):
        for copy in self.late_halves(self.mf, self.mf):
            copy.wait_recv()
        self.copy_own().wait()

        @pl.when(self.d < self.nz - 1)
        def _():
            self.late_line(self.d, 0).start()

        @pl.when(self.d > 0)
        def _():
            self.late_line(self.d, 1).start()

    def late_step(self, t):
        d, nz = (self.d, self.nz)
        left = d - 1 - t
        right = d + 1 + t

        @pl.when(left >= 0)
        def _():
            self.late_line(left, 0).wait_recv()

            @pl.when(d < nz - 1)
            def _():
                self.late_line(left, 0).start()

        @pl.when(right < nz)
        def _():
            self.late_line(right, 1).wait_recv()

            @pl.when(d > 0)
            def _():
                self.late_line(right, 1).start()

    def last_pass(self):
        @pl.when(self.d == self.nz - 1)
        def _():
            self.pass_on(0)

        if self.nz > 1:
            @pl.when(self.d == 0)
            def _():
                self.pass_on(self.nz - 1)

        if self.first == self.cols:
            self.copy_own().wait()
        for slot in range(3):
            self.core(slot).start()

    def take_diagonal(self):
        def take(piece, carry):
            for copy in self.diagonal(piece):
                copy.wait_recv()
            return carry

        lax.fori_loop(0, self.nz, take, 0)
        self.core(3).start()
        if self.first < self.cols:
            self.core(4).start()

    def steps(self):
        late = self.first < self.cols
        early = [functools.partial(self.step, t) for t in range(self.nz - 1)] + [self.last_pass]
        late = []
        if self.first < self.cols:
            late = [self.late_turn, self.late_start]
            late += [functools.partial(self.late_step, t) for t in range(self.nz - 1)]
        todo = []
        while early or late:
            todo += early[:1] + late[:1]
            early, late = (early[1:], late[1:])
        return todo

    def complete(self):
        for slot in range(5 if self.first < self.cols else 4):
            self.core(slot, True).wait_recv()

    def finish(self):
        d, nz = (self.d, self.nz)
        late = self.first < self.cols
        for slot in range(5 if late else 4):
            self.core(slot).wait_send()
        if late:
            for copy in self.late_across() + self.late_halves(self.mx, self.my):
                copy.wait_send()

        def done(piece, carry):
            for copy in self.across(piece):
                copy.wait_send()
            for copy in self.relay(piece):
                copy.wait_send()

            @pl.when(jnp.logical_and(piece <= d, d < nz - 1))
            def _():
                self.line(piece, 0).wait_send()
                if late:
                    self.late_line(piece, 0).wait_send()

            @pl.when(jnp.logical_and(piece >= d, d > 0))
            def _():
                self.line(piece, 1).wait_send()
                if late:
                    self.late_line(piece, 1).wait_send()

            return carry

        lax.fori_loop(0, nz, done, 0)


def gather_sems(count, nz):
    dma = pltpu.SemaphoreType.DMA
    piece = [dma((count, nz))] * 8
    return (
        [dma((count, 2, nz))] * 2 + piece + [dma((count, 4))] * 2 + [dma((count, 2, nz))] * 2
        + [dma((count, 5))] * 2 + [dma((count,))]
    )


class Reduce:
    def __init__(self, nz, chunks, ring, ins, outs, refs):
        n = len(chunks)
        self.nz, self.chunks, self.ring, self.ins, self.outs, self.n = (nz, chunks, ring, ins, outs, n)
        self.accs, self.sends1, self.recvs1, self.sends2, self.recvs2, self.lines = (
            refs[i * n : (i + 1) * n] for i in range(6)
        )
        refs = refs[6 * n :]
        kinds = sorted(set(ring))
        self.buffers = {kind: refs[3 * i : 3 * i + 3] for i, kind in enumerate(kinds)}
        (self.ld, self.cs, self.cr, self.s1s, self.s1r, self.s2s, self.s2r, self.zs, self.zr) = refs[
            3 * len(kinds) :
        ]
        self.turns = [ring[:k].count(kind) for k, kind in enumerate(ring)]
        self.r = lax.axis_index("role")
        self.d = lax.axis_index("dp")
        m = lax.axis_index("mp")
        self.mx, self.my = (shift_of(m, 1), shift_of(m, 2))
        self.columns = (shift_of(m, 3), self.mx, self.my, m)

    def part(self, k, column, first):
        array, start, width = self.chunks[k]
        return self.ins[array].at[column, pl.ds(first, self.nz), :, pl.ds(start, width)]

    def core(self, k, j):
        return remote(
            self.part(k, self.columns[j], (1 - self.r) * self.nz), self.accs[k].at[j], self.cs.at[k, j], self.cr.at[k, j],
            {"role": 1 - self.r},
        )

    def loaded(self, k, j):
        far_ring, near_ring, own_ring = self.buffers[self.ring[k]]
        if j == 0:
            return far_ring.at[self.turns[k] % 3]
        if j == 3:
            return own_ring.at[self.turns[k] % 2]
        return near_ring.at[self.turns[k] % 2, j - 1]

    def load(self, k, j):
        return pltpu.make_async_copy(self.part(k, self.columns[j], self.r * self.nz), self.loaded(k, j), self.ld.at[k, j])

    def first(self, k, piece):
        half = self.chunks[k][2] // 2
        low, high = (pl.ds(0, half), pl.ds(half, half))
        return (
            remote(self.sends1[k].at[piece, :, low], self.recvs1[k].at[piece, :, low],
                   self.s1s.at[k, 0, piece], self.s1r.at[k, 0, piece], {"mp": self.my}),
            remote(self.sends1[k].at[piece, :, high], self.recvs1[k].at[piece, :, high],
                   self.s1s.at[k, 1, piece], self.s1r.at[k, 1, piece], {"mp": self.mx}),
        )

    def second(self, k, piece):
        return (
            remote(self.sends2[k].at[0, piece], self.recvs2[k].at[0, piece],
                   self.s2s.at[k, 0, piece], self.s2r.at[k, 0, piece], {"mp": self.mx}),
            remote(self.sends2[k].at[1, piece], self.recvs2[k].at[1, piece],
                   self.s2s.at[k, 1, piece], self.s2r.at[k, 1, piece], {"mp": self.my}),
        )

    def right(self, k, piece):
        return remote(self.accs[k].at[3, piece], self.lines[k].at[piece], self.zs.at[k, piece],
                      self.zr.at[k, piece], {"dp": self.d + 1})

    def left(self, k, piece):
        slot = jnp.where(piece == self.d - 1, self.nz, piece)
        return remote(self.accs[k].at[3, piece], self.lines[k].at[slot], self.zs.at[k, piece],
                      self.zr.at[k, slot], {"dp": self.d - 1})

    def line_in(self, k, slot):
        return remote(self.lines[k].at[slot], self.lines[k].at[slot], self.zs.at[k, 0], self.zr.at[k, slot],
                      {"role": 1 - self.r})

    def each(self, body):
        def step(t, carry):
            off = self.nz - 1 - t

            @pl.when(self.d + off < self.nz)
            def _():
                body(self.d + off)

            @pl.when(self.d - off >= 0)
            def _():
                body(self.d - off)

            return carry

        lax.fori_loop(0, self.nz - 1, step, 0)
        body(self.d)

    def fetch(self, k):
        for j in range(4):
            self.core(k, j).start()
        self.load(k, 0).start()

    def combine(self, k, j):
        self.core(k, j).wait_recv()
        self.load(k, j).wait()

    def to_far(self, k):
        self.load(k, 1).start()
        self.load(k, 2).start()
        self.combine(k, 0)

        def send_far(piece):
            self.sends1[k][piece] = (self.accs[k][0, piece] + self.loaded(k, 0)[piece]).astype(self.sends1[k].dtype)
            for copy in self.first(k, piece):
                copy.start()

        self.each(send_far)

    def to_near(self, k):
        half = self.chunks[k][2] // 2
        self.load(k, 3).start()
        self.combine(k, 1)
        self.combine(k, 2)

        def send_near(piece):
            for copy in self.first(k, piece):
                copy.wait_recv()
            relayed = self.recvs1[k][piece].astype(jnp.float32)
            lane = lax.broadcasted_iota(jnp.int32, relayed.shape, 1)
            self.sends2[k][0, piece] = (
                self.accs[k][1, piece] + self.loaded(k, 1)[piece] + jnp.where(lane < half, relayed, 0.0)
            ).astype(self.sends2[k].dtype)
            self.sends2[k][1, piece] = (
                self.accs[k][2, piece] + self.loaded(k, 2)[piece] + jnp.where(lane < half, 0.0, relayed)
            ).astype(self.sends2[k].dtype)
            for copy in self.second(k, piece):
                copy.start()

        self.each(send_near)

    def to_line(self, k):
        self.combine(k, 3)

        def pass_on(piece):
            for copy in self.second(k, piece):
                copy.wait_recv()
            self.accs[k][3, piece] += (
                self.loaded(k, 3)[piece]
                + self.recvs2[k][0, piece].astype(jnp.float32)
                + self.recvs2[k][1, piece].astype(jnp.float32)
            )

            @pl.when(piece > self.d)
            def _():
                @pl.when(self.d > 0)
                def _():
                    self.line_in(k, piece).wait_recv()
                    self.accs[k][3, piece] += self.lines[k][piece]

                self.right(k, piece).start()

            @pl.when(piece < self.d)
            def _():
                @pl.when(self.d < self.nz - 1)
                def _():
                    self.line_in(k, piece).wait_recv()
                    self.accs[k][3, piece] += self.lines[k][piece]

                self.left(k, piece).start()

        self.each(pass_on)

    def to_own(self, k):
        self.combine(k, 3)

        def add(piece):
            for copy in self.second(k, piece):
                copy.wait_recv()
            self.accs[k][3, piece] += (
                self.loaded(k, 3)[piece]
                + self.recvs2[k][0, piece].astype(jnp.float32)
                + self.recvs2[k][1, piece].astype(jnp.float32)
            )

        self.each(add)

    def along(self, k, hop):
        nz = self.nz

        def forward(piece):
            if hop > 0:
                self.line_in(k, piece).wait_recv()
                self.accs[k][3, piece] += self.lines[k][piece]

        @pl.when(self.d == hop)
        def _():
            def send(t, carry):
                forward(nz - 1 - t)
                self.right(k, nz - 1 - t).start()
                return carry

            lax.fori_loop(0, nz - 1 - hop, send, 0)

        @pl.when(self.d == nz - 1 - hop)
        def _():
            def send(piece, carry):
                forward(piece)
                self.left(k, piece).start()
                return carry

            lax.fori_loop(0, nz - 1 - hop, send, 0)

    def land(self, k):
        array, start, width = self.chunks[k]

        @pl.when(self.d > 0)
        def _():
            self.line_in(k, self.d).wait_recv()
            self.accs[k][3, self.d] += self.lines[k][self.d]

        @pl.when(self.d < self.nz - 1)
        def _():
            self.line_in(k, self.nz).wait_recv()
            self.accs[k][3, self.d] += self.lines[k][self.nz]

        total = self.accs[k][3, self.d]
        self.outs[array][:, start : start + width] = total
        return jnp.sum(total * total, keepdims=True)

    def finish(self):
        for k in range(self.n):
            for j in range(4):
                self.core(k, j).wait_send()

            def done(piece, carry):
                for copy in self.first(k, piece):
                    copy.wait_send()
                for copy in self.second(k, piece):
                    copy.wait_send()

                @pl.when(piece != self.d)
                def _():
                    self.right(k, piece).wait_send()

                return carry

            lax.fori_loop(0, self.nz, done, 0)


def reduce_ring(grads, chunks):
    shapes = [(grads[array].shape[2], width) for array, _, width in chunks]
    kinds = sorted(set(shapes))
    return (shapes, kinds, tuple(kinds.index(s) for s in shapes))


def reduce_scratch(grads, wire_types, chunks, nz):
    groups = 4
    n = len(chunks)
    dma = pltpu.SemaphoreType.DMA
    shapes, kinds, ring = reduce_ring(grads, chunks)
    wires = [wire_types[array] for array, _, _ in chunks]
    return (
        [pltpu.VMEM((groups, nz, *s), jnp.float32) for s in shapes]
        + [pltpu.VMEM((nz, *s), t) for s, t in zip(shapes, wires)] * 2
        + [pltpu.VMEM((2, nz, *s), t) for s, t in zip(shapes, wires)] * 2
        + [pltpu.VMEM((nz + 1, *s), jnp.float32) for s in shapes]
        + [
            pltpu.VMEM((*slots, nz, *kinds[kind]), jnp.float32)
            for kind in range(len(kinds))
            for slots in (
                (min(3, ring.count(kind)),),
                (min(2, ring.count(kind)), 2),
                (min(2, ring.count(kind)),),
            )
        ]
        + [dma((n, groups))] * 3
        + [dma((n, 2, nz))] * 4
        + [dma((n, nz)), dma((n, nz + 1))]
    )


def peers(nz):
    r = lax.axis_index("role")
    d = lax.axis_index("dp")
    m = lax.axis_index("mp")
    group = [{"role": role, "mp": shift_of(m, by)} for role in (r, 1 - r) for by in range(4)][1:]
    return (group, [{"dp": lax.rem(d + j, nz)} for j in range(1, nz)])


def reduce_kernel(nz, chunks, ring, count, stats_in, *refs):
    ins = refs[:count]
    outs = refs[count : 2 * count]
    stats_out, near, near_in, far_in, ns, nr, fs, fr = refs[2 * count : 2 * count + 8]
    work = Reduce(nz, chunks, ring, ins, outs, refs[2 * count + 8 :])
    n = len(chunks)
    r = lax.axis_index("role")
    d = lax.axis_index("dp")
    m = lax.axis_index("mp")
    groups = 4
    group, far = peers(nz)
    greet(group + far)
    ahead = 2
    for k in range(min(ahead, n)):
        work.fetch(k)
    squares = jnp.zeros((1, 1), jnp.float32)
    for step in range(n + 3):
        if step + ahead < n:
            work.fetch(step + ahead)
        if step < n:
            work.to_far(step)
        if 0 <= step - 1 < n:
            work.to_near(step - 1)
        if 0 <= step - 2 < n:
            work.to_line(step - 2)
        if 0 <= step - 3 < n:
            squares += work.land(step - 3)

    mine = r * groups + m
    row = lax.broadcasted_iota(jnp.int32, (8, 128), 0)
    near[...] = stats_in[...] + jnp.where(row == 1, squares, 0.0)
    near_in[mine] = near[...]
    copies = []
    for j, peer in enumerate(group):
        copies.append(remote(near, near_in.at[mine], ns.at[j], nr.at[mine], peer))
        copies[-1].start()
    for j, peer in enumerate(group):
        slot = peer["role"] * groups + peer["mp"]
        remote(near, near_in.at[slot], ns.at[j], nr.at[slot], peer).wait_recv()
    for copy in copies:
        copy.wait_send()
    summed = near_in[0]
    for j in range(1, 2 * groups):
        summed += near_in[j]
    near[...] = summed
    far_in[d] = summed
    copies = []
    for j, peer in enumerate(far):
        copies.append(remote(near, far_in.at[d], fs.at[j], fr.at[d], peer))
        copies[-1].start()
    for j, peer in enumerate(far):
        slot = peer["dp"]
        remote(near, far_in.at[slot], fs.at[j], fr.at[slot], peer).wait_recv()
    for copy in copies:
        copy.wait_send()
    summed = far_in[0]
    for j in range(1, nz):
        summed += far_in[j]
    stats_out[...] = summed
    work.finish()


def reduce_all(grads, wire_types, chunks, stats):
    nz = lax.axis_size("dp")
    groups = lax.axis_size("mp")
    count = len(grads)
    dma = pltpu.SemaphoreType.DMA
    vmem = pl.BlockSpec(memory_space=pltpu.VMEM)
    return pl.pallas_call(
        functools.partial(reduce_kernel, nz, chunks, reduce_ring(grads, chunks)[2], count),
        out_shape=[jax.ShapeDtypeStruct(g.shape[2:], jnp.float32) for g in grads]
        + [jax.ShapeDtypeStruct((8, 128), jnp.float32)],
        in_specs=[vmem] + [pl.BlockSpec(memory_space=pl.ANY)] * count,
        out_specs=[vmem] * (count + 1),
        scratch_shapes=[
            pltpu.VMEM((8, 128), jnp.float32),
            pltpu.VMEM((2 * groups, 8, 128), jnp.float32),
            pltpu.VMEM((nz, 8, 128), jnp.float32),
            dma((2 * groups,)),
            dma((2 * groups,)),
            dma((nz,)),
            dma((nz,)),
        ]
        + reduce_scratch(grads, wire_types, chunks, nz),
        compiler_params=pltpu.CompilerParams(
            collective_id=2, has_side_effects=True, vmem_limit_bytes=60 * 2**20
        ),
    )(stats, *grads)


def dot(left, right):
    return lax.dot_general(left, right, (((1,), (0,)), ((), ())), preferred_element_type=F32)


def dot_rt(left, right):
    return lax.dot_general(left, right, (((1,), (1,)), ((), ())), preferred_element_type=F32)


def dot_lt(left, right):
    return lax.dot_general(left, right, (((0,), (0,)), ((), ())), preferred_element_type=F32)


def chain(term, count):
    total = term(0)
    for g in range(1, count):
        total += term(g)
    return total


def head_lanes(lanes, size, head):
    lane = lax.broadcasted_iota(jnp.int32, (1, lanes), 1)
    return jnp.logical_and(lane >= head * size, lane < (head + 1) * size)


def only(mask, value):
    return jnp.where(mask, value, jnp.zeros_like(value))


def turn(value, by):
    return pltpu.roll(value, by % value.shape[1], 1)


def stats_of(stream):
    mean = jnp.mean(stream, -1, keepdims=True)
    cent = stream - mean
    scale = lax.rsqrt(jnp.mean(cent * cent, -1, keepdims=True) + 1e-06)
    return (cent * scale, scale)


def norm_back_of(normed, scale, gain, grad):
    gain_grad = jnp.sum(grad * normed, 0, keepdims=True)
    scaled = grad * gain
    inner = (
        scaled
        - jnp.mean(scaled, -1, keepdims=True)
        - normed * jnp.mean(scaled * normed, -1, keepdims=True)
    )
    return (scale * inner, gain_grad)


def normal_cdf(hidden):
    return 0.5 * (1.0 + lax.erf(hidden * ROOT_HALF))


def encoder_forward(sizes, asked, pix, place, bias, bank, gains, keep_refs, finish):
    local, hidden, size = sizes
    groups = bank.shape[0]
    heads = local // size
    up = 4 * local
    down = up + hidden
    emb = down + hidden
    wide = local + 64
    saving = keep_refs is not None
    if saving:
        (norm1, scale1, mixer_in, qs, ks, vs, probs_out, mixed_out, norm2, scale2, dense, slope,
         active) = keep_refs
    terms = None
    for g in range(groups):
        term = dot_rt(pix[g], bank[g, :, emb : emb + wide])
        terms = term if terms is None else terms + term
    start = place() + terms
    normed, scale = stats_of(start)
    a = (normed * gains[0]).astype(BF)
    if saving:
        norm1[...] = normed
        scale1[...] = scale
        mixer_in[...] = a
    yield
    terms = None
    for g in range(groups):
        t = dot(a, bank[g, :, : 3 * local + 64]).astype(BF).astype(F32)
        q = t[:asked, :wide].astype(BF)
        k = turn(t, -local)[:, :wide].astype(BF)
        v = t[:, 2 * local :].astype(BF)
        if saving:
            qs[g] = q
            ks[g] = k
            vs[g] = v
        mixed = jnp.zeros((asked, wide), F32)
        for h in range(heads):
            mask = head_lanes(wide, size, h)
            score = dot_rt(only(mask, q), k) * size**-0.5 + bias[...]
            score = jnp.exp(score - jnp.max(score, -1, keepdims=True))
            probs = score / jnp.sum(score, -1, keepdims=True)
            if saving:
                probs_out[g * heads + h] = probs
            mixed += only(mask, dot(probs.astype(BF), v))
        mixed = turn(mixed, 64).astype(BF)
        if saving:
            mixed_out[g] = mixed
        term = dot_rt(mixed, bank[g, :, up - wide : up])
        terms = term if terms is None else terms + term
        yield
    middle = start[:asked] + terms
    normed, scale = stats_of(middle)
    b = (normed * gains[1]).astype(BF)
    if saving:
        norm2[...] = normed
        scale2[...] = scale
        dense[...] = b
    terms = None
    for g in range(groups):
        pre = dot(b, bank[g, :, up:down])
        cdf = normal_cdf(pre)
        act = (pre * cdf).astype(BF)
        if saving:
            slope[g] = cdf + pre * jnp.exp(-0.5 * pre * pre) * INVERSE_ROOT
            active[g] = act
        term = dot_rt(act, bank[g, :, down:emb])
        terms = term if terms is None else terms + term
        yield
    finish(middle + terms)


def front_kernel(nz, sizes, asked, firsts, *refs):
    local, hidden, size = sizes
    wide = local + 64
    sources, refs = (refs[:4], refs[4:])
    (half, tables, shuffle, bias_t, bias_s, hot), refs = (refs[:6], refs[6:])
    (bank_out, pbank_out, context, wanted, pix_s, vec_rows, total), refs = (refs[:7], refs[7:])
    keep_refs, refs = (refs[:13], refs[13:])
    (vec_all, tbank, bank, pix_t, px, pr, own_sem, out_sem), sems = (refs[:8], refs[8:])
    r = lax.axis_index("role")
    d = lax.axis_index("dp")
    m = lax.axis_index("mp")
    groups = tbank.shape[0]
    width = tbank.shape[1]
    nears = [{"mp": shift_of(m, by)} for by in range(1, groups)]
    greet([{"role": 1 - r}] + nears + [{"dp": lax.rem(d + j, nz)} for j in range(1, nz)])
    targets = (vec_all, tbank, bank, pbank_out)
    arrays = [
        Gather(k, sources[k], targets[k], sources[k].shape[-2], sources[k].shape[-1], firsts[k],
               sems, (r, d, m), nz)
        for k in range(4)
    ]
    small, teach, learn, guess = arrays

    def pixel(j):
        peer = shift_of(m, j)
        return remote(half.at[peer], pix_t.at[m], px.at[j], pr.at[j], {"mp": peer})

    def pixel_in(j):
        peer = shift_of(m, j)
        return remote(half.at[peer], pix_t.at[peer], px.at[j], pr.at[j], {"mp": peer})

    own_pixel = pltpu.make_async_copy(half.at[m], pix_t.at[m], own_sem.at[0])
    own_pixel.start()
    small.start()
    for j in range(1, groups):
        pixel(j).start()
    teach.start()
    for step in small.steps():
        step()

    def place():
        rows = tables[...].astype(F32)
        return rows[:, :width] + rows[:, width : 2 * width] + rows[:, 2 * width :]

    def place_shuffled():
        rows = dot(shuffle[...], tables[...])
        return rows[:, :width] + rows[:, width : 2 * width] + rows[:, 2 * width :]

    for j, step in enumerate(teach.steps()):
        if j == 3:
            learn.start()
        step()
        if j == 1:
            small.take_diagonal()
    small.complete()

    share = vec_rows.shape[1] * 4 // (vec_all.shape[0] * vec_all.shape[1])
    lanes = vec_all.shape[3]
    lane = lax.broadcasted_iota(jnp.int32, (1, lanes), 1)

    def vector_row(kind, j):
        row = jnp.zeros((1, width), F32)
        count = width // share
        for c in range(count):
            flat = j * count + c
            piece = vec_all[flat % groups, flat // groups].astype(F32)[kind : kind + 1]
            piece = only(lane < share, piece)
            row += turn(jnp.concatenate([piece, jnp.zeros((1, width - lanes), F32)], 1), c * share)
        return row

    gains_t = [vector_row(1, j) for j in range(2)]
    rows_s = [vector_row(0, j) for j in range(4)]
    vec_rows[...] = jnp.concatenate(rows_s, 0)
    counts = jnp.zeros((1, 1), F32)
    for c in range(groups):
        for o in range(vec_all.shape[1]):
            counts += vec_all[c, o].astype(F32)[2:3, :1]
    total[...] = jnp.broadcast_to(counts, total.shape)
    own_pixel.wait()
    for j in range(1, groups):
        pixel_in(j).wait_recv()
    for g in range(groups):
        pix_s[g] = dot(shuffle[...], pix_t[g]).astype(BF)

    def teacher_rows(latent):
        chosen = dot(hot[...], stats_of(latent)[0].astype(BF))
        for g in range(groups):
            wanted[g] = turn(chosen, -g * local)[:, :wide].astype(BF)

    def student_rows(latent):
        at = lax.broadcasted_iota(jnp.int32, (1, wide), 1)
        for g in range(groups):
            context[g] = only(at >= 64, turn(latent, 64 - g * local)[:, :wide]).astype(BF)

    teacher = encoder_forward(
        sizes, pix_t.shape[1], pix_t, place, bias_t, tbank, gains_t, None, teacher_rows
    )
    student = encoder_forward(
        sizes, asked, pix_s, place_shuffled, bias_s, bank, rows_s[:2], keep_refs, student_rows
    )

    def advance(work, parts):
        for _ in range(parts):
            next(work, None)

    def bank_copy(g):
        return pltpu.make_async_copy(bank.at[g], bank_out.at[g], out_sem.at[g])

    steps = learn.steps()
    for j, step in enumerate(steps):
        if j == 3:
            guess.start()
        step()
        if j == 1:
            teach.take_diagonal()
        if j == 3:
            teach.complete()
        if j > 3:
            advance(teacher, 2)
    for j, step in enumerate(guess.steps()):
        step()
        if j == 1:
            learn.take_diagonal()
            advance(teacher, 100)
            learn.complete()
            for g in range(groups):
                bank_copy(g).start()
        if j > 1:
            advance(student, 1)
    guess.take_diagonal()
    advance(student, 100)
    for g in range(groups):
        bank_copy(g).wait()
    guess.complete()
    for j in range(1, groups):
        pixel(j).wait_send()
    for array in arrays:
        array.finish()


def run_front(packs, half, tables, shuffle, keep_t, keep_s, hot, sizes, asked):
    local, hidden, size = sizes
    nz = lax.axis_size("dp")
    groups = lax.axis_size("mp")
    owners = lax.axis_size("role") * nz
    vec, target, master, predictor = packs
    rows = half.shape[1]
    width = target.shape[0] * owners
    columns = target.shape[1]
    wide = local + 64
    make = jax.ShapeDtypeStruct
    hbm = pl.BlockSpec(memory_space=pl.ANY)
    vmem = pl.BlockSpec(memory_space=pltpu.VMEM)
    dma = pltpu.SemaphoreType.DMA
    bank = make((groups, width, columns), BF)
    outs = [
        bank,
        make((groups, owners, *predictor.shape[1:]), BF),
        make((groups, asked, wide), BF),
        make((groups, hot.shape[0], wide), BF),
        make((groups, rows, wide), BF),
        make((4, width), F32),
        make((8, 128), F32),
        make((rows, width), F32),
        make((rows, 1), F32),
        make((rows, width), BF),
        make((groups, asked, wide), BF),
        make((groups, rows, wide), BF),
        make((groups, rows, wide), BF),
        make((HEADS, asked, rows), F32),
        make((groups, asked, wide), BF),
        make((asked, width), F32),
        make((asked, 1), F32),
        make((asked, width), BF),
        make((groups, asked, hidden), F32),
        make((groups, asked, hidden), BF),
    ]

    def first(cols):
        return cols - (cols // 5 // 256) * 256

    firsts = (vec.shape[2], first(columns), first(columns), first(predictor.shape[2]))
    bias_t, bias_s = (((keep - 1.0) * 1e9)[None, :] for keep in (keep_t, keep_s))
    return pl.pallas_call(
        functools.partial(front_kernel, nz, sizes, asked, firsts),
        out_shape=outs,
        in_specs=[hbm] * 5 + [vmem] * 5,
        out_specs=[hbm] * 2 + [vmem] * (len(outs) - 2),
        scratch_shapes=[
            pltpu.VMEM((groups, owners, *vec.shape[1:]), BF),
            pltpu.VMEM(bank.shape, BF),
            pltpu.VMEM(bank.shape, BF),
            pltpu.VMEM((groups, rows, wide), BF),
            dma((groups,)),
            dma((groups,)),
            dma((1,)),
            dma((groups,)),
        ]
        + gather_sems(4, nz),
        compiler_params=pltpu.CompilerParams(
            collective_id=1, has_side_effects=True, vmem_limit_bytes=60 * 2**20
        ),
    )(vec, target, master, predictor, half, tables, shuffle, bias_t, bias_s, hot)


def predictor_kernel(
    sizes, ctx, wanted, tables, shuffle, hot, keep, weight, total, bank, vec_rows,
    grad_ctx, grads, small, loss_out, probs_s, q_s, k_s, v_s, mixed_s, slope_s, active_s, dt_s
):
    local, plocal, phidden, size, blocks = sizes
    groups = bank.shape[0]
    heads = plocal // size
    lanes = 128
    up = 4 * plocal
    down = up + phidden
    head_at = down + phidden
    entry_at = head_at + local
    wide = local + 64
    nctx = ctx.shape[1]
    asked = hot.shape[0]
    rows = nctx + asked
    tlen = asked // blocks
    pwidth = groups * plocal
    first, second, final, token = (
        vec_rows[i : i + 1, j : j + pwidth] for i in (2, 3) for j in (0, pwidth)
    )
    root = size**-0.5
    key = lax.broadcasted_iota(jnp.int32, (asked, rows), 1) - nctx
    query = lax.broadcasted_iota(jnp.int32, (asked, rows), 0)
    reached = jnp.logical_or(key < 0, key // tlen == query // tlen)
    bias = (only(reached, jnp.broadcast_to(keep[...], (asked, rows))) - 1.0) * 1e9

    def places(chosen):
        found = dot(chosen, tables[...])
        return found[:, :pwidth] + found[:, pwidth : 2 * pwidth] + found[:, 2 * pwidth :]


    entry = places(shuffle[:nctx]) + chain(
        lambda g: dot_rt(ctx[g], bank[g, :, entry_at - 64 : entry_at + local]), groups
    )
    tgt_in = places(hot[...]) + token
    norm_c, scale_c = stats_of(entry)
    norm_t, scale_t = stats_of(tgt_in)
    a_c = (norm_c * first).astype(BF)
    a_t = (norm_t * first).astype(BF)
    a = jnp.concatenate([a_c, a_t], 0)

    def attend(g):
        t = dot(a, bank[g, :, :up]).astype(BF).astype(F32)
        q = t[nctx:, :lanes].astype(BF)
        k = turn(t, -plocal)[:, :lanes].astype(BF)
        v = turn(t, -2 * plocal)[:, :lanes].astype(BF)
        q_s[g] = q
        k_s[g] = k
        v_s[g] = v
        mixed = jnp.zeros((asked, lanes), F32)
        for h in range(heads):
            mask = head_lanes(lanes, size, h)
            score = dot_rt(only(mask, q), k) * root + bias
            score = jnp.exp(score - jnp.max(score, -1, keepdims=True))
            probs = score / jnp.sum(score, -1, keepdims=True)
            probs_s[g * heads + h] = probs
            mixed += only(mask, dot(probs.astype(BF), v))
        mixed = turn(mixed, lanes - plocal).astype(BF)
        mixed_s[g] = mixed
        return dot_rt(mixed, bank[g, :, up - lanes : up])

    middle = tgt_in + chain(attend, groups)
    norm2, scale2 = stats_of(middle)
    b = (norm2 * second).astype(BF)

    def feed(g):
        pre = dot(b, bank[g, :, up:down])
        cdf = normal_cdf(pre)
        slope_s[g] = cdf + pre * jnp.exp(-0.5 * pre * pre) * INVERSE_ROOT
        act = (pre * cdf).astype(BF)
        active_s[g] = act
        return dot_rt(act, bank[g, :, down:head_at])

    out = middle + chain(feed, groups)
    norm_f, scale_f = stats_of(out)
    head_in = (norm_f * final).astype(BF)
    lane = lax.broadcasted_iota(jnp.int32, (1, wide), 1)
    losses = jnp.zeros((1, 1), F32)
    row_weight = weight[...]

    def judge(g):
        nonlocal losses
        pred = dot(head_in, bank[g, :, head_at : head_at + wide])
        diff = only(lane < local, pred - wanted[g].astype(F32))
        losses += jnp.sum(row_weight * diff * diff, keepdims=True)
        grad = (2.0 * row_weight * diff / total[0:1, 0:1]).astype(BF)
        g_head = dot_lt(head_in, grad)
        grads[g, :, head_at : head_at + lanes] = g_head[:, :lanes]
        grads[g, :, head_at + lanes : head_at + wide] = g_head[:, lanes:]
        return dot_rt(grad, bank[g, :, head_at : head_at + wide])

    grad_out, g_final = norm_back_of(norm_f, scale_f, final, chain(judge, groups))
    loss_out[...] = jnp.broadcast_to(losses, loss_out.shape)

    branch = grad_out.astype(BF)

    def feed_back(g):
        grads[g, :, down:head_at] = dot_lt(branch, active_s[g])
        grad_pre = (dot(branch, bank[g, :, down:head_at]) * slope_s[g]).astype(BF)
        grads[g, :, up:down] = dot_lt(b, grad_pre)
        return dot_rt(grad_pre, bank[g, :, up:down])

    grad_norm, g_second = norm_back_of(norm2, scale2, second, chain(feed_back, groups))
    grad_mid = grad_out + grad_norm
    mixer = grad_mid.astype(BF)

    def attend_back(g):
        g_o = dot_lt(mixer, mixed_s[g])
        gm = turn(dot(mixer, bank[g, :, up - lanes : up]), plocal - lanes).astype(BF)
        q, k, v = (q_s[g], k_s[g], v_s[g])
        valid = head_lanes(lanes, plocal, 0)
        gm = only(valid, gm)
        qv = only(valid, q)
        block = lax.broadcasted_iota(jnp.int32, (asked, 1), 0) // tlen
        q_spread = jnp.concatenate([only(block == i, qv) for i in range(blocks)], 1)
        gm_spread = jnp.concatenate([only(block == i, gm) for i in range(blocks)], 1)
        dqs, dkt, dvt, dkc, dvc = ([], [], [], [], [])
        for h in range(heads):
            mask = head_lanes(lanes, size, h)
            masks = jnp.concatenate([mask] * blocks, 1)
            probs = probs_s[g * heads + h]
            gmh = only(mask, gm)
            grad_probs = dot_rt(gmh, v)
            ds = (probs * (grad_probs - jnp.sum(grad_probs * probs, -1, keepdims=True))).astype(BF)
            pb = probs.astype(BF)
            qh = only(mask, qv)
            dqs.append(dot(ds, only(mask, k)))
            dkt.append(dot_lt(ds[:, nctx:], qh))
            dvt.append(dot_lt(pb[:, nctx:], gmh))
            dkc.append(dot_lt(ds[:, :nctx], only(masks, q_spread)))
            dvc.append(dot_lt(pb[:, :nctx], only(masks, gm_spread)))
        dq = (sum(dqs[1:], dqs[0]) * root).astype(BF).astype(F32)
        dk = (sum(dkt[1:], dkt[0]) * root).astype(BF).astype(F32)
        dv = sum(dvt[1:], dvt[0]).astype(BF).astype(F32)
        kc = (sum(dkc[1:], dkc[0]) * root).astype(BF).astype(F32)
        vc = sum(dvc[1:], dvc[0]).astype(BF).astype(F32)
        kc = chain(lambda i: kc[:, i * lanes : (i + 1) * lanes], blocks)
        vc = chain(lambda i: vc[:, i * lanes : (i + 1) * lanes], blocks)

        def lay(query, keyed, valued):
            count = keyed.shape[0]
            blank = jnp.zeros((count, up - lanes), F32)
            wideq = 0.0 if query is None else jnp.concatenate([query, blank], 1)
            return (
                wideq
                + turn(jnp.concatenate([keyed, blank], 1), plocal)
                + turn(jnp.concatenate([valued, blank], 1), 2 * plocal)
            )

        dt_t = lay(dq, dk, dv).astype(BF)
        dt_c = lay(None, kc, vc)
        high = dt_c.astype(BF)
        low = (dt_c - high.astype(F32)).astype(BF)
        dt = jnp.concatenate([high, dt_t], 0)
        dt_s[g] = jnp.concatenate([dt, low], 0)
        g_qkv = dot_lt(jnp.concatenate([a, a_c], 0), jnp.concatenate([dt, low], 0))
        grads[g, :, : up - lanes] = g_qkv[:, : up - lanes]
        grads[g, :, up - lanes : up] = g_qkv[:, up - lanes :] + g_o

    for g in range(groups):
        attend_back(g)
    grad_a = chain(lambda g: dot_rt(dt_s[g], bank[g, :, :up]), groups)
    grad_in_t, g_first_t = norm_back_of(norm_t, scale_t, first, grad_a[nctx:rows])
    grad_in_c, g_first_c = norm_back_of(
        norm_c, scale_c, first, grad_a[:nctx] + grad_a[rows:]
    )
    g_token = jnp.sum(grad_in_t + grad_mid, 0, keepdims=True)
    small[...] = jnp.concatenate([g_first_t + g_first_c, g_second, g_final, g_token], 0)
    grad_entry = grad_in_c.astype(BF)
    width = groups * local
    grad_context = jnp.zeros((nctx, width), F32)
    for g in range(groups):
        g_entry = dot_lt(grad_entry, ctx[g])
        grads[g, :, entry_at - 64 : entry_at + 64] += g_entry[:, :lanes]
        grads[g, :, entry_at + 64 : entry_at + local] = g_entry[:, lanes:]
        part = only(lane >= 64, dot(grad_entry, bank[g, :, entry_at - 64 : entry_at + local]))
        full = jnp.concatenate([part, jnp.zeros((nctx, width - wide), F32)], 1)
        grad_context += turn(full, g * local - 64)
    grad_ctx[...] = grad_context


def run_predictor(ctx, wanted, tables, shuffle, hot, keep, weight, total, bank, vec_rows, sizes):
    local, plocal, phidden, size, blocks = sizes
    groups = bank.shape[0]
    nctx = ctx.shape[1]
    pwidth = groups * plocal
    asked = hot.shape[0]
    rows = nctx + asked
    make = jax.ShapeDtypeStruct
    outs = [
        make((nctx, groups * local), F32),
        make(bank.shape, F32),
        make((4, pwidth), F32),
        make((8, 128), F32),
    ]
    ins = [ctx, wanted, tables, shuffle, hot, keep, weight, total, bank, vec_rows]
    vmem = pl.BlockSpec(memory_space=pltpu.VMEM)
    scratch = [
        pltpu.VMEM((HEADS, asked, rows), F32),
        pltpu.VMEM((groups, asked, 128), BF),
        pltpu.VMEM((groups, rows, 128), BF),
        pltpu.VMEM((groups, rows, 128), BF),
        pltpu.VMEM((groups, asked, 128), BF),
        pltpu.VMEM((groups, asked, phidden), F32),
        pltpu.VMEM((groups, asked, phidden), BF),
        pltpu.VMEM((groups, rows + nctx, 4 * plocal), BF),
    ]
    return pl.pallas_call(
        functools.partial(predictor_kernel, sizes),
        out_shape=outs,
        in_specs=[vmem] * len(ins),
        out_specs=[vmem] * len(outs),
        scratch_shapes=scratch,
        compiler_params=pltpu.CompilerParams(vmem_limit_bytes=56 * 2**20),
    )(*ins)


def encoder_back_kernel(
    sizes, nz, chunks, ring, grad_ctx, pix, norm1, scale1, mixer_in, qs, ks, vs, probs_in, mixed_in, norm2, scale2,
    dense, slope, active, bank, gains, pgrads, grads, small, psum, squares, wide_s, tail_s, dt_s,
    sems, *refs
):
    local, hidden, size = sizes
    groups = bank.shape[0]
    heads = local // size
    up = 4 * local
    down = up + hidden
    emb = down + hidden
    wide = local + 64
    span = 3 * local + 64
    asked = grad_ctx.shape[0]
    rows = norm1.shape[0]
    first, second = (gains[0:1], gains[1:2])
    root = size**-0.5
    work = Reduce(nz, chunks, ring, (pgrads,), (psum,), refs)
    group, far = peers(nz)
    greet(group + far)
    n = len(chunks)
    stages = [functools.partial(work.to_far, k) for k in range(n)]
    stages += [functools.partial(work.to_near, k) for k in range(n)]
    stages += [functools.partial(work.to_own, k) for k in range(n)]
    stages += [functools.partial(work.along, k, hop) for hop in range(nz - 1) for k in range(n)]
    for k in range(n):
        work.fetch(k)

    def serve(count=1):
        for stage in stages[:count]:
            stage()
        del stages[:count]

    grad_out = grad_ctx[...]
    branch = grad_out.astype(BF)

    def ship(g, start, width):
        return pltpu.make_async_copy(
            wide_s.at[g % 2, :, pl.ds(0, width)],
            grads.at[g, :, pl.ds(start, width)],
            sems.at[g % 2],
        )

    def feed_back(g):
        if g >= 2:
            ship(g - 2, up, 2 * hidden).wait()
        wide_s[g % 2, :, hidden : 2 * hidden] = dot_lt(branch, active[g])
        grad_pre = (dot(branch, bank[g, :, down:emb]) * slope[g]).astype(BF)
        wide_s[g % 2, :, :hidden] = dot_lt(dense[...], grad_pre)
        ship(g, up, 2 * hidden).start()
        serve()
        return dot_rt(grad_pre, bank[g, :, up:down])

    grad_norm, g_second = norm_back_of(norm2[...], scale2[...], second, chain(feed_back, groups))
    grad_mid = grad_out + grad_norm
    mixer = grad_mid.astype(BF)
    for g in range(groups - 2, groups):
        ship(g, up, 2 * hidden).wait()
    valid = head_lanes(wide, local, 0)

    def attend_back(g):
        g_o = dot_lt(mixer, mixed_in[g])
        gm = turn(dot(mixer, bank[g, :, up - wide : up]), -64).astype(BF)
        q, k, v = (only(valid, qs[g]), ks[g], vs[g])
        gm = only(valid, gm)
        dqs, dks, dvs = ([], [], [])
        for h in range(heads):
            mask = head_lanes(wide, size, h)
            probs = probs_in[g * heads + h]
            gmh = only(mask, gm)
            grad_probs = dot_rt(gmh, v)
            ds = (probs * (grad_probs - jnp.sum(grad_probs * probs, -1, keepdims=True))).astype(BF)
            dqs.append(dot(ds, only(mask, k)))
            dks.append(dot_lt(ds, only(mask, q)))
            dvs.append(dot_lt(probs.astype(BF), gmh))
        dq = (sum(dqs[1:], dqs[0]) * root).astype(BF).astype(F32)
        dk = (sum(dks[1:], dks[0]) * root).astype(BF).astype(F32)
        dv = sum(dvs[1:], dvs[0]).astype(BF).astype(F32)
        dq = jnp.concatenate([dq, jnp.zeros((rows - asked, wide), F32)], 0)
        blank = jnp.zeros((rows, span - wide), F32)
        dt = (
            jnp.concatenate([dq, blank], 1)
            + turn(jnp.concatenate([dk, blank], 1), local)
            + jnp.concatenate([blank, dv], 1)
        ).astype(BF)
        dt_s[g] = dt
        g_qkv = dot_lt(mixer_in[...], dt)
        if g >= 2:
            ship(g - 2, 0, up).wait()
        slot = wide_s.at[g % 2]
        slot[:, : up - wide] = g_qkv[:, : up - wide]
        slot[:, up - wide : span] = g_qkv[:, up - wide :] + g_o[:, : span - up + wide]
        slot[:, span:up] = g_o[:, span - up + wide :]
        ship(g, 0, up).start()

    for g in range(groups):
        attend_back(g)
        serve(2 if g < 2 else 1)
    grad_a = chain(lambda g: dot_rt(dt_s[g], bank[g, :, :span]), groups)
    grad_start, g_first = norm_back_of(norm1[...], scale1[...], first, grad_a)
    grad_start = (
        grad_start + jnp.concatenate([grad_mid, jnp.zeros((rows - asked, grad_mid.shape[1]), F32)], 0)
    ).astype(BF)
    small[...] = jnp.concatenate([g_first, g_second], 0)

    def tail(g):
        return pltpu.make_async_copy(
            tail_s.at[g], grads.at[g, :, pl.ds(emb, wide)], sems.at[2 + g]
        )

    for g in range(groups):
        tail_s[g] = dot_lt(grad_start, pix[g])
        tail(g).start()
        serve()
    serve(len(stages))
    for g in range(groups - 2, groups):
        ship(g, 0, up).wait()
    total = jnp.zeros((1, 1), F32)
    for k in range(n):
        total += work.land(k)
    squares[...] = jnp.broadcast_to(total, squares.shape)
    for g in range(groups):
        tail(g).wait()
    work.finish()


def run_encoder_back(grad_ctx, pix, saved, bank, gains, sizes, pgrads, chunks):
    local, hidden, size = sizes
    groups, width, columns = bank.shape
    rows = pix.shape[1]
    make = jax.ShapeDtypeStruct
    nz = lax.axis_size("dp")
    ins = [grad_ctx, pix, *saved, bank, gains]
    hbm = pl.BlockSpec(memory_space=pl.ANY)
    vmem = pl.BlockSpec(memory_space=pltpu.VMEM)
    return pl.pallas_call(
        functools.partial(encoder_back_kernel, sizes, nz, chunks, reduce_ring([pgrads], chunks)[2]),
        out_shape=[
            make(bank.shape, F32),
            make((2, width), F32),
            make(pgrads.shape[2:], F32),
            make((8, 128), F32),
        ],
        in_specs=[vmem] * len(ins) + [hbm],
        out_specs=[hbm, vmem, vmem, vmem],
        scratch_shapes=[
            pltpu.VMEM((2, width, 2 * hidden), F32),
            pltpu.VMEM((groups, width, local + 64), F32),
            pltpu.VMEM((groups, rows, 3 * local + 64), BF),
            pltpu.SemaphoreType.DMA((2 + groups,)),
        ]
        + reduce_scratch([pgrads], (BF,), chunks, nz),
        compiler_params=pltpu.CompilerParams(
            collective_id=3, has_side_effects=True, vmem_limit_bytes=60 * 2**20
        ),
    )(*ins, pgrads)


def per_device(
    pixels,
    context_slots,
    context_count,
    target_slots,
    target_count,
    encoder_in,
    encoder_out,
    predictor_in,
    predictor_out,
    vectors,
    first_encoder_in,
    first_encoder_out,
    first_predictor_in,
    first_predictor_out,
    first_vectors,
    second_encoder_in,
    second_encoder_out,
    second_predictor_in,
    second_predictor_out,
    second_vectors,
    target_encoder_in,
    target_encoder_out,
    target_vectors,
):
    groups = lax.axis_size("mp")
    owners = lax.axis_size("role") * lax.axis_size("dp")
    width = encoder_in.shape[0] * owners
    pwidth = predictor_in.shape[0] * owners
    local, plocal = (width // groups, pwidth // groups)
    pixel = pixels.shape[2]
    hidden = encoder_in.shape[1] - 3 * local
    phidden = predictor_in.shape[1] - 3 * plocal - local
    patches = pixels.shape[1]
    image = lax.axis_index("role") * groups + lax.axis_index("mp")

    slots = lax.dynamic_index_in_dim(context_slots, image, 0, keepdims=False)
    count = lax.dynamic_index_in_dim(context_count, image, 0, keepdims=False)
    tslots = lax.dynamic_index_in_dim(target_slots, image, 0, keepdims=False)
    tcount = lax.dynamic_index_in_dim(target_count, image, 0, keepdims=False)
    nctx = slots.shape[0]
    blocks, tlen = tslots.shape
    rows = -(-patches // 16) * 16
    share = vectors.shape[0]

    patch = jnp.arange(patches)
    hits = slots[:, None] == patch[None, :]
    member = jnp.any(hits, 0)
    order = jnp.where(
        member,
        jnp.sum(jnp.where(hits, jnp.arange(nctx)[:, None], 0), 0),
        nctx + jnp.cumsum(1 - member.astype(jnp.int32)) - 1,
    )
    order = jnp.pad(order, (0, rows - patches), constant_values=-1)
    slot_of = jnp.arange(rows)
    shuffle = (order[None, :] == slot_of[:, None]).astype(BF)
    ckeep = (jnp.arange(nctx) < count).astype(F32)
    tkeep = (jnp.arange(tlen)[None, :] < tcount[:, None]).astype(F32)
    tflat = tslots.reshape(-1)
    keep = jnp.concatenate([ckeep, tkeep.reshape(-1)])[None, :]
    hot = (tflat[:, None] == slot_of[None, :]).astype(BF)

    vec = jnp.stack([vectors, target_vectors, jnp.broadcast_to(jnp.sum(tcount).astype(F32), (share,))])
    vec = jnp.pad(vec, ((0, 13), (0, -share % LANES))).astype(BF)
    half = lax.dynamic_slice_in_dim(pixels, lax.axis_index("role") * groups, groups, 0)
    half = jnp.pad(half, ((0, 0), (0, rows - patches), (0, 64)))
    sizes = (local, hidden, width // HEADS)
    bank, pbank, context, wanted, student_pix, vec_rows, total, *saved = run_front(
        (
            vec[None],
            pack_encoder(target_encoder_in, target_encoder_out, local, pixel),
            pack_encoder(encoder_in, encoder_out, local, pixel),
            pack_predictor(predictor_in, predictor_out, local, plocal, phidden)[None],
        ),
        half,
        np.pad(in_three(sincos(width)), ((0, rows - patches), (0, 0))),
        shuffle,
        (slot_of < patches).astype(F32),
        (slot_of < count).astype(F32),
        hot,
        sizes,
        nctx,
    )
    target_total = total[0, 0]
    grad_context, g_pbank, p_small, loss = run_predictor(
        context,
        wanted,
        np.pad(in_three(sincos(pwidth)), ((0, rows - patches), (0, 0))),
        shuffle,
        hot,
        keep,
        tkeep.reshape(-1, 1),
        total,
        pbank.reshape(groups, pwidth, -1),
        vec_rows,
        (local, plocal, phidden, pwidth // HEADS, blocks),
    )
    g_bank, e_small, r_pbank, p_squares = run_encoder_back(
        grad_context, student_pix, saved, bank, vec_rows, sizes,
        g_pbank.reshape(pbank.shape), chunk_list([(0, g_pbank.shape[2], 768)]),
    )
    g_vec = jnp.concatenate([e_small.reshape(-1), p_small.reshape(-1)])
    g_vec = g_vec.reshape(owners, groups, 1, -1).transpose(1, 0, 2, 3)
    row = jnp.arange(8)[:, None]
    r_bank, r_vec, stats = reduce_all(
        [
            g_bank.reshape(groups, owners, width // owners, -1),
            jnp.pad(g_vec, ((0, 0), (0, 0), (0, 7), (0, -share % (2 * LANES)))),
        ],
        (BF, F32),
        chunk_list([(0, g_bank.shape[2], 512), (1, -(-share // 256) * 256, 256)]),
        jnp.where(row == 0, loss, jnp.where(row == 1, p_squares, 0.0)),
    )
    r_pin, r_pout = unpack_predictor(r_pbank, local, plocal, phidden)
    r_in, r_out = unpack_encoder(r_bank, local, hidden, pixel)
    r_vec = r_vec[0, :share]
    loss_total, squares = (stats[0, 0], stats[1, 0])
    grad_norm = jnp.sqrt(squares)
    scale = jnp.minimum(1.0, CLIP / (grad_norm + 1e-06))
    new_in, m_in, v_in = adamw(
        encoder_in, r_in, first_encoder_in, second_encoder_in, scale, RATE_MATRIX, DECAY
    )
    new_out, m_out, v_out = adamw(
        encoder_out, r_out, first_encoder_out, second_encoder_out, scale, RATE_MATRIX, DECAY
    )
    new_pin, m_pin, v_pin = adamw(
        predictor_in, r_pin, first_predictor_in, second_predictor_in, scale, RATE_MATRIX, DECAY
    )
    new_pout, m_pout, v_pout = adamw(
        predictor_out, r_pout, first_predictor_out, second_predictor_out, scale, RATE_MATRIX, DECAY
    )
    new_vec, m_vec, v_vec = adamw(
        vectors, r_vec, first_vectors, second_vectors, scale, RATE_VECTOR, 0.0
    )
    ema_in = MOMENTUM_EMA * target_encoder_in + (1.0 - MOMENTUM_EMA) * new_in
    ema_out = MOMENTUM_EMA * target_encoder_out + (1.0 - MOMENTUM_EMA) * new_out
    ema_vec = MOMENTUM_EMA * target_vectors + (1.0 - MOMENTUM_EMA) * new_vec
    return (
        new_in, new_out, new_pin, new_pout, new_vec,
        m_in, m_out, m_pin, m_pout, m_vec,
        v_in, v_out, v_pin, v_pout, v_vec,
        ema_in, ema_out, ema_vec,
        loss_total, target_total, grad_norm,
    )


def solution(mesh):
    bank_in, bank_out, small = (
        P(("role", "dp"), "mp"),
        P("mp", ("role", "dp")),
        P(("role", "dp", "mp")),
    )
    five = (bank_in, bank_out, bank_in, bank_out, small)
    three = (bank_in, bank_out, small)
    return jax.shard_map(
        per_device,
        mesh=mesh,
        in_specs=(
            P("dp", None, "mp"),
            P("dp", None),
            P("dp"),
            P("dp", None, None),
            P("dp", None),
        )
        + five * 3
        + three,
        out_specs=five * 3 + three + (P(), P(), P()),
        check_vma=False,
    )
```

```python
import functools

import jax
import jax.numpy as jnp
import numpy as np
from jax import lax
from jax.experimental import pallas as pl
from jax.experimental.pallas import tpu as pltpu
from jax.sharding import PartitionSpec as P

HEADS = 12
GRID = 14
STEP = 10

BETA_ONE = 0.9
BETA_TWO = 0.999
ADAM_EPS = 1e-08
RATE_MATRIX = 0.03
RATE_VECTOR = 0.3
DECAY = 0.05
MOMENTUM_EMA = 0.9
CLIP = 0.1
ROOT_HALF = 0.7071067811865476
INVERSE_ROOT = 0.3989422804014327

BF = jnp.bfloat16
F32 = jnp.float32
LANES = 128


def sincos(width):
    quarter = width // 4
    omega = 1.0 / 10000.0 ** (np.arange(quarter, dtype=np.float64) / quarter)
    place = np.arange(GRID * GRID)
    rows = (place // GRID)[:, None] * omega[None, :]
    cols = (place % GRID)[:, None] * omega[None, :]
    return np.concatenate([np.sin(rows), np.cos(rows), np.sin(cols), np.cos(cols)], -1).astype(
        np.float32
    )


def in_three(table):
    parts, rest = ([], table)
    for _ in range(3):
        parts.append(rest.astype(jnp.bfloat16))
        rest = rest - parts[-1].astype(np.float32)
    return np.concatenate(parts, 1)


def chunk_list(arrays):
    return tuple(
        (array, start, min(step, columns - start))
        for array, columns, step in arrays
        for start in range(0, columns, step)
    )


def pack_encoder(w_in, w_out, local, pixel):
    turned = w_out.T
    used = w_in.shape[1] + turned.shape[1]
    return jnp.concatenate(
        [
            w_in[:, : 3 * local],
            turned[:, pixel : pixel + local],
            w_in[:, 3 * local :],
            turned[:, pixel + local :],
            turned[:, :pixel],
            jnp.zeros((w_in.shape[0], -used % (2 * LANES)), F32),
        ],
        1,
    ).astype(BF)


def pack_predictor(p_in, p_out, local, plocal, phidden):
    turned = p_out.T
    return jnp.concatenate(
        [
            p_in[:, : 3 * plocal],
            turned[:, local : local + plocal],
            p_in[:, 3 * plocal : 3 * plocal + phidden],
            turned[:, local + plocal :],
            p_in[:, 3 * plocal + phidden :],
            turned[:, :local],
        ],
        1,
    ).astype(BF)


def adamw(weight, grad, first, second, scale, rate, decay):
    grad = grad * scale
    first = BETA_ONE * first + (1.0 - BETA_ONE) * grad
    second = BETA_TWO * second + (1.0 - BETA_TWO) * grad * grad
    mean_hat = first / (1.0 - BETA_ONE**STEP)
    square_hat = second / (1.0 - BETA_TWO**STEP)
    return (
        weight - rate * (mean_hat / (jnp.sqrt(square_hat) + ADAM_EPS) + decay * weight),
        first,
        second,
    )


def shift_of(rank, by):
    return jnp.bitwise_xor(rank, by)


def greet(peers):
    barrier = pltpu.get_barrier_semaphore()
    for peer in peers:
        pl.semaphore_signal(barrier, inc=1, device_id=peer, device_id_type=pl.DeviceIdType.MESH)
    pl.semaphore_wait(barrier, len(peers))


def remote(src, dst, send, recv, where):
    return pltpu.make_async_remote_copy(
        src_ref=src, dst_ref=dst, send_sem=send, recv_sem=recv,
        device_id=where, device_id_type=pl.DeviceIdType.MESH,
    )


class Gather:
    def __init__(self, place, source, target, rows, cols, first, sems, where, nz):
        (self.zs, self.zr, self.xs, self.xr, self.ys, self.yr, self.rxs, self.rxr, self.rys,
         self.ryr, self.bs, self.br, self.bzs, self.bzr, self.cs, self.cr, self.own) = sems
        self.k = place
        self.source, self.target = (source, target)
        self.rows, self.cols, self.first, self.nz = (rows, cols, first, nz)
        self.r, self.d, self.m = where
        self.base = self.r * nz
        self.mx, self.my, self.mf = (shift_of(self.m, by) for by in (1, 2, 3))

    def at(self, column, owner, count, start, width):
        if len(self.target.shape) == 4:
            return self.target.at[column, pl.ds(owner, count), :, pl.ds(start, width)]
        row = pl.multiple_of(owner * self.rows, self.rows)
        return self.target.at[column, pl.ds(row, count * self.rows), pl.ds(start, width)]

    def mine(self, start, width):
        if len(self.target.shape) == 4:
            return self.source.at[:, :, pl.ds(start, width)]
        return self.source.at[:, pl.ds(start, width)]

    def line(self, piece, way, own=False):
        spot = self.at(self.m, self.base + piece, 1, 0, self.first)
        return remote(
            self.mine(0, self.first) if own else spot, spot,
            self.zs.at[self.k, way, piece], self.zr.at[self.k, way, piece],
            {"dp": self.d + 1 - 2 * way},
        )

    def across(self, piece, own=False):
        spot = self.at(self.m, self.base + piece, 1, 0, self.first)
        source = self.mine(0, self.first) if own else spot
        return (
            remote(source, spot, self.xs.at[self.k, piece], self.xr.at[self.k, piece], {"mp": self.mx}),
            remote(source, spot, self.ys.at[self.k, piece], self.yr.at[self.k, piece], {"mp": self.my}),
        )

    def arrived(self, piece):
        return [
            remote(spot, spot, send.at[self.k, piece], recv.at[self.k, piece], {"mp": peer})
            for spot, send, recv, peer in (
                (self.at(self.mx, self.base + piece, 1, 0, self.first), self.xs, self.xr, self.mx),
                (self.at(self.my, self.base + piece, 1, 0, self.first), self.ys, self.yr, self.my),
            )
        ]

    def halves(self, low, high, piece):
        half = self.first // 2 if self.first % 256 == 0 else self.first
        one = self.at(low, self.base + piece, 1, 0, half)
        copies = [remote(one, one, self.rys.at[self.k, piece], self.ryr.at[self.k, piece], {"mp": self.my})]
        if half < self.first:
            two = self.at(high, self.base + piece, 1, half, half)
            copies.append(
                remote(two, two, self.rxs.at[self.k, piece], self.rxr.at[self.k, piece], {"mp": self.mx})
            )
        return copies

    def relay(self, piece):
        return self.halves(self.mx, self.my, piece)

    def diagonal(self, piece):
        return self.halves(self.mf, self.mf, piece)

    def late_across(self):
        width = self.cols - self.first
        spot = self.at(self.m, self.base + self.d, 1, self.first, width)
        source = self.mine(self.first, width)
        return (
            remote(source, spot, self.bs.at[self.k, 0], self.br.at[self.k, 0], {"mp": self.mx}),
            remote(source, spot, self.bs.at[self.k, 1], self.br.at[self.k, 1], {"mp": self.my}),
        )

    def late_arrived(self):
        width = self.cols - self.first
        spots = [self.at(c, self.base + self.d, 1, self.first, width) for c in (self.mx, self.my)]
        return [
            remote(spot, spot, self.bs.at[self.k, i], self.br.at[self.k, i], {"mp": peer})
            for i, (spot, peer) in enumerate(zip(spots, (self.mx, self.my)))
        ]

    def late_halves(self, low, high):
        half = (self.cols - self.first) // 2
        one = self.at(low, self.base + self.d, 1, self.first, half)
        two = self.at(high, self.base + self.d, 1, self.first + half, half)
        return (
            remote(one, one, self.bs.at[self.k, 2], self.br.at[self.k, 2], {"mp": self.my}),
            remote(two, two, self.bs.at[self.k, 3], self.br.at[self.k, 3], {"mp": self.mx}),
        )

    def late_line(self, piece, way):
        spot = self.at(slice(None), self.base + piece, 1, self.first, self.cols - self.first)
        return remote(
            spot, spot, self.bzs.at[self.k, way, piece], self.bzr.at[self.k, way, piece],
            {"dp": self.d + 1 - 2 * way},
        )

    def core(self, slot, incoming=False):
        base = (1 - self.r) * self.nz if incoming else self.base
        if slot == 4:
            spot = self.at(slice(None), base, self.nz, self.first, self.cols - self.first)
        else:
            column = (self.m, self.mx, self.my, self.mf)[slot]
            spot = self.at(column, base, self.nz, 0, self.first)
        return remote(spot, spot, self.cs.at[self.k, slot], self.cr.at[self.k, slot], {"role": 1 - self.r})

    def copy_own(self):
        return pltpu.make_async_copy(
            self.mine(0, self.cols), self.at(self.m, self.base + self.d, 1, 0, self.cols),
            self.own.at[self.k],
        )

    def start(self):
        d, nz = (self.d, self.nz)

        @pl.when(d < nz - 1)
        def _():
            self.line(d, 0, True).start()

        @pl.when(d > 0)
        def _():
            self.line(d, 1, True).start()

        for copy in self.across(d, True):
            copy.start()
        if self.first < self.cols:
            for copy in self.late_across():
                copy.start()
        self.copy_own().start()

    def pass_on(self, piece):
        for copy in self.arrived(piece):
            copy.wait_recv()
        for copy in self.relay(piece):
            copy.start()

    def step(self, t):
        d, nz = (self.d, self.nz)
        left = d - 1 - t
        right = d + 1 + t

        @pl.when(left >= 0)
        def _():
            self.line(left, 0).wait_recv()

            @pl.when(d < nz - 1)
            def _():
                self.line(left, 0).start()

            for copy in self.across(left):
                copy.start()

        @pl.when(right < nz)
        def _():
            self.line(right, 1).wait_recv()

            @pl.when(d > 0)
            def _():
                self.line(right, 1).start()

            for copy in self.across(right):
                copy.start()

        if t == 0:
            self.pass_on(d)
        else:
            @pl.when(left + 1 >= 0)
            def _():
                self.pass_on(left + 1)

            @pl.when(right - 1 < nz)
            def _():
                self.pass_on(right - 1)

    def late_turn(self):
        for copy in self.late_arrived():
            copy.wait_recv()
        for copy in self.late_halves(self.mx, self.my):
            copy.start()

    def late_start(self):
        for copy in self.late_halves(self.mf, self.mf):
            copy.wait_recv()
        self.copy_own().wait()

        @pl.when(self.d < self.nz - 1)
        def _():
            self.late_line(self.d, 0).start()

        @pl.when(self.d > 0)
        def _():
            self.late_line(self.d, 1).start()

    def late_step(self, t):
        d, nz = (self.d, self.nz)
        left = d - 1 - t
        right = d + 1 + t

        @pl.when(left >= 0)
        def _():
            self.late_line(left, 0).wait_recv()

            @pl.when(d < nz - 1)
            def _():
                self.late_line(left, 0).start()

        @pl.when(right < nz)
        def _():
            self.late_line(right, 1).wait_recv()

            @pl.when(d > 0)
            def _():
                self.late_line(right, 1).start()

    def last_pass(self):
        @pl.when(self.d == self.nz - 1)
        def _():
            self.pass_on(0)

        if self.nz > 1:
            @pl.when(self.d == 0)
            def _():
                self.pass_on(self.nz - 1)

        if self.first == self.cols:
            self.copy_own().wait()
        for slot in range(3):
            self.core(slot).start()

    def take_diagonal(self):
        def take(piece, carry):
            for copy in self.diagonal(piece):
                copy.wait_recv()
            return carry

        lax.fori_loop(0, self.nz, take, 0)
        self.core(3).start()
        if self.first < self.cols:
            self.core(4).start()

    def steps(self):
        late = self.first < self.cols
        early = [functools.partial(self.step, t) for t in range(self.nz - 1)] + [self.last_pass]
        late = []
        if self.first < self.cols:
            late = [self.late_turn, self.late_start]
            late += [functools.partial(self.late_step, t) for t in range(self.nz - 1)]
        todo = []
        while early or late:
            todo += early[:1] + late[:1]
            early, late = (early[1:], late[1:])
        return todo

    def complete(self):
        for slot in range(5 if self.first < self.cols else 4):
            self.core(slot, True).wait_recv()

    def finish(self):
        d, nz = (self.d, self.nz)
        late = self.first < self.cols
        for slot in range(5 if late else 4):
            self.core(slot).wait_send()
        if late:
            for copy in self.late_across() + self.late_halves(self.mx, self.my):
                copy.wait_send()

        def done(piece, carry):
            for copy in self.across(piece):
                copy.wait_send()
            for copy in self.relay(piece):
                copy.wait_send()

            @pl.when(jnp.logical_and(piece <= d, d < nz - 1))
            def _():
                self.line(piece, 0).wait_send()
                if late:
                    self.late_line(piece, 0).wait_send()

            @pl.when(jnp.logical_and(piece >= d, d > 0))
            def _():
                self.line(piece, 1).wait_send()
                if late:
                    self.late_line(piece, 1).wait_send()

            return carry

        lax.fori_loop(0, nz, done, 0)


def gather_sems(count, nz):
    dma = pltpu.SemaphoreType.DMA
    piece = [dma((count, nz))] * 8
    return (
        [dma((count, 2, nz))] * 2 + piece + [dma((count, 4))] * 2 + [dma((count, 2, nz))] * 2
        + [dma((count, 5))] * 2 + [dma((count,))]
    )


def reduce_kernel(nz, chunks, ring, count, stats_in, *refs):
    n = len(chunks)
    ins = refs[:count]
    outs = refs[count : 2 * count]
    stats_out = refs[2 * count]
    rest = refs[2 * count + 1 :]
    accs = rest[:n]
    sends1 = rest[n : 2 * n]
    recvs1 = rest[2 * n : 3 * n]
    sends2 = rest[3 * n : 4 * n]
    recvs2 = rest[4 * n : 5 * n]
    lines = rest[5 * n : 6 * n]
    rest = rest[6 * n :]
    kinds = sorted(set(ring))
    buffers = {kind: rest[3 * i : 3 * i + 3] for i, kind in enumerate(kinds)}
    (near, near_in, far_in, ld, cs, cr, s1s, s1r, s2s, s2r, zs, zr, ns, nr, fs, fr) = rest[
        3 * len(kinds) :
    ]
    turns = [ring[:k].count(kind) for k, kind in enumerate(ring)]
    r = lax.axis_index("role")
    d = lax.axis_index("dp")
    m = lax.axis_index("mp")
    groups = 4
    mx = shift_of(m, 1)
    my = shift_of(m, 2)
    mf = shift_of(m, 3)
    columns = (mf, mx, my, m)
    group = [
        {"role": role, "mp": shift_of(m, by)}
        for role in (r, 1 - r)
        for by in range(groups)
    ][1:]
    far = [{"dp": lax.rem(d + j, nz)} for j in range(1, nz)]
    greet(group + far)

    def part(k, column, first):
        array, start, width = chunks[k]
        return ins[array].at[column, pl.ds(first, nz), :, pl.ds(start, width)]

    def core(k, j):
        return remote(
            part(k, columns[j], (1 - r) * nz), accs[k].at[j], cs.at[k, j], cr.at[k, j],
            {"role": 1 - r},
        )

    def loaded(k, j):
        far_ring, near_ring, own_ring = buffers[ring[k]]
        if j == 0:
            return far_ring.at[turns[k] % 3]
        if j == 3:
            return own_ring.at[turns[k] % 2]
        return near_ring.at[turns[k] % 2, j - 1]

    def load(k, j):
        return pltpu.make_async_copy(part(k, columns[j], r * nz), loaded(k, j), ld.at[k, j])

    def first(k, piece):
        half = chunks[k][2] // 2
        low, high = (pl.ds(0, half), pl.ds(half, half))
        return (
            remote(sends1[k].at[piece, :, low], recvs1[k].at[piece, :, low],
                   s1s.at[k, 0, piece], s1r.at[k, 0, piece], {"mp": my}),
            remote(sends1[k].at[piece, :, high], recvs1[k].at[piece, :, high],
                   s1s.at[k, 1, piece], s1r.at[k, 1, piece], {"mp": mx}),
        )

    def second(k, piece):
        return (
            remote(sends2[k].at[0, piece], recvs2[k].at[0, piece],
                   s2s.at[k, 0, piece], s2r.at[k, 0, piece], {"mp": mx}),
            remote(sends2[k].at[1, piece], recvs2[k].at[1, piece],
                   s2s.at[k, 1, piece], s2r.at[k, 1, piece], {"mp": my}),
        )

    def right(k, piece):
        return remote(accs[k].at[3, piece], lines[k].at[piece], zs.at[k, piece],
                      zr.at[k, piece], {"dp": d + 1})

    def left(k, piece):
        slot = jnp.where(piece == d - 1, nz, piece)
        return remote(accs[k].at[3, piece], lines[k].at[slot], zs.at[k, piece],
                      zr.at[k, slot], {"dp": d - 1})

    def line_in(k, slot):
        return remote(lines[k].at[slot], lines[k].at[slot], zs.at[k, 0], zr.at[k, slot],
                      {"role": 1 - r})

    def each(body):
        def step(t, carry):
            off = nz - 1 - t

            @pl.when(d + off < nz)
            def _():
                body(d + off)

            @pl.when(d - off >= 0)
            def _():
                body(d - off)

            return carry

        lax.fori_loop(0, nz - 1, step, 0)
        body(d)

    def fetch(k):
        for j in range(groups):
            core(k, j).start()
        load(k, 0).start()

    def combine(k, j):
        core(k, j).wait_recv()
        load(k, j).wait()

    def to_far(k):
        load(k, 1).start()
        load(k, 2).start()
        combine(k, 0)

        def send_far(piece):
            sends1[k][piece] = (accs[k][0, piece] + loaded(k, 0)[piece]).astype(sends1[k].dtype)
            for copy in first(k, piece):
                copy.start()

        each(send_far)

    def to_near(k):
        half = chunks[k][2] // 2
        load(k, 3).start()
        combine(k, 1)
        combine(k, 2)

        def send_near(piece):
            for copy in first(k, piece):
                copy.wait_recv()
            relayed = recvs1[k][piece].astype(jnp.float32)
            lane = lax.broadcasted_iota(jnp.int32, relayed.shape, 1)
            sends2[k][0, piece] = (
                accs[k][1, piece] + loaded(k, 1)[piece] + jnp.where(lane < half, relayed, 0.0)
            ).astype(sends2[k].dtype)
            sends2[k][1, piece] = (
                accs[k][2, piece] + loaded(k, 2)[piece] + jnp.where(lane < half, 0.0, relayed)
            ).astype(sends2[k].dtype)
            for copy in second(k, piece):
                copy.start()

        each(send_near)

    def to_line(k):
        combine(k, 3)

        def pass_on(piece):
            for copy in second(k, piece):
                copy.wait_recv()
            accs[k][3, piece] += (
                loaded(k, 3)[piece]
                + recvs2[k][0, piece].astype(jnp.float32)
                + recvs2[k][1, piece].astype(jnp.float32)
            )

            @pl.when(piece > d)
            def _():
                @pl.when(d > 0)
                def _():
                    line_in(k, piece).wait_recv()
                    accs[k][3, piece] += lines[k][piece]

                right(k, piece).start()

            @pl.when(piece < d)
            def _():
                @pl.when(d < nz - 1)
                def _():
                    line_in(k, piece).wait_recv()
                    accs[k][3, piece] += lines[k][piece]

                left(k, piece).start()

        each(pass_on)

    def land(k):
        array, start, width = chunks[k]

        @pl.when(d > 0)
        def _():
            line_in(k, d).wait_recv()
            accs[k][3, d] += lines[k][d]

        @pl.when(d < nz - 1)
        def _():
            line_in(k, nz).wait_recv()
            accs[k][3, d] += lines[k][nz]

        total = accs[k][3, d]
        outs[array][:, start : start + width] = total
        return jnp.sum(total * total, keepdims=True)

    ahead = 2
    for k in range(min(ahead, n)):
        fetch(k)
    squares = jnp.zeros((1, 1), jnp.float32)
    for step in range(n + 3):
        if step + ahead < n:
            fetch(step + ahead)
        if step < n:
            to_far(step)
        if 0 <= step - 1 < n:
            to_near(step - 1)
        if 0 <= step - 2 < n:
            to_line(step - 2)
        if 0 <= step - 3 < n:
            squares += land(step - 3)

    mine = r * groups + m
    row = lax.broadcasted_iota(jnp.int32, (8, 128), 0)
    near[...] = jnp.where(row == 0, stats_in[...], squares)
    near_in[mine] = near[...]
    copies = []
    for j, peer in enumerate(group):
        copies.append(remote(near, near_in.at[mine], ns.at[j], nr.at[mine], peer))
        copies[-1].start()
    for j, peer in enumerate(group):
        slot = peer["role"] * groups + peer["mp"]
        remote(near, near_in.at[slot], ns.at[j], nr.at[slot], peer).wait_recv()
    for copy in copies:
        copy.wait_send()
    summed = near_in[0]
    for j in range(1, 2 * groups):
        summed += near_in[j]
    near[...] = summed
    far_in[d] = summed
    copies = []
    for j, peer in enumerate(far):
        copies.append(remote(near, far_in.at[d], fs.at[j], fr.at[d], peer))
        copies[-1].start()
    for j, peer in enumerate(far):
        slot = peer["dp"]
        remote(near, far_in.at[slot], fs.at[j], fr.at[slot], peer).wait_recv()
    for copy in copies:
        copy.wait_send()
    summed = far_in[0]
    for j in range(1, nz):
        summed += far_in[j]
    stats_out[...] = summed

    for k in range(n):
        for j in range(groups):
            core(k, j).wait_send()

        def done(piece, carry):
            for copy in first(k, piece):
                copy.wait_send()
            for copy in second(k, piece):
                copy.wait_send()

            @pl.when(piece != d)
            def _():
                right(k, piece).wait_send()

            return carry

        lax.fori_loop(0, nz, done, 0)


def reduce_all(grads, wire_types, chunks, stats):
    nz = lax.axis_size("dp")
    groups = lax.axis_size("mp")
    count = len(grads)
    n = len(chunks)
    dma = pltpu.SemaphoreType.DMA
    shapes = [(grads[array].shape[2], width) for array, _, width in chunks]
    kinds = sorted(set(shapes))
    ring = tuple(kinds.index(s) for s in shapes)
    wires = [wire_types[array] for array, _, _ in chunks]
    vmem = pl.BlockSpec(memory_space=pltpu.VMEM)
    scratch = (
        [pltpu.VMEM((groups, nz, *s), jnp.float32) for s in shapes]
        + [pltpu.VMEM((nz, *s), t) for s, t in zip(shapes, wires)] * 2
        + [pltpu.VMEM((2, nz, *s), t) for s, t in zip(shapes, wires)] * 2
        + [pltpu.VMEM((nz + 1, *s), jnp.float32) for s in shapes]
        + [
            pltpu.VMEM((*slots, nz, *kinds[kind]), jnp.float32)
            for kind in range(len(kinds))
            for slots in ((min(3, ring.count(kind)),), (min(2, ring.count(kind)), 2), (min(2, ring.count(kind)),))
        ]
        + [
            pltpu.VMEM((8, 128), jnp.float32),
            pltpu.VMEM((2 * groups, 8, 128), jnp.float32),
            pltpu.VMEM((nz, 8, 128), jnp.float32),
            dma((n, groups)),
            dma((n, groups)),
            dma((n, groups)),
            dma((n, 2, nz)),
            dma((n, 2, nz)),
            dma((n, 2, nz)),
            dma((n, 2, nz)),
            dma((n, nz)),
            dma((n, nz + 1)),
            dma((2 * groups,)),
            dma((2 * groups,)),
            dma((nz,)),
            dma((nz,)),
        ]
    )
    return pl.pallas_call(
        functools.partial(reduce_kernel, nz, chunks, ring, count),
        out_shape=[jax.ShapeDtypeStruct(g.shape[2:], jnp.float32) for g in grads]
        + [jax.ShapeDtypeStruct((8, 128), jnp.float32)],
        in_specs=[vmem] + [pl.BlockSpec(memory_space=pl.ANY)] * count,
        out_specs=[vmem] * (count + 1),
        scratch_shapes=scratch,
        compiler_params=pltpu.CompilerParams(
            collective_id=2, has_side_effects=True, vmem_limit_bytes=59 * 2**20
        ),
    )(stats, *grads)


def dot(left, right):
    return lax.dot_general(left, right, (((1,), (0,)), ((), ())), preferred_element_type=F32)


def dot_rt(left, right):
    return lax.dot_general(left, right, (((1,), (1,)), ((), ())), preferred_element_type=F32)


def dot_lt(left, right):
    return lax.dot_general(left, right, (((0,), (0,)), ((), ())), preferred_element_type=F32)


def chain(term, count):
    total = term(0)
    for g in range(1, count):
        total += term(g)
    return total


def head_lanes(lanes, size, head):
    lane = lax.broadcasted_iota(jnp.int32, (1, lanes), 1)
    return jnp.logical_and(lane >= head * size, lane < (head + 1) * size)


def only(mask, value):
    return jnp.where(mask, value, jnp.zeros_like(value))


def turn(value, by):
    return pltpu.roll(value, by % value.shape[1], 1)


def stats_of(stream):
    mean = jnp.mean(stream, -1, keepdims=True)
    cent = stream - mean
    scale = lax.rsqrt(jnp.mean(cent * cent, -1, keepdims=True) + 1e-06)
    return (cent * scale, scale)


def norm_back_of(normed, scale, gain, grad):
    gain_grad = jnp.sum(grad * normed, 0, keepdims=True)
    scaled = grad * gain
    inner = (
        scaled
        - jnp.mean(scaled, -1, keepdims=True)
        - normed * jnp.mean(scaled * normed, -1, keepdims=True)
    )
    return (scale * inner, gain_grad)


def normal_cdf(hidden):
    return 0.5 * (1.0 + lax.erf(hidden * ROOT_HALF))


def encoder_forward(sizes, asked, pix, place, bias, bank, gains, keep_refs, finish):
    local, hidden, size = sizes
    groups = bank.shape[0]
    heads = local // size
    up = 4 * local
    down = up + hidden
    emb = down + hidden
    wide = local + 64
    saving = keep_refs is not None
    if saving:
        (norm1, scale1, mixer_in, qs, ks, vs, probs_out, mixed_out, norm2, scale2, dense, slope,
         active) = keep_refs
    terms = None
    for g in range(groups):
        term = dot_rt(pix[g], bank[g, :, emb : emb + wide])
        terms = term if terms is None else terms + term
    start = place() + terms
    normed, scale = stats_of(start)
    a = (normed * gains[0]).astype(BF)
    if saving:
        norm1[...] = normed
        scale1[...] = scale
        mixer_in[...] = a
    yield
    terms = None
    for g in range(groups):
        t = dot(a, bank[g, :, : 3 * local + 64]).astype(BF).astype(F32)
        q = t[:asked, :wide].astype(BF)
        k = turn(t, -local)[:, :wide].astype(BF)
        v = t[:, 2 * local :].astype(BF)
        if saving:
            qs[g] = q
            ks[g] = k
            vs[g] = v
        mixed = jnp.zeros((asked, wide), F32)
        for h in range(heads):
            mask = head_lanes(wide, size, h)
            score = dot_rt(only(mask, q), k) * size**-0.5 + bias[...]
            score = jnp.exp(score - jnp.max(score, -1, keepdims=True))
            probs = score / jnp.sum(score, -1, keepdims=True)
            if saving:
                probs_out[g * heads + h] = probs
            mixed += only(mask, dot(probs.astype(BF), v))
        mixed = turn(mixed, 64).astype(BF)
        if saving:
            mixed_out[g] = mixed
        term = dot_rt(mixed, bank[g, :, up - wide : up])
        terms = term if terms is None else terms + term
        yield
    middle = start[:asked] + terms
    normed, scale = stats_of(middle)
    b = (normed * gains[1]).astype(BF)
    if saving:
        norm2[...] = normed
        scale2[...] = scale
        dense[...] = b
    terms = None
    for g in range(groups):
        pre = dot(b, bank[g, :, up:down])
        cdf = normal_cdf(pre)
        act = (pre * cdf).astype(BF)
        if saving:
            slope[g] = cdf + pre * jnp.exp(-0.5 * pre * pre) * INVERSE_ROOT
            active[g] = act
        term = dot_rt(act, bank[g, :, down:emb])
        terms = term if terms is None else terms + term
        yield
    finish(middle + terms)


def front_kernel(nz, sizes, asked, firsts, *refs):
    local, hidden, size = sizes
    wide = local + 64
    sources, refs = (refs[:4], refs[4:])
    (half, tables, shuffle, bias_t, bias_s, hot), refs = (refs[:6], refs[6:])
    (bank_out, pbank_out, context, wanted, pix_s, vec_rows, total), refs = (refs[:7], refs[7:])
    keep_refs, refs = (refs[:13], refs[13:])
    (vec_all, tbank, bank, pix_t, px, pr, own_sem, out_sem), sems = (refs[:8], refs[8:])
    r = lax.axis_index("role")
    d = lax.axis_index("dp")
    m = lax.axis_index("mp")
    groups = tbank.shape[0]
    width = tbank.shape[1]
    nears = [{"mp": shift_of(m, by)} for by in range(1, groups)]
    greet([{"role": 1 - r}] + nears + [{"dp": lax.rem(d + j, nz)} for j in range(1, nz)])
    targets = (vec_all, tbank, bank, pbank_out)
    arrays = [
        Gather(k, sources[k], targets[k], sources[k].shape[-2], sources[k].shape[-1], firsts[k],
               sems, (r, d, m), nz)
        for k in range(4)
    ]
    small, teach, learn, guess = arrays

    def pixel(j):
        peer = shift_of(m, j)
        return remote(half.at[peer], pix_t.at[m], px.at[j], pr.at[j], {"mp": peer})

    def pixel_in(j):
        peer = shift_of(m, j)
        return remote(half.at[peer], pix_t.at[peer], px.at[j], pr.at[j], {"mp": peer})

    own_pixel = pltpu.make_async_copy(half.at[m], pix_t.at[m], own_sem.at[0])
    own_pixel.start()
    small.start()
    for j in range(1, groups):
        pixel(j).start()
    teach.start()
    for step in small.steps():
        step()

    def place():
        rows = tables[...].astype(F32)
        return rows[:, :width] + rows[:, width : 2 * width] + rows[:, 2 * width :]

    def place_shuffled():
        rows = dot(shuffle[...], tables[...])
        return rows[:, :width] + rows[:, width : 2 * width] + rows[:, 2 * width :]

    for j, step in enumerate(teach.steps()):
        if j == 3:
            learn.start()
        step()
        if j == 1:
            small.take_diagonal()
    small.complete()

    share = vec_rows.shape[1] * 4 // (vec_all.shape[0] * vec_all.shape[1])
    lanes = vec_all.shape[3]
    lane = lax.broadcasted_iota(jnp.int32, (1, lanes), 1)

    def vector_row(kind, j):
        row = jnp.zeros((1, width), F32)
        count = width // share
        for c in range(count):
            flat = j * count + c
            piece = vec_all[flat % groups, flat // groups].astype(F32)[kind : kind + 1]
            piece = only(lane < share, piece)
            row += turn(jnp.concatenate([piece, jnp.zeros((1, width - lanes), F32)], 1), c * share)
        return row

    gains_t = [vector_row(1, j) for j in range(2)]
    rows_s = [vector_row(0, j) for j in range(4)]
    vec_rows[...] = jnp.concatenate(rows_s, 0)
    counts = jnp.zeros((1, 1), F32)
    for c in range(groups):
        for o in range(vec_all.shape[1]):
            counts += vec_all[c, o].astype(F32)[2:3, :1]
    total[...] = jnp.broadcast_to(counts, total.shape)
    own_pixel.wait()
    for j in range(1, groups):
        pixel_in(j).wait_recv()
    for g in range(groups):
        pix_s[g] = dot(shuffle[...], pix_t[g]).astype(BF)

    def teacher_rows(latent):
        chosen = dot(hot[...], stats_of(latent)[0].astype(BF))
        for g in range(groups):
            wanted[g] = turn(chosen, -g * local)[:, :wide].astype(BF)

    def student_rows(latent):
        at = lax.broadcasted_iota(jnp.int32, (1, wide), 1)
        for g in range(groups):
            context[g] = only(at >= 64, turn(latent, 64 - g * local)[:, :wide]).astype(BF)

    teacher = encoder_forward(
        sizes, pix_t.shape[1], pix_t, place, bias_t, tbank, gains_t, None, teacher_rows
    )
    student = encoder_forward(
        sizes, asked, pix_s, place_shuffled, bias_s, bank, rows_s[:2], keep_refs, student_rows
    )

    def advance(work, parts):
        for _ in range(parts):
            next(work, None)

    def bank_copy(g):
        return pltpu.make_async_copy(bank.at[g], bank_out.at[g], out_sem.at[g])

    steps = learn.steps()
    for j, step in enumerate(steps):
        if j == 3:
            guess.start()
        step()
        if j == 1:
            teach.take_diagonal()
        if j == 3:
            teach.complete()
        if j > 3:
            advance(teacher, 2)
    for j, step in enumerate(guess.steps()):
        step()
        if j == 1:
            learn.take_diagonal()
            advance(teacher, 100)
            learn.complete()
            for g in range(groups):
                bank_copy(g).start()
        if j > 1:
            advance(student, 1)
    guess.take_diagonal()
    advance(student, 100)
    for g in range(groups):
        bank_copy(g).wait()
    guess.complete()
    for j in range(1, groups):
        pixel(j).wait_send()
    for array in arrays:
        array.finish()


def run_front(packs, half, tables, shuffle, keep_t, keep_s, hot, sizes, asked):
    local, hidden, size = sizes
    nz = lax.axis_size("dp")
    groups = lax.axis_size("mp")
    owners = lax.axis_size("role") * nz
    vec, target, master, predictor = packs
    rows = half.shape[1]
    width = target.shape[0] * owners
    columns = target.shape[1]
    wide = local + 64
    make = jax.ShapeDtypeStruct
    hbm = pl.BlockSpec(memory_space=pl.ANY)
    vmem = pl.BlockSpec(memory_space=pltpu.VMEM)
    dma = pltpu.SemaphoreType.DMA
    bank = make((groups, width, columns), BF)
    outs = [
        bank,
        make((groups, owners, *predictor.shape[1:]), BF),
        make((groups, asked, wide), BF),
        make((groups, hot.shape[0], wide), BF),
        make((groups, rows, wide), BF),
        make((4, width), F32),
        make((8, 128), F32),
        make((rows, width), F32),
        make((rows, 1), F32),
        make((rows, width), BF),
        make((groups, asked, wide), BF),
        make((groups, rows, wide), BF),
        make((groups, rows, wide), BF),
        make((HEADS, asked, rows), F32),
        make((groups, asked, wide), BF),
        make((asked, width), F32),
        make((asked, 1), F32),
        make((asked, width), BF),
        make((groups, asked, hidden), F32),
        make((groups, asked, hidden), BF),
    ]

    def first(cols):
        return cols - (cols // 5 // 256) * 256

    firsts = (vec.shape[2], first(columns), first(columns), first(predictor.shape[2]))
    bias_t, bias_s = (((keep - 1.0) * 1e9)[None, :] for keep in (keep_t, keep_s))
    return pl.pallas_call(
        functools.partial(front_kernel, nz, sizes, asked, firsts),
        out_shape=outs,
        in_specs=[hbm] * 5 + [vmem] * 5,
        out_specs=[hbm] * 2 + [vmem] * (len(outs) - 2),
        scratch_shapes=[
            pltpu.VMEM((groups, owners, *vec.shape[1:]), BF),
            pltpu.VMEM(bank.shape, BF),
            pltpu.VMEM(bank.shape, BF),
            pltpu.VMEM((groups, rows, wide), BF),
            dma((groups,)),
            dma((groups,)),
            dma((1,)),
            dma((groups,)),
        ]
        + gather_sems(4, nz),
        compiler_params=pltpu.CompilerParams(
            collective_id=1, has_side_effects=True, vmem_limit_bytes=50 * 2**20
        ),
    )(vec, target, master, predictor, half, tables, shuffle, bias_t, bias_s, hot)


def predictor_kernel(
    sizes, ctx, wanted, tables, shuffle, hot, keep, weight, total, bank, vec_rows,
    grad_ctx, grads, small, loss_out, probs_s, q_s, k_s, v_s, mixed_s, slope_s, active_s, dt_s
):
    local, plocal, phidden, size, blocks = sizes
    groups = bank.shape[0]
    heads = plocal // size
    lanes = 128
    up = 4 * plocal
    down = up + phidden
    head_at = down + phidden
    entry_at = head_at + local
    wide = local + 64
    nctx = ctx.shape[1]
    asked = hot.shape[0]
    rows = nctx + asked
    tlen = asked // blocks
    pwidth = groups * plocal
    first, second, final, token = (
        vec_rows[i : i + 1, j : j + pwidth] for i in (2, 3) for j in (0, pwidth)
    )
    root = size**-0.5
    key = lax.broadcasted_iota(jnp.int32, (asked, rows), 1) - nctx
    query = lax.broadcasted_iota(jnp.int32, (asked, rows), 0)
    reached = jnp.logical_or(key < 0, key // tlen == query // tlen)
    bias = (only(reached, jnp.broadcast_to(keep[...], (asked, rows))) - 1.0) * 1e9

    def places(chosen):
        found = dot(chosen, tables[...])
        return found[:, :pwidth] + found[:, pwidth : 2 * pwidth] + found[:, 2 * pwidth :]


    entry = places(shuffle[:nctx]) + chain(
        lambda g: dot_rt(ctx[g], bank[g, :, entry_at - 64 : entry_at + local]), groups
    )
    tgt_in = places(hot[...]) + token
    norm_c, scale_c = stats_of(entry)
    norm_t, scale_t = stats_of(tgt_in)
    a_c = (norm_c * first).astype(BF)
    a_t = (norm_t * first).astype(BF)
    a = jnp.concatenate([a_c, a_t], 0)

    def attend(g):
        t = dot(a, bank[g, :, :up]).astype(BF).astype(F32)
        q = t[nctx:, :lanes].astype(BF)
        k = turn(t, -plocal)[:, :lanes].astype(BF)
        v = turn(t, -2 * plocal)[:, :lanes].astype(BF)
        q_s[g] = q
        k_s[g] = k
        v_s[g] = v
        mixed = jnp.zeros((asked, lanes), F32)
        for h in range(heads):
            mask = head_lanes(lanes, size, h)
            score = dot_rt(only(mask, q), k) * root + bias
            score = jnp.exp(score - jnp.max(score, -1, keepdims=True))
            probs = score / jnp.sum(score, -1, keepdims=True)
            probs_s[g * heads + h] = probs
            mixed += only(mask, dot(probs.astype(BF), v))
        mixed = turn(mixed, lanes - plocal).astype(BF)
        mixed_s[g] = mixed
        return dot_rt(mixed, bank[g, :, up - lanes : up])

    middle = tgt_in + chain(attend, groups)
    norm2, scale2 = stats_of(middle)
    b = (norm2 * second).astype(BF)

    def feed(g):
        pre = dot(b, bank[g, :, up:down])
        cdf = normal_cdf(pre)
        slope_s[g] = cdf + pre * jnp.exp(-0.5 * pre * pre) * INVERSE_ROOT
        act = (pre * cdf).astype(BF)
        active_s[g] = act
        return dot_rt(act, bank[g, :, down:head_at])

    out = middle + chain(feed, groups)
    norm_f, scale_f = stats_of(out)
    head_in = (norm_f * final).astype(BF)
    lane = lax.broadcasted_iota(jnp.int32, (1, wide), 1)
    losses = jnp.zeros((1, 1), F32)
    row_weight = weight[...]

    def judge(g):
        nonlocal losses
        pred = dot(head_in, bank[g, :, head_at : head_at + wide])
        diff = only(lane < local, pred - wanted[g].astype(F32))
        losses += jnp.sum(row_weight * diff * diff, keepdims=True)
        grad = (2.0 * row_weight * diff / total[0:1, 0:1]).astype(BF)
        g_head = dot_lt(head_in, grad)
        grads[g, :, head_at : head_at + lanes] = g_head[:, :lanes]
        grads[g, :, head_at + lanes : head_at + wide] = g_head[:, lanes:]
        return dot_rt(grad, bank[g, :, head_at : head_at + wide])

    grad_out, g_final = norm_back_of(norm_f, scale_f, final, chain(judge, groups))
    loss_out[...] = jnp.broadcast_to(losses, loss_out.shape)

    branch = grad_out.astype(BF)

    def feed_back(g):
        grads[g, :, down:head_at] = dot_lt(branch, active_s[g])
        grad_pre = (dot(branch, bank[g, :, down:head_at]) * slope_s[g]).astype(BF)
        grads[g, :, up:down] = dot_lt(b, grad_pre)
        return dot_rt(grad_pre, bank[g, :, up:down])

    grad_norm, g_second = norm_back_of(norm2, scale2, second, chain(feed_back, groups))
    grad_mid = grad_out + grad_norm
    mixer = grad_mid.astype(BF)

    def attend_back(g):
        g_o = dot_lt(mixer, mixed_s[g])
        gm = turn(dot(mixer, bank[g, :, up - lanes : up]), plocal - lanes).astype(BF)
        q, k, v = (q_s[g], k_s[g], v_s[g])
        valid = head_lanes(lanes, plocal, 0)
        gm = only(valid, gm)
        qv = only(valid, q)
        block = lax.broadcasted_iota(jnp.int32, (asked, 1), 0) // tlen
        q_spread = jnp.concatenate([only(block == i, qv) for i in range(blocks)], 1)
        gm_spread = jnp.concatenate([only(block == i, gm) for i in range(blocks)], 1)
        dqs, dkt, dvt, dkc, dvc = ([], [], [], [], [])
        for h in range(heads):
            mask = head_lanes(lanes, size, h)
            masks = jnp.concatenate([mask] * blocks, 1)
            probs = probs_s[g * heads + h]
            gmh = only(mask, gm)
            grad_probs = dot_rt(gmh, v)
            ds = (probs * (grad_probs - jnp.sum(grad_probs * probs, -1, keepdims=True))).astype(BF)
            pb = probs.astype(BF)
            qh = only(mask, qv)
            dqs.append(dot(ds, only(mask, k)))
            dkt.append(dot_lt(ds[:, nctx:], qh))
            dvt.append(dot_lt(pb[:, nctx:], gmh))
            dkc.append(dot_lt(ds[:, :nctx], only(masks, q_spread)))
            dvc.append(dot_lt(pb[:, :nctx], only(masks, gm_spread)))
        dq = (sum(dqs[1:], dqs[0]) * root).astype(BF).astype(F32)
        dk = (sum(dkt[1:], dkt[0]) * root).astype(BF).astype(F32)
        dv = sum(dvt[1:], dvt[0]).astype(BF).astype(F32)
        kc = (sum(dkc[1:], dkc[0]) * root).astype(BF).astype(F32)
        vc = sum(dvc[1:], dvc[0]).astype(BF).astype(F32)
        kc = chain(lambda i: kc[:, i * lanes : (i + 1) * lanes], blocks)
        vc = chain(lambda i: vc[:, i * lanes : (i + 1) * lanes], blocks)

        def lay(query, keyed, valued):
            count = keyed.shape[0]
            blank = jnp.zeros((count, up - lanes), F32)
            wideq = 0.0 if query is None else jnp.concatenate([query, blank], 1)
            return (
                wideq
                + turn(jnp.concatenate([keyed, blank], 1), plocal)
                + turn(jnp.concatenate([valued, blank], 1), 2 * plocal)
            )

        dt_t = lay(dq, dk, dv).astype(BF)
        dt_c = lay(None, kc, vc)
        high = dt_c.astype(BF)
        low = (dt_c - high.astype(F32)).astype(BF)
        dt = jnp.concatenate([high, dt_t], 0)
        dt_s[g] = jnp.concatenate([dt, low], 0)
        g_qkv = dot_lt(jnp.concatenate([a, a_c], 0), jnp.concatenate([dt, low], 0))
        grads[g, :, : up - lanes] = g_qkv[:, : up - lanes]
        grads[g, :, up - lanes : up] = g_qkv[:, up - lanes :] + g_o

    for g in range(groups):
        attend_back(g)
    grad_a = chain(lambda g: dot_rt(dt_s[g], bank[g, :, :up]), groups)
    grad_in_t, g_first_t = norm_back_of(norm_t, scale_t, first, grad_a[nctx:rows])
    grad_in_c, g_first_c = norm_back_of(
        norm_c, scale_c, first, grad_a[:nctx] + grad_a[rows:]
    )
    g_token = jnp.sum(grad_in_t + grad_mid, 0, keepdims=True)
    small[...] = jnp.concatenate([g_first_t + g_first_c, g_second, g_final, g_token], 0)
    grad_entry = grad_in_c.astype(BF)
    width = groups * local
    grad_context = jnp.zeros((nctx, width), F32)
    for g in range(groups):
        g_entry = dot_lt(grad_entry, ctx[g])
        grads[g, :, entry_at - 64 : entry_at + 64] += g_entry[:, :lanes]
        grads[g, :, entry_at + 64 : entry_at + local] = g_entry[:, lanes:]
        part = only(lane >= 64, dot(grad_entry, bank[g, :, entry_at - 64 : entry_at + local]))
        full = jnp.concatenate([part, jnp.zeros((nctx, width - wide), F32)], 1)
        grad_context += turn(full, g * local - 64)
    grad_ctx[...] = grad_context


def run_predictor(ctx, wanted, tables, shuffle, hot, keep, weight, total, bank, vec_rows, sizes):
    local, plocal, phidden, size, blocks = sizes
    groups = bank.shape[0]
    nctx = ctx.shape[1]
    pwidth = groups * plocal
    asked = hot.shape[0]
    rows = nctx + asked
    make = jax.ShapeDtypeStruct
    outs = [
        make((nctx, groups * local), F32),
        make(bank.shape, F32),
        make((4, pwidth), F32),
        make((8, 128), F32),
    ]
    ins = [ctx, wanted, tables, shuffle, hot, keep, weight, total, bank, vec_rows]
    vmem = pl.BlockSpec(memory_space=pltpu.VMEM)
    scratch = [
        pltpu.VMEM((HEADS, asked, rows), F32),
        pltpu.VMEM((groups, asked, 128), BF),
        pltpu.VMEM((groups, rows, 128), BF),
        pltpu.VMEM((groups, rows, 128), BF),
        pltpu.VMEM((groups, asked, 128), BF),
        pltpu.VMEM((groups, asked, phidden), F32),
        pltpu.VMEM((groups, asked, phidden), BF),
        pltpu.VMEM((groups, rows + nctx, 4 * plocal), BF),
    ]
    return pl.pallas_call(
        functools.partial(predictor_kernel, sizes),
        out_shape=outs,
        in_specs=[vmem] * len(ins),
        out_specs=[vmem] * len(outs),
        scratch_shapes=scratch,
        compiler_params=pltpu.CompilerParams(vmem_limit_bytes=48 * 2**20),
    )(*ins)


def encoder_back_kernel(
    sizes, grad_ctx, pix, norm1, scale1, mixer_in, qs, ks, vs, probs_in, mixed_in, norm2, scale2,
    dense, slope, active, bank, gains, grads, small, wide_s, tail_s, dt_s, sems
):
    local, hidden, size = sizes
    groups = bank.shape[0]
    heads = local // size
    up = 4 * local
    down = up + hidden
    emb = down + hidden
    wide = local + 64
    span = 3 * local + 64
    asked = grad_ctx.shape[0]
    rows = norm1.shape[0]
    first, second = (gains[0:1], gains[1:2])
    root = size**-0.5
    grad_out = grad_ctx[...]
    branch = grad_out.astype(BF)

    def ship(g, start, width):
        return pltpu.make_async_copy(
            wide_s.at[g % 2, :, pl.ds(start, width)],
            grads.at[g, :, pl.ds(start, width)],
            sems.at[g % 2],
        )

    def feed_back(g):
        if g >= 2:
            ship(g - 2, up, 2 * hidden).wait()
        wide_s[g % 2, :, down:emb] = dot_lt(branch, active[g])
        grad_pre = (dot(branch, bank[g, :, down:emb]) * slope[g]).astype(BF)
        wide_s[g % 2, :, up:down] = dot_lt(dense[...], grad_pre)
        ship(g, up, 2 * hidden).start()
        return dot_rt(grad_pre, bank[g, :, up:down])

    grad_norm, g_second = norm_back_of(norm2[...], scale2[...], second, chain(feed_back, groups))
    grad_mid = grad_out + grad_norm
    mixer = grad_mid.astype(BF)
    for g in range(groups - 2, groups):
        ship(g, up, 2 * hidden).wait()
    valid = head_lanes(wide, local, 0)

    def attend_back(g):
        g_o = dot_lt(mixer, mixed_in[g])
        gm = turn(dot(mixer, bank[g, :, up - wide : up]), -64).astype(BF)
        q, k, v = (only(valid, qs[g]), ks[g], vs[g])
        gm = only(valid, gm)
        dqs, dks, dvs = ([], [], [])
        for h in range(heads):
            mask = head_lanes(wide, size, h)
            probs = probs_in[g * heads + h]
            gmh = only(mask, gm)
            grad_probs = dot_rt(gmh, v)
            ds = (probs * (grad_probs - jnp.sum(grad_probs * probs, -1, keepdims=True))).astype(BF)
            dqs.append(dot(ds, only(mask, k)))
            dks.append(dot_lt(ds, only(mask, q)))
            dvs.append(dot_lt(probs.astype(BF), gmh))
        dq = (sum(dqs[1:], dqs[0]) * root).astype(BF).astype(F32)
        dk = (sum(dks[1:], dks[0]) * root).astype(BF).astype(F32)
        dv = sum(dvs[1:], dvs[0]).astype(BF).astype(F32)
        dq = jnp.concatenate([dq, jnp.zeros((rows - asked, wide), F32)], 0)
        blank = jnp.zeros((rows, span - wide), F32)
        dt = (
            jnp.concatenate([dq, blank], 1)
            + turn(jnp.concatenate([dk, blank], 1), local)
            + jnp.concatenate([blank, dv], 1)
        ).astype(BF)
        dt_s[g] = dt
        g_qkv = dot_lt(mixer_in[...], dt)
        if g >= 2:
            ship(g - 2, 0, up).wait()
        slot = wide_s.at[g % 2]
        slot[:, : up - wide] = g_qkv[:, : up - wide]
        slot[:, up - wide : span] = g_qkv[:, up - wide :] + g_o[:, : span - up + wide]
        slot[:, span:up] = g_o[:, span - up + wide :]
        ship(g, 0, up).start()

    for g in range(groups):
        attend_back(g)
    grad_a = chain(lambda g: dot_rt(dt_s[g], bank[g, :, :span]), groups)
    grad_start, g_first = norm_back_of(norm1[...], scale1[...], first, grad_a)
    grad_start = (
        grad_start + jnp.concatenate([grad_mid, jnp.zeros((rows - asked, grad_mid.shape[1]), F32)], 0)
    ).astype(BF)
    small[...] = jnp.concatenate([g_first, g_second], 0)

    def tail(g):
        return pltpu.make_async_copy(
            tail_s.at[g], grads.at[g, :, pl.ds(emb, wide)], sems.at[2 + g]
        )

    for g in range(groups):
        tail_s[g] = dot_lt(grad_start, pix[g])
        tail(g).start()
    for g in range(groups - 2, groups):
        ship(g, 0, up).wait()
    for g in range(groups):
        tail(g).wait()


def run_encoder_back(grad_ctx, pix, saved, bank, gains, sizes):
    local, hidden, size = sizes
    groups, width, columns = bank.shape
    rows = pix.shape[1]
    make = jax.ShapeDtypeStruct
    ins = [grad_ctx, pix, *saved, bank, gains]
    vmem = pl.BlockSpec(memory_space=pltpu.VMEM)
    return pl.pallas_call(
        functools.partial(encoder_back_kernel, sizes),
        out_shape=[make(bank.shape, F32), make((2, width), F32)],
        in_specs=[vmem] * len(ins),
        out_specs=[pl.BlockSpec(memory_space=pl.ANY), vmem],
        scratch_shapes=[
            pltpu.VMEM((2, width, 4 * local + 2 * hidden), F32),
            pltpu.VMEM((groups, width, local + 64), F32),
            pltpu.VMEM((groups, rows, 3 * local + 64), BF),
            pltpu.SemaphoreType.DMA((2 + groups,)),
        ],
        compiler_params=pltpu.CompilerParams(vmem_limit_bytes=58 * 2**20),
    )(*ins)


def update_kernel(sizes, stats, bank, pbank, *refs):
    local, hidden, pixel, plocal, phidden = sizes
    sources, outs, ins, sems = (refs[:14], refs[14:28], refs[28:42], refs[42])
    copies = [
        pltpu.make_async_copy(source, ref, sems.at[i])
        for i, (source, ref) in enumerate(zip(sources, ins))
    ]
    for copy in copies:
        copy.start()
    norm = jnp.sqrt(stats[1:2, 0:1])
    scale = jnp.minimum(1.0, CLIP / (norm + 1e-06))

    def side_by_side(packed, parts):
        whole = packed[...]
        total = sum(width for _, width in parts)
        lane = lax.broadcasted_iota(jnp.int32, (1, whole.shape[1]), 1)
        at, result = (0, whole)
        for first, width in parts:
            moved = turn(whole, at - first) if at != first else whole
            result = jnp.where(lane >= at, moved, result)
            at += width
        return result[:, :total]

    def step(which, grad, target=None):
        for i in (which, 4 + which, 8 + which):
            copies[i].wait()
        weight, first, second = (ins[i][...] for i in (which, 4 + which, 8 + which))
        new, first, second = adamw(weight, grad, first, second, scale, RATE_MATRIX, DECAY)
        for i, value in ((which, new), (4 + which, first), (8 + which, second)):
            outs[i][...] = value
        if target is not None:
            copies[target].wait()
            outs[target][...] = MOMENTUM_EMA * ins[target][...] + (1.0 - MOMENTUM_EMA) * new

    up = 4 * local
    down = up + hidden
    emb = down + hidden
    step(0, side_by_side(bank, ((0, 3 * local), (up, hidden))), 12)
    step(1, side_by_side(bank, ((emb, pixel), (3 * local, local), (down, hidden))), 13)
    up = 4 * plocal
    down = up + phidden
    head = down + phidden
    step(2, side_by_side(pbank, ((0, 3 * plocal), (up, phidden), (head, local))))
    step(3, side_by_side(pbank, ((head + local, local), (3 * plocal, plocal), (down, phidden))))


def run_update(stats, bank, pbank, arrays, sizes):
    vmem = pl.BlockSpec(memory_space=pltpu.VMEM)
    arrays = [a.T if i % 2 else a for i, a in enumerate(arrays)]
    results = pl.pallas_call(
        functools.partial(update_kernel, sizes),
        out_shape=[jax.ShapeDtypeStruct(a.shape, F32) for a in arrays],
        in_specs=[vmem] * 3 + [pl.BlockSpec(memory_space=pl.ANY)] * len(arrays),
        out_specs=[vmem] * len(arrays),
        scratch_shapes=[pltpu.VMEM(a.shape, F32) for a in arrays]
        + [pltpu.SemaphoreType.DMA((len(arrays),))],
        compiler_params=pltpu.CompilerParams(vmem_limit_bytes=60 * 2**20),
    )(stats, bank, pbank, *arrays)
    return [a.T if i % 2 else a for i, a in enumerate(results)]


def per_device(
    pixels,
    context_slots,
    context_count,
    target_slots,
    target_count,
    encoder_in,
    encoder_out,
    predictor_in,
    predictor_out,
    vectors,
    first_encoder_in,
    first_encoder_out,
    first_predictor_in,
    first_predictor_out,
    first_vectors,
    second_encoder_in,
    second_encoder_out,
    second_predictor_in,
    second_predictor_out,
    second_vectors,
    target_encoder_in,
    target_encoder_out,
    target_vectors,
):
    groups = lax.axis_size("mp")
    owners = lax.axis_size("role") * lax.axis_size("dp")
    width = encoder_in.shape[0] * owners
    pwidth = predictor_in.shape[0] * owners
    local, plocal = (width // groups, pwidth // groups)
    pixel = pixels.shape[2]
    hidden = encoder_in.shape[1] - 3 * local
    phidden = predictor_in.shape[1] - 3 * plocal - local
    patches = pixels.shape[1]
    image = lax.axis_index("role") * groups + lax.axis_index("mp")

    slots = lax.dynamic_index_in_dim(context_slots, image, 0, keepdims=False)
    count = lax.dynamic_index_in_dim(context_count, image, 0, keepdims=False)
    tslots = lax.dynamic_index_in_dim(target_slots, image, 0, keepdims=False)
    tcount = lax.dynamic_index_in_dim(target_count, image, 0, keepdims=False)
    nctx = slots.shape[0]
    blocks, tlen = tslots.shape
    rows = -(-patches // 16) * 16
    share = vectors.shape[0]

    patch = jnp.arange(patches)
    hits = slots[:, None] == patch[None, :]
    member = jnp.any(hits, 0)
    order = jnp.where(
        member,
        jnp.sum(jnp.where(hits, jnp.arange(nctx)[:, None], 0), 0),
        nctx + jnp.cumsum(1 - member.astype(jnp.int32)) - 1,
    )
    order = jnp.pad(order, (0, rows - patches), constant_values=-1)
    slot_of = jnp.arange(rows)
    shuffle = (order[None, :] == slot_of[:, None]).astype(BF)
    ckeep = (jnp.arange(nctx) < count).astype(F32)
    tkeep = (jnp.arange(tlen)[None, :] < tcount[:, None]).astype(F32)
    tflat = tslots.reshape(-1)
    keep = jnp.concatenate([ckeep, tkeep.reshape(-1)])[None, :]
    hot = (tflat[:, None] == slot_of[None, :]).astype(BF)

    vec = jnp.stack([vectors, target_vectors, jnp.broadcast_to(jnp.sum(tcount).astype(F32), (share,))])
    vec = jnp.pad(vec, ((0, 13), (0, -share % LANES))).astype(BF)
    half = lax.dynamic_slice_in_dim(pixels, lax.axis_index("role") * groups, groups, 0)
    half = jnp.pad(half, ((0, 0), (0, rows - patches), (0, 64)))
    sizes = (local, hidden, width // HEADS)
    bank, pbank, context, wanted, student_pix, vec_rows, total, *saved = run_front(
        (
            vec[None],
            pack_encoder(target_encoder_in, target_encoder_out, local, pixel),
            pack_encoder(encoder_in, encoder_out, local, pixel),
            pack_predictor(predictor_in, predictor_out, local, plocal, phidden)[None],
        ),
        half,
        np.pad(in_three(sincos(width)), ((0, rows - patches), (0, 0))),
        shuffle,
        (slot_of < patches).astype(F32),
        (slot_of < count).astype(F32),
        hot,
        sizes,
        nctx,
    )
    target_total = total[0, 0]
    grad_context, g_pbank, p_small, loss = run_predictor(
        context,
        wanted,
        np.pad(in_three(sincos(pwidth)), ((0, rows - patches), (0, 0))),
        shuffle,
        hot,
        keep,
        tkeep.reshape(-1, 1),
        total,
        pbank.reshape(groups, pwidth, -1),
        vec_rows,
        (local, plocal, phidden, pwidth // HEADS, blocks),
    )
    g_bank, e_small = run_encoder_back(grad_context, student_pix, saved, bank, vec_rows, sizes)
    g_vec = jnp.concatenate([e_small.reshape(-1), p_small.reshape(-1)])
    g_vec = g_vec.reshape(owners, groups, 1, -1).transpose(1, 0, 2, 3)
    r_bank, r_pbank, r_vec, stats = reduce_all(
        [
            g_bank.reshape(groups, owners, width // owners, -1),
            g_pbank.reshape(pbank.shape),
            jnp.pad(g_vec, ((0, 0), (0, 0), (0, 7), (0, -share % (2 * LANES)))),
        ],
        (BF, BF, F32),
        chunk_list([(1, g_pbank.shape[2], 768), (0, g_bank.shape[2], 512), (2, -(-share // 256) * 256, 256)]),
        loss,
    )
    r_vec = r_vec[0, :share]
    loss_total, squares = (stats[0, 0], stats[1, 0])
    grad_norm = jnp.sqrt(squares)
    scale = jnp.minimum(1.0, CLIP / (grad_norm + 1e-06))
    (
        new_in, new_out, new_pin, new_pout,
        m_in, m_out, m_pin, m_pout,
        v_in, v_out, v_pin, v_pout,
        ema_in, ema_out,
    ) = run_update(
        stats,
        r_bank,
        r_pbank,
        (
            encoder_in, encoder_out, predictor_in, predictor_out,
            first_encoder_in, first_encoder_out, first_predictor_in, first_predictor_out,
            second_encoder_in, second_encoder_out, second_predictor_in, second_predictor_out,
            target_encoder_in, target_encoder_out,
        ),
        (local, hidden, pixel, plocal, phidden),
    )
    new_vec, m_vec, v_vec = adamw(
        vectors, r_vec, first_vectors, second_vectors, scale, RATE_VECTOR, 0.0
    )
    ema_vec = MOMENTUM_EMA * target_vectors + (1.0 - MOMENTUM_EMA) * new_vec
    return (
        new_in, new_out, new_pin, new_pout, new_vec,
        m_in, m_out, m_pin, m_pout, m_vec,
        v_in, v_out, v_pin, v_pout, v_vec,
        ema_in, ema_out, ema_vec,
        loss_total, target_total, grad_norm,
    )


def solution(mesh):
    bank_in, bank_out, small = (
        P(("role", "dp"), "mp"),
        P("mp", ("role", "dp")),
        P(("role", "dp", "mp")),
    )
    five = (bank_in, bank_out, bank_in, bank_out, small)
    three = (bank_in, bank_out, small)
    return jax.shard_map(
        per_device,
        mesh=mesh,
        in_specs=(
            P("dp", None, "mp"),
            P("dp", None),
            P("dp"),
            P("dp", None, None),
            P("dp", None),
        )
        + five * 3
        + three,
        out_specs=five * 3 + three + (P(), P(), P()),
        check_vma=False,
    )
```

```python
import functools

import jax
import jax.numpy as jnp
import numpy as np
from jax import lax
from jax.experimental import pallas as pl
from jax.experimental.pallas import tpu as pltpu
from jax.sharding import PartitionSpec as P

HEADS = 12
GRID = 14
STEP = 10

BETA_ONE = 0.9
BETA_TWO = 0.999
ADAM_EPS = 1e-08
RATE_MATRIX = 0.03
RATE_VECTOR = 0.3
DECAY = 0.05
MOMENTUM_EMA = 0.9
CLIP = 0.1
ROOT_HALF = 0.7071067811865476
INVERSE_ROOT = 0.3989422804014327

BF = jnp.bfloat16
F32 = jnp.float32
LANES = 128


def sincos(width):
    quarter = width // 4
    omega = 1.0 / 10000.0 ** (np.arange(quarter, dtype=np.float64) / quarter)
    place = np.arange(GRID * GRID)
    rows = (place // GRID)[:, None] * omega[None, :]
    cols = (place % GRID)[:, None] * omega[None, :]
    return np.concatenate([np.sin(rows), np.cos(rows), np.sin(cols), np.cos(cols)], -1).astype(
        np.float32
    )


def in_three(table):
    parts, rest = ([], table)
    for _ in range(3):
        parts.append(rest.astype(jnp.bfloat16))
        rest = rest - parts[-1].astype(np.float32)
    return np.concatenate(parts, 1)


def chunk_list(arrays):
    return tuple(
        (array, start, min(step, columns - start))
        for array, columns, step in arrays
        for start in range(0, columns, step)
    )


def pack_encoder(w_in, w_out, local, pixel):
    turned = w_out.T
    used = w_in.shape[1] + turned.shape[1]
    return jnp.concatenate(
        [
            w_in[:, : 3 * local],
            turned[:, pixel : pixel + local],
            w_in[:, 3 * local :],
            turned[:, pixel + local :],
            turned[:, :pixel],
            jnp.zeros((w_in.shape[0], -used % (2 * LANES)), F32),
        ],
        1,
    ).astype(BF)


def pack_predictor(p_in, p_out, local, plocal, phidden):
    turned = p_out.T
    return jnp.concatenate(
        [
            p_in[:, : 3 * plocal],
            turned[:, local : local + plocal],
            p_in[:, 3 * plocal : 3 * plocal + phidden],
            turned[:, local + plocal :],
            p_in[:, 3 * plocal + phidden :],
            turned[:, :local],
        ],
        1,
    ).astype(BF)


def adamw(weight, grad, first, second, scale, rate, decay):
    grad = grad * scale
    first = BETA_ONE * first + (1.0 - BETA_ONE) * grad
    second = BETA_TWO * second + (1.0 - BETA_TWO) * grad * grad
    mean_hat = first / (1.0 - BETA_ONE**STEP)
    square_hat = second / (1.0 - BETA_TWO**STEP)
    return (
        weight - rate * (mean_hat / (jnp.sqrt(square_hat) + ADAM_EPS) + decay * weight),
        first,
        second,
    )


def shift_of(rank, by):
    return jnp.bitwise_xor(rank, by)


def greet(peers):
    barrier = pltpu.get_barrier_semaphore()
    for peer in peers:
        pl.semaphore_signal(barrier, inc=1, device_id=peer, device_id_type=pl.DeviceIdType.MESH)
    pl.semaphore_wait(barrier, len(peers))


def remote(src, dst, send, recv, where):
    return pltpu.make_async_remote_copy(
        src_ref=src, dst_ref=dst, send_sem=send, recv_sem=recv,
        device_id=where, device_id_type=pl.DeviceIdType.MESH,
    )


class Gather:
    def __init__(self, place, source, target, rows, cols, first, sems, where, nz):
        (self.zs, self.zr, self.xs, self.xr, self.ys, self.yr, self.rxs, self.rxr, self.rys,
         self.ryr, self.bs, self.br, self.bzs, self.bzr, self.cs, self.cr, self.own) = sems
        self.k = place
        self.source, self.target = (source, target)
        self.rows, self.cols, self.first, self.nz = (rows, cols, first, nz)
        self.r, self.d, self.m = where
        self.base = self.r * nz
        self.mx, self.my, self.mf = (shift_of(self.m, by) for by in (1, 2, 3))

    def at(self, column, owner, count, start, width):
        if len(self.target.shape) == 4:
            return self.target.at[column, pl.ds(owner, count), :, pl.ds(start, width)]
        row = pl.multiple_of(owner * self.rows, self.rows)
        return self.target.at[column, pl.ds(row, count * self.rows), pl.ds(start, width)]

    def mine(self, start, width):
        if len(self.target.shape) == 4:
            return self.source.at[:, :, pl.ds(start, width)]
        return self.source.at[:, pl.ds(start, width)]

    def line(self, piece, way, own=False):
        spot = self.at(self.m, self.base + piece, 1, 0, self.first)
        return remote(
            self.mine(0, self.first) if own else spot, spot,
            self.zs.at[self.k, way, piece], self.zr.at[self.k, way, piece],
            {"dp": self.d + 1 - 2 * way},
        )

    def across(self, piece, own=False):
        spot = self.at(self.m, self.base + piece, 1, 0, self.first)
        source = self.mine(0, self.first) if own else spot
        return (
            remote(source, spot, self.xs.at[self.k, piece], self.xr.at[self.k, piece], {"mp": self.mx}),
            remote(source, spot, self.ys.at[self.k, piece], self.yr.at[self.k, piece], {"mp": self.my}),
        )

    def arrived(self, piece):
        return [
            remote(spot, spot, send.at[self.k, piece], recv.at[self.k, piece], {"mp": peer})
            for spot, send, recv, peer in (
                (self.at(self.mx, self.base + piece, 1, 0, self.first), self.xs, self.xr, self.mx),
                (self.at(self.my, self.base + piece, 1, 0, self.first), self.ys, self.yr, self.my),
            )
        ]

    def halves(self, low, high, piece):
        half = self.first // 2 if self.first % 256 == 0 else self.first
        one = self.at(low, self.base + piece, 1, 0, half)
        copies = [remote(one, one, self.rys.at[self.k, piece], self.ryr.at[self.k, piece], {"mp": self.my})]
        if half < self.first:
            two = self.at(high, self.base + piece, 1, half, half)
            copies.append(
                remote(two, two, self.rxs.at[self.k, piece], self.rxr.at[self.k, piece], {"mp": self.mx})
            )
        return copies

    def relay(self, piece):
        return self.halves(self.mx, self.my, piece)

    def diagonal(self, piece):
        return self.halves(self.mf, self.mf, piece)

    def late_across(self):
        width = self.cols - self.first
        spot = self.at(self.m, self.base + self.d, 1, self.first, width)
        source = self.mine(self.first, width)
        return (
            remote(source, spot, self.bs.at[self.k, 0], self.br.at[self.k, 0], {"mp": self.mx}),
            remote(source, spot, self.bs.at[self.k, 1], self.br.at[self.k, 1], {"mp": self.my}),
        )

    def late_arrived(self):
        width = self.cols - self.first
        spots = [self.at(c, self.base + self.d, 1, self.first, width) for c in (self.mx, self.my)]
        return [
            remote(spot, spot, self.bs.at[self.k, i], self.br.at[self.k, i], {"mp": peer})
            for i, (spot, peer) in enumerate(zip(spots, (self.mx, self.my)))
        ]

    def late_halves(self, low, high):
        half = (self.cols - self.first) // 2
        one = self.at(low, self.base + self.d, 1, self.first, half)
        two = self.at(high, self.base + self.d, 1, self.first + half, half)
        return (
            remote(one, one, self.bs.at[self.k, 2], self.br.at[self.k, 2], {"mp": self.my}),
            remote(two, two, self.bs.at[self.k, 3], self.br.at[self.k, 3], {"mp": self.mx}),
        )

    def late_line(self, piece, way):
        spot = self.at(slice(None), self.base + piece, 1, self.first, self.cols - self.first)
        return remote(
            spot, spot, self.bzs.at[self.k, way, piece], self.bzr.at[self.k, way, piece],
            {"dp": self.d + 1 - 2 * way},
        )

    def core(self, slot, incoming=False):
        base = (1 - self.r) * self.nz if incoming else self.base
        if slot == 4:
            spot = self.at(slice(None), base, self.nz, self.first, self.cols - self.first)
        else:
            column = (self.m, self.mx, self.my, self.mf)[slot]
            spot = self.at(column, base, self.nz, 0, self.first)
        return remote(spot, spot, self.cs.at[self.k, slot], self.cr.at[self.k, slot], {"role": 1 - self.r})

    def copy_own(self):
        return pltpu.make_async_copy(
            self.mine(0, self.cols), self.at(self.m, self.base + self.d, 1, 0, self.cols),
            self.own.at[self.k],
        )

    def start(self):
        d, nz = (self.d, self.nz)

        @pl.when(d < nz - 1)
        def _():
            self.line(d, 0, True).start()

        @pl.when(d > 0)
        def _():
            self.line(d, 1, True).start()

        for copy in self.across(d, True):
            copy.start()
        if self.first < self.cols:
            for copy in self.late_across():
                copy.start()
        self.copy_own().start()

    def pass_on(self, piece):
        for copy in self.arrived(piece):
            copy.wait_recv()
        for copy in self.relay(piece):
            copy.start()

    def step(self, t):
        d, nz = (self.d, self.nz)
        left = d - 1 - t
        right = d + 1 + t

        @pl.when(left >= 0)
        def _():
            self.line(left, 0).wait_recv()

            @pl.when(d < nz - 1)
            def _():
                self.line(left, 0).start()

            for copy in self.across(left):
                copy.start()

        @pl.when(right < nz)
        def _():
            self.line(right, 1).wait_recv()

            @pl.when(d > 0)
            def _():
                self.line(right, 1).start()

            for copy in self.across(right):
                copy.start()

        if t == 0:
            self.pass_on(d)
        else:
            @pl.when(left + 1 >= 0)
            def _():
                self.pass_on(left + 1)

            @pl.when(right - 1 < nz)
            def _():
                self.pass_on(right - 1)

    def late_turn(self):
        for copy in self.late_arrived():
            copy.wait_recv()
        for copy in self.late_halves(self.mx, self.my):
            copy.start()

    def late_start(self):
        for copy in self.late_halves(self.mf, self.mf):
            copy.wait_recv()
        self.copy_own().wait()

        @pl.when(self.d < self.nz - 1)
        def _():
            self.late_line(self.d, 0).start()

        @pl.when(self.d > 0)
        def _():
            self.late_line(self.d, 1).start()

    def late_step(self, t):
        d, nz = (self.d, self.nz)
        left = d - 1 - t
        right = d + 1 + t

        @pl.when(left >= 0)
        def _():
            self.late_line(left, 0).wait_recv()

            @pl.when(d < nz - 1)
            def _():
                self.late_line(left, 0).start()

        @pl.when(right < nz)
        def _():
            self.late_line(right, 1).wait_recv()

            @pl.when(d > 0)
            def _():
                self.late_line(right, 1).start()

    def last_pass(self):
        @pl.when(self.d == self.nz - 1)
        def _():
            self.pass_on(0)

        if self.nz > 1:
            @pl.when(self.d == 0)
            def _():
                self.pass_on(self.nz - 1)

        if self.first == self.cols:
            self.copy_own().wait()
        for slot in range(3):
            self.core(slot).start()

    def take_diagonal(self):
        def take(piece, carry):
            for copy in self.diagonal(piece):
                copy.wait_recv()
            return carry

        lax.fori_loop(0, self.nz, take, 0)
        self.core(3).start()
        if self.first < self.cols:
            self.core(4).start()

    def steps(self):
        late = self.first < self.cols
        early = [functools.partial(self.step, t) for t in range(self.nz - 1)] + [self.last_pass]
        late = []
        if self.first < self.cols:
            late = [self.late_turn, self.late_start]
            late += [functools.partial(self.late_step, t) for t in range(self.nz - 1)]
        todo = []
        while early or late:
            todo += early[:1] + late[:1]
            early, late = (early[1:], late[1:])
        return todo

    def complete(self):
        for slot in range(5 if self.first < self.cols else 4):
            self.core(slot, True).wait_recv()

    def finish(self):
        d, nz = (self.d, self.nz)
        late = self.first < self.cols
        for slot in range(5 if late else 4):
            self.core(slot).wait_send()
        if late:
            for copy in self.late_across() + self.late_halves(self.mx, self.my):
                copy.wait_send()

        def done(piece, carry):
            for copy in self.across(piece):
                copy.wait_send()
            for copy in self.relay(piece):
                copy.wait_send()

            @pl.when(jnp.logical_and(piece <= d, d < nz - 1))
            def _():
                self.line(piece, 0).wait_send()
                if late:
                    self.late_line(piece, 0).wait_send()

            @pl.when(jnp.logical_and(piece >= d, d > 0))
            def _():
                self.line(piece, 1).wait_send()
                if late:
                    self.late_line(piece, 1).wait_send()

            return carry

        lax.fori_loop(0, nz, done, 0)


def gather_sems(count, nz):
    dma = pltpu.SemaphoreType.DMA
    piece = [dma((count, nz))] * 8
    return (
        [dma((count, 2, nz))] * 2 + piece + [dma((count, 4))] * 2 + [dma((count, 2, nz))] * 2
        + [dma((count, 5))] * 2 + [dma((count,))]
    )


def reduce_kernel(nz, chunks, ring, count, stats_in, *refs):
    n = len(chunks)
    ins = refs[:count]
    outs = refs[count : 2 * count]
    stats_out = refs[2 * count]
    rest = refs[2 * count + 1 :]
    accs = rest[:n]
    sends1 = rest[n : 2 * n]
    recvs1 = rest[2 * n : 3 * n]
    sends2 = rest[3 * n : 4 * n]
    recvs2 = rest[4 * n : 5 * n]
    lines = rest[5 * n : 6 * n]
    rest = rest[6 * n :]
    kinds = sorted(set(ring))
    buffers = {kind: rest[3 * i : 3 * i + 3] for i, kind in enumerate(kinds)}
    (near, near_in, far_in, ld, cs, cr, s1s, s1r, s2s, s2r, zs, zr, ns, nr, fs, fr) = rest[
        3 * len(kinds) :
    ]
    turns = [ring[:k].count(kind) for k, kind in enumerate(ring)]
    r = lax.axis_index("role")
    d = lax.axis_index("dp")
    m = lax.axis_index("mp")
    groups = 4
    mx = shift_of(m, 1)
    my = shift_of(m, 2)
    mf = shift_of(m, 3)
    columns = (mf, mx, my, m)
    group = [
        {"role": role, "mp": shift_of(m, by)}
        for role in (r, 1 - r)
        for by in range(groups)
    ][1:]
    far = [{"dp": lax.rem(d + j, nz)} for j in range(1, nz)]
    greet(group + far)

    def part(k, column, first):
        array, start, width = chunks[k]
        return ins[array].at[column, pl.ds(first, nz), :, pl.ds(start, width)]

    def core(k, j):
        return remote(
            part(k, columns[j], (1 - r) * nz), accs[k].at[j], cs.at[k, j], cr.at[k, j],
            {"role": 1 - r},
        )

    def loaded(k, j):
        far_ring, near_ring, own_ring = buffers[ring[k]]
        if j == 0:
            return far_ring.at[turns[k] % 3]
        if j == 3:
            return own_ring.at[turns[k] % 2]
        return near_ring.at[turns[k] % 2, j - 1]

    def load(k, j):
        return pltpu.make_async_copy(part(k, columns[j], r * nz), loaded(k, j), ld.at[k, j])

    def first(k, piece):
        half = chunks[k][2] // 2
        low, high = (pl.ds(0, half), pl.ds(half, half))
        return (
            remote(sends1[k].at[piece, :, low], recvs1[k].at[piece, :, low],
                   s1s.at[k, 0, piece], s1r.at[k, 0, piece], {"mp": my}),
            remote(sends1[k].at[piece, :, high], recvs1[k].at[piece, :, high],
                   s1s.at[k, 1, piece], s1r.at[k, 1, piece], {"mp": mx}),
        )

    def second(k, piece):
        return (
            remote(sends2[k].at[0, piece], recvs2[k].at[0, piece],
                   s2s.at[k, 0, piece], s2r.at[k, 0, piece], {"mp": mx}),
            remote(sends2[k].at[1, piece], recvs2[k].at[1, piece],
                   s2s.at[k, 1, piece], s2r.at[k, 1, piece], {"mp": my}),
        )

    def right(k, piece):
        return remote(accs[k].at[3, piece], lines[k].at[piece], zs.at[k, piece],
                      zr.at[k, piece], {"dp": d + 1})

    def left(k, piece):
        slot = jnp.where(piece == d - 1, nz, piece)
        return remote(accs[k].at[3, piece], lines[k].at[slot], zs.at[k, piece],
                      zr.at[k, slot], {"dp": d - 1})

    def line_in(k, slot):
        return remote(lines[k].at[slot], lines[k].at[slot], zs.at[k, 0], zr.at[k, slot],
                      {"role": 1 - r})

    def each(body):
        def step(t, carry):
            off = nz - 1 - t

            @pl.when(d + off < nz)
            def _():
                body(d + off)

            @pl.when(d - off >= 0)
            def _():
                body(d - off)

            return carry

        lax.fori_loop(0, nz - 1, step, 0)
        body(d)

    def fetch(k):
        for j in range(groups):
            core(k, j).start()
        load(k, 0).start()

    def combine(k, j):
        core(k, j).wait_recv()
        load(k, j).wait()

    def to_far(k):
        load(k, 1).start()
        load(k, 2).start()
        combine(k, 0)

        def send_far(piece):
            sends1[k][piece] = (accs[k][0, piece] + loaded(k, 0)[piece]).astype(sends1[k].dtype)
            for copy in first(k, piece):
                copy.start()

        each(send_far)

    def to_near(k):
        half = chunks[k][2] // 2
        load(k, 3).start()
        combine(k, 1)
        combine(k, 2)

        def send_near(piece):
            for copy in first(k, piece):
                copy.wait_recv()
            relayed = recvs1[k][piece].astype(jnp.float32)
            lane = lax.broadcasted_iota(jnp.int32, relayed.shape, 1)
            sends2[k][0, piece] = (
                accs[k][1, piece] + loaded(k, 1)[piece] + jnp.where(lane < half, relayed, 0.0)
            ).astype(sends2[k].dtype)
            sends2[k][1, piece] = (
                accs[k][2, piece] + loaded(k, 2)[piece] + jnp.where(lane < half, 0.0, relayed)
            ).astype(sends2[k].dtype)
            for copy in second(k, piece):
                copy.start()

        each(send_near)

    def to_line(k):
        combine(k, 3)

        def pass_on(piece):
            for copy in second(k, piece):
                copy.wait_recv()
            accs[k][3, piece] += (
                loaded(k, 3)[piece]
                + recvs2[k][0, piece].astype(jnp.float32)
                + recvs2[k][1, piece].astype(jnp.float32)
            )

            @pl.when(piece > d)
            def _():
                @pl.when(d > 0)
                def _():
                    line_in(k, piece).wait_recv()
                    accs[k][3, piece] += lines[k][piece]

                right(k, piece).start()

            @pl.when(piece < d)
            def _():
                @pl.when(d < nz - 1)
                def _():
                    line_in(k, piece).wait_recv()
                    accs[k][3, piece] += lines[k][piece]

                left(k, piece).start()

        each(pass_on)

    def land(k):
        array, start, width = chunks[k]

        @pl.when(d > 0)
        def _():
            line_in(k, d).wait_recv()
            accs[k][3, d] += lines[k][d]

        @pl.when(d < nz - 1)
        def _():
            line_in(k, nz).wait_recv()
            accs[k][3, d] += lines[k][nz]

        total = accs[k][3, d]
        outs[array][:, start : start + width] = total
        return jnp.sum(total * total, keepdims=True)

    ahead = 2
    for k in range(min(ahead, n)):
        fetch(k)
    squares = jnp.zeros((1, 1), jnp.float32)
    for step in range(n + 3):
        if step + ahead < n:
            fetch(step + ahead)
        if step < n:
            to_far(step)
        if 0 <= step - 1 < n:
            to_near(step - 1)
        if 0 <= step - 2 < n:
            to_line(step - 2)
        if 0 <= step - 3 < n:
            squares += land(step - 3)

    mine = r * groups + m
    row = lax.broadcasted_iota(jnp.int32, (8, 128), 0)
    near[...] = jnp.where(row == 0, stats_in[...], squares)
    near_in[mine] = near[...]
    copies = []
    for j, peer in enumerate(group):
        copies.append(remote(near, near_in.at[mine], ns.at[j], nr.at[mine], peer))
        copies[-1].start()
    for j, peer in enumerate(group):
        slot = peer["role"] * groups + peer["mp"]
        remote(near, near_in.at[slot], ns.at[j], nr.at[slot], peer).wait_recv()
    for copy in copies:
        copy.wait_send()
    summed = near_in[0]
    for j in range(1, 2 * groups):
        summed += near_in[j]
    near[...] = summed
    far_in[d] = summed
    copies = []
    for j, peer in enumerate(far):
        copies.append(remote(near, far_in.at[d], fs.at[j], fr.at[d], peer))
        copies[-1].start()
    for j, peer in enumerate(far):
        slot = peer["dp"]
        remote(near, far_in.at[slot], fs.at[j], fr.at[slot], peer).wait_recv()
    for copy in copies:
        copy.wait_send()
    summed = far_in[0]
    for j in range(1, nz):
        summed += far_in[j]
    stats_out[...] = summed

    for k in range(n):
        for j in range(groups):
            core(k, j).wait_send()

        def done(piece, carry):
            for copy in first(k, piece):
                copy.wait_send()
            for copy in second(k, piece):
                copy.wait_send()

            @pl.when(piece != d)
            def _():
                right(k, piece).wait_send()

            return carry

        lax.fori_loop(0, nz, done, 0)


def reduce_all(grads, wire_types, chunks, stats):
    nz = lax.axis_size("dp")
    groups = lax.axis_size("mp")
    count = len(grads)
    n = len(chunks)
    dma = pltpu.SemaphoreType.DMA
    shapes = [(grads[array].shape[2], width) for array, _, width in chunks]
    kinds = sorted(set(shapes))
    ring = tuple(kinds.index(s) for s in shapes)
    wires = [wire_types[array] for array, _, _ in chunks]
    vmem = pl.BlockSpec(memory_space=pltpu.VMEM)
    scratch = (
        [pltpu.VMEM((groups, nz, *s), jnp.float32) for s in shapes]
        + [pltpu.VMEM((nz, *s), t) for s, t in zip(shapes, wires)] * 2
        + [pltpu.VMEM((2, nz, *s), t) for s, t in zip(shapes, wires)] * 2
        + [pltpu.VMEM((nz + 1, *s), jnp.float32) for s in shapes]
        + [
            pltpu.VMEM((*slots, nz, *kinds[kind]), jnp.float32)
            for kind in range(len(kinds))
            for slots in ((min(3, ring.count(kind)),), (min(2, ring.count(kind)), 2), (min(2, ring.count(kind)),))
        ]
        + [
            pltpu.VMEM((8, 128), jnp.float32),
            pltpu.VMEM((2 * groups, 8, 128), jnp.float32),
            pltpu.VMEM((nz, 8, 128), jnp.float32),
            dma((n, groups)),
            dma((n, groups)),
            dma((n, groups)),
            dma((n, 2, nz)),
            dma((n, 2, nz)),
            dma((n, 2, nz)),
            dma((n, 2, nz)),
            dma((n, nz)),
            dma((n, nz + 1)),
            dma((2 * groups,)),
            dma((2 * groups,)),
            dma((nz,)),
            dma((nz,)),
        ]
    )
    return pl.pallas_call(
        functools.partial(reduce_kernel, nz, chunks, ring, count),
        out_shape=[jax.ShapeDtypeStruct(g.shape[2:], jnp.float32) for g in grads]
        + [jax.ShapeDtypeStruct((8, 128), jnp.float32)],
        in_specs=[vmem] + [pl.BlockSpec(memory_space=pl.ANY)] * count,
        out_specs=[vmem] * (count + 1),
        scratch_shapes=scratch,
        compiler_params=pltpu.CompilerParams(
            collective_id=2, has_side_effects=True, vmem_limit_bytes=59 * 2**20
        ),
    )(stats, *grads)


def dot(left, right):
    return lax.dot_general(left, right, (((1,), (0,)), ((), ())), preferred_element_type=F32)


def dot_rt(left, right):
    return lax.dot_general(left, right, (((1,), (1,)), ((), ())), preferred_element_type=F32)


def dot_lt(left, right):
    return lax.dot_general(left, right, (((0,), (0,)), ((), ())), preferred_element_type=F32)


def chain(term, count):
    total = term(0)
    for g in range(1, count):
        total += term(g)
    return total


def head_lanes(lanes, size, head):
    lane = lax.broadcasted_iota(jnp.int32, (1, lanes), 1)
    return jnp.logical_and(lane >= head * size, lane < (head + 1) * size)


def only(mask, value):
    return jnp.where(mask, value, jnp.zeros_like(value))


def turn(value, by):
    return pltpu.roll(value, by % value.shape[1], 1)


def stats_of(stream):
    mean = jnp.mean(stream, -1, keepdims=True)
    cent = stream - mean
    scale = lax.rsqrt(jnp.mean(cent * cent, -1, keepdims=True) + 1e-06)
    return (cent * scale, scale)


def norm_back_of(normed, scale, gain, grad):
    gain_grad = jnp.sum(grad * normed, 0, keepdims=True)
    scaled = grad * gain
    inner = (
        scaled
        - jnp.mean(scaled, -1, keepdims=True)
        - normed * jnp.mean(scaled * normed, -1, keepdims=True)
    )
    return (scale * inner, gain_grad)


def normal_cdf(hidden):
    return 0.5 * (1.0 + lax.erf(hidden * ROOT_HALF))


def encoder_forward(sizes, asked, pix, place, bias, bank, gains, keep_refs, finish):
    local, hidden, size = sizes
    groups = bank.shape[0]
    heads = local // size
    up = 4 * local
    down = up + hidden
    emb = down + hidden
    wide = local + 64
    saving = keep_refs is not None
    if saving:
        (norm1, scale1, mixer_in, qs, ks, vs, probs_out, mixed_out, norm2, scale2, dense, slope,
         active) = keep_refs
    terms = None
    for g in range(groups):
        term = dot_rt(pix[g], bank[g, :, emb : emb + wide])
        terms = term if terms is None else terms + term
    start = place() + terms
    normed, scale = stats_of(start)
    a = (normed * gains[0]).astype(BF)
    if saving:
        norm1[...] = normed
        scale1[...] = scale
        mixer_in[...] = a
    yield
    terms = None
    for g in range(groups):
        t = dot(a, bank[g, :, : 3 * local + 64]).astype(BF).astype(F32)
        q = t[:asked, :wide].astype(BF)
        k = turn(t, -local)[:, :wide].astype(BF)
        v = t[:, 2 * local :].astype(BF)
        if saving:
            qs[g] = q
            ks[g] = k
            vs[g] = v
        mixed = jnp.zeros((asked, wide), F32)
        for h in range(heads):
            mask = head_lanes(wide, size, h)
            score = dot_rt(only(mask, q), k) * size**-0.5 + bias[...]
            score = jnp.exp(score - jnp.max(score, -1, keepdims=True))
            probs = score * (1.0 / jnp.sum(score, -1, keepdims=True))
            if saving:
                probs_out[g * heads + h] = probs
            mixed += only(mask, dot(probs.astype(BF), v))
        mixed = turn(mixed, 64).astype(BF)
        if saving:
            mixed_out[g] = mixed
        term = dot_rt(mixed, bank[g, :, up - wide : up])
        terms = term if terms is None else terms + term
        yield
    middle = start[:asked] + terms
    normed, scale = stats_of(middle)
    b = (normed * gains[1]).astype(BF)
    if saving:
        norm2[...] = normed
        scale2[...] = scale
        dense[...] = b
    terms = None
    for g in range(groups):
        pre = dot(b, bank[g, :, up:down])
        cdf = normal_cdf(pre)
        act = (pre * cdf).astype(BF)
        if saving:
            slope[g] = cdf + pre * jnp.exp(-0.5 * pre * pre) * INVERSE_ROOT
            active[g] = act
        term = dot_rt(act, bank[g, :, down:emb])
        terms = term if terms is None else terms + term
        yield
    finish(middle + terms)


def front_kernel(nz, sizes, asked, firsts, *refs):
    local, hidden, size = sizes
    wide = local + 64
    sources, refs = (refs[:4], refs[4:])
    (half, tables, shuffle, bias_t, bias_s, hot), refs = (refs[:6], refs[6:])
    (bank_out, pbank_out, context, wanted, pix_s, vec_rows, total), refs = (refs[:7], refs[7:])
    keep_refs, refs = (refs[:13], refs[13:])
    (vec_all, tbank, bank, pix_t, px, pr, own_sem, out_sem), sems = (refs[:8], refs[8:])
    r = lax.axis_index("role")
    d = lax.axis_index("dp")
    m = lax.axis_index("mp")
    groups = tbank.shape[0]
    width = tbank.shape[1]
    nears = [{"mp": shift_of(m, by)} for by in range(1, groups)]
    greet([{"role": 1 - r}] + nears + [{"dp": lax.rem(d + j, nz)} for j in range(1, nz)])
    targets = (vec_all, tbank, bank, pbank_out)
    arrays = [
        Gather(k, sources[k], targets[k], sources[k].shape[-2], sources[k].shape[-1], firsts[k],
               sems, (r, d, m), nz)
        for k in range(4)
    ]
    small, teach, learn, guess = arrays

    def pixel(j):
        peer = shift_of(m, j)
        return remote(half.at[peer], pix_t.at[m], px.at[j], pr.at[j], {"mp": peer})

    def pixel_in(j):
        peer = shift_of(m, j)
        return remote(half.at[peer], pix_t.at[peer], px.at[j], pr.at[j], {"mp": peer})

    own_pixel = pltpu.make_async_copy(half.at[m], pix_t.at[m], own_sem.at[0])
    own_pixel.start()
    small.start()
    for j in range(1, groups):
        pixel(j).start()
    teach.start()
    for step in small.steps():
        step()

    def place():
        rows = tables[...].astype(F32)
        return rows[:, :width] + rows[:, width : 2 * width] + rows[:, 2 * width :]

    def place_shuffled():
        rows = dot(shuffle[...], tables[...])
        return rows[:, :width] + rows[:, width : 2 * width] + rows[:, 2 * width :]

    for j, step in enumerate(teach.steps()):
        if j == 3:
            learn.start()
        step()
        if j == 1:
            small.take_diagonal()
    small.complete()

    share = vec_rows.shape[1] * 4 // (vec_all.shape[0] * vec_all.shape[1])
    lanes = vec_all.shape[3]
    lane = lax.broadcasted_iota(jnp.int32, (1, lanes), 1)

    def vector_row(kind, j):
        row = jnp.zeros((1, width), F32)
        count = width // share
        for c in range(count):
            flat = j * count + c
            piece = vec_all[flat % groups, flat // groups].astype(F32)[kind : kind + 1]
            piece = only(lane < share, piece)
            row += turn(jnp.concatenate([piece, jnp.zeros((1, width - lanes), F32)], 1), c * share)
        return row

    gains_t = [vector_row(1, j) for j in range(2)]
    rows_s = [vector_row(0, j) for j in range(4)]
    vec_rows[...] = jnp.concatenate(rows_s, 0)
    counts = jnp.zeros((1, 1), F32)
    for c in range(groups):
        for o in range(vec_all.shape[1]):
            counts += vec_all[c, o].astype(F32)[2:3, :1]
    total[...] = jnp.broadcast_to(counts, total.shape)
    own_pixel.wait()
    for j in range(1, groups):
        pixel_in(j).wait_recv()
    for g in range(groups):
        pix_s[g] = dot(shuffle[...], pix_t[g]).astype(BF)

    def teacher_rows(latent):
        chosen = dot(hot[...], stats_of(latent)[0].astype(BF))
        for g in range(groups):
            wanted[g] = turn(chosen, -g * local)[:, :wide].astype(BF)

    def student_rows(latent):
        at = lax.broadcasted_iota(jnp.int32, (1, wide), 1)
        for g in range(groups):
            context[g] = only(at >= 64, turn(latent, 64 - g * local)[:, :wide]).astype(BF)

    teacher = encoder_forward(
        sizes, pix_t.shape[1], pix_t, place, bias_t, tbank, gains_t, None, teacher_rows
    )
    student = encoder_forward(
        sizes, asked, pix_s, place_shuffled, bias_s, bank, rows_s[:2], keep_refs, student_rows
    )

    def advance(work, parts):
        for _ in range(parts):
            next(work, None)

    def bank_copy(g):
        return pltpu.make_async_copy(bank.at[g], bank_out.at[g], out_sem.at[g])

    steps = learn.steps()
    for j, step in enumerate(steps):
        if j == 3:
            guess.start()
        step()
        if j == 1:
            teach.take_diagonal()
        if j == 3:
            teach.complete()
        if j > 3:
            advance(teacher, 2)
    for j, step in enumerate(guess.steps()):
        step()
        if j == 1:
            learn.take_diagonal()
            advance(teacher, 100)
            learn.complete()
            for g in range(groups):
                bank_copy(g).start()
        if j > 1:
            advance(student, 1)
    guess.take_diagonal()
    advance(student, 100)
    for g in range(groups):
        bank_copy(g).wait()
    guess.complete()
    for j in range(1, groups):
        pixel(j).wait_send()
    for array in arrays:
        array.finish()


def run_front(packs, half, tables, shuffle, keep_t, keep_s, hot, sizes, asked):
    local, hidden, size = sizes
    nz = lax.axis_size("dp")
    groups = lax.axis_size("mp")
    owners = lax.axis_size("role") * nz
    vec, target, master, predictor = packs
    rows = half.shape[1]
    width = target.shape[0] * owners
    columns = target.shape[1]
    wide = local + 64
    make = jax.ShapeDtypeStruct
    hbm = pl.BlockSpec(memory_space=pl.ANY)
    vmem = pl.BlockSpec(memory_space=pltpu.VMEM)
    dma = pltpu.SemaphoreType.DMA
    bank = make((groups, width, columns), BF)
    outs = [
        bank,
        make((groups, owners, *predictor.shape[1:]), BF),
        make((groups, asked, wide), BF),
        make((groups, hot.shape[0], wide), BF),
        make((groups, rows, wide), BF),
        make((4, width), F32),
        make((8, 128), F32),
        make((rows, width), F32),
        make((rows, 1), F32),
        make((rows, width), BF),
        make((groups, asked, wide), BF),
        make((groups, rows, wide), BF),
        make((groups, rows, wide), BF),
        make((HEADS, asked, rows), F32),
        make((groups, asked, wide), BF),
        make((asked, width), F32),
        make((asked, 1), F32),
        make((asked, width), BF),
        make((groups, asked, hidden), F32),
        make((groups, asked, hidden), BF),
    ]

    def first(cols):
        return cols - (cols // 5 // 256) * 256

    firsts = (vec.shape[2], first(columns), first(columns), first(predictor.shape[2]))
    bias_t, bias_s = (((keep - 1.0) * 1e9)[None, :] for keep in (keep_t, keep_s))
    return pl.pallas_call(
        functools.partial(front_kernel, nz, sizes, asked, firsts),
        out_shape=outs,
        in_specs=[hbm] * 5 + [vmem] * 5,
        out_specs=[hbm] * 2 + [vmem] * (len(outs) - 2),
        scratch_shapes=[
            pltpu.VMEM((groups, owners, *vec.shape[1:]), BF),
            pltpu.VMEM(bank.shape, BF),
            pltpu.VMEM(bank.shape, BF),
            pltpu.VMEM((groups, rows, wide), BF),
            dma((groups,)),
            dma((groups,)),
            dma((1,)),
            dma((groups,)),
        ]
        + gather_sems(4, nz),
        compiler_params=pltpu.CompilerParams(
            collective_id=1, has_side_effects=True, vmem_limit_bytes=50 * 2**20
        ),
    )(vec, target, master, predictor, half, tables, shuffle, bias_t, bias_s, hot)


def predictor_kernel(
    sizes, ctx, wanted, tables, shuffle, hot, keep, weight, total, bank, vec_rows,
    grad_ctx, grads, small, loss_out, probs_s, q_s, k_s, v_s, mixed_s, slope_s, active_s, dt_s
):
    local, plocal, phidden, size, blocks = sizes
    groups = bank.shape[0]
    heads = plocal // size
    lanes = 128
    up = 4 * plocal
    down = up + phidden
    head_at = down + phidden
    entry_at = head_at + local
    wide = local + 64
    nctx = ctx.shape[1]
    asked = hot.shape[0]
    rows = nctx + asked
    tlen = asked // blocks
    pwidth = groups * plocal
    first, second, final, token = (
        vec_rows[i : i + 1, j : j + pwidth] for i in (2, 3) for j in (0, pwidth)
    )
    root = size**-0.5
    key = lax.broadcasted_iota(jnp.int32, (asked, rows), 1) - nctx
    query = lax.broadcasted_iota(jnp.int32, (asked, rows), 0)
    reached = jnp.logical_or(key < 0, key // tlen == query // tlen)
    bias = (only(reached, jnp.broadcast_to(keep[...], (asked, rows))) - 1.0) * 1e9

    def places(chosen):
        found = dot(chosen, tables[...])
        return found[:, :pwidth] + found[:, pwidth : 2 * pwidth] + found[:, 2 * pwidth :]


    entry = places(shuffle[:nctx]) + chain(
        lambda g: dot_rt(ctx[g], bank[g, :, entry_at - 64 : entry_at + local]), groups
    )
    tgt_in = places(hot[...]) + token
    norm_c, scale_c = stats_of(entry)
    norm_t, scale_t = stats_of(tgt_in)
    a_c = (norm_c * first).astype(BF)
    a_t = (norm_t * first).astype(BF)
    a = jnp.concatenate([a_c, a_t], 0)

    def attend(g):
        t = dot(a, bank[g, :, :up]).astype(BF).astype(F32)
        q = t[nctx:, :lanes].astype(BF)
        k = turn(t, -plocal)[:, :lanes].astype(BF)
        v = turn(t, -2 * plocal)[:, :lanes].astype(BF)
        q_s[g] = q
        k_s[g] = k
        v_s[g] = v
        mixed = jnp.zeros((asked, lanes), F32)
        for h in range(heads):
            mask = head_lanes(lanes, size, h)
            score = dot_rt(only(mask, q), k) * root + bias
            score = jnp.exp(score - jnp.max(score, -1, keepdims=True))
            probs = score * (1.0 / jnp.sum(score, -1, keepdims=True))
            probs_s[g * heads + h] = probs
            mixed += only(mask, dot(probs.astype(BF), v))
        mixed = turn(mixed, lanes - plocal).astype(BF)
        mixed_s[g] = mixed
        return dot_rt(mixed, bank[g, :, up - lanes : up])

    middle = tgt_in + chain(attend, groups)
    norm2, scale2 = stats_of(middle)
    b = (norm2 * second).astype(BF)

    def feed(g):
        pre = dot(b, bank[g, :, up:down])
        cdf = normal_cdf(pre)
        slope_s[g] = cdf + pre * jnp.exp(-0.5 * pre * pre) * INVERSE_ROOT
        act = (pre * cdf).astype(BF)
        active_s[g] = act
        return dot_rt(act, bank[g, :, down:head_at])

    out = middle + chain(feed, groups)
    norm_f, scale_f = stats_of(out)
    head_in = (norm_f * final).astype(BF)
    lane = lax.broadcasted_iota(jnp.int32, (1, wide), 1)
    losses = jnp.zeros((1, 1), F32)
    row_weight = weight[...]

    def judge(g):
        nonlocal losses
        pred = dot(head_in, bank[g, :, head_at : head_at + wide])
        diff = only(lane < local, pred - wanted[g].astype(F32))
        losses += jnp.sum(row_weight * diff * diff, keepdims=True)
        grad = (diff * (2.0 * row_weight / total[0:1, 0:1])).astype(BF)
        g_head = dot_lt(head_in, grad)
        grads[g, :, head_at : head_at + lanes] = g_head[:, :lanes]
        grads[g, :, head_at + lanes : head_at + wide] = g_head[:, lanes:]
        return dot_rt(grad, bank[g, :, head_at : head_at + wide])

    grad_out, g_final = norm_back_of(norm_f, scale_f, final, chain(judge, groups))
    loss_out[...] = jnp.broadcast_to(losses, loss_out.shape)

    branch = grad_out.astype(BF)

    def feed_back(g):
        grads[g, :, down:head_at] = dot_lt(branch, active_s[g])
        grad_pre = (dot(branch, bank[g, :, down:head_at]) * slope_s[g]).astype(BF)
        grads[g, :, up:down] = dot_lt(b, grad_pre)
        return dot_rt(grad_pre, bank[g, :, up:down])

    grad_norm, g_second = norm_back_of(norm2, scale2, second, chain(feed_back, groups))
    grad_mid = grad_out + grad_norm
    mixer = grad_mid.astype(BF)

    def attend_back(g):
        g_o = dot_lt(mixer, mixed_s[g])
        gm = turn(dot(mixer, bank[g, :, up - lanes : up]), plocal - lanes).astype(BF)
        q, k, v = (q_s[g], k_s[g], v_s[g])
        valid = head_lanes(lanes, plocal, 0)
        gm = only(valid, gm)
        qv = only(valid, q)
        block = lax.broadcasted_iota(jnp.int32, (asked, 1), 0) // tlen
        q_spread = jnp.concatenate([only(block == i, qv) for i in range(blocks)], 1)
        gm_spread = jnp.concatenate([only(block == i, gm) for i in range(blocks)], 1)
        dqs, dkt, dvt, dkc, dvc = ([], [], [], [], [])
        for h in range(heads):
            mask = head_lanes(lanes, size, h)
            masks = jnp.concatenate([mask] * blocks, 1)
            probs = probs_s[g * heads + h]
            gmh = only(mask, gm)
            grad_probs = dot_rt(gmh, v)
            ds = (probs * (grad_probs - jnp.sum(grad_probs * probs, -1, keepdims=True))).astype(BF)
            pb = probs.astype(BF)
            qh = only(mask, qv)
            dqs.append(dot(ds, only(mask, k)))
            dkt.append(dot_lt(ds[:, nctx:], qh))
            dvt.append(dot_lt(pb[:, nctx:], gmh))
            dkc.append(dot_lt(ds[:, :nctx], only(masks, q_spread)))
            dvc.append(dot_lt(pb[:, :nctx], only(masks, gm_spread)))
        dq = (sum(dqs[1:], dqs[0]) * root).astype(BF).astype(F32)
        dk = (sum(dkt[1:], dkt[0]) * root).astype(BF).astype(F32)
        dv = sum(dvt[1:], dvt[0]).astype(BF).astype(F32)
        kc = (sum(dkc[1:], dkc[0]) * root).astype(BF).astype(F32)
        vc = sum(dvc[1:], dvc[0]).astype(BF).astype(F32)
        kc = chain(lambda i: kc[:, i * lanes : (i + 1) * lanes], blocks)
        vc = chain(lambda i: vc[:, i * lanes : (i + 1) * lanes], blocks)

        def lay(query, keyed, valued):
            count = keyed.shape[0]
            blank = jnp.zeros((count, up - lanes), F32)
            wideq = 0.0 if query is None else jnp.concatenate([query, blank], 1)
            return (
                wideq
                + turn(jnp.concatenate([keyed, blank], 1), plocal)
                + turn(jnp.concatenate([valued, blank], 1), 2 * plocal)
            )

        dt_t = lay(dq, dk, dv).astype(BF)
        dt_c = lay(None, kc, vc)
        high = dt_c.astype(BF)
        low = (dt_c - high.astype(F32)).astype(BF)
        dt = jnp.concatenate([high, dt_t], 0)
        dt_s[g] = jnp.concatenate([dt, low], 0)
        g_qkv = dot_lt(jnp.concatenate([a, a_c], 0), jnp.concatenate([dt, low], 0))
        grads[g, :, : up - lanes] = g_qkv[:, : up - lanes]
        grads[g, :, up - lanes : up] = g_qkv[:, up - lanes :] + g_o

    for g in range(groups):
        attend_back(g)
    grad_a = chain(lambda g: dot_rt(dt_s[g], bank[g, :, :up]), groups)
    grad_in_t, g_first_t = norm_back_of(norm_t, scale_t, first, grad_a[nctx:rows])
    grad_in_c, g_first_c = norm_back_of(
        norm_c, scale_c, first, grad_a[:nctx] + grad_a[rows:]
    )
    g_token = jnp.sum(grad_in_t + grad_mid, 0, keepdims=True)
    small[...] = jnp.concatenate([g_first_t + g_first_c, g_second, g_final, g_token], 0)
    grad_entry = grad_in_c.astype(BF)
    width = groups * local
    grad_context = jnp.zeros((nctx, width), F32)
    for g in range(groups):
        g_entry = dot_lt(grad_entry, ctx[g])
        grads[g, :, entry_at - 64 : entry_at + 64] += g_entry[:, :lanes]
        grads[g, :, entry_at + 64 : entry_at + local] = g_entry[:, lanes:]
        part = only(lane >= 64, dot(grad_entry, bank[g, :, entry_at - 64 : entry_at + local]))
        full = jnp.concatenate([part, jnp.zeros((nctx, width - wide), F32)], 1)
        grad_context += turn(full, g * local - 64)
    grad_ctx[...] = grad_context


def run_predictor(ctx, wanted, tables, shuffle, hot, keep, weight, total, bank, vec_rows, sizes):
    local, plocal, phidden, size, blocks = sizes
    groups = bank.shape[0]
    nctx = ctx.shape[1]
    pwidth = groups * plocal
    asked = hot.shape[0]
    rows = nctx + asked
    make = jax.ShapeDtypeStruct
    outs = [
        make((nctx, groups * local), F32),
        make(bank.shape, F32),
        make((4, pwidth), F32),
        make((8, 128), F32),
    ]
    ins = [ctx, wanted, tables, shuffle, hot, keep, weight, total, bank, vec_rows]
    vmem = pl.BlockSpec(memory_space=pltpu.VMEM)
    scratch = [
        pltpu.VMEM((HEADS, asked, rows), F32),
        pltpu.VMEM((groups, asked, 128), BF),
        pltpu.VMEM((groups, rows, 128), BF),
        pltpu.VMEM((groups, rows, 128), BF),
        pltpu.VMEM((groups, asked, 128), BF),
        pltpu.VMEM((groups, asked, phidden), F32),
        pltpu.VMEM((groups, asked, phidden), BF),
        pltpu.VMEM((groups, rows + nctx, 4 * plocal), BF),
    ]
    return pl.pallas_call(
        functools.partial(predictor_kernel, sizes),
        out_shape=outs,
        in_specs=[vmem] * len(ins),
        out_specs=[vmem] * len(outs),
        scratch_shapes=scratch,
        compiler_params=pltpu.CompilerParams(vmem_limit_bytes=48 * 2**20),
    )(*ins)


def encoder_back_kernel(
    sizes, grad_ctx, pix, norm1, scale1, mixer_in, qs, ks, vs, probs_in, mixed_in, norm2, scale2,
    dense, slope, active, bank, gains, grads, small, wide_s, tail_s, dt_s, sems
):
    local, hidden, size = sizes
    groups = bank.shape[0]
    heads = local // size
    up = 4 * local
    down = up + hidden
    emb = down + hidden
    wide = local + 64
    span = 3 * local + 64
    asked = grad_ctx.shape[0]
    rows = norm1.shape[0]
    first, second = (gains[0:1], gains[1:2])
    root = size**-0.5
    grad_out = grad_ctx[...]
    branch = grad_out.astype(BF)

    def ship(g, start, width):
        return pltpu.make_async_copy(
            wide_s.at[g % 2, :, pl.ds(start, width)],
            grads.at[g, :, pl.ds(start, width)],
            sems.at[g % 2],
        )

    def feed_back(g):
        if g >= 2:
            ship(g - 2, up, 2 * hidden).wait()
        wide_s[g % 2, :, down:emb] = dot_lt(branch, active[g])
        grad_pre = (dot(branch, bank[g, :, down:emb]) * slope[g]).astype(BF)
        wide_s[g % 2, :, up:down] = dot_lt(dense[...], grad_pre)
        ship(g, up, 2 * hidden).start()
        return dot_rt(grad_pre, bank[g, :, up:down])

    grad_norm, g_second = norm_back_of(norm2[...], scale2[...], second, chain(feed_back, groups))
    grad_mid = grad_out + grad_norm
    mixer = grad_mid.astype(BF)
    for g in range(groups - 2, groups):
        ship(g, up, 2 * hidden).wait()
    valid = head_lanes(wide, local, 0)

    def attend_back(g):
        g_o = dot_lt(mixer, mixed_in[g])
        gm = turn(dot(mixer, bank[g, :, up - wide : up]), -64).astype(BF)
        q, k, v = (only(valid, qs[g]), ks[g], vs[g])
        gm = only(valid, gm)
        dqs, dks, dvs = ([], [], [])
        for h in range(heads):
            mask = head_lanes(wide, size, h)
            probs = probs_in[g * heads + h]
            gmh = only(mask, gm)
            grad_probs = dot_rt(gmh, v)
            ds = (probs * (grad_probs - jnp.sum(grad_probs * probs, -1, keepdims=True))).astype(BF)
            dqs.append(dot(ds, only(mask, k)))
            dks.append(dot_lt(ds, only(mask, q)))
            dvs.append(dot_lt(probs.astype(BF), gmh))
        dq = (sum(dqs[1:], dqs[0]) * root).astype(BF).astype(F32)
        dk = (sum(dks[1:], dks[0]) * root).astype(BF).astype(F32)
        dv = sum(dvs[1:], dvs[0]).astype(BF).astype(F32)
        dq = jnp.concatenate([dq, jnp.zeros((rows - asked, wide), F32)], 0)
        blank = jnp.zeros((rows, span - wide), F32)
        dt = (
            jnp.concatenate([dq, blank], 1)
            + turn(jnp.concatenate([dk, blank], 1), local)
            + jnp.concatenate([blank, dv], 1)
        ).astype(BF)
        dt_s[g] = dt
        g_qkv = dot_lt(mixer_in[...], dt)
        if g >= 2:
            ship(g - 2, 0, up).wait()
        slot = wide_s.at[g % 2]
        slot[:, : up - wide] = g_qkv[:, : up - wide]
        slot[:, up - wide : span] = g_qkv[:, up - wide :] + g_o[:, : span - up + wide]
        slot[:, span:up] = g_o[:, span - up + wide :]
        ship(g, 0, up).start()

    for g in range(groups):
        attend_back(g)
    grad_a = chain(lambda g: dot_rt(dt_s[g], bank[g, :, :span]), groups)
    grad_start, g_first = norm_back_of(norm1[...], scale1[...], first, grad_a)
    grad_start = (
        grad_start + jnp.concatenate([grad_mid, jnp.zeros((rows - asked, grad_mid.shape[1]), F32)], 0)
    ).astype(BF)
    small[...] = jnp.concatenate([g_first, g_second], 0)

    def tail(g):
        return pltpu.make_async_copy(
            tail_s.at[g], grads.at[g, :, pl.ds(emb, wide)], sems.at[2 + g]
        )

    for g in range(groups):
        tail_s[g] = dot_lt(grad_start, pix[g])
        tail(g).start()
    for g in range(groups - 2, groups):
        ship(g, 0, up).wait()
    for g in range(groups):
        tail(g).wait()


def run_encoder_back(grad_ctx, pix, saved, bank, gains, sizes):
    local, hidden, size = sizes
    groups, width, columns = bank.shape
    rows = pix.shape[1]
    make = jax.ShapeDtypeStruct
    ins = [grad_ctx, pix, *saved, bank, gains]
    vmem = pl.BlockSpec(memory_space=pltpu.VMEM)
    return pl.pallas_call(
        functools.partial(encoder_back_kernel, sizes),
        out_shape=[make(bank.shape, F32), make((2, width), F32)],
        in_specs=[vmem] * len(ins),
        out_specs=[pl.BlockSpec(memory_space=pl.ANY), vmem],
        scratch_shapes=[
            pltpu.VMEM((2, width, 4 * local + 2 * hidden), F32),
            pltpu.VMEM((groups, width, local + 64), F32),
            pltpu.VMEM((groups, rows, 3 * local + 64), BF),
            pltpu.SemaphoreType.DMA((2 + groups,)),
        ],
        compiler_params=pltpu.CompilerParams(vmem_limit_bytes=58 * 2**20),
    )(*ins)


def update_kernel(sizes, stats, bank, pbank, *refs):
    local, hidden, pixel, plocal, phidden = sizes
    sources, outs, ins, sems = (refs[:14], refs[14:28], refs[28:42], refs[42])
    copies = [
        pltpu.make_async_copy(source, ref, sems.at[i])
        for i, (source, ref) in enumerate(zip(sources, ins))
    ]
    for copy in copies:
        copy.start()
    norm = jnp.sqrt(stats[1:2, 0:1])
    scale = jnp.minimum(1.0, CLIP / (norm + 1e-06))

    def side_by_side(packed, parts):
        whole = packed[...]
        total = sum(width for _, width in parts)
        lane = lax.broadcasted_iota(jnp.int32, (1, whole.shape[1]), 1)
        at, result = (0, whole)
        for first, width in parts:
            moved = turn(whole, at - first) if at != first else whole
            result = jnp.where(lane >= at, moved, result)
            at += width
        return result[:, :total]

    def step(which, grad, target=None):
        for i in (which, 4 + which, 8 + which):
            copies[i].wait()
        weight, first, second = (ins[i][...] for i in (which, 4 + which, 8 + which))
        new, first, second = adamw(weight, grad, first, second, scale, RATE_MATRIX, DECAY)
        for i, value in ((which, new), (4 + which, first), (8 + which, second)):
            outs[i][...] = value
        if target is not None:
            copies[target].wait()
            outs[target][...] = MOMENTUM_EMA * ins[target][...] + (1.0 - MOMENTUM_EMA) * new

    up = 4 * local
    down = up + hidden
    emb = down + hidden
    step(0, side_by_side(bank, ((0, 3 * local), (up, hidden))), 12)
    step(1, side_by_side(bank, ((emb, pixel), (3 * local, local), (down, hidden))), 13)
    up = 4 * plocal
    down = up + phidden
    head = down + phidden
    step(2, side_by_side(pbank, ((0, 3 * plocal), (up, phidden), (head, local))))
    step(3, side_by_side(pbank, ((head + local, local), (3 * plocal, plocal), (down, phidden))))


def run_update(stats, bank, pbank, arrays, sizes):
    vmem = pl.BlockSpec(memory_space=pltpu.VMEM)
    arrays = [a.T if i % 2 else a for i, a in enumerate(arrays)]
    results = pl.pallas_call(
        functools.partial(update_kernel, sizes),
        out_shape=[jax.ShapeDtypeStruct(a.shape, F32) for a in arrays],
        in_specs=[vmem] * 3 + [pl.BlockSpec(memory_space=pl.ANY)] * len(arrays),
        out_specs=[vmem] * len(arrays),
        scratch_shapes=[pltpu.VMEM(a.shape, F32) for a in arrays]
        + [pltpu.SemaphoreType.DMA((len(arrays),))],
        compiler_params=pltpu.CompilerParams(vmem_limit_bytes=60 * 2**20),
    )(stats, bank, pbank, *arrays)
    return [a.T if i % 2 else a for i, a in enumerate(results)]


def per_device(
    pixels,
    context_slots,
    context_count,
    target_slots,
    target_count,
    encoder_in,
    encoder_out,
    predictor_in,
    predictor_out,
    vectors,
    first_encoder_in,
    first_encoder_out,
    first_predictor_in,
    first_predictor_out,
    first_vectors,
    second_encoder_in,
    second_encoder_out,
    second_predictor_in,
    second_predictor_out,
    second_vectors,
    target_encoder_in,
    target_encoder_out,
    target_vectors,
):
    groups = lax.axis_size("mp")
    owners = lax.axis_size("role") * lax.axis_size("dp")
    width = encoder_in.shape[0] * owners
    pwidth = predictor_in.shape[0] * owners
    local, plocal = (width // groups, pwidth // groups)
    pixel = pixels.shape[2]
    hidden = encoder_in.shape[1] - 3 * local
    phidden = predictor_in.shape[1] - 3 * plocal - local
    patches = pixels.shape[1]
    image = lax.axis_index("role") * groups + lax.axis_index("mp")

    slots = lax.dynamic_index_in_dim(context_slots, image, 0, keepdims=False)
    count = lax.dynamic_index_in_dim(context_count, image, 0, keepdims=False)
    tslots = lax.dynamic_index_in_dim(target_slots, image, 0, keepdims=False)
    tcount = lax.dynamic_index_in_dim(target_count, image, 0, keepdims=False)
    nctx = slots.shape[0]
    blocks, tlen = tslots.shape
    rows = -(-patches // 16) * 16
    share = vectors.shape[0]

    patch = jnp.arange(patches)
    hits = slots[:, None] == patch[None, :]
    member = jnp.any(hits, 0)
    order = jnp.where(
        member,
        jnp.sum(jnp.where(hits, jnp.arange(nctx)[:, None], 0), 0),
        nctx + jnp.cumsum(1 - member.astype(jnp.int32)) - 1,
    )
    order = jnp.pad(order, (0, rows - patches), constant_values=-1)
    slot_of = jnp.arange(rows)
    shuffle = (order[None, :] == slot_of[:, None]).astype(BF)
    ckeep = (jnp.arange(nctx) < count).astype(F32)
    tkeep = (jnp.arange(tlen)[None, :] < tcount[:, None]).astype(F32)
    tflat = tslots.reshape(-1)
    keep = jnp.concatenate([ckeep, tkeep.reshape(-1)])[None, :]
    hot = (tflat[:, None] == slot_of[None, :]).astype(BF)

    vec = jnp.stack([vectors, target_vectors, jnp.broadcast_to(jnp.sum(tcount).astype(F32), (share,))])
    vec = jnp.pad(vec, ((0, 13), (0, -share % LANES))).astype(BF)
    half = lax.dynamic_slice_in_dim(pixels, lax.axis_index("role") * groups, groups, 0)
    half = jnp.pad(half, ((0, 0), (0, rows - patches), (0, 64)))
    sizes = (local, hidden, width // HEADS)
    bank, pbank, context, wanted, student_pix, vec_rows, total, *saved = run_front(
        (
            vec[None],
            pack_encoder(target_encoder_in, target_encoder_out, local, pixel),
            pack_encoder(encoder_in, encoder_out, local, pixel),
            pack_predictor(predictor_in, predictor_out, local, plocal, phidden)[None],
        ),
        half,
        np.pad(in_three(sincos(width)), ((0, rows - patches), (0, 0))),
        shuffle,
        (slot_of < patches).astype(F32),
        (slot_of < count).astype(F32),
        hot,
        sizes,
        nctx,
    )
    target_total = total[0, 0]
    grad_context, g_pbank, p_small, loss = run_predictor(
        context,
        wanted,
        np.pad(in_three(sincos(pwidth)), ((0, rows - patches), (0, 0))),
        shuffle,
        hot,
        keep,
        tkeep.reshape(-1, 1),
        total,
        pbank.reshape(groups, pwidth, -1),
        vec_rows,
        (local, plocal, phidden, pwidth // HEADS, blocks),
    )
    g_bank, e_small = run_encoder_back(grad_context, student_pix, saved, bank, vec_rows, sizes)
    g_vec = jnp.concatenate([e_small.reshape(-1), p_small.reshape(-1)])
    g_vec = g_vec.reshape(owners, groups, 1, -1).transpose(1, 0, 2, 3)
    r_bank, r_pbank, r_vec, stats = reduce_all(
        [
            g_bank.reshape(groups, owners, width // owners, -1),
            g_pbank.reshape(pbank.shape),
            jnp.pad(g_vec, ((0, 0), (0, 0), (0, 7), (0, -share % (2 * LANES)))),
        ],
        (BF, BF, F32),
        chunk_list([(1, g_pbank.shape[2], 768), (0, g_bank.shape[2], 512), (2, -(-share // 256) * 256, 256)]),
        loss,
    )
    r_vec = r_vec[0, :share]
    loss_total, squares = (stats[0, 0], stats[1, 0])
    grad_norm = jnp.sqrt(squares)
    scale = jnp.minimum(1.0, CLIP / (grad_norm + 1e-06))
    (
        new_in, new_out, new_pin, new_pout,
        m_in, m_out, m_pin, m_pout,
        v_in, v_out, v_pin, v_pout,
        ema_in, ema_out,
    ) = run_update(
        stats,
        r_bank,
        r_pbank,
        (
            encoder_in, encoder_out, predictor_in, predictor_out,
            first_encoder_in, first_encoder_out, first_predictor_in, first_predictor_out,
            second_encoder_in, second_encoder_out, second_predictor_in, second_predictor_out,
            target_encoder_in, target_encoder_out,
        ),
        (local, hidden, pixel, plocal, phidden),
    )
    new_vec, m_vec, v_vec = adamw(
        vectors, r_vec, first_vectors, second_vectors, scale, RATE_VECTOR, 0.0
    )
    ema_vec = MOMENTUM_EMA * target_vectors + (1.0 - MOMENTUM_EMA) * new_vec
    return (
        new_in, new_out, new_pin, new_pout, new_vec,
        m_in, m_out, m_pin, m_pout, m_vec,
        v_in, v_out, v_pin, v_pout, v_vec,
        ema_in, ema_out, ema_vec,
        loss_total, target_total, grad_norm,
    )


def solution(mesh):
    bank_in, bank_out, small = (
        P(("role", "dp"), "mp"),
        P("mp", ("role", "dp")),
        P(("role", "dp", "mp")),
    )
    five = (bank_in, bank_out, bank_in, bank_out, small)
    three = (bank_in, bank_out, small)
    return jax.shard_map(
        per_device,
        mesh=mesh,
        in_specs=(
            P("dp", None, "mp"),
            P("dp", None),
            P("dp"),
            P("dp", None, None),
            P("dp", None),
        )
        + five * 3
        + three,
        out_specs=five * 3 + three + (P(), P(), P()),
        check_vma=False,
    )
```
